32 devices in a mesh: group: 2 (over x), expert: 16 (over z, y, core).
Axes of the slice: x: 2, y: 2, z: 4, core: 2. Of those that a mesh axis runs over, the one named last changes fastest.
Arguments:
- tokens: bfloat16 [4096, 1024], P(('group', 'expert')), parts along dimension 0, may hold values from -6 to 6
- cotangent: bfloat16 [4096, 1024], P(('group', 'expert')), parts along dimension 0, may hold values from -6 to 6
- routes: int32 [4096, 2], P(('group', 'expert')), parts along dimension 0, may hold values from 0 to 3, all different within a row; in each aligned block of 128 rows (0 to 127, 128 to 255, ...) at most 96 rows name the same one
- gate_nums: int32 [4096, 2], P(('group', 'expert')), parts along dimension 0, may hold values from 1 to 8
- gain: float32 [1024], replicated, may hold values from 0.5 to 1.5
- w_gate: bfloat16 [16, 1024, 1024], P('expert'), may hold values from -0.1875 to 0.1875
- w_up: bfloat16 [16, 1024, 1024], P('expert'), may hold values from -0.1875 to 0.1875
- w_down: bfloat16 [16, 1024, 1024], P('expert'), may hold values from -0.1875 to 0.1875
Outputs:
- mixed: bfloat16 [4096, 1024], P(('group', 'expert')), parts along dimension 0
- grad_down: bfloat16 [32, 1024, 1024], P(('group', 'expert')), parts along dimension 0
The draws below stay inside these ranges and needn't reach their ends.
There are 2 independent parts, one for each index of `group`. The reference program is written for one: setup_inputs(seed, part) draws one part's arguments, and reference() takes and returns one part's arrays. A program takes and returns all parts, laid end to end along the dimension named above; an argument that names none is the same for every part. Nothing has to cross between parts.
Inputs may be any that keep to these rules, and one draw needn't show every extreme that they name: In each aligned block of 128 frames (the frames of one device) no expert is named by more than 96 routes, a bound that some block reaches; a frame names 2 different experts.
All inputs are finite; a program needn't handle non-finite values.
Results may differ from the reference program's by a relative error of at most 0.0072.
Values may be sent and summed in bfloat16 or wider, within the bound.
No kernel may reach another device: no remote copies, remote signals or barrier semaphores. Data moves between devices by JAX's collectives and lax.ppermute only.
A program may use at most 64 MiB of HBM per device.

```python
import math
import jax
import jax.numpy as jnp
import numpy as np
from jax import lax

D = 1024
TOP = 2
HSPLIT = 4
TOK_DEV = 128
FF_DEV = 1024
EXPERTS = 4
CAP = 96
TOKENS = 2048
N_EXPERT = 16


def set_ends(values, rng, least, top_value):
    shape = values.shape
    place = [jax.random.randint(jax.random.fold_in(rng, axis), (), 0, shape[axis]) for axis in range(len(shape))]
    values = values.at[tuple(place)].set(least)
    longest = shape.index(max(shape))
    place[longest] = (place[longest] + 1) % shape[longest]
    return values.at[tuple(place)].set(top_value)


def steps_of(own_key, shape, cuts, least, top_value):
    level, own = 1.0, jax.random.fold_in(own_key, 6)
    for axis_at, shards_of in cuts:
        steps = jnp.exp(jax.random.uniform(jax.random.fold_in(own, axis_at), (shards_of,), jnp.float32, least / len(cuts), top_value / len(cuts)))
        level = level * jnp.repeat(steps, shape[axis_at] // shards_of).reshape([-1 if axis == axis_at else 1 for axis in range(len(shape))])
    return level


def assign_block(rng, own, number, rows, amount, top, limit, skew):
    order = jax.random.permutation(rng, amount)
    heavy_load, common = portions_of(amount, rows * top, limit, skew, True), portions_of(amount, rows * top, limit, skew, False)
    places = jnp.arange(amount)

    def named(sizes, rotation):
        used = int((sizes > 0).sum())
        fixed = max(1, used // 4)
        shifted = fixed + (places - fixed + rotation * (used - fixed)) % max(1, amount - fixed)
        return jnp.zeros((amount,), jnp.int32).at[order[jnp.where(places < fixed, places, shifted)]].set(jnp.asarray(sizes, jnp.int32))

    sizes = jnp.where(number % 4 == 0, named(heavy_load, number // 4), named(common, number - number // 4 - 1))
    mixed = jax.random.permutation(jax.random.fold_in(own, 3), amount)
    giver, receiver = mixed[0:amount // 2 * 2:2], mixed[1:amount // 2 * 2:2]
    room = jnp.minimum(sizes[giver] - 1, limit - sizes[receiver]) // 2
    room = jnp.where((giver == order[0]) | (receiver == order[0]) | (sizes[receiver] == 0), 0, jnp.maximum(room, 0))
    shifted = jax.random.randint(jax.random.fold_in(own, 4), (amount // 2,), 0, 1 << 20) % (room + 1)
    sizes = sizes.at[giver].add(-shifted).at[receiver].add(shifted)
    members = jnp.searchsorted(jnp.cumsum(sizes), jnp.arange(rows * top), side="right").astype(jnp.int32)
    grid = members.reshape(top, rows).T
    grid = grid[jax.random.permutation(jax.random.fold_in(own, 1), rows)]
    rotation = jax.random.randint(jax.random.fold_in(own, 2), (rows, 1), 0, top)
    return jnp.take_along_axis(grid, (jnp.arange(top)[None, :] + rotation) % top, axis=1)


def portions_of(amount, total, bound, lean, full):
    portions = [(1 << 20) // math.isqrt(standing ** lean) + 1 for standing in range(1, amount + 1)]
    largest = bound if full else min(bound, max(-(-total // amount), total * portions[0] // sum(portions)))
    least = 1 if total - largest >= amount - 1 else 0
    holding, spare = [largest] + [least] * (amount - 1), total - largest - least * (amount - 1)
    while spare > 0:
        movable = [i for i in range(1, amount) if holding[i] < largest] or [i for i in range(1, amount) if holding[i] < bound]
        pool, left = sum([portions[i] for i in movable]), spare
        for i in movable:
            addition = min(bound - holding[i], max(1, left * portions[i] // pool), spare)
            holding[i] = holding[i] + addition
            spare = spare - addition
    return np.array(holding)


def normal_values(own_key, dims, spread, bound, pieces=(), kind=jnp.bfloat16):
    drawn = jax.random.normal(own_key, dims, jnp.float32) * spread
    if len(pieces) > 0:
        drawn = steps_of(own_key, dims, pieces, -0.22, 0.18) * drawn
    return jnp.clip(drawn, min=-bound, max=bound).astype(kind)


def setup_inputs(seed: int = 0, part: int = 0) -> dict:
    streams_of = jax.random.split(jax.random.key(seed), 9)
    part_splits = jax.random.split(jax.random.fold_in(streams_of[8], part), 9)
    tokens = normal_values(part_splits[0], (TOKENS, D), 1.0, 6.0, ((0, 16),))
    cotangent = normal_values(part_splits[1], (TOKENS, D), 1.0, 6.0, ((0, 16),))
    routes_keys = jax.random.split(jax.random.fold_in(part_splits[2], 1), TOKENS // TOK_DEV)
    routes_turns = jax.random.permutation(jax.random.fold_in(part_splits[2], 3), TOKENS // TOK_DEV)
    routes = jax.vmap(lambda own, number: assign_block(jax.random.fold_in(part_splits[2], 2), own, number, TOK_DEV, EXPERTS, TOP, CAP, 2))(routes_keys, routes_turns).reshape((TOKENS, TOP))
    gate_nums = set_ends(jax.random.randint(part_splits[3], (TOKENS, TOP), 1, 9), jax.random.fold_in(part_splits[3], 1), 1, 8).astype(jnp.int32)
    gain = jnp.clip(1.0 + 0.1 * jax.random.normal(streams_of[4], (D,), jnp.float32), 0.5, 1.5)
    w_gate = normal_values(streams_of[5], (EXPERTS * HSPLIT, D, FF_DEV), D ** -0.5, 0.1875, ((0, 16),))
    w_up = normal_values(streams_of[6], (EXPERTS * HSPLIT, D, FF_DEV), D ** -0.5, 0.1875, ((0, 16),))
    w_down = normal_values(streams_of[7], (EXPERTS * HSPLIT, FF_DEV, D), FF_DEV ** -0.5, 0.1875, ((0, 16),))
    return {"tokens": tokens, "cotangent": cotangent, "routes": routes, "gate_nums": gate_nums, "gain": gain, "w_gate": w_gate, "w_up": w_up, "w_down": w_down}


def reference(tokens, cotangent, routes, gate_nums, gain, w_gate, w_up, w_down):
    frames = tokens.astype(jnp.float32)
    inverse = lax.rsqrt(lax.optimization_barrier(jnp.mean(frames * frames, -1, keepdims=True)) + 1e-06)
    normed = (frames * inverse * gain).astype(jnp.bfloat16)
    numerators = gate_nums.astype(jnp.float32)
    gates = numerators / lax.optimization_barrier(jnp.sum(numerators, -1, keepdims=True))
    scaled = (gates[:, :, None] * cotangent.astype(jnp.float32)[:, None, :]).astype(jnp.bfloat16)
    blocks = N_EXPERT
    routes_dev = TOK_DEV * TOP
    flat_routes = routes.reshape(blocks, routes_dev)
    onehot = (flat_routes[:, :, None] == jnp.arange(EXPERTS, dtype=jnp.int32)[None, None, :]).astype(jnp.int32)
    within = lax.optimization_barrier(jnp.sum((jnp.cumsum(onehot, axis=1) - 1) * onehot, -1))
    slot_index = (flat_routes * CAP + within).astype(jnp.int32)
    sources = jnp.arange(blocks, dtype=jnp.int32)[:, None]
    row_copies = jnp.repeat(normed.reshape(blocks, TOK_DEV, D), TOP, axis=1)
    rows_buffer = jnp.zeros((blocks, EXPERTS * CAP, D), jnp.bfloat16).at[sources, slot_index].set(row_copies)
    grads_buffer = jnp.zeros((blocks, EXPERTS * CAP, D), jnp.bfloat16).at[sources, slot_index].set(scaled.reshape(blocks, routes_dev, D))

    def expert_work(device):
        start = (device // HSPLIT * CAP).astype(jnp.int32)
        rows = lax.dynamic_slice_in_dim(rows_buffer, start, CAP, 1).reshape(blocks * CAP, D)
        cot_rows = lax.dynamic_slice_in_dim(grads_buffer, start, CAP, 1).reshape(blocks * CAP, D)
        pre_gate = jnp.dot(rows, w_gate[device], preferred_element_type=jnp.float32)
        pre_up = jnp.dot(rows, w_up[device], preferred_element_type=jnp.float32)
        hidden = (jax.nn.silu(pre_gate) * pre_up).astype(jnp.bfloat16)
        partial_value = jnp.dot(hidden, w_down[device], preferred_element_type=jnp.float32).astype(jnp.bfloat16)
        grad_block = jnp.dot(hidden.T, cot_rows, preferred_element_type=jnp.float32).astype(jnp.bfloat16)
        return (partial_value, grad_block)
    partials, grad_down = lax.map(expert_work, jnp.arange(N_EXPERT, dtype=jnp.int32))
    summed = lax.optimization_barrier(jnp.sum(partials.reshape(EXPERTS, HSPLIT, blocks, CAP, D).astype(jnp.float32), axis=1))
    summed = jnp.transpose(summed, (1, 0, 2, 3)).reshape(blocks, EXPERTS * CAP, D)
    picked = jnp.take_along_axis(summed, slot_index[:, :, None], axis=1)
    branch = lax.optimization_barrier(jnp.sum(picked.reshape(TOKENS, TOP, D) * gates[:, :, None], axis=1))
    mixed = (frames + branch).astype(jnp.bfloat16)
    return (mixed, grad_down)
```

```python
import functools

import jax
import jax.numpy as jnp
from jax import lax
from jax.experimental import pallas as pl
from jax.experimental.pallas import tpu as pltpu
from jax.sharding import PartitionSpec as P

HSPLIT = 4
TILE = 256
F32 = jnp.float32
BF16 = jnp.bfloat16


def whole(count):
    return [pl.BlockSpec(memory_space=pltpu.VMEM)] * count


def params(mib):
    return pltpu.CompilerParams(vmem_limit_bytes=mib << 20)


def named_by(routes, plane, experts):
    rows = routes.shape[0]
    expert = lax.broadcasted_iota(jnp.int32, (rows, experts), 1) ^ plane
    member = jnp.zeros((rows, experts), jnp.bool_)
    for k in range(routes.shape[1]):
        member = member | (routes[:, k : k + 1] == expert)
    return member


def gate_of(routes, numerators, plane, experts):
    rows = routes.shape[0]
    expert = lax.broadcasted_iota(jnp.int32, (rows, experts), 1) ^ plane
    gates = numerators / jnp.sum(numerators, -1, keepdims=True)
    gate = jnp.zeros((rows, experts), F32)
    for k in range(routes.shape[1]):
        gate = gate + jnp.where(routes[:, k : k + 1] == expert, gates[:, k : k + 1], 0.0)
    return gate


def placing_of(member, capacity):
    rows, experts = member.shape
    ones = member.astype(F32).astype(BF16)
    first = lax.broadcasted_iota(jnp.int32, (rows, rows), 0)
    second = lax.broadcasted_iota(jnp.int32, (rows, rows), 1)
    upto = (first <= second).astype(F32).astype(BF16)
    same = (first == second).astype(F32).astype(BF16)
    over_rows = (((0,), (0,)), ((), ()))
    count = lax.dot_general(ones, upto, over_rows, preferred_element_type=F32)
    here = lax.dot_general(ones, same, over_rows, preferred_element_type=F32)
    place = jnp.where(here > 0.5, count, 0.0).astype(jnp.int32) - 1
    slots = lax.broadcasted_iota(jnp.int32, (capacity, rows), 0)
    return [
        (slots == place[s : s + 1, :]).astype(F32).astype(BF16) for s in range(experts)
    ]


def send_rows_kernel(experts, plane_ref, tokens_ref, gain_ref, routes_ref, *outs):
    frames = tokens_ref[...].astype(F32)
    inverse = lax.rsqrt(jnp.mean(frames * frames, -1, keepdims=True) + 1e-06)
    normed = (frames * inverse * gain_ref[...]).astype(BF16)
    member = named_by(routes_ref[...], plane_ref[0], experts)
    for out, placing in zip(outs, placing_of(member, outs[0].shape[0])):
        out[...] = jnp.dot(placing, normed, preferred_element_type=F32).astype(BF16)


def send_grads_kernel(experts, plane_ref, cot_ref, routes_ref, nums_ref, *outs):
    cot = cot_ref[...].astype(F32)
    routes = routes_ref[...]
    member = named_by(routes, plane_ref[0], experts)
    gate = gate_of(routes, nums_ref[...].astype(F32), plane_ref[0], experts)
    for s, (out, placing) in enumerate(zip(outs, placing_of(member, outs[0].shape[0]))):
        scaled = (gate[:, s : s + 1] * cot).astype(BF16)
        out[...] = jnp.dot(placing, scaled, preferred_element_type=F32).astype(BF16)


def ffn_kernel(shifts, *refs):
    pieces, refs = refs[: 4 * shifts], refs[4 * shifts :]
    gate_ref, up_ref, down_ref, hidden_ref = refs[:4]
    keeps, sends, rows_ref = refs[4 : 4 + shifts], refs[4 + shifts : 4 + 2 * shifts], refs[-1]
    capacity = pieces[0].shape[0]
    for i, piece in enumerate(pieces):
        rows_ref[i * capacity : (i + 1) * capacity, :] = piece[...]
    width = gate_ref.shape[2]

    @pl.loop(0, width // TILE)
    def _(j):
        columns = pl.ds(pl.multiple_of(j * TILE, TILE), TILE)
        rows = rows_ref[...]
        pre_gate = jnp.dot(rows, gate_ref[0, :, columns], preferred_element_type=F32)
        pre_up = jnp.dot(rows, up_ref[0, :, columns], preferred_element_type=F32)
        hidden_ref[:, columns] = (pre_gate * lax.logistic(pre_gate) * pre_up).astype(BF16)

    @pl.loop(0, down_ref.shape[2] // TILE)
    def _(j):
        columns = pl.ds(pl.multiple_of(j * TILE, TILE), TILE)
        value = jnp.dot(
            hidden_ref[...], down_ref[0, :, columns], preferred_element_type=F32
        ).astype(BF16)
        for i in range(shifts):
            at = 4 * i * capacity
            keeps[i][:, columns] = value[at : at + 2 * capacity]
            sends[i][:, columns] = value[at + 2 * capacity : at + 4 * capacity]


def grad_kernel(chunks, per_chunk, *refs):
    hiddens, pieces = refs[:chunks], refs[chunks : chunks + chunks * per_chunk]
    out_ref, cot_ref = refs[-2:]
    capacity = pieces[0].shape[0]
    for i, piece in enumerate(pieces):
        cot_ref[i * capacity : (i + 1) * capacity, :] = piece[...]
    rows = capacity * per_chunk

    @pl.loop(0, out_ref.shape[2] // TILE)
    def _(j):
        columns = pl.ds(pl.multiple_of(j * TILE, TILE), TILE)
        total = jnp.zeros((out_ref.shape[1], TILE), F32)
        for i, hidden in enumerate(hiddens):
            total = total + lax.dot_general(
                hidden[...],
                cot_ref[i * rows : (i + 1) * rows, columns],
                (((0,), (0,)), ((), ())),
                preferred_element_type=F32,
            )
        out_ref[0, :, columns] = total.astype(BF16)


def combine_kernel(experts, plane_ref, tokens_ref, routes_ref, nums_ref, *refs):
    values, out = refs[:-1], refs[-1]
    routes = routes_ref[...]
    rows = routes.shape[0]
    capacity = values[0].shape[0]
    member = named_by(routes, plane_ref[0], experts)
    gate = gate_of(routes, nums_ref[...].astype(F32), plane_ref[0], experts)
    first = lax.broadcasted_iota(jnp.int32, (rows, rows), 0)
    second = lax.broadcasted_iota(jnp.int32, (rows, rows), 1)
    before = (second <= first).astype(F32).astype(BF16)
    count = jnp.dot(before, member.astype(F32).astype(BF16), preferred_element_type=F32)
    place = jnp.where(member, count, 0.0).astype(jnp.int32) - 1
    slots = lax.broadcasted_iota(jnp.int32, (rows, capacity), 1)
    total = jnp.zeros(tokens_ref.shape, F32)
    for s, value in enumerate(values):
        picking = (slots == place[:, s : s + 1]).astype(F32).astype(BF16)
        picked = jnp.dot(picking, value[...], preferred_element_type=F32)
        total = total + gate[:, s : s + 1] * picked
    out[...] = (tokens_ref[...].astype(F32) + total).astype(BF16)


def on_device(tokens, cotangent, routes, gate_nums, gain, w_gate, w_up, w_down):
    devices = lax.axis_size("expert")
    experts = devices // HSPLIT
    rows_here, width = tokens.shape
    hidden_width = w_gate.shape[2]
    top_count = routes.shape[1]
    capacity = HSPLIT * (3 * top_count * rows_here // (2 * experts * HSPLIT))
    capacity = -(-capacity // 16) * 16
    chunks = min(4, experts)
    shifts = experts // chunks
    plane = (lax.axis_index("expert") // HSPLIT).astype(jnp.int32).reshape(1)
    scalar = pl.BlockSpec(memory_space=pltpu.SMEM)

    def swap(value, mask):
        return lax.ppermute(value, "expert", [(i, i ^ mask) for i in range(devices)])

    piece = jax.ShapeDtypeStruct((capacity, width), BF16)
    placed_flops = 2 * experts * capacity * rows_here * width
    send_rows = pl.pallas_call(
        functools.partial(send_rows_kernel, experts),
        out_shape=[piece] * experts,
        in_specs=[scalar] + whole(3),
        out_specs=whole(experts),
        compiler_params=params(16),
        cost_estimate=pl.CostEstimate(
            flops=placed_flops, bytes_accessed=2 << 20, transcendentals=0
        ),
        name="send_rows",
    )(plane, tokens, gain.reshape(1, -1), routes)
    send_grads = pl.pallas_call(
        functools.partial(send_grads_kernel, experts),
        out_shape=[piece] * experts,
        in_specs=[scalar] + whole(3),
        out_specs=whole(experts),
        compiler_params=params(16),
        cost_estimate=pl.CostEstimate(
            flops=placed_flops, bytes_accessed=2 << 20, transcendentals=0
        ),
        name="send_grads",
    )(plane, cotangent, routes, gate_nums)

    def spread(value, shift):
        mine = value if shift == 0 else swap(value, shift * HSPLIT)
        other = swap(mine, 2)
        return [mine, other, swap(mine, 1), swap(other, 1)]

    rows = [spread(send_rows[s], s) for s in range(experts)]
    grads = [spread(send_grads[s], s) for s in range(experts)]

    rows_chunk = 4 * shifts * capacity
    hiddens, returned = [], []
    for chunk in range(chunks):
        pieces = [p for s in range(chunk * shifts, (chunk + 1) * shifts) for p in rows[s]]
        half = jax.ShapeDtypeStruct((2 * capacity, width), BF16)
        outs = pl.pallas_call(
            functools.partial(ffn_kernel, shifts),
            out_shape=[jax.ShapeDtypeStruct((rows_chunk, hidden_width), BF16)] + [half] * (2 * shifts),
            in_specs=whole(len(pieces) + 3),
            out_specs=whole(1 + 2 * shifts),
            scratch_shapes=[pltpu.VMEM((rows_chunk, width), BF16)],
            compiler_params=params(28),
            cost_estimate=pl.CostEstimate(
                flops=6 * rows_chunk * width * hidden_width,
                bytes_accessed=8 << 20,
                transcendentals=0,
            ),
            name="ffn",
        )(*pieces, w_gate, w_up, w_down)
        hiddens.append(outs[0])
        for i in range(shifts):
            keep, send = outs[1 + i], outs[1 + shifts + i]
            received = swap(send, 1)
            both = keep.astype(F32) + received.astype(F32)
            to_send = both[capacity:].astype(BF16)
            other = swap(to_send, 2)
            mine = (both[:capacity] + other.astype(F32)).astype(BF16)
            shift = chunk * shifts + i
            returned.append(mine if shift == 0 else swap(mine, shift * HSPLIT))

    grad_pieces = [p for s in range(experts) for p in grads[s]]
    grad_down = pl.pallas_call(
        functools.partial(grad_kernel, chunks, 4 * shifts),
        out_shape=jax.ShapeDtypeStruct((1, hidden_width, width), BF16),
        in_specs=whole(chunks + len(grad_pieces)),
        out_specs=whole(1)[0],
        scratch_shapes=[pltpu.VMEM((chunks * rows_chunk, width), BF16)],
        compiler_params=params(32),
        cost_estimate=pl.CostEstimate(
            flops=2 * chunks * rows_chunk * width * hidden_width,
            bytes_accessed=8 << 20,
            transcendentals=0,
        ),
        name="grad",
    )(*hiddens, *grad_pieces)
    mixed = pl.pallas_call(
        functools.partial(combine_kernel, experts),
        out_shape=jax.ShapeDtypeStruct(tokens.shape, BF16),
        in_specs=[scalar] + whole(3 + experts),
        out_specs=whole(1)[0],
        compiler_params=params(16),
        cost_estimate=pl.CostEstimate(
            flops=placed_flops, bytes_accessed=2 << 20, transcendentals=0
        ),
        name="combine",
    )(plane, tokens, routes, gate_nums, *returned)
    return (mixed, grad_down)


def solution(mesh):
    placed = (
        P(("group", "expert"), None),
        P(("group", "expert"), None),
        P(("group", "expert"), None),
        P(("group", "expert"), None),
        P(),
        P("expert", None, None),
        P("expert", None, None),
        P("expert", None, None),
    )
    return jax.shard_map(
        on_device,
        mesh=mesh,
        in_specs=placed,
        out_specs=(P(("group", "expert"), None), P(("group", "expert"), None, None)),
        check_vma=False,
    )
```

```python
import functools

import jax
import jax.numpy as jnp
from jax import lax
from jax.experimental import pallas as pl
from jax.experimental.pallas import tpu as pltpu
from jax.sharding import PartitionSpec as P

HSPLIT = 4
GROUPS = 4
TILE = 256
LINK_WORK = 10 << 30
F32 = jnp.float32
BF16 = jnp.bfloat16


def after(value, *earlier):
    return lax.optimization_barrier((value,) + earlier)[0]


def whole(count):
    return [pl.BlockSpec(memory_space=pltpu.VMEM)] * count


def call(kernel, mib, name, moved=0, **keywords):
    return pl.pallas_call(
        kernel,
        compiler_params=pltpu.CompilerParams(vmem_limit_bytes=mib << 20),
        cost_estimate=pl.CostEstimate(flops=moved, bytes_accessed=0, transcendentals=0),
        name=name,
        **keywords,
    )


def experts_of(plane, experts, rows):
    return lax.broadcasted_iota(jnp.int32, (experts, rows), 0) ^ plane


def placing_of(routes, plane, experts, capacity):
    rows = routes.shape[1]
    expert = experts_of(plane, experts, rows)
    member = jnp.zeros((experts, rows), jnp.bool_)
    for k in range(routes.shape[0]):
        member = member | (routes[k : k + 1, :] == expert)
    first = lax.broadcasted_iota(jnp.int32, (rows, rows), 0)
    second = lax.broadcasted_iota(jnp.int32, (rows, rows), 1)
    upto = (first <= second).astype(F32).astype(BF16)
    ones = member.astype(F32)
    count = jnp.dot(ones.astype(BF16), upto, preferred_element_type=F32)
    place = (ones * count).astype(jnp.int32) - 1
    slots = lax.broadcasted_iota(jnp.int32, (capacity, rows), 0)
    return [(slots == place[s : s + 1, :]).astype(F32) for s in range(experts)]


def gates_of(routes, numbers, plane, experts):
    expert = experts_of(plane, experts, routes.shape[1])
    numerators = numbers.astype(F32)
    gates = numerators / jnp.sum(numerators, 0, keepdims=True)
    gate = jnp.zeros(expert.shape, F32)
    for k in range(routes.shape[0]):
        gate = gate + jnp.where(routes[k : k + 1, :] == expert, gates[k : k + 1, :], 0.0)
    return gate


def fetch(semaphores, *pairs):
    copies = [
        pltpu.make_async_copy(source, target, semaphores.at[i])
        for i, (source, target) in enumerate(pairs)
    ]
    for copy in copies:
        copy.start()
    return copies


def send_rows_kernel(experts, plane_ref, tokens_hbm, gain_hbm, routes_hbm, *refs):
    outs = refs[:experts]
    tokens_ref, gain_ref, routes_ref, semaphores = refs[experts:]
    copies = fetch(
        semaphores, (routes_hbm, routes_ref), (gain_hbm, gain_ref), (tokens_hbm, tokens_ref)
    )
    copies[0].wait()
    placings = placing_of(routes_ref[...], plane_ref[0], experts, outs[0].shape[0])
    copies[1].wait()
    copies[2].wait()
    frames = tokens_ref[...].astype(F32)
    inverse = lax.rsqrt(jnp.mean(frames * frames, -1, keepdims=True) + 1e-06)
    normed = (frames * inverse * gain_ref[...]).astype(BF16)
    for out, placing in zip(outs, placings):
        out[...] = jnp.dot(placing.astype(BF16), normed, preferred_element_type=F32).astype(BF16)


def send_grads_kernel(experts, plane_ref, cot_hbm, routes_hbm, nums_hbm, *refs):
    outs = refs[:experts]
    cot_ref, routes_ref, nums_ref, semaphores = refs[experts:]
    copies = fetch(
        semaphores, (routes_hbm, routes_ref), (nums_hbm, nums_ref), (cot_hbm, cot_ref)
    )
    copies[0].wait()
    copies[1].wait()
    routes = routes_ref[...]
    placings = placing_of(routes, plane_ref[0], experts, outs[0].shape[0])
    gates = gates_of(routes, nums_ref[...], plane_ref[0], experts)
    copies[2].wait()
    cot = cot_ref[...]
    for s, (out, placing) in enumerate(zip(outs, placings)):
        picked = jnp.dot(placing.astype(BF16), cot, preferred_element_type=F32)
        gate = jnp.sum(placing * gates[s : s + 1, :], -1, keepdims=True)
        out[...] = (gate * picked).astype(BF16)


def load_kernel(*refs):
    sources, outs, semaphores = refs[:3], refs[3:6], refs[6]
    copies = fetch(semaphores, *[(s.at[0], o) for s, o in zip(sources, outs)])
    for copy in copies:
        copy.wait()


def nothing(*refs):
    pass


def through(values, name, moved=0):
    count = len(values)
    return call(
        nothing,
        4,
        name,
        moved,
        out_shape=[jax.ShapeDtypeStruct(v.shape, v.dtype) for v in values],
        in_specs=whole(count),
        out_specs=whole(count),
        input_output_aliases={i: i for i in range(count)},
    )(*values)


def ffn_kernel(count, *refs):
    pieces, refs = refs[:count], refs[count:]
    gate_ref, up_ref, down_ref, turned_ref, keep_ref, send_ref, rows_ref, hidden_ref = refs
    at = 0
    for piece in pieces:
        rows_ref[at : at + piece.shape[0], :] = piece[...]
        at += piece.shape[0]
    rows = rows_ref[...]
    half = keep_ref.shape[0]
    for j in range(gate_ref.shape[1] // TILE):
        columns = slice(j * TILE, (j + 1) * TILE)
        pre_gate = jnp.dot(rows, gate_ref[:, columns], preferred_element_type=F32)
        pre_up = jnp.dot(rows, up_ref[:, columns], preferred_element_type=F32)
        hidden = pre_gate * lax.logistic(pre_gate) * pre_up
        hidden_ref[:, columns] = hidden.astype(BF16)
        turned_ref[columns, :] = hidden.T.astype(BF16)
    for j in range(down_ref.shape[1] // TILE):
        columns = slice(j * TILE, (j + 1) * TILE)
        value = jnp.dot(
            hidden_ref[...], down_ref[:, columns], preferred_element_type=F32
        ).astype(BF16)
        keep_ref[:, columns] = value[:half]
        send_ref[:, columns] = value[half:]


def grad_kernel(plan, turned_count, *refs):
    turned, pieces = refs[:turned_count], refs[turned_count:-3]
    out_ref, hidden_ref, cot_ref = refs[-3:]
    for i, start, rows, at in plan:
        cot_ref[at : at + rows, :] = pieces[i][start : start + rows, :]
    at = 0
    for value in turned:
        hidden_ref[:, at : at + value.shape[1]] = value[...]
        at += value.shape[1]
    for j in range(out_ref.shape[2] // TILE):
        columns = slice(j * TILE, (j + 1) * TILE)
        out_ref[0, :, columns] = jnp.dot(
            hidden_ref[...], cot_ref[:, columns], preferred_element_type=F32
        ).astype(BF16)


def combine_kernel(experts, plane_ref, tokens_ref, routes_ref, nums_ref, *refs):
    values, out = refs[:-1], refs[-1]
    routes = routes_ref[...]
    placings = placing_of(routes, plane_ref[0], experts, values[0].shape[0])
    gates = gates_of(routes, nums_ref[...], plane_ref[0], experts)
    fill = -experts % 8
    if fill:
        gates = jnp.concatenate([gates, jnp.zeros((fill, gates.shape[1]), F32)], 0)
    gates = gates.T
    total = tokens_ref[...].astype(F32)
    for s, value in enumerate(values):
        picked = lax.dot_general(
            placings[s].astype(BF16),
            value[...],
            (((0,), (0,)), ((), ())),
            preferred_element_type=F32,
        )
        total = total + gates[:, s : s + 1] * picked
    out[...] = total.astype(BF16)


def on_device(tokens, cotangent, routes, gate_nums, gain, w_gate, w_up, w_down):
    devices = lax.axis_size("expert")
    experts = devices // HSPLIT
    rows_here, width = tokens.shape
    hidden_width = w_gate.shape[2]
    top_count = routes.shape[1]
    capacity = HSPLIT * (3 * top_count * rows_here // (2 * experts * HSPLIT))
    capacity = -(-capacity // 16) * 16
    shifts = max(1, experts // GROUPS)
    groups = [list(range(g, g + shifts)) for g in range(0, experts, shifts)]
    height = shifts * capacity
    plane = (lax.axis_index("expert") // HSPLIT).astype(jnp.int32).reshape(1)
    routes, gate_nums, gain = routes.T, gate_nums.T, gain.reshape(1, -1)
    scalar = pl.BlockSpec(memory_space=pltpu.SMEM)
    anywhere = pl.BlockSpec(memory_space=pl.ANY)
    piece = jax.ShapeDtypeStruct((capacity, width), BF16)
    live = {}

    def swap(value, mask):
        return lax.ppermute(value, "expert", [(i, i ^ mask) for i in range(devices)])

    def sync():
        values = lax.optimization_barrier(tuple(live.values()))
        live.update(zip(list(live), values))

    def join(parts):
        return parts[0] if len(parts) == 1 else jnp.concatenate(parts, 0)

    flying = {}

    def launch(name, value, mask):
        flying[name] = swap(value, mask)

    def land():
        names = list(flying)
        landed = dict(zip(names, through([flying.pop(n) for n in names], "land", LINK_WORK)))
        for name, value in landed.items():
            if name[0] == "y":
                live[name[1:]] = join([live.pop(("sent",) + name[1:]), value])
            elif name[0] == "fold":
                gs = name[1]
                keep, crossed = live.pop(("keep", gs)), live.pop(("crossed", gs))
                rows = value.shape[0]
                total = keep[:rows].astype(F32) + crossed[:rows].astype(F32)
                total = (total + value.astype(F32)).astype(BF16)
                for i, s in enumerate([s for g in gs for s in groups[g]]):
                    live["R", s] = total[i * capacity : (i + 1) * capacity]
            else:
                live[name] = value
        return next(iter(landed.values()))

    def across(kind, g):
        for s in groups[g]:
            if s:
                launch((kind, s), live[kind, s], s * HSPLIT)

    def along(kind, *gs):
        own = join([live.pop((kind, s)) for g in gs for s in groups[g]])
        live["sent", kind, "own", gs] = own
        launch(("y", kind, "own", gs), own, 2)

    def core(kind, *gs):
        live[kind, "other", gs] = swap(live[kind, "own", gs], 1)

    def ffn(*gs):
        pieces = [live.pop(("N", "own", gs)), live.pop(("N", "other", gs))]
        half = jax.ShapeDtypeStruct(pieces[0].shape, BF16)
        rows = 2 * half.shape[0]
        live["turned", gs], live["keep", gs], live["send", gs] = call(
            functools.partial(ffn_kernel, len(pieces)),
            24,
            "ffn",
            out_shape=[jax.ShapeDtypeStruct((hidden_width, rows), BF16), half, half],
            in_specs=whole(len(pieces) + 3),
            out_specs=whole(3),
            scratch_shapes=[
                pltpu.VMEM((rows, width), BF16),
                pltpu.VMEM((rows, hidden_width), BF16),
            ],
        )(*pieces, live["w", 0], live["w", 1], live["w", 2])

    def cross(*gs):
        live["crossed", gs] = swap(live.pop(("send", gs)), 1)

    def fold_core(earlier, *gs):
        keep, crossed = live["keep", gs], after(live["crossed", gs], earlier)
        rows = keep.shape[0] // 2
        both = keep[rows:].astype(F32) + crossed[rows:].astype(F32)
        live["across", gs] = both.astype(BF16)

    def fold_row(*gs):
        launch(("fold", gs), live.pop(("across", gs)), 2)

    def back(g):
        across("R", g)

    def send_rows():
        values = call(
            functools.partial(send_rows_kernel, experts),
            16,
            "send_rows",
            out_shape=[piece] * experts,
            in_specs=[scalar] + [anywhere] * 3,
            out_specs=whole(experts),
            scratch_shapes=[
                pltpu.VMEM(tokens.shape, BF16),
                pltpu.VMEM(gain.shape, F32),
                pltpu.VMEM(routes.shape, jnp.int32),
                pltpu.SemaphoreType.DMA((3,)),
            ],
        )(plane, tokens, gain, routes)
        live.update({("N", s): value for s, value in enumerate(values)})

    def send_grads():
        values = call(
            functools.partial(send_grads_kernel, experts),
            16,
            "send_grads",
            out_shape=[piece] * experts,
            in_specs=[scalar] + [anywhere] * 3,
            out_specs=whole(experts),
            scratch_shapes=[
                pltpu.VMEM(cotangent.shape, BF16),
                pltpu.VMEM(routes.shape, jnp.int32),
                pltpu.VMEM(gate_nums.shape, jnp.int32),
                pltpu.SemaphoreType.DMA((3,)),
            ],
        )(plane, after(cotangent, live["N", experts - 1]), routes, gate_nums)
        live.update({("C", s): value for s, value in enumerate(values)})

    def load():
        weight = jax.ShapeDtypeStruct((width, hidden_width), BF16)
        values = call(
            load_kernel,
            16,
            "load",
            out_shape=[weight, weight, jax.ShapeDtypeStruct((hidden_width, width), BF16)],
            in_specs=[anywhere] * 3,
            out_specs=whole(3),
            scratch_shapes=[pltpu.SemaphoreType.DMA((3,))],
        )(after(w_gate, live["C", experts - 1]), w_up, w_down)
        live.update({("w", i): value for i, value in enumerate(values)})

    send_rows()
    if shifts > 1:
        across("N", 0)
        land()
    sync()
    along("N", 0)
    for g in (1, 2):
        across("N", g)
    send_grads()
    if shifts > 1:
        across("C", 0)
        land()
    along("C", 0)
    load()
    land()
    sync()
    across("N", 3)
    across("C", 1)
    along("N", 1, 2)
    core("N", 0)
    ffn(0)
    cross(0)
    fold_core(land(), 0)
    sync()
    across("C", 2)
    along("N", 3)
    fold_row(0)
    core("N", 1, 2)
    ffn(1, 2)
    cross(1, 2)
    fold_core(land(), 1, 2)
    sync()
    across("C", 3)
    fold_row(1, 2)
    core("N", 3)
    ffn(3)
    cross(3)
    core("C", 0)
    fold_core(land(), 3)
    sync()
    if shifts > 1:
        back(0)
    back(1)
    back(2)
    fold_row(3)
    along("C", 1)
    land()
    sync()
    back(3)
    along("C", 2, 3)
    core("C", 1)
    land()
    sync()
    core("C", 2, 3)

    places, at = {}, 0
    turned = [(0,), (1, 2), (3,)]
    for gs in turned:
        for half in ("own", "other"):
            for side in range(2):
                for g in gs:
                    places[half, side, g] = at
                    at += height
    pieces, plan = [], []
    for gs in [(0,), (1,), (2, 3)]:
        for half in ("own", "other"):
            for side in range(2):
                for i, g in enumerate(gs):
                    start = (side * len(gs) + i) * height
                    plan.append((len(pieces), start, height, places[half, side, g]))
            pieces.append(live["C", half, gs])
    grad_down = call(
        functools.partial(grad_kernel, plan, len(turned)),
        24,
        "grad",
        out_shape=jax.ShapeDtypeStruct((1, hidden_width, width), BF16),
        in_specs=whole(len(turned) + len(pieces)),
        out_specs=whole(1)[0],
        scratch_shapes=[
            pltpu.VMEM((hidden_width, at), BF16),
            pltpu.VMEM((at, width), BF16),
        ],
    )(*[live["turned", gs] for gs in turned], *pieces)
    mixed = call(
        functools.partial(combine_kernel, experts),
        16,
        "combine",
        out_shape=jax.ShapeDtypeStruct(tokens.shape, BF16),
        in_specs=[scalar] + whole(3 + experts),
        out_specs=whole(1)[0],
    )(plane, tokens, routes, gate_nums, *[live["R", s] for s in range(experts)])
    return (mixed, grad_down)


def solution(mesh):
    placed = (
        P(("group", "expert"), None),
        P(("group", "expert"), None),
        P(("group", "expert"), None),
        P(("group", "expert"), None),
        P(),
        P("expert", None, None),
        P("expert", None, None),
        P("expert", None, None),
    )
    return jax.shard_map(
        on_device,
        mesh=mesh,
        in_specs=placed,
        out_specs=(P(("group", "expert"), None), P(("group", "expert"), None, None)),
        check_vma=False,
    )
```

```python
import functools

import jax
import jax.numpy as jnp
from jax import lax
from jax.experimental import pallas as pl
from jax.experimental.pallas import tpu as pltpu
from jax.sharding import PartitionSpec as P

HSPLIT = 4
GROUPS = 4
JOINED = ((1, 2), (2, 3))
TILE = 256
LINK_WORK = int(8 * 2**30)
F32 = jnp.float32
BF16 = jnp.bfloat16


def after(value, *earlier):
    return lax.optimization_barrier((value,) + earlier)[0]


def whole(count):
    return [pl.BlockSpec(memory_space=pltpu.VMEM)] * count


def call(kernel, mib, name, moved=0, **keywords):
    return pl.pallas_call(
        kernel,
        compiler_params=pltpu.CompilerParams(vmem_limit_bytes=mib << 20),
        cost_estimate=pl.CostEstimate(flops=moved, bytes_accessed=0, transcendentals=0),
        name=name,
        **keywords,
    )


def experts_of(plane, experts, rows):
    return lax.broadcasted_iota(jnp.int32, (experts, rows), 0) ^ plane


def placing_of(routes, plane, experts, capacity):
    rows = routes.shape[1]
    expert = experts_of(plane, experts, rows)
    member = jnp.zeros((experts, rows), jnp.bool_)
    for k in range(routes.shape[0]):
        member = member | (routes[k : k + 1, :] == expert)
    first = lax.broadcasted_iota(jnp.int32, (rows, rows), 0)
    second = lax.broadcasted_iota(jnp.int32, (rows, rows), 1)
    upto = (first <= second).astype(F32).astype(BF16)
    ones = member.astype(F32)
    count = jnp.dot(ones.astype(BF16), upto, preferred_element_type=F32)
    place = (ones * count).astype(jnp.int32) - 1
    slots = lax.broadcasted_iota(jnp.int32, (capacity, rows), 0)
    return [(slots == place[s : s + 1, :]).astype(F32) for s in range(experts)]


def gates_of(routes, numbers, plane, experts):
    expert = experts_of(plane, experts, routes.shape[1])
    numerators = numbers.astype(F32)
    gates = numerators / jnp.sum(numerators, 0, keepdims=True)
    gate = jnp.zeros(expert.shape, F32)
    for k in range(routes.shape[0]):
        gate = gate + jnp.where(routes[k : k + 1, :] == expert, gates[k : k + 1, :], 0.0)
    return gate


def fetch(semaphores, *pairs):
    copies = [
        pltpu.make_async_copy(source, target, semaphores.at[i])
        for i, (source, target) in enumerate(pairs)
    ]
    for copy in copies:
        copy.start()
    return copies


def send_rows_kernel(experts, plane_ref, tokens_hbm, gain_hbm, routes_hbm, *refs):
    outs = refs[:experts]
    tokens_ref, gain_ref, routes_ref, semaphores = refs[experts:]
    copies = fetch(
        semaphores, (routes_hbm, routes_ref), (gain_hbm, gain_ref), (tokens_hbm, tokens_ref)
    )
    copies[0].wait()
    placings = placing_of(routes_ref[...], plane_ref[0], experts, outs[0].shape[0])
    copies[1].wait()
    copies[2].wait()
    frames = tokens_ref[...].astype(F32)
    inverse = lax.rsqrt(jnp.mean(frames * frames, -1, keepdims=True) + 1e-06)
    normed = (frames * inverse * gain_ref[...]).astype(BF16)
    for out, placing in zip(outs, placings):
        out[...] = jnp.dot(placing.astype(BF16), normed, preferred_element_type=F32).astype(BF16)


def send_grads_kernel(experts, plane_ref, cot_hbm, routes_hbm, nums_hbm, *refs):
    outs = refs[:experts]
    cot_ref, routes_ref, nums_ref, semaphores = refs[experts:]
    copies = fetch(
        semaphores, (routes_hbm, routes_ref), (nums_hbm, nums_ref), (cot_hbm, cot_ref)
    )
    copies[0].wait()
    copies[1].wait()
    routes = routes_ref[...]
    placings = placing_of(routes, plane_ref[0], experts, outs[0].shape[0])
    gates = gates_of(routes, nums_ref[...], plane_ref[0], experts)
    copies[2].wait()
    cot = cot_ref[...]
    for s, (out, placing) in enumerate(zip(outs, placings)):
        picked = jnp.dot(placing.astype(BF16), cot, preferred_element_type=F32)
        gate = jnp.sum(placing * gates[s : s + 1, :], -1, keepdims=True)
        out[...] = (gate * picked).astype(BF16)


def load_kernel(*refs):
    sources, outs, semaphores = refs[:3], refs[3:6], refs[6]
    copies = fetch(semaphores, *[(s.at[0], o) for s, o in zip(sources, outs)])
    for copy in copies:
        copy.wait()


def nothing(*refs):
    pass


def through(values, name, moved=0):
    count = len(values)
    return call(
        nothing,
        4,
        name,
        moved,
        out_shape=[jax.ShapeDtypeStruct(v.shape, v.dtype) for v in values],
        in_specs=whole(count),
        out_specs=whole(count),
        input_output_aliases={i: i for i in range(count)},
    )(*values)


def ffn_kernel(count, *refs):
    pieces, refs = refs[:count], refs[count:]
    gate_ref, up_ref, down_ref, turned_ref, keep_ref, send_ref, rows_ref, hidden_ref = refs
    at = 0
    for piece in pieces:
        rows_ref[at : at + piece.shape[0], :] = piece[...]
        at += piece.shape[0]
    rows = rows_ref[...]
    half = keep_ref.shape[0]
    for j in range(gate_ref.shape[1] // TILE):
        columns = slice(j * TILE, (j + 1) * TILE)
        pre_gate = jnp.dot(rows, gate_ref[:, columns], preferred_element_type=F32)
        pre_up = jnp.dot(rows, up_ref[:, columns], preferred_element_type=F32)
        hidden = pre_gate * lax.logistic(pre_gate) * pre_up
        hidden_ref[:, columns] = hidden.astype(BF16)
        turned_ref[columns, :] = hidden.T.astype(BF16)
    for j in range(down_ref.shape[1] // TILE):
        columns = slice(j * TILE, (j + 1) * TILE)
        value = jnp.dot(
            hidden_ref[...], down_ref[:, columns], preferred_element_type=F32
        ).astype(BF16)
        keep_ref[:, columns] = value[:half]
        send_ref[:, columns] = value[half:]


def grad_kernel(plan, earlier_count, *refs):
    earlier, refs = refs[:earlier_count], refs[earlier_count:]
    out_ref, hidden_ref, cot_ref = refs[-3:]
    at = 0
    for turned, column, piece, row, count in plan:
        hidden_ref[:, at : at + count] = refs[turned][:, column : column + count]
        cot_ref[at : at + count, :] = refs[piece][row : row + count, :]
        at += count
    for j in range(cot_ref.shape[1] // TILE):
        columns = slice(j * TILE, (j + 1) * TILE)
        total = jnp.dot(hidden_ref[...], cot_ref[:, columns], preferred_element_type=F32)
        if earlier:
            out_ref[0, :, columns] = (earlier[0][0, :, columns] + total).astype(BF16)
        else:
            out_ref[0, :, columns] = total


def combine_kernel(experts, plane_ref, tokens_ref, routes_ref, nums_ref, *refs):
    values, out = refs[:-1], refs[-1]
    routes = routes_ref[...]
    placings = placing_of(routes, plane_ref[0], experts, values[0].shape[0])
    gates = gates_of(routes, nums_ref[...], plane_ref[0], experts)
    fill = -experts % 8
    if fill:
        gates = jnp.concatenate([gates, jnp.zeros((fill, gates.shape[1]), F32)], 0)
    gates = gates.T
    total = tokens_ref[...].astype(F32)
    for s, value in enumerate(values):
        picked = lax.dot_general(
            placings[s].astype(BF16),
            value[...],
            (((0,), (0,)), ((), ())),
            preferred_element_type=F32,
        )
        total = total + gates[:, s : s + 1] * picked
    out[...] = total.astype(BF16)


def on_device(tokens, cotangent, routes, gate_nums, gain, w_gate, w_up, w_down):
    devices = lax.axis_size("expert")
    experts = devices // HSPLIT
    rows_here, width = tokens.shape
    hidden_width = w_gate.shape[2]
    top_count = routes.shape[1]
    capacity = HSPLIT * (3 * top_count * rows_here // (2 * experts * HSPLIT))
    capacity = -(-capacity // 16) * 16
    shifts = max(1, experts // GROUPS)
    groups = [list(range(g, g + shifts)) for g in range(0, experts, shifts)]
    height = shifts * capacity
    plane = (lax.axis_index("expert") // HSPLIT).astype(jnp.int32).reshape(1)
    routes, gate_nums, gain = routes.T, gate_nums.T, gain.reshape(1, -1)
    scalar = pl.BlockSpec(memory_space=pltpu.SMEM)
    anywhere = pl.BlockSpec(memory_space=pl.ANY)
    piece = jax.ShapeDtypeStruct((capacity, width), BF16)
    live = {}

    def swap(value, mask):
        return lax.ppermute(value, "expert", [(i, i ^ mask) for i in range(devices)])

    def sync():
        values = lax.optimization_barrier(tuple(live.values()))
        live.update(zip(list(live), values))

    def join(parts):
        return parts[0] if len(parts) == 1 else jnp.concatenate(parts, 0)

    flying, last = {}, []

    def launch(name, value, mask):
        flying[name] = swap(value, mask)

    def land(*names):
        values = tuple(flying.pop(n) for n in names) + tuple(last)
        landed = through(lax.optimization_barrier(values)[: len(names)], "land", LINK_WORK)
        last[:] = landed[:1]
        for name, value in zip(names, landed):
            if name[0] == "y":
                live[name[1:]] = join([live.pop(("sent",) + name[1:]), value])
            elif name[0] == "fold":
                gs = name[1]
                keep, crossed = live.pop(("keep", gs)), live.pop(("crossed", gs))
                rows = value.shape[0]
                total = keep[:rows].astype(F32) + crossed[:rows].astype(F32)
                total = (total + value.astype(F32)).astype(BF16)
                for i, s in enumerate([s for g in gs for s in groups[g]]):
                    live["R", s] = total[i * capacity : (i + 1) * capacity]
            else:
                live[name] = value
        return landed[0]

    def planes(kind, *gs):
        return [(kind, s) for g in gs for s in groups[g] if s]

    def rows(kind, *gs):
        return ("y", kind, "own", gs)

    def across(kind, g):
        for s in groups[g]:
            if s:
                launch((kind, s), live[kind, s], s * HSPLIT)

    def along(kind, *gs):
        own = join([live.pop((kind, s)) for g in gs for s in groups[g]])
        live["sent", kind, "own", gs] = own
        launch(("y", kind, "own", gs), own, 2)

    def core(kind, *gs):
        own = join([live[kind, "own", (g,)] for g in gs])
        live[kind, "other", gs] = swap(own, 1)

    def core_joined(kind, gs):
        live[kind, "other", gs] = swap(live[kind, "own", gs], 1)

    def ffn(*gs):
        pieces = [live.pop(("N", "own", gs)), live.pop(("N", "other", gs))]
        half = jax.ShapeDtypeStruct(pieces[0].shape, BF16)
        rows = 2 * half.shape[0]
        live["turned", gs], live["keep", gs], live["send", gs] = call(
            functools.partial(ffn_kernel, len(pieces)),
            24,
            "ffn",
            out_shape=[jax.ShapeDtypeStruct((hidden_width, rows), BF16), half, half],
            in_specs=whole(len(pieces) + 3),
            out_specs=whole(3),
            scratch_shapes=[
                pltpu.VMEM((rows, width), BF16),
                pltpu.VMEM((rows, hidden_width), BF16),
            ],
        )(*pieces, live["w", 0], live["w", 1], live["w", 2])
        last.append(live["turned", gs])

    def cross(*gs):
        live["crossed", gs] = swap(live.pop(("send", gs)), 1)

    def fold_core(earlier, *gs):
        keep, crossed = live["keep", gs], after(live["crossed", gs], earlier)
        rows = keep.shape[0] // 2
        both = keep[rows:].astype(F32) + crossed[rows:].astype(F32)
        live["across", gs] = both.astype(BF16)
        last.append(live["across", gs])

    def fold_row(*gs):
        launch(("fold", gs), live.pop(("across", gs)), 2)

    def back(g):
        across("R", g)

    def send_rows():
        values = call(
            functools.partial(send_rows_kernel, experts),
            16,
            "send_rows",
            out_shape=[piece] * experts,
            in_specs=[scalar] + [anywhere] * 3,
            out_specs=whole(experts),
            scratch_shapes=[
                pltpu.VMEM(tokens.shape, BF16),
                pltpu.VMEM(gain.shape, F32),
                pltpu.VMEM(routes.shape, jnp.int32),
                pltpu.SemaphoreType.DMA((3,)),
            ],
        )(plane, tokens, gain, routes)
        live.update({("N", s): value for s, value in enumerate(values)})

    def send_grads():
        values = call(
            functools.partial(send_grads_kernel, experts),
            16,
            "send_grads",
            out_shape=[piece] * experts,
            in_specs=[scalar] + [anywhere] * 3,
            out_specs=whole(experts),
            scratch_shapes=[
                pltpu.VMEM(cotangent.shape, BF16),
                pltpu.VMEM(routes.shape, jnp.int32),
                pltpu.VMEM(gate_nums.shape, jnp.int32),
                pltpu.SemaphoreType.DMA((3,)),
            ],
        )(plane, after(cotangent, live["N", experts - 1]), routes, gate_nums)
        live.update({("C", s): value for s, value in enumerate(values)})

    def load():
        weight = jax.ShapeDtypeStruct((width, hidden_width), BF16)
        values = call(
            load_kernel,
            16,
            "load",
            out_shape=[weight, weight, jax.ShapeDtypeStruct((hidden_width, width), BF16)],
            in_specs=[anywhere] * 3,
            out_specs=whole(3),
            scratch_shapes=[pltpu.SemaphoreType.DMA((3,))],
        )(after(w_gate, live["C", experts - 1]), w_up, w_down)
        live.update({("w", i): value for i, value in enumerate(values)})

    def grad(turned, pieces, earlier):
        columns = {}
        for i, gs in enumerate(turned):
            at = 0
            for half in ("own", "other"):
                for side in range(2):
                    for g in gs:
                        columns[half, side, g] = (i, at)
                        at += height
        plan = []
        for i, (half, gs) in enumerate(pieces):
            row = 0
            for parts in [gs] if gs in JOINED else [(g,) for g in gs]:
                for side in range(2):
                    for g in parts:
                        where, at = columns[half, side, g]
                        plan.append((where, at, len(turned) + i, row, height))
                        row += height
        total = sum(step[-1] for step in plan)
        kind = F32 if earlier is None else BF16
        return call(
            functools.partial(grad_kernel, plan, 0 if earlier is None else 1),
            24,
            "grad",
            out_shape=jax.ShapeDtypeStruct((1, hidden_width, width), kind),
            in_specs=whole(len(turned) + len(pieces) + (earlier is not None)),
            out_specs=whole(1)[0],
            scratch_shapes=[
                pltpu.VMEM((hidden_width, total), BF16),
                pltpu.VMEM((total, width), BF16),
            ],
        )(
            *([] if earlier is None else [earlier]),
            *[live["turned", gs] for gs in turned],
            *[live["C", half, gs] for half, gs in pieces],
        )

    send_rows()
    if shifts > 1:
        across("N", 0)
        land(*planes("N", 0))
    sync()
    for g in (1, 2):
        across("N", g)
    along("N", 0)
    send_grads()
    if shifts > 1:
        across("C", 0)
        land(*planes("C", 0))
    along("C", 0)
    load()
    land(rows("N", 0))
    sync()
    core_joined("N", (0,))
    land(*planes("N", 1, 2))
    sync()
    along("N", 1, 2)
    across("N", 3)
    across("C", 1)
    land(rows("C", 0))
    sync()
    ffn(0)
    cross(0)
    fold_core(land(*planes("N", 3), *planes("C", 1)), 0)
    sync()
    fold_row(0)
    across("C", 2)
    land(rows("N", 1, 2))
    sync()
    along("N", 3)
    core_joined("N", (1, 2))
    ffn(1, 2)
    cross(1, 2)
    land(("fold", (0,)))
    sync()
    along("C", 1)
    fold_core(land(*planes("C", 2)), 1, 2)
    sync()
    fold_row(1, 2)
    across("C", 3)
    land(rows("N", 3))
    sync()
    core_joined("N", (3,))
    ffn(3)
    cross(3)
    fold_core(land(rows("C", 1)), 3)
    sync()
    fold_row(3)
    core("C", 0, 1)
    land(*planes("C", 3))
    sync()
    land(("fold", (1, 2)))
    sync()
    along("C", 2, 3)
    if shifts > 1:
        back(0)
    back(1)
    back(2)
    land(("fold", (3,)))
    sync()
    back(3)
    first = grad([(0,), (1, 2)], [("own", (0,)), ("own", (1,)), ("other", (0, 1))], None)
    live["first"] = first
    last.append(first)
    if shifts > 1:
        land(*planes("R", 0))
    land(*planes("R", 1, 2))
    sync()
    land(rows("C", 2, 3))
    sync()
    core_joined("C", (2, 3))
    land(*planes("R", 3))
    grad_down = grad([(1, 2), (3,)], [("own", (2, 3)), ("other", (2, 3))], live["first"])
    mixed = call(
        functools.partial(combine_kernel, experts),
        16,
        "combine",
        out_shape=jax.ShapeDtypeStruct(tokens.shape, BF16),
        in_specs=[scalar] + whole(3 + experts),
        out_specs=whole(1)[0],
    )(plane, tokens, routes, gate_nums, *[live["R", s] for s in range(experts)])
    return (mixed, grad_down)


def solution(mesh):
    placed = (
        P(("group", "expert"), None),
        P(("group", "expert"), None),
        P(("group", "expert"), None),
        P(("group", "expert"), None),
        P(),
        P("expert", None, None),
        P("expert", None, None),
        P("expert", None, None),
    )
    return jax.shard_map(
        on_device,
        mesh=mesh,
        in_specs=placed,
        out_specs=(P(("group", "expert"), None), P(("group", "expert"), None, None)),
        check_vma=False,
    )
```

```python
import functools

import jax
import jax.numpy as jnp
from jax import lax
from jax.experimental import pallas as pl
from jax.experimental.pallas import tpu as pltpu
from jax.sharding import PartitionSpec as P

HSPLIT = 4
TILE = 256
PER_STEP = 4
F32 = jnp.float32
BF16 = jnp.bfloat16
OVER_ROWS = (((0,), (0,)), ((), ()))


def whole(count):
    return [pl.BlockSpec(memory_space=pltpu.VMEM)] * count


def call(kernel, mib, name, flops, **keywords):
    return pl.pallas_call(
        kernel,
        compiler_params=pltpu.CompilerParams(vmem_limit_bytes=mib << 20),
        cost_estimate=pl.CostEstimate(flops=flops, bytes_accessed=4 << 20, transcendentals=0),
        name=name,
        **keywords,
    )


def placing_of(meta, expert, capacity):
    rows = meta.shape[1]
    top = meta.shape[0] // 2
    routes, numerators = meta[:top], meta[top:].astype(F32)
    named = (routes == expert).astype(F32)
    member = jnp.sum(named, 0, keepdims=True)
    gates = numerators / jnp.sum(numerators, 0, keepdims=True)
    gate = jnp.sum(named * gates, 0, keepdims=True)
    first = lax.broadcasted_iota(jnp.int32, (rows, rows), 0)
    second = lax.broadcasted_iota(jnp.int32, (rows, rows), 1)
    upto = (first <= second).astype(F32).astype(BF16)
    count = jnp.dot(
        jnp.broadcast_to(member, (16, rows)).astype(BF16), upto, preferred_element_type=F32
    )[:1]
    place = (member * count).astype(jnp.int32) - 1
    slots = lax.broadcasted_iota(jnp.int32, (capacity, rows), 0)
    placing = (slots == place).astype(F32)
    return placing.astype(BF16), jnp.sum(placing * gate, -1, keepdims=True)


def normed_kernel(tokens_ref, gain_ref, out_ref):
    frames = tokens_ref[...].astype(F32)
    inverse = lax.rsqrt(jnp.mean(frames * frames, -1, keepdims=True) + 1e-06)
    out_ref[...] = (frames * inverse * gain_ref[...]).astype(BF16)


def ffn_kernel(
    capacity, expert_ref, meta_ref, frames_ref, gate_ref, up_ref, down_ref, turned_ref, out_ref, *scratch
):
    rows_ref, hidden_ref, value_ref = scratch
    block = meta_ref.shape[2]
    height = PER_STEP * capacity

    @pl.loop(0, meta_ref.shape[0] // PER_STEP)
    def _(step):
        placings = [
            placing_of(meta_ref[step * PER_STEP + b], expert_ref[0], capacity)
            for b in range(PER_STEP)
        ]
        for b, (placing, _) in enumerate(placings):
            at = pl.multiple_of((step * PER_STEP + b) * block, block)
            rows_ref[b * capacity : (b + 1) * capacity, :] = jnp.dot(
                placing, frames_ref[pl.ds(at, block), :], preferred_element_type=F32
            ).astype(BF16)
        rows = rows_ref[...]
        for j in range(gate_ref.shape[2] // TILE):
            columns = slice(j * TILE, (j + 1) * TILE)
            pre_gate = jnp.dot(rows, gate_ref[0, :, columns], preferred_element_type=F32)
            pre_up = jnp.dot(rows, up_ref[0, :, columns], preferred_element_type=F32)
            hidden = pre_gate * lax.logistic(pre_gate) * pre_up
            hidden_ref[:, columns] = hidden.astype(BF16)
            at = pl.multiple_of(step * height, 128)
            turned_ref[columns, pl.ds(at, height)] = hidden.T.astype(BF16)
        for j in range(down_ref.shape[2] // TILE):
            columns = slice(j * TILE, (j + 1) * TILE)
            value_ref[...] = jnp.dot(
                hidden_ref[...], down_ref[0, :, columns], preferred_element_type=F32
            )
            for b, (placing, gate) in enumerate(placings):
                at = pl.multiple_of((step * PER_STEP + b) * block, block)
                value = (value_ref[b * capacity : (b + 1) * capacity, :] * gate).astype(BF16)
                out_ref[pl.ds(at, block), columns] = lax.dot_general(
                    placing, value, OVER_ROWS, preferred_element_type=F32
                ).astype(BF16)


def grad_kernel(capacity, expert_ref, meta_ref, cot_ref, turned_ref, out_ref, rows_ref):
    block = meta_ref.shape[2]

    @pl.loop(0, meta_ref.shape[0])
    def _(b):
        placing, gate = placing_of(meta_ref[b], expert_ref[0], capacity)
        at = pl.multiple_of(b * block, block)
        picked = jnp.dot(placing, cot_ref[pl.ds(at, block), :], preferred_element_type=F32)
        to = pl.multiple_of(b * capacity, 16)
        rows_ref[pl.ds(to, capacity), :] = (picked * gate).astype(BF16)

    for j in range(out_ref.shape[2] // TILE):
        columns = slice(j * TILE, (j + 1) * TILE)
        out_ref[0, :, columns] = jnp.dot(
            turned_ref[...], rows_ref[:, columns], preferred_element_type=F32
        ).astype(BF16)


def on_device(tokens, cotangent, routes, gate_nums, gain, w_gate, w_up, w_down):
    devices = lax.axis_size("expert")
    experts = devices // HSPLIT
    block, width = tokens.shape
    hidden_width = w_gate.shape[2]
    top_count = routes.shape[1]
    capacity = HSPLIT * (3 * top_count * block // (2 * experts * HSPLIT))
    capacity = -(-capacity // 32) * 32
    rows = devices * capacity
    expert = (lax.axis_index("expert") // HSPLIT).astype(jnp.int32).reshape(1)
    scalar = pl.BlockSpec(memory_space=pltpu.SMEM)

    meta = jnp.concatenate([routes.T, gate_nums.T], 0)[None]
    normed = call(
        normed_kernel,
        16,
        "normed",
        0,
        out_shape=jax.ShapeDtypeStruct(tokens.shape, BF16),
        in_specs=whole(2),
        out_specs=whole(1)[0],
    )(tokens, gain.reshape(1, -1))
    meta = lax.all_gather(meta, "expert", axis=0, tiled=True)
    frames = lax.all_gather(normed, "expert", axis=0, tiled=True)
    cots = lax.all_gather(cotangent, "expert", axis=0, tiled=True)
    turned, dense = call(
        functools.partial(ffn_kernel, capacity),
        40,
        "ffn",
        6 * rows * width * hidden_width,
        out_shape=[
            jax.ShapeDtypeStruct((hidden_width, rows), BF16),
            jax.ShapeDtypeStruct((devices * block, width), BF16),
        ],
        in_specs=[scalar] + whole(5),
        out_specs=whole(2),
        scratch_shapes=[
            pltpu.VMEM((PER_STEP * capacity, width), BF16),
            pltpu.VMEM((PER_STEP * capacity, hidden_width), BF16),
            pltpu.VMEM((PER_STEP * capacity, TILE), F32),
        ],
    )(expert, meta, frames, w_gate, w_up, w_down)
    branch = lax.psum_scatter(dense, "expert", scatter_dimension=0, tiled=True)
    grad_down = call(
        functools.partial(grad_kernel, capacity),
        40,
        "grad",
        2 * rows * width * hidden_width,
        out_shape=jax.ShapeDtypeStruct((1, hidden_width, width), BF16),
        in_specs=[scalar] + whole(3),
        out_specs=whole(1)[0],
        scratch_shapes=[pltpu.VMEM((rows, width), BF16)],
    )(expert, meta, cots, turned)
    mixed = (tokens.astype(F32) + branch.astype(F32)).astype(BF16)
    return (mixed, grad_down)


def solution(mesh):
    placed = (
        P(("group", "expert"), None),
        P(("group", "expert"), None),
        P(("group", "expert"), None),
        P(("group", "expert"), None),
        P(),
        P("expert", None, None),
        P("expert", None, None),
        P("expert", None, None),
    )
    return jax.shard_map(
        on_device,
        mesh=mesh,
        in_specs=placed,
        out_specs=(P(("group", "expert"), None), P(("group", "expert"), None, None)),
        check_vma=False,
    )
```

```python
import functools

import jax
import jax.numpy as jnp
from jax import lax
from jax.experimental import pallas as pl
from jax.experimental.pallas import tpu as pltpu
from jax.sharding import PartitionSpec as P

HSPLIT = 4
GROUPS = 4
JOINED = ((1, 2), (2, 3))
TILE = 256
LINK_WORK = 10 << 30
F32 = jnp.float32
BF16 = jnp.bfloat16


def after(value, *earlier):
    return lax.optimization_barrier((value,) + earlier)[0]


def whole(count):
    return [pl.BlockSpec(memory_space=pltpu.VMEM)] * count


def call(kernel, mib, name, moved=0, **keywords):
    return pl.pallas_call(
        kernel,
        compiler_params=pltpu.CompilerParams(vmem_limit_bytes=mib << 20),
        cost_estimate=pl.CostEstimate(flops=moved, bytes_accessed=0, transcendentals=0),
        name=name,
        **keywords,
    )


def experts_of(plane, experts, rows):
    return lax.broadcasted_iota(jnp.int32, (experts, rows), 0) ^ plane


def placing_of(routes, plane, experts, capacity):
    rows = routes.shape[1]
    expert = experts_of(plane, experts, rows)
    member = jnp.zeros((experts, rows), jnp.bool_)
    for k in range(routes.shape[0]):
        member = member | (routes[k : k + 1, :] == expert)
    first = lax.broadcasted_iota(jnp.int32, (rows, rows), 0)
    second = lax.broadcasted_iota(jnp.int32, (rows, rows), 1)
    upto = (first <= second).astype(F32).astype(BF16)
    ones = member.astype(F32)
    count = jnp.dot(ones.astype(BF16), upto, preferred_element_type=F32)
    place = (ones * count).astype(jnp.int32) - 1
    slots = lax.broadcasted_iota(jnp.int32, (capacity, rows), 0)
    return [(slots == place[s : s + 1, :]).astype(F32) for s in range(experts)]


def gates_of(routes, numbers, plane, experts):
    expert = experts_of(plane, experts, routes.shape[1])
    numerators = numbers.astype(F32)
    gates = numerators / jnp.sum(numerators, 0, keepdims=True)
    gate = jnp.zeros(expert.shape, F32)
    for k in range(routes.shape[0]):
        gate = gate + jnp.where(routes[k : k + 1, :] == expert, gates[k : k + 1, :], 0.0)
    return gate


def fetch(semaphores, *pairs):
    copies = [
        pltpu.make_async_copy(source, target, semaphores.at[i])
        for i, (source, target) in enumerate(pairs)
    ]
    for copy in copies:
        copy.start()
    return copies


def send_kernel(experts, plane_ref, *refs):
    sources, refs = refs[:5], refs[5:]
    row_outs, grad_outs = refs[:experts], refs[experts : 2 * experts]
    targets, semaphores = refs[2 * experts : -1], refs[-1]
    tokens_ref, cot_ref, routes_ref, nums_ref, gain_ref = targets
    copies = fetch(semaphores, *zip(sources, targets))
    copies[2].wait()
    copies[3].wait()
    routes = routes_ref[...]
    placings = placing_of(routes, plane_ref[0], experts, row_outs[0].shape[0])
    gates = gates_of(routes, nums_ref[...], plane_ref[0], experts)
    copies[4].wait()
    copies[0].wait()
    frames = tokens_ref[...].astype(F32)
    inverse = lax.rsqrt(jnp.mean(frames * frames, -1, keepdims=True) + 1e-06)
    normed = (frames * inverse * gain_ref[...]).astype(BF16)
    for out, placing in zip(row_outs, placings):
        out[...] = jnp.dot(placing.astype(BF16), normed, preferred_element_type=F32).astype(BF16)
    copies[1].wait()
    cot = cot_ref[...]
    for s, (out, placing) in enumerate(zip(grad_outs, placings)):
        picked = jnp.dot(placing.astype(BF16), cot, preferred_element_type=F32)
        gate = jnp.sum(placing * gates[s : s + 1, :], -1, keepdims=True)
        out[...] = (gate * picked).astype(BF16)


def load_kernel(*refs):
    sources, outs, semaphores = refs[:3], refs[3:6], refs[6]
    copies = fetch(semaphores, *[(s.at[0], o) for s, o in zip(sources, outs)])
    for copy in copies:
        copy.wait()


def nothing(*refs):
    pass


def through(values, name, moved=0):
    count = len(values)
    return call(
        nothing,
        4,
        name,
        moved,
        out_shape=[jax.ShapeDtypeStruct(v.shape, v.dtype) for v in values],
        in_specs=whole(count),
        out_specs=whole(count),
        input_output_aliases={i: i for i in range(count)},
    )(*values)


def ffn_kernel(count, *refs):
    pieces, refs = refs[:count], refs[count:]
    gate_ref, up_ref, down_ref, turned_ref, keep_ref, send_ref, rows_ref, hidden_ref = refs
    at = 0
    for piece in pieces:
        rows_ref[at : at + piece.shape[0], :] = piece[...]
        at += piece.shape[0]
    rows = rows_ref[...]
    half = keep_ref.shape[0]
    for j in range(gate_ref.shape[1] // TILE):
        columns = slice(j * TILE, (j + 1) * TILE)
        pre_gate = jnp.dot(rows, gate_ref[:, columns], preferred_element_type=F32)
        pre_up = jnp.dot(rows, up_ref[:, columns], preferred_element_type=F32)
        hidden = pre_gate * lax.logistic(pre_gate) * pre_up
        hidden_ref[:, columns] = hidden.astype(BF16)
        turned_ref[columns, :] = hidden.T.astype(BF16)
    for j in range(down_ref.shape[1] // TILE):
        columns = slice(j * TILE, (j + 1) * TILE)
        value = jnp.dot(
            hidden_ref[...], down_ref[:, columns], preferred_element_type=F32
        ).astype(BF16)
        keep_ref[:, columns] = value[:half]
        send_ref[:, columns] = value[half:]


def gather_grad(plan, refs, hidden_ref, cot_ref):
    at = 0
    for turned, column, piece, row, count in plan:
        hidden_ref[:, at : at + count] = refs[turned][:, column : column + count]
        cot_ref[at : at + count, :] = refs[piece][row : row + count, :]
        at += count


def first_grad_kernel(plan, *refs):
    out_ref, hidden_ref, cot_ref = refs[-3:]
    gather_grad(plan, refs, hidden_ref, cot_ref)
    for j in range(out_ref.shape[0] // TILE):
        part = slice(j * TILE, (j + 1) * TILE)
        out_ref[part, :] = jnp.dot(
            hidden_ref[part, :], cot_ref[...], preferred_element_type=F32
        )


def last_grad_kernel(plan, first_ref, *refs):
    out_hbm, out_ref, hidden_ref, cot_ref, semaphores = refs[-5:]
    gather_grad(plan, refs, hidden_ref, cot_ref)
    copies = []
    for j in range(first_ref.shape[0] // TILE):
        part = slice(j * TILE, (j + 1) * TILE)
        total = jnp.dot(hidden_ref[part, :], cot_ref[...], preferred_element_type=F32)
        out_ref[part, :] = (first_ref[part, :] + total).astype(BF16)
        copies.append(
            pltpu.make_async_copy(out_ref.at[part, :], out_hbm.at[0, part, :], semaphores.at[j])
        )
        copies[-1].start()
    for copy in copies:
        copy.wait()


def combine_kernel(experts, plane_ref, tokens_ref, routes_ref, nums_ref, *refs):
    values, out = refs[:-1], refs[-1]
    routes = routes_ref[...]
    placings = placing_of(routes, plane_ref[0], experts, values[0].shape[0])
    gates = gates_of(routes, nums_ref[...], plane_ref[0], experts)
    fill = -experts % 8
    if fill:
        gates = jnp.concatenate([gates, jnp.zeros((fill, gates.shape[1]), F32)], 0)
    gates = gates.T
    total = tokens_ref[...].astype(F32)
    for s, value in enumerate(values):
        picked = lax.dot_general(
            placings[s].astype(BF16),
            value[...],
            (((0,), (0,)), ((), ())),
            preferred_element_type=F32,
        )
        total = total + gates[:, s : s + 1] * picked
    out[...] = total.astype(BF16)


def on_device(tokens, cotangent, routes, gate_nums, gain, w_gate, w_up, w_down):
    devices = lax.axis_size("expert")
    experts = devices // HSPLIT
    rows_here, width = tokens.shape
    hidden_width = w_gate.shape[2]
    top_count = routes.shape[1]
    capacity = HSPLIT * (3 * top_count * rows_here // (2 * experts * HSPLIT))
    capacity = -(-capacity // 16) * 16
    shifts = max(1, experts // GROUPS)
    groups = [list(range(g, g + shifts)) for g in range(0, experts, shifts)]
    height = shifts * capacity
    plane = (lax.axis_index("expert") // HSPLIT).astype(jnp.int32).reshape(1)
    routes, gate_nums, gain = routes.T, gate_nums.T, gain.reshape(1, -1)
    scalar = pl.BlockSpec(memory_space=pltpu.SMEM)
    anywhere = pl.BlockSpec(memory_space=pl.ANY)
    piece = jax.ShapeDtypeStruct((capacity, width), BF16)
    live = {}

    def swap(value, mask):
        return lax.ppermute(value, "expert", [(i, i ^ mask) for i in range(devices)])

    def sync():
        values = lax.optimization_barrier(tuple(live.values()))
        live.update(zip(list(live), values))

    def join(parts):
        return parts[0] if len(parts) == 1 else jnp.concatenate(parts, 0)

    flying = {}

    def launch(name, value, mask):
        flying[name] = swap(value, mask)

    def land(*earlier):
        names = list(flying)
        values = [flying.pop(name) for name in names]
        values = lax.optimization_barrier(tuple(values) + earlier)[: len(names)]
        values = through(values, "land", LINK_WORK)
        for name, value in zip(names, values):
            if name[0] != "y":
                live[name] = value
                continue
            at = 0
            for kind, gs in name[1:]:
                here = live.pop(("sent", kind, gs))
                came = value[at : at + here.shape[0]]
                at += here.shape[0]
                if kind != "fold":
                    live[kind, "own", gs] = join([here, came])
                    continue
                keep, crossed = live.pop(("keep", gs)), live.pop(("crossed", gs))
                rows = came.shape[0]
                total = keep[:rows].astype(F32) + crossed[:rows].astype(F32)
                total = (total + came.astype(F32)).astype(BF16)
                for i, s in enumerate([s for g in gs for s in groups[g]]):
                    live["R", s] = total[i * capacity : (i + 1) * capacity]
        return values[0]

    def across(kind, *gs):
        for s in [s for g in gs for s in groups[g]]:
            if s:
                launch((kind, s), live[kind, s], s * HSPLIT)

    def along(*items):
        for kind, gs in items:
            if kind == "fold":
                value = live.pop(("across", gs))
            else:
                value = join([live.pop((kind, s)) for g in gs for s in groups[g]])
            live["sent", kind, gs] = value
        launch(("y",) + items, join([live["sent", kind, gs] for kind, gs in items]), 2)

    def core(kind, *tuples):
        gs = tuple(g for part in tuples for g in part)
        live[kind, "other", gs] = swap(join([live[kind, "own", part] for part in tuples]), 1)

    def ffn(*gs):
        pieces = [live.pop(("N", "own", gs)), live.pop(("N", "other", gs))]
        half = jax.ShapeDtypeStruct(pieces[0].shape, BF16)
        rows = 2 * half.shape[0]
        live["turned", gs], live["keep", gs], live["send", gs] = call(
            functools.partial(ffn_kernel, len(pieces)),
            24,
            "ffn",
            out_shape=[jax.ShapeDtypeStruct((hidden_width, rows), BF16), half, half],
            in_specs=whole(len(pieces) + 3),
            out_specs=whole(3),
            scratch_shapes=[
                pltpu.VMEM((rows, width), BF16),
                pltpu.VMEM((rows, hidden_width), BF16),
            ],
        )(*pieces, live["w", 0], live["w", 1], live["w", 2])

    def cross(*gs):
        live["crossed", gs] = swap(live.pop(("send", gs)), 1)

    def fold_core(earlier, *gs):
        keep, crossed = live["keep", gs], after(live["crossed", gs], earlier)
        rows = keep.shape[0] // 2
        both = keep[rows:].astype(F32) + crossed[rows:].astype(F32)
        live["across", gs] = both.astype(BF16)

    def in_hbm(*values):
        return [pltpu.with_memory_space_constraint(v, pltpu.HBM) for v in values]

    def send():
        sources = (tokens, cotangent, routes, gate_nums, gain)
        values = call(
            functools.partial(send_kernel, experts),
            16,
            "send",
            out_shape=[piece] * (2 * experts),
            in_specs=[scalar] + [anywhere] * len(sources),
            out_specs=whole(2 * experts),
            scratch_shapes=[pltpu.VMEM(v.shape, v.dtype) for v in sources]
            + [pltpu.SemaphoreType.DMA((len(sources),))],
        )(plane, *in_hbm(*sources))
        live.update({("N", s): value for s, value in enumerate(values[:experts])})
        live.update({("C", s): value for s, value in enumerate(values[experts:])})

    def load():
        weight = jax.ShapeDtypeStruct((width, hidden_width), BF16)
        values = call(
            load_kernel,
            16,
            "load",
            out_shape=[weight, weight, jax.ShapeDtypeStruct((hidden_width, width), BF16)],
            in_specs=[anywhere] * 3,
            out_specs=whole(3),
            scratch_shapes=[pltpu.SemaphoreType.DMA((3,))],
        )(*in_hbm(after(w_gate, live["C", experts - 1]), w_up, w_down))
        live.update({("w", i): value for i, value in enumerate(values)})

    def grad_call(turned, pieces):
        columns = {}
        for i, gs in enumerate(turned):
            at = 0
            for half in ("own", "other"):
                for side in range(2):
                    for g in gs:
                        columns[half, side, g] = (i, at)
                        at += height
        plan = []
        for i, (half, gs) in enumerate(pieces):
            row = 0
            for parts in [gs] if gs in JOINED else [(g,) for g in gs]:
                for side in range(2):
                    for g in parts:
                        where, at = columns[half, side, g]
                        plan.append((where, at, len(turned) + i, row, height))
                        row += height
        total = sum(step[-1] for step in plan)
        sides = [pltpu.VMEM((hidden_width, total), BF16), pltpu.VMEM((total, width), BF16)]
        values = [live["turned", gs] for gs in turned]
        values += [live["C", half, gs] for half, gs in pieces]
        return plan, sides, values

    def first_grad(turned, pieces):
        plan, sides, values = grad_call(turned, pieces)
        live["first"] = call(
            functools.partial(first_grad_kernel, plan),
            24,
            "first_grad",
            out_shape=jax.ShapeDtypeStruct((hidden_width, width), F32),
            in_specs=whole(len(values)),
            out_specs=whole(1)[0],
            scratch_shapes=sides,
        )(*values)

    def last_grad(turned, pieces):
        plan, sides, values = grad_call(turned, pieces)
        return call(
            functools.partial(last_grad_kernel, plan),
            24,
            "last_grad",
            out_shape=jax.ShapeDtypeStruct((1, hidden_width, width), BF16),
            in_specs=whole(1 + len(values)),
            out_specs=anywhere,
            scratch_shapes=[pltpu.VMEM((hidden_width, width), BF16)]
            + sides
            + [pltpu.SemaphoreType.DMA((hidden_width // TILE,))],
        )(live["first"], *values)

    send()
    if shifts > 1:
        across("N", 0)
        across("C", 0)
        land()
    sync()
    across("N", 1, 2)
    along(("N", (0,)), ("C", (0,)))
    load()
    land()
    sync()
    across("N", 3)
    across("C", 1)
    along(("N", (1, 2)))
    core("N", (0,))
    ffn(0)
    cross(0)
    fold_core(land(), 0)
    sync()
    across("C", 2)
    along(("N", (3,)), ("fold", (0,)))
    core("N", (1, 2))
    ffn(1, 2)
    cross(1, 2)
    fold_core(land(), 1, 2)
    sync()
    across("C", 3)
    along(("fold", (1, 2)))
    core("N", (3,))
    ffn(3)
    cross(3)
    fold_core(land(), 3)
    sync()
    if shifts > 1:
        across("R", 0)
    across("R", 1, 2)
    along(("fold", (3,)), ("C", (1,)))
    land()
    sync()
    across("R", 3)
    along(("C", (2, 3)))
    core("C", (0,), (1,))
    first_grad([(0,), (1, 2)], [("own", (0,)), ("own", (1,)), ("other", (0, 1))])
    land(live["first"])
    sync()
    core("C", (2, 3))
    grad_down = last_grad([(1, 2), (3,)], [("own", (2, 3)), ("other", (2, 3))])
    mixed = call(
        functools.partial(combine_kernel, experts),
        16,
        "combine",
        out_shape=jax.ShapeDtypeStruct(tokens.shape, BF16),
        in_specs=[scalar] + whole(3 + experts),
        out_specs=whole(1)[0],
    )(plane, tokens, routes, gate_nums, *[live["R", s] for s in range(experts)])
    return (mixed, grad_down)


def solution(mesh):
    placed = (
        P(("group", "expert"), None),
        P(("group", "expert"), None),
        P(("group", "expert"), None),
        P(("group", "expert"), None),
        P(),
        P("expert", None, None),
        P("expert", None, None),
        P("expert", None, None),
    )
    return jax.shard_map(
        on_device,
        mesh=mesh,
        in_specs=placed,
        out_specs=(P(("group", "expert"), None), P(("group", "expert"), None, None)),
        check_vma=False,
    )
```

```python
import functools

import jax
import jax.numpy as jnp
from jax import lax
from jax.experimental import pallas as pl
from jax.experimental.pallas import tpu as pltpu
from jax.sharding import PartitionSpec as P

HSPLIT = 4
GROUPS = 4
JOINED = ((1, 2), (2, 3))
TILE = 256
LINK_WORK = 10 << 30
F32 = jnp.float32
BF16 = jnp.bfloat16


def after(value, *earlier):
    return lax.optimization_barrier((value,) + earlier)[0]


def whole(count):
    return [pl.BlockSpec(memory_space=pltpu.VMEM)] * count


def call(kernel, mib, name, moved=0, **keywords):
    return pl.pallas_call(
        kernel,
        compiler_params=pltpu.CompilerParams(vmem_limit_bytes=mib << 20),
        cost_estimate=pl.CostEstimate(flops=moved, bytes_accessed=0, transcendentals=0),
        name=name,
        **keywords,
    )


def experts_of(plane, experts, rows):
    return lax.broadcasted_iota(jnp.int32, (experts, rows), 0) ^ plane


def placing_of(routes, plane, experts, capacity):
    rows = routes.shape[1]
    expert = experts_of(plane, experts, rows)
    member = jnp.zeros((experts, rows), jnp.bool_)
    for k in range(routes.shape[0]):
        member = member | (routes[k : k + 1, :] == expert)
    first = lax.broadcasted_iota(jnp.int32, (rows, rows), 0)
    second = lax.broadcasted_iota(jnp.int32, (rows, rows), 1)
    upto = (first <= second).astype(F32).astype(BF16)
    ones = member.astype(F32)
    count = jnp.dot(ones.astype(BF16), upto, preferred_element_type=F32)
    place = (ones * count).astype(jnp.int32) - 1
    slots = lax.broadcasted_iota(jnp.int32, (capacity, rows), 0)
    return [(slots == place[s : s + 1, :]).astype(F32) for s in range(experts)]


def gates_of(routes, numbers, plane, experts):
    expert = experts_of(plane, experts, routes.shape[1])
    numerators = numbers.astype(F32)
    gates = numerators / jnp.sum(numerators, 0, keepdims=True)
    gate = jnp.zeros(expert.shape, F32)
    for k in range(routes.shape[0]):
        gate = gate + jnp.where(routes[k : k + 1, :] == expert, gates[k : k + 1, :], 0.0)
    return gate


def fetch(semaphores, *pairs):
    copies = [
        pltpu.make_async_copy(source, target, semaphores.at[i])
        for i, (source, target) in enumerate(pairs)
    ]
    for copy in copies:
        copy.start()
    return copies


def send_kernel(experts, plane_ref, *refs):
    sources, refs = refs[:5], refs[5:]
    row_outs, grad_outs = refs[:experts], refs[experts : 2 * experts]
    targets, semaphores = refs[2 * experts : -1], refs[-1]
    tokens_ref, cot_ref, routes_ref, nums_ref, gain_ref = targets
    copies = fetch(semaphores, *zip(sources, targets))
    copies[2].wait()
    copies[3].wait()
    routes = routes_ref[...]
    placings = placing_of(routes, plane_ref[0], experts, row_outs[0].shape[0])
    gates = gates_of(routes, nums_ref[...], plane_ref[0], experts)
    copies[4].wait()
    copies[0].wait()
    frames = tokens_ref[...].astype(F32)
    inverse = lax.rsqrt(jnp.mean(frames * frames, -1, keepdims=True) + 1e-06)
    normed = (frames * inverse * gain_ref[...]).astype(BF16)
    for out, placing in zip(row_outs, placings):
        out[...] = jnp.dot(placing.astype(BF16), normed, preferred_element_type=F32).astype(BF16)
    copies[1].wait()
    cot = cot_ref[...]
    for s, (out, placing) in enumerate(zip(grad_outs, placings)):
        picked = jnp.dot(placing.astype(BF16), cot, preferred_element_type=F32)
        gate = jnp.sum(placing * gates[s : s + 1, :], -1, keepdims=True)
        out[...] = (gate * picked).astype(BF16)


def load_kernel(*refs):
    sources, outs, semaphores = refs[:3], refs[3:6], refs[6]
    copies = fetch(semaphores, *[(s.at[0], o) for s, o in zip(sources, outs)])
    for copy in copies:
        copy.wait()


def nothing(*refs):
    pass


def through(values, name, moved=0):
    count = len(values)
    return call(
        nothing,
        4,
        name,
        moved,
        out_shape=[jax.ShapeDtypeStruct(v.shape, v.dtype) for v in values],
        in_specs=whole(count),
        out_specs=whole(count),
        input_output_aliases={i: i for i in range(count)},
    )(*values)


def ffn_kernel(count, *refs):
    pieces, refs = refs[:count], refs[count:]
    gate_ref, up_ref, down_ref, turned_ref, keep_ref, send_ref, rows_ref, hidden_ref = refs
    at = 0
    for piece in pieces:
        rows_ref[at : at + piece.shape[0], :] = piece[...]
        at += piece.shape[0]
    rows = rows_ref[...]
    half = keep_ref.shape[0]
    for j in range(gate_ref.shape[1] // TILE):
        columns = slice(j * TILE, (j + 1) * TILE)
        pre_gate = jnp.dot(rows, gate_ref[:, columns], preferred_element_type=F32)
        pre_up = jnp.dot(rows, up_ref[:, columns], preferred_element_type=F32)
        hidden = pre_gate * lax.logistic(pre_gate) * pre_up
        hidden_ref[:, columns] = hidden.astype(BF16)
        turned_ref[columns, :] = hidden.T.astype(BF16)
    for j in range(down_ref.shape[1] // TILE):
        columns = slice(j * TILE, (j + 1) * TILE)
        value = jnp.dot(
            hidden_ref[...], down_ref[:, columns], preferred_element_type=F32
        ).astype(BF16)
        keep_ref[:, columns] = value[:half]
        send_ref[:, columns] = value[half:]


def gather_grad(plan, refs, hidden_ref, cot_ref):
    at = 0
    for turned, column, piece, row, count in plan:
        hidden_ref[:, at : at + count] = refs[turned][:, column : column + count]
        cot_ref[at : at + count, :] = refs[piece][row : row + count, :]
        at += count


def first_grad_kernel(plan, *refs):
    out_ref, hidden_ref, cot_ref = refs[-3:]
    gather_grad(plan, refs, hidden_ref, cot_ref)
    for j in range(out_ref.shape[0] // TILE):
        part = slice(j * TILE, (j + 1) * TILE)
        out_ref[part, :] = jnp.dot(
            hidden_ref[part, :], cot_ref[...], preferred_element_type=F32
        )


def last_grad_kernel(plan, first_ref, *refs):
    out_hbm, out_ref, hidden_ref, cot_ref, semaphores = refs[-5:]
    gather_grad(plan, refs, hidden_ref, cot_ref)
    copies = []
    for j in range(first_ref.shape[0] // TILE):
        part = slice(j * TILE, (j + 1) * TILE)
        total = jnp.dot(hidden_ref[part, :], cot_ref[...], preferred_element_type=F32)
        out_ref[part, :] = (first_ref[part, :] + total).astype(BF16)
        copies.append(
            pltpu.make_async_copy(out_ref.at[part, :], out_hbm.at[0, part, :], semaphores.at[j])
        )
        copies[-1].start()
    for copy in copies:
        copy.wait()


def combine_kernel(experts, plane_ref, tokens_ref, routes_ref, nums_ref, *refs):
    values, out = refs[:-1], refs[-1]
    routes = routes_ref[...]
    placings = placing_of(routes, plane_ref[0], experts, values[0].shape[0])
    gates = gates_of(routes, nums_ref[...], plane_ref[0], experts)
    fill = -experts % 8
    if fill:
        gates = jnp.concatenate([gates, jnp.zeros((fill, gates.shape[1]), F32)], 0)
    gates = gates.T
    total = tokens_ref[...].astype(F32)
    for s, value in enumerate(values):
        picked = lax.dot_general(
            placings[s].astype(BF16),
            value[...],
            (((0,), (0,)), ((), ())),
            preferred_element_type=F32,
        )
        total = total + gates[:, s : s + 1] * picked
    out[...] = total.astype(BF16)


def on_device(tokens, cotangent, routes, gate_nums, gain, w_gate, w_up, w_down):
    devices = lax.axis_size("expert")
    experts = devices // HSPLIT
    rows_here, width = tokens.shape
    hidden_width = w_gate.shape[2]
    top_count = routes.shape[1]
    capacity = HSPLIT * (3 * top_count * rows_here // (2 * experts * HSPLIT))
    capacity = -(-capacity // 16) * 16
    shifts = max(1, experts // GROUPS)
    groups = [list(range(g, g + shifts)) for g in range(0, experts, shifts)]
    height = shifts * capacity
    plane = (lax.axis_index("expert") // HSPLIT).astype(jnp.int32).reshape(1)
    routes, gate_nums, gain = routes.T, gate_nums.T, gain.reshape(1, -1)
    scalar = pl.BlockSpec(memory_space=pltpu.SMEM)
    anywhere = pl.BlockSpec(memory_space=pl.ANY)
    piece = jax.ShapeDtypeStruct((capacity, width), BF16)
    live = {}

    def swap(value, mask):
        return lax.ppermute(value, "expert", [(i, i ^ mask) for i in range(devices)])

    def sync():
        values = lax.optimization_barrier(tuple(live.values()))
        live.update(zip(list(live), values))

    def join(parts):
        return parts[0] if len(parts) == 1 else jnp.concatenate(parts, 0)

    flying = {}

    def launch(name, value, mask):
        flying[name] = swap(value, mask)

    def land(*earlier):
        names = list(flying)
        values = [flying.pop(name) for name in names]
        if earlier:
            values = lax.optimization_barrier(tuple(values) + earlier)[: len(names)]
        values = through(values, "land", LINK_WORK)
        for name, value in zip(names, values):
            if name[0] != "y":
                live[name] = value
                continue
            at = 0
            for kind, gs in name[1:]:
                here = live.pop(("sent", kind, gs))
                came = value[at : at + here.shape[0]]
                at += here.shape[0]
                if kind != "fold":
                    live[kind, "own", gs] = join([here, came])
                    continue
                keep, crossed = live.pop(("keep", gs)), live.pop(("crossed", gs))
                rows = came.shape[0]
                total = keep[:rows].astype(F32) + crossed[:rows].astype(F32)
                total = (total + came.astype(F32)).astype(BF16)
                for i, s in enumerate([s for g in gs for s in groups[g]]):
                    live["R", s] = total[i * capacity : (i + 1) * capacity]
        return values[0]

    def across(kind, *gs):
        for s in [s for g in gs for s in groups[g]]:
            if s:
                launch((kind, s), live[kind, s], s * HSPLIT)

    def along(*items):
        for kind, gs in items:
            if kind == "fold":
                value = live.pop(("across", gs))
            else:
                value = join([live.pop((kind, s)) for g in gs for s in groups[g]])
            live["sent", kind, gs] = value
        launch(("y",) + items, join([live["sent", kind, gs] for kind, gs in items]), 2)

    def core(kind, *tuples):
        gs = tuple(g for part in tuples for g in part)
        live[kind, "other", gs] = swap(join([live[kind, "own", part] for part in tuples]), 1)

    def ffn(*gs):
        pieces = [live.pop(("N", "own", gs)), live.pop(("N", "other", gs))]
        half = jax.ShapeDtypeStruct(pieces[0].shape, BF16)
        rows = 2 * half.shape[0]
        live["turned", gs], live["keep", gs], live["send", gs] = call(
            functools.partial(ffn_kernel, len(pieces)),
            24,
            "ffn",
            out_shape=[jax.ShapeDtypeStruct((hidden_width, rows), BF16), half, half],
            in_specs=whole(len(pieces) + 3),
            out_specs=whole(3),
            scratch_shapes=[
                pltpu.VMEM((rows, width), BF16),
                pltpu.VMEM((rows, hidden_width), BF16),
            ],
        )(*pieces, live["w", 0], live["w", 1], live["w", 2])

    def cross(*gs):
        live["crossed", gs] = swap(live.pop(("send", gs)), 1)

    def fold_core(earlier, *gs):
        keep, crossed = live["keep", gs], after(live["crossed", gs], earlier)
        rows = keep.shape[0] // 2
        both = keep[rows:].astype(F32) + crossed[rows:].astype(F32)
        live["across", gs] = both.astype(BF16)

    def in_hbm(*values):
        return [pltpu.with_memory_space_constraint(v, pltpu.HBM) for v in values]

    def send():
        sources = (tokens, cotangent, routes, gate_nums, gain)
        values = call(
            functools.partial(send_kernel, experts),
            16,
            "send",
            out_shape=[piece] * (2 * experts),
            in_specs=[scalar] + [anywhere] * len(sources),
            out_specs=whole(2 * experts),
            scratch_shapes=[pltpu.VMEM(v.shape, v.dtype) for v in sources]
            + [pltpu.SemaphoreType.DMA((len(sources),))],
        )(plane, *in_hbm(*sources))
        live.update({("N", s): value for s, value in enumerate(values[:experts])})
        live.update({("C", s): value for s, value in enumerate(values[experts:])})

    def load():
        weight = jax.ShapeDtypeStruct((width, hidden_width), BF16)
        values = call(
            load_kernel,
            16,
            "load",
            out_shape=[weight, weight, jax.ShapeDtypeStruct((hidden_width, width), BF16)],
            in_specs=[anywhere] * 3,
            out_specs=whole(3),
            scratch_shapes=[pltpu.SemaphoreType.DMA((3,))],
        )(*in_hbm(after(w_gate, live["C", experts - 1]), w_up, w_down))
        live.update({("w", i): value for i, value in enumerate(values)})

    def grad_call(turned, pieces):
        columns = {}
        for i, gs in enumerate(turned):
            at = 0
            for half in ("own", "other"):
                for side in range(2):
                    for g in gs:
                        columns[half, side, g] = (i, at)
                        at += height
        plan = []
        for i, (half, gs) in enumerate(pieces):
            row = 0
            for parts in [gs] if gs in JOINED else [(g,) for g in gs]:
                for side in range(2):
                    for g in parts:
                        where, at = columns[half, side, g]
                        plan.append((where, at, len(turned) + i, row, height))
                        row += height
        total = sum(step[-1] for step in plan)
        sides = [pltpu.VMEM((hidden_width, total), BF16), pltpu.VMEM((total, width), BF16)]
        values = [live["turned", gs] for gs in turned]
        values += [live["C", half, gs] for half, gs in pieces]
        return plan, sides, values

    def first_grad(turned, pieces):
        plan, sides, values = grad_call(turned, pieces)
        live["first"] = call(
            functools.partial(first_grad_kernel, plan),
            24,
            "first_grad",
            out_shape=jax.ShapeDtypeStruct((hidden_width, width), F32),
            in_specs=whole(len(values)),
            out_specs=whole(1)[0],
            scratch_shapes=sides,
        )(*values)

    def last_grad(turned, pieces):
        plan, sides, values = grad_call(turned, pieces)
        return call(
            functools.partial(last_grad_kernel, plan),
            24,
            "last_grad",
            out_shape=jax.ShapeDtypeStruct((1, hidden_width, width), BF16),
            in_specs=whole(1 + len(values)),
            out_specs=anywhere,
            scratch_shapes=[pltpu.VMEM((hidden_width, width), BF16)]
            + sides
            + [pltpu.SemaphoreType.DMA((hidden_width // TILE,))],
        )(live["first"], *values)

    send()
    if shifts > 1:
        across("N", 0)
        across("C", 0)
        land()
    sync()
    across("N", 1, 2)
    along(("N", (0,)), ("C", (0,)))
    load()
    land()
    sync()
    across("N", 3)
    across("C", 1)
    along(("N", (1, 2)))
    core("N", (0,))
    ffn(0)
    cross(0)
    fold_core(land(), 0)
    sync()
    across("C", 2)
    along(("N", (3,)), ("fold", (0,)))
    core("N", (1, 2))
    ffn(1, 2)
    cross(1, 2)
    fold_core(land(), 1, 2)
    sync()
    across("C", 3)
    along(("fold", (1, 2)))
    core("N", (3,))
    ffn(3)
    cross(3)
    fold_core(land(), 3)
    sync()
    if shifts > 1:
        across("R", 0)
    across("R", 1, 2)
    along(("fold", (3,)), ("C", (1,)))
    land()
    sync()
    across("R", 3)
    along(("C", (2, 3)))
    core("C", (0,), (1,))
    first_grad([(0,), (1, 2)], [("own", (0,)), ("own", (1,)), ("other", (0, 1))])
    land(live["first"])
    sync()
    core("C", (2, 3))
    grad_down = last_grad([(1, 2), (3,)], [("own", (2, 3)), ("other", (2, 3))])
    mixed = call(
        functools.partial(combine_kernel, experts),
        16,
        "combine",
        out_shape=jax.ShapeDtypeStruct(tokens.shape, BF16),
        in_specs=[scalar] + whole(3 + experts),
        out_specs=whole(1)[0],
    )(plane, tokens, routes, gate_nums, *[live["R", s] for s in range(experts)])
    return (mixed, grad_down)


def solution(mesh):
    placed = (
        P(("group", "expert"), None),
        P(("group", "expert"), None),
        P(("group", "expert"), None),
        P(("group", "expert"), None),
        P(),
        P("expert", None, None),
        P("expert", None, None),
        P("expert", None, None),
    )
    return jax.shard_map(
        on_device,
        mesh=mesh,
        in_specs=placed,
        out_specs=(P(("group", "expert"), None), P(("group", "expert"), None, None)),
        check_vma=False,
    )
```

```python
import functools

import jax
import jax.numpy as jnp
from jax import lax
from jax.experimental import pallas as pl
from jax.experimental.pallas import tpu as pltpu
from jax.sharding import PartitionSpec as P

HSPLIT = 4
GROUPS = 4
JOINED = ((1, 2), (2, 3))
TILE = 256
LINK_WORK = 10 << 30
F32 = jnp.float32
BF16 = jnp.bfloat16


def after(value, *earlier):
    return lax.optimization_barrier((value,) + earlier)[0]


def whole(count):
    return [pl.BlockSpec(memory_space=pltpu.VMEM)] * count


def call(kernel, mib, name, moved=0, **keywords):
    return pl.pallas_call(
        kernel,
        compiler_params=pltpu.CompilerParams(vmem_limit_bytes=mib << 20),
        cost_estimate=pl.CostEstimate(flops=moved, bytes_accessed=0, transcendentals=0),
        name=name,
        **keywords,
    )


def experts_of(plane, experts, rows):
    ahead = lax.broadcasted_iota(jnp.int32, (experts, rows), 0) + plane
    return jnp.where(ahead >= experts, ahead - experts, ahead)


def placing_of(routes, plane, experts, capacity):
    rows = routes.shape[1]
    expert = experts_of(plane, experts, rows)
    member = jnp.zeros((experts, rows), jnp.bool_)
    for k in range(routes.shape[0]):
        member = member | (routes[k : k + 1, :] == expert)
    first = lax.broadcasted_iota(jnp.int32, (rows, rows), 0)
    second = lax.broadcasted_iota(jnp.int32, (rows, rows), 1)
    upto = (first <= second).astype(F32).astype(BF16)
    ones = member.astype(F32)
    count = jnp.dot(ones.astype(BF16), upto, preferred_element_type=F32)
    place = (ones * count).astype(jnp.int32) - 1
    slots = lax.broadcasted_iota(jnp.int32, (capacity, rows), 0)
    return [(slots == place[s : s + 1, :]).astype(F32) for s in range(experts)]


def gates_of(routes, numbers, plane, experts):
    expert = experts_of(plane, experts, routes.shape[1])
    numerators = numbers.astype(F32)
    gates = numerators / jnp.sum(numerators, 0, keepdims=True)
    gate = jnp.zeros(expert.shape, F32)
    for k in range(routes.shape[0]):
        gate = gate + jnp.where(routes[k : k + 1, :] == expert, gates[k : k + 1, :], 0.0)
    return gate


def fetch(semaphores, *pairs):
    copies = [
        pltpu.make_async_copy(source, target, semaphores.at[i])
        for i, (source, target) in enumerate(pairs)
    ]
    for copy in copies:
        copy.start()
    return copies


def send_kernel(experts, plane_ref, *refs):
    sources, refs = refs[:5], refs[5:]
    row_outs, grad_outs = refs[:experts], refs[experts : 2 * experts]
    targets, semaphores = refs[2 * experts : -1], refs[-1]
    tokens_ref, cot_ref, routes_ref, nums_ref, gain_ref = targets
    copies = fetch(semaphores, *zip(sources, targets))
    copies[2].wait()
    copies[3].wait()
    routes = routes_ref[...]
    placings = placing_of(routes, plane_ref[0], experts, row_outs[0].shape[0])
    gates = gates_of(routes, nums_ref[...], plane_ref[0], experts)
    copies[4].wait()
    copies[0].wait()
    frames = tokens_ref[...].astype(F32)
    inverse = lax.rsqrt(jnp.mean(frames * frames, -1, keepdims=True) + 1e-06)
    normed = (frames * inverse * gain_ref[...]).astype(BF16)
    for out, placing in zip(row_outs, placings):
        out[...] = jnp.dot(placing.astype(BF16), normed, preferred_element_type=F32).astype(BF16)
    copies[1].wait()
    cot = cot_ref[...]
    for s, (out, placing) in enumerate(zip(grad_outs, placings)):
        picked = jnp.dot(placing.astype(BF16), cot, preferred_element_type=F32)
        gate = jnp.sum(placing * gates[s : s + 1, :], -1, keepdims=True)
        out[...] = (gate * picked).astype(BF16)


def load_kernel(*refs):
    sources, outs, semaphores = refs[:3], refs[3:6], refs[6]
    copies = fetch(semaphores, *[(s.at[0], o) for s, o in zip(sources, outs)])
    for copy in copies:
        copy.wait()


def nothing(*refs):
    pass


def through(values, name, moved=0):
    count = len(values)
    return call(
        nothing,
        4,
        name,
        moved,
        out_shape=[jax.ShapeDtypeStruct(v.shape, v.dtype) for v in values],
        in_specs=whole(count),
        out_specs=whole(count),
        input_output_aliases={i: i for i in range(count)},
    )(*values)


def ffn_kernel(count, *refs):
    pieces, refs = refs[:count], refs[count:]
    gate_ref, up_ref, down_ref, turned_ref, keep_ref, send_ref, rows_ref, hidden_ref = refs
    at = 0
    for piece in pieces:
        rows_ref[at : at + piece.shape[0], :] = piece[...]
        at += piece.shape[0]
    rows = rows_ref[...]
    half = keep_ref.shape[0]
    for j in range(gate_ref.shape[1] // TILE):
        columns = slice(j * TILE, (j + 1) * TILE)
        pre_gate = jnp.dot(rows, gate_ref[:, columns], preferred_element_type=F32)
        pre_up = jnp.dot(rows, up_ref[:, columns], preferred_element_type=F32)
        hidden = pre_gate * lax.logistic(pre_gate) * pre_up
        hidden_ref[:, columns] = hidden.astype(BF16)
        turned_ref[columns, :] = hidden.T.astype(BF16)
    for j in range(down_ref.shape[1] // TILE):
        columns = slice(j * TILE, (j + 1) * TILE)
        value = jnp.dot(
            hidden_ref[...], down_ref[:, columns], preferred_element_type=F32
        ).astype(BF16)
        keep_ref[:, columns] = value[:half]
        send_ref[:, columns] = value[half:]


def gather_grad(plan, refs, hidden_ref, cot_ref):
    at = 0
    for turned, column, piece, row, count in plan:
        hidden_ref[:, at : at + count] = refs[turned][:, column : column + count]
        cot_ref[at : at + count, :] = refs[piece][row : row + count, :]
        at += count


def first_grad_kernel(plan, *refs):
    out_ref, hidden_ref, cot_ref = refs[-3:]
    gather_grad(plan, refs, hidden_ref, cot_ref)
    for j in range(out_ref.shape[0] // TILE):
        part = slice(j * TILE, (j + 1) * TILE)
        out_ref[part, :] = jnp.dot(
            hidden_ref[part, :], cot_ref[...], preferred_element_type=F32
        )


def last_grad_kernel(plan, first_ref, *refs):
    out_hbm, out_ref, hidden_ref, cot_ref, semaphores = refs[-5:]
    gather_grad(plan, refs, hidden_ref, cot_ref)
    copies = []
    for j in range(first_ref.shape[0] // TILE):
        part = slice(j * TILE, (j + 1) * TILE)
        total = jnp.dot(hidden_ref[part, :], cot_ref[...], preferred_element_type=F32)
        out_ref[part, :] = (first_ref[part, :] + total).astype(BF16)
        copies.append(
            pltpu.make_async_copy(out_ref.at[part, :], out_hbm.at[0, part, :], semaphores.at[j])
        )
        copies[-1].start()
    for copy in copies:
        copy.wait()


def combine_kernel(experts, plane_ref, tokens_ref, routes_ref, nums_ref, *refs):
    values, out = refs[:-1], refs[-1]
    routes = routes_ref[...]
    placings = placing_of(routes, plane_ref[0], experts, values[0].shape[0])
    gates = gates_of(routes, nums_ref[...], plane_ref[0], experts)
    fill = -experts % 8
    if fill:
        gates = jnp.concatenate([gates, jnp.zeros((fill, gates.shape[1]), F32)], 0)
    gates = gates.T
    total = tokens_ref[...].astype(F32)
    for s, value in enumerate(values):
        picked = lax.dot_general(
            placings[s].astype(BF16),
            value[...],
            (((0,), (0,)), ((), ())),
            preferred_element_type=F32,
        )
        total = total + gates[:, s : s + 1] * picked
    out[...] = total.astype(BF16)


def on_device(tokens, cotangent, routes, gate_nums, gain, w_gate, w_up, w_down):
    devices = lax.axis_size("expert")
    experts = devices // HSPLIT
    rows_here, width = tokens.shape
    hidden_width = w_gate.shape[2]
    top_count = routes.shape[1]
    capacity = HSPLIT * (3 * top_count * rows_here // (2 * experts * HSPLIT))
    capacity = -(-capacity // 16) * 16
    shifts = max(1, experts // GROUPS)
    turns = sorted(range(experts), key=lambda s: (min(s, experts - s), s))
    groups = [turns[g : g + shifts] for g in range(0, experts, shifts)]
    height = shifts * capacity
    plane = (lax.axis_index("expert") // HSPLIT).astype(jnp.int32).reshape(1)
    routes, gate_nums, gain = routes.T, gate_nums.T, gain.reshape(1, -1)
    scalar = pl.BlockSpec(memory_space=pltpu.SMEM)
    anywhere = pl.BlockSpec(memory_space=pl.ANY)
    piece = jax.ShapeDtypeStruct((capacity, width), BF16)
    live = {}

    def swap(value, mask):
        return lax.ppermute(value, "expert", [(i, i ^ mask) for i in range(devices)])

    def turn(value, steps):
        to = [(i, (i + steps * HSPLIT) % devices) for i in range(devices)]
        return lax.ppermute(value, "expert", to)

    def sync():
        values = lax.optimization_barrier(tuple(live.values()))
        live.update(zip(list(live), values))

    def join(parts):
        return parts[0] if len(parts) == 1 else jnp.concatenate(parts, 0)

    flying = {}

    def land(*earlier):
        names = list(flying)
        values = [flying.pop(name) for name in names]
        if earlier:
            values = lax.optimization_barrier(tuple(values) + earlier)[: len(names)]
        values = through(values, "land", LINK_WORK)
        for name, value in zip(names, values):
            if name[0] != "y":
                live[name] = value
                continue
            at = 0
            for kind, gs in name[1:]:
                here = live.pop(("sent", kind, gs))
                came = value[at : at + here.shape[0]]
                at += here.shape[0]
                if kind != "fold":
                    live[kind, "own", gs] = join([here, came])
                    continue
                keep, crossed = live.pop(("keep", gs)), live.pop(("crossed", gs))
                rows = came.shape[0]
                total = keep[:rows].astype(F32) + crossed[:rows].astype(F32)
                total = (total + came.astype(F32)).astype(BF16)
                for i, s in enumerate([s for g in gs for s in groups[g]]):
                    live["R", s] = total[i * capacity : (i + 1) * capacity]
        return values[0]

    def across(kind, *gs):
        for s in [s for g in gs for s in groups[g]]:
            if s:
                flying[kind, s] = turn(live[kind, s], -s if kind == "R" else s)

    def along(*items):
        for kind, gs in items:
            if kind == "fold":
                value = live.pop(("across", gs))
            else:
                value = join([live.pop((kind, s)) for g in gs for s in groups[g]])
            live["sent", kind, gs] = value
        flying[("y",) + items] = swap(join([live["sent", kind, gs] for kind, gs in items]), 2)

    def core(kind, *tuples):
        gs = tuple(g for part in tuples for g in part)
        live[kind, "other", gs] = swap(join([live[kind, "own", part] for part in tuples]), 1)

    def ffn(*gs):
        pieces = [live.pop(("N", "own", gs)), live.pop(("N", "other", gs))]
        half = jax.ShapeDtypeStruct(pieces[0].shape, BF16)
        rows = 2 * half.shape[0]
        live["turned", gs], live["keep", gs], live["send", gs] = call(
            functools.partial(ffn_kernel, len(pieces)),
            24,
            "ffn",
            out_shape=[jax.ShapeDtypeStruct((hidden_width, rows), BF16), half, half],
            in_specs=whole(len(pieces) + 3),
            out_specs=whole(3),
            scratch_shapes=[
                pltpu.VMEM((rows, width), BF16),
                pltpu.VMEM((rows, hidden_width), BF16),
            ],
        )(*pieces, live["w", 0], live["w", 1], live["w", 2])

    def cross(*gs):
        live["crossed", gs] = swap(live.pop(("send", gs)), 1)

    def fold_core(earlier, *gs):
        keep, crossed = live["keep", gs], after(live["crossed", gs], earlier)
        rows = keep.shape[0] // 2
        both = keep[rows:].astype(F32) + crossed[rows:].astype(F32)
        live["across", gs] = both.astype(BF16)

    def in_hbm(*values):
        return [pltpu.with_memory_space_constraint(v, pltpu.HBM) for v in values]

    def send():
        sources = (tokens, cotangent, routes, gate_nums, gain)
        values = call(
            functools.partial(send_kernel, experts),
            16,
            "send",
            out_shape=[piece] * (2 * experts),
            in_specs=[scalar] + [anywhere] * len(sources),
            out_specs=whole(2 * experts),
            scratch_shapes=[pltpu.VMEM(v.shape, v.dtype) for v in sources]
            + [pltpu.SemaphoreType.DMA((len(sources),))],
        )(plane, *in_hbm(*sources))
        live.update({("N", s): value for s, value in enumerate(values[:experts])})
        live.update({("C", s): value for s, value in enumerate(values[experts:])})

    def load():
        weight = jax.ShapeDtypeStruct((width, hidden_width), BF16)
        values = call(
            load_kernel,
            16,
            "load",
            out_shape=[weight, weight, jax.ShapeDtypeStruct((hidden_width, width), BF16)],
            in_specs=[anywhere] * 3,
            out_specs=whole(3),
            scratch_shapes=[pltpu.SemaphoreType.DMA((3,))],
        )(*in_hbm(after(w_gate, live["C", groups[-1][-1]]), w_up, w_down))
        live.update({("w", i): value for i, value in enumerate(values)})

    def grad_call(turned, pieces):
        columns = {}
        for i, gs in enumerate(turned):
            at = 0
            for half in ("own", "other"):
                for side in range(2):
                    for g in gs:
                        columns[half, side, g] = (i, at)
                        at += height
        plan = []
        for i, (half, gs) in enumerate(pieces):
            row = 0
            for parts in [gs] if gs in JOINED else [(g,) for g in gs]:
                for side in range(2):
                    for g in parts:
                        where, at = columns[half, side, g]
                        plan.append((where, at, len(turned) + i, row, height))
                        row += height
        total = sum(step[-1] for step in plan)
        sides = [pltpu.VMEM((hidden_width, total), BF16), pltpu.VMEM((total, width), BF16)]
        values = [live["turned", gs] for gs in turned]
        values += [live["C", half, gs] for half, gs in pieces]
        return plan, sides, values

    def first_grad(turned, pieces):
        plan, sides, values = grad_call(turned, pieces)
        live["first"] = call(
            functools.partial(first_grad_kernel, plan),
            24,
            "first_grad",
            out_shape=jax.ShapeDtypeStruct((hidden_width, width), F32),
            in_specs=whole(len(values)),
            out_specs=whole(1)[0],
            scratch_shapes=sides,
        )(*values)

    def last_grad(turned, pieces):
        plan, sides, values = grad_call(turned, pieces)
        return call(
            functools.partial(last_grad_kernel, plan),
            24,
            "last_grad",
            out_shape=jax.ShapeDtypeStruct((1, hidden_width, width), BF16),
            in_specs=whole(1 + len(values)),
            out_specs=anywhere,
            scratch_shapes=[pltpu.VMEM((hidden_width, width), BF16)]
            + sides
            + [pltpu.SemaphoreType.DMA((hidden_width // TILE,))],
        )(live["first"], *values)

    send()
    if shifts > 1:
        across("N", 0)
        across("C", 0)
        land()
    sync()
    across("N", 1, 2)
    along(("N", (0,)), ("C", (0,)))
    load()
    land()
    sync()
    across("N", 3)
    along(("N", (1, 2)))
    core("N", (0,))
    ffn(0)
    cross(0)
    fold_core(land(), 0)
    sync()
    across("C", 1, 2)
    along(("N", (3,)), ("fold", (0,)))
    core("N", (1, 2))
    ffn(1, 2)
    cross(1, 2)
    fold_core(land(), 1, 2)
    sync()
    across("C", 3)
    along(("fold", (1, 2)))
    core("N", (3,))
    ffn(3)
    cross(3)
    fold_core(land(), 3)
    sync()
    if shifts > 1:
        across("R", 0)
    across("R", 1, 2)
    along(("fold", (3,)), ("C", (1,)))
    land()
    sync()
    across("R", 3)
    along(("C", (2, 3)))
    core("C", (0,), (1,))
    first_grad([(0,), (1, 2)], [("own", (0,)), ("own", (1,)), ("other", (0, 1))])
    land(live["first"])
    sync()
    core("C", (2, 3))
    grad_down = last_grad([(1, 2), (3,)], [("own", (2, 3)), ("other", (2, 3))])
    mixed = call(
        functools.partial(combine_kernel, experts),
        16,
        "combine",
        out_shape=jax.ShapeDtypeStruct(tokens.shape, BF16),
        in_specs=[scalar] + whole(3 + experts),
        out_specs=whole(1)[0],
    )(plane, tokens, routes, gate_nums, *[live["R", s] for s in range(experts)])
    return (mixed, grad_down)


def solution(mesh):
    placed = (
        P(("group", "expert"), None),
        P(("group", "expert"), None),
        P(("group", "expert"), None),
        P(("group", "expert"), None),
        P(),
        P("expert", None, None),
        P("expert", None, None),
        P("expert", None, None),
    )
    return jax.shard_map(
        on_device,
        mesh=mesh,
        in_specs=placed,
        out_specs=(P(("group", "expert"), None), P(("group", "expert"), None, None)),
        check_vma=False,
    )
```

```python
import functools

import jax
import jax.numpy as jnp
from jax import lax
from jax.experimental import pallas as pl
from jax.experimental.pallas import tpu as pltpu
from jax.sharding import PartitionSpec as P

HSPLIT = 4
GROUPS = 4
JOINED = ((1, 2), (2, 3))
TILE = 256
LINK_WORK = 10 << 30
LAST_WORK = 0
F32 = jnp.float32
BF16 = jnp.bfloat16


def after(value, *earlier):
    return lax.optimization_barrier((value,) + earlier)[0]


def whole(count):
    return [pl.BlockSpec(memory_space=pltpu.VMEM)] * count


def call(kernel, mib, name, moved=0, **keywords):
    return pl.pallas_call(
        kernel,
        compiler_params=pltpu.CompilerParams(vmem_limit_bytes=mib << 20),
        cost_estimate=pl.CostEstimate(flops=moved, bytes_accessed=0, transcendentals=0),
        name=name,
        **keywords,
    )


def experts_of(plane, experts, rows):
    ahead = lax.broadcasted_iota(jnp.int32, (experts, rows), 0) + plane
    return jnp.where(ahead >= experts, ahead - experts, ahead)


def placing_of(routes, plane, experts, capacity):
    rows = routes.shape[1]
    expert = experts_of(plane, experts, rows)
    member = jnp.zeros((experts, rows), jnp.bool_)
    for k in range(routes.shape[0]):
        member = member | (routes[k : k + 1, :] == expert)
    first = lax.broadcasted_iota(jnp.int32, (rows, rows), 0)
    second = lax.broadcasted_iota(jnp.int32, (rows, rows), 1)
    upto = (first <= second).astype(F32).astype(BF16)
    ones = member.astype(F32)
    count = jnp.dot(ones.astype(BF16), upto, preferred_element_type=F32)
    place = (ones * count).astype(jnp.int32) - 1
    slots = lax.broadcasted_iota(jnp.int32, (capacity, rows), 0)
    return [(slots == place[s : s + 1, :]).astype(F32) for s in range(experts)]


def gates_of(routes, numbers, plane, experts):
    expert = experts_of(plane, experts, routes.shape[1])
    numerators = numbers.astype(F32)
    gates = numerators / jnp.sum(numerators, 0, keepdims=True)
    gate = jnp.zeros(expert.shape, F32)
    for k in range(routes.shape[0]):
        gate = gate + jnp.where(routes[k : k + 1, :] == expert, gates[k : k + 1, :], 0.0)
    return gate


def fetch(semaphores, *pairs):
    copies = [
        pltpu.make_async_copy(source, target, semaphores.at[i])
        for i, (source, target) in enumerate(pairs)
    ]
    for copy in copies:
        copy.start()
    return copies


def send_kernel(experts, plane_ref, *refs):
    sources, refs = refs[:5], refs[5:]
    row_outs, grad_outs = refs[:experts], refs[experts : 2 * experts]
    targets, semaphores = refs[2 * experts : -1], refs[-1]
    tokens_ref, cot_ref, routes_ref, nums_ref, gain_ref = targets
    copies = fetch(semaphores, *zip(sources, targets))
    copies[2].wait()
    copies[3].wait()
    routes = routes_ref[...]
    placings = placing_of(routes, plane_ref[0], experts, row_outs[0].shape[0])
    gates = gates_of(routes, nums_ref[...], plane_ref[0], experts)
    copies[4].wait()
    copies[0].wait()
    frames = tokens_ref[...].astype(F32)
    inverse = lax.rsqrt(jnp.mean(frames * frames, -1, keepdims=True) + 1e-06)
    normed = (frames * inverse * gain_ref[...]).astype(BF16)
    for out, placing in zip(row_outs, placings):
        out[...] = jnp.dot(placing.astype(BF16), normed, preferred_element_type=F32).astype(BF16)
    copies[1].wait()
    cot = cot_ref[...]
    for s, (out, placing) in enumerate(zip(grad_outs, placings)):
        picked = jnp.dot(placing.astype(BF16), cot, preferred_element_type=F32)
        gate = jnp.sum(placing * gates[s : s + 1, :], -1, keepdims=True)
        out[...] = (gate * picked).astype(BF16)


def load_kernel(*refs):
    sources, outs, semaphores = refs[:3], refs[3:6], refs[6]
    copies = fetch(semaphores, *[(s.at[0], o) for s, o in zip(sources, outs)])
    for copy in copies:
        copy.wait()


def nothing(*refs):
    pass


def through(values, name, moved=0):
    count = len(values)
    return call(
        nothing,
        4,
        name,
        moved,
        out_shape=[jax.ShapeDtypeStruct(v.shape, v.dtype) for v in values],
        in_specs=whole(count),
        out_specs=whole(count),
        input_output_aliases={i: i for i in range(count)},
    )(*values)


def ffn_kernel(count, *refs):
    pieces, refs = refs[:count], refs[count:]
    gate_ref, up_ref, down_ref, turned_ref, keep_ref, send_ref, rows_ref, hidden_ref = refs
    at = 0
    for piece in pieces:
        rows_ref[at : at + piece.shape[0], :] = piece[...]
        at += piece.shape[0]
    rows = rows_ref[...]
    half = keep_ref.shape[0]
    for j in range(gate_ref.shape[1] // TILE):
        columns = slice(j * TILE, (j + 1) * TILE)
        pre_gate = jnp.dot(rows, gate_ref[:, columns], preferred_element_type=F32)
        pre_up = jnp.dot(rows, up_ref[:, columns], preferred_element_type=F32)
        hidden = pre_gate * lax.logistic(pre_gate) * pre_up
        hidden_ref[:, columns] = hidden.astype(BF16)
        turned_ref[columns, :] = hidden.T.astype(BF16)
    for j in range(down_ref.shape[1] // TILE):
        columns = slice(j * TILE, (j + 1) * TILE)
        value = jnp.dot(
            hidden_ref[...], down_ref[:, columns], preferred_element_type=F32
        ).astype(BF16)
        keep_ref[:, columns] = value[:half]
        send_ref[:, columns] = value[half:]


def gather_grad(plan, refs, hidden_ref, cot_ref):
    at = 0
    for turned, column, piece, row, count in plan:
        hidden_ref[:, at : at + count] = refs[turned][:, column : column + count]
        cot_ref[at : at + count, :] = refs[piece][row : row + count, :]
        at += count


def first_grad_kernel(plan, *refs):
    out_ref, hidden_ref, cot_ref = refs[-3:]
    gather_grad(plan, refs, hidden_ref, cot_ref)
    for j in range(out_ref.shape[0] // TILE):
        part = slice(j * TILE, (j + 1) * TILE)
        out_ref[part, :] = jnp.dot(
            hidden_ref[part, :], cot_ref[...], preferred_element_type=F32
        )


def last_grad_kernel(plan, first_ref, *refs):
    out_hbm, out_ref, hidden_ref, cot_ref, semaphores = refs[-5:]
    gather_grad(plan, refs, hidden_ref, cot_ref)
    copies = []
    for j in range(first_ref.shape[0] // TILE):
        part = slice(j * TILE, (j + 1) * TILE)
        total = jnp.dot(hidden_ref[part, :], cot_ref[...], preferred_element_type=F32)
        out_ref[part, :] = (first_ref[part, :] + total).astype(BF16)
        copies.append(
            pltpu.make_async_copy(out_ref.at[part, :], out_hbm.at[0, part, :], semaphores.at[j])
        )
        copies[-1].start()
    for copy in copies:
        copy.wait()


def combine_kernel(experts, plane_ref, tokens_ref, routes_ref, nums_ref, *refs):
    values, out = refs[:-1], refs[-1]
    routes = routes_ref[...]
    placings = placing_of(routes, plane_ref[0], experts, values[0].shape[0])
    gates = gates_of(routes, nums_ref[...], plane_ref[0], experts)
    fill = -experts % 8
    if fill:
        gates = jnp.concatenate([gates, jnp.zeros((fill, gates.shape[1]), F32)], 0)
    gates = gates.T
    total = tokens_ref[...].astype(F32)
    for s, value in enumerate(values):
        picked = lax.dot_general(
            placings[s].astype(BF16),
            value[...],
            (((0,), (0,)), ((), ())),
            preferred_element_type=F32,
        )
        total = total + gates[:, s : s + 1] * picked
    out[...] = total.astype(BF16)


def on_device(tokens, cotangent, routes, gate_nums, gain, w_gate, w_up, w_down):
    devices = lax.axis_size("expert")
    experts = devices // HSPLIT
    rows_here, width = tokens.shape
    hidden_width = w_gate.shape[2]
    top_count = routes.shape[1]
    capacity = HSPLIT * (3 * top_count * rows_here // (2 * experts * HSPLIT))
    capacity = -(-capacity // 16) * 16
    shifts = max(1, experts // GROUPS)
    turns = sorted(range(experts), key=lambda s: (min(s, experts - s), s))
    groups = [turns[g : g + shifts] for g in range(0, experts, shifts)]
    height = shifts * capacity
    plane = (lax.axis_index("expert") // HSPLIT).astype(jnp.int32).reshape(1)
    routes, gate_nums, gain = routes.T, gate_nums.T, gain.reshape(1, -1)
    scalar = pl.BlockSpec(memory_space=pltpu.SMEM)
    anywhere = pl.BlockSpec(memory_space=pl.ANY)
    piece = jax.ShapeDtypeStruct((capacity, width), BF16)
    live = {}

    def swap(value, mask):
        return lax.ppermute(value, "expert", [(i, i ^ mask) for i in range(devices)])

    def turn(value, steps):
        to = [(i, (i + steps * HSPLIT) % devices) for i in range(devices)]
        return lax.ppermute(value, "expert", to)

    def sync():
        values = lax.optimization_barrier(tuple(live.values()))
        live.update(zip(list(live), values))

    def join(parts):
        return parts[0] if len(parts) == 1 else jnp.concatenate(parts, 0)

    flying = {}

    def land(*earlier, sooner=()):
        names = [name for name in flying if name[0] != "y"]
        first = list(flying) != names and len(names) > 0
        if first:
            values = [flying.pop(name) for name in names]
            if sooner:
                values = lax.optimization_barrier(tuple(values) + sooner)[: len(names)]
            values = through(values, "land_planes", LINK_WORK)
            live.update(zip(names, values))
            earlier += (values[0],)
        names = list(flying)
        values = [flying.pop(name) for name in names]
        if earlier:
            values = lax.optimization_barrier(tuple(values) + earlier)[: len(names)]
        values = through(values, "land", LAST_WORK if first else LINK_WORK)
        for name, value in zip(names, values):
            if name[0] != "y":
                live[name] = value
                continue
            at = 0
            for kind, gs in name[1:]:
                here = live.pop(("sent", kind, gs))
                came = value[at : at + here.shape[0]]
                at += here.shape[0]
                if kind != "fold":
                    live[kind, "own", gs] = join([here, came])
                    continue
                keep, crossed = live.pop(("keep", gs)), live.pop(("crossed", gs))
                rows = came.shape[0]
                total = keep[:rows].astype(F32) + crossed[:rows].astype(F32)
                total = (total + came.astype(F32)).astype(BF16)
                for i, s in enumerate([s for g in gs for s in groups[g]]):
                    live["R", s] = total[i * capacity : (i + 1) * capacity]
        return values[0]

    def across(kind, *gs):
        for s in [s for g in gs for s in groups[g]]:
            if s:
                flying[kind, s] = turn(live[kind, s], -s if kind == "R" else s)

    def along(*items):
        for kind, gs in items:
            if kind == "fold":
                value = live.pop(("across", gs))
            else:
                value = join([live.pop((kind, s)) for g in gs for s in groups[g]])
            live["sent", kind, gs] = value
        flying[("y",) + items] = swap(join([live["sent", kind, gs] for kind, gs in items]), 2)

    def core(kind, *tuples):
        gs = tuple(g for part in tuples for g in part)
        live[kind, "other", gs] = swap(join([live[kind, "own", part] for part in tuples]), 1)

    def ffn(*gs):
        pieces = [live.pop(("N", "own", gs)), live.pop(("N", "other", gs))]
        half = jax.ShapeDtypeStruct(pieces[0].shape, BF16)
        rows = 2 * half.shape[0]
        live["turned", gs], live["keep", gs], live["send", gs] = call(
            functools.partial(ffn_kernel, len(pieces)),
            24,
            "ffn",
            out_shape=[jax.ShapeDtypeStruct((hidden_width, rows), BF16), half, half],
            in_specs=whole(len(pieces) + 3),
            out_specs=whole(3),
            scratch_shapes=[
                pltpu.VMEM((rows, width), BF16),
                pltpu.VMEM((rows, hidden_width), BF16),
            ],
        )(*pieces, live["w", 0], live["w", 1], live["w", 2])

    def cross(*gs):
        live["crossed", gs] = swap(live.pop(("send", gs)), 1)

    def fold_core(earlier, *gs):
        keep, crossed = live["keep", gs], after(live["crossed", gs], earlier)
        rows = keep.shape[0] // 2
        both = keep[rows:].astype(F32) + crossed[rows:].astype(F32)
        live["across", gs] = both.astype(BF16)

    def in_hbm(*values):
        return [pltpu.with_memory_space_constraint(v, pltpu.HBM) for v in values]

    def send():
        sources = (tokens, cotangent, routes, gate_nums, gain)
        values = call(
            functools.partial(send_kernel, experts),
            16,
            "send",
            out_shape=[piece] * (2 * experts),
            in_specs=[scalar] + [anywhere] * len(sources),
            out_specs=whole(2 * experts),
            scratch_shapes=[pltpu.VMEM(v.shape, v.dtype) for v in sources]
            + [pltpu.SemaphoreType.DMA((len(sources),))],
        )(plane, *in_hbm(*sources))
        live.update({("N", s): value for s, value in enumerate(values[:experts])})
        live.update({("C", s): value for s, value in enumerate(values[experts:])})

    def load():
        weight = jax.ShapeDtypeStruct((width, hidden_width), BF16)
        values = call(
            load_kernel,
            16,
            "load",
            out_shape=[weight, weight, jax.ShapeDtypeStruct((hidden_width, width), BF16)],
            in_specs=[anywhere] * 3,
            out_specs=whole(3),
            scratch_shapes=[pltpu.SemaphoreType.DMA((3,))],
        )(*in_hbm(after(w_gate, live["C", groups[-1][-1]]), w_up, w_down))
        live.update({("w", i): value for i, value in enumerate(values)})

    def grad_call(turned, pieces):
        columns = {}
        for i, gs in enumerate(turned):
            at = 0
            for half in ("own", "other"):
                for side in range(2):
                    for g in gs:
                        columns[half, side, g] = (i, at)
                        at += height
        plan = []
        for i, (half, gs) in enumerate(pieces):
            row = 0
            for parts in [gs] if gs in JOINED else [(g,) for g in gs]:
                for side in range(2):
                    for g in parts:
                        where, at = columns[half, side, g]
                        plan.append((where, at, len(turned) + i, row, height))
                        row += height
        total = sum(step[-1] for step in plan)
        sides = [pltpu.VMEM((hidden_width, total), BF16), pltpu.VMEM((total, width), BF16)]
        values = [live["turned", gs] for gs in turned]
        values += [live["C", half, gs] for half, gs in pieces]
        return plan, sides, values

    def first_grad(turned, pieces):
        plan, sides, values = grad_call(turned, pieces)
        live["first"] = call(
            functools.partial(first_grad_kernel, plan),
            24,
            "first_grad",
            out_shape=jax.ShapeDtypeStruct((hidden_width, width), F32),
            in_specs=whole(len(values)),
            out_specs=whole(1)[0],
            scratch_shapes=sides,
        )(*values)

    def last_grad(turned, pieces):
        plan, sides, values = grad_call(turned, pieces)
        return call(
            functools.partial(last_grad_kernel, plan),
            24,
            "last_grad",
            out_shape=jax.ShapeDtypeStruct((1, hidden_width, width), BF16),
            in_specs=whole(1 + len(values)),
            out_specs=anywhere,
            scratch_shapes=[pltpu.VMEM((hidden_width, width), BF16)]
            + sides
            + [pltpu.SemaphoreType.DMA((hidden_width // TILE,))],
        )(live["first"], *values)

    send()
    if shifts > 1:
        across("N", 0)
        across("C", 0)
        land()
    sync()
    across("N", 1, 2)
    along(("N", (0,)), ("C", (0,)))
    load()
    land()
    sync()
    across("N", 3)
    along(("N", (1, 2)))
    core("N", (0,))
    ffn(0)
    cross(0)
    fold_core(land(), 0)
    sync()
    across("C", 1, 2)
    along(("N", (3,)), ("fold", (0,)))
    core("N", (1, 2))
    ffn(1, 2)
    cross(1, 2)
    fold_core(land(), 1, 2)
    sync()
    across("C", 3)
    along(("fold", (1, 2)))
    core("N", (3,))
    ffn(3)
    cross(3)
    fold_core(land(live["crossed", (3,)]), 3)
    sync()
    if shifts > 1:
        across("R", 0)
    across("R", 1, 2)
    along(("fold", (3,)), ("C", (1,)))
    land()
    sync()
    across("R", 3)
    along(("C", (2, 3)))
    core("C", (0,), (1,))
    first_grad([(0,), (1, 2)], [("own", (0,)), ("own", (1,)), ("other", (0, 1))])
    land(sooner=(live["first"],))
    sync()
    core("C", (2, 3))
    grad_down = last_grad([(1, 2), (3,)], [("own", (2, 3)), ("other", (2, 3))])
    mixed = call(
        functools.partial(combine_kernel, experts),
        16,
        "combine",
        out_shape=jax.ShapeDtypeStruct(tokens.shape, BF16),
        in_specs=[scalar] + whole(3 + experts),
        out_specs=whole(1)[0],
    )(plane, tokens, routes, gate_nums, *[live["R", s] for s in range(experts)])
    return (mixed, grad_down)


def solution(mesh):
    placed = (
        P(("group", "expert"), None),
        P(("group", "expert"), None),
        P(("group", "expert"), None),
        P(("group", "expert"), None),
        P(),
        P("expert", None, None),
        P("expert", None, None),
        P("expert", None, None),
    )
    return jax.shard_map(
        on_device,
        mesh=mesh,
        in_specs=placed,
        out_specs=(P(("group", "expert"), None), P(("group", "expert"), None, None)),
        check_vma=False,
    )
```

```python
import functools

import jax
import jax.numpy as jnp
from jax import lax
from jax.experimental import pallas as pl
from jax.experimental.pallas import tpu as pltpu
from jax.sharding import PartitionSpec as P

HSPLIT = 4
GROUPS = 4
PLAN = (
    ("yN0 zN1 zN2 loadW0", ""),
    ("yC0 zN3", "yN0 zN1 zN2"),
    ("cN0 yN1 zC1", "yC0 zN3 cN0"),
    ("ffnN0 cR0 cC0 yN3 zC2", "yN1 zC1 cR0 cC0"),
    ("cN1 yN2 zC3", "yN3 zC2 cN1"),
    ("ffnN1 cR1 cN3 yR0", "yN2 zC3 cR1 cN3"),
    ("ffnN3 cR3 cN2 yR1", "yR0 cR3 cN2"),
    ("ffnN2 cR2 totalR0 yR3", "yR1 cR2"),
    ("totalR1 zR1 yR2", "yR3"),
    ("totalR3 zR3 yC1", "yR2 zR1"),
    ("totalR2 zR2 yC2", "yC1 zR3"),
    ("cC1 yC3", "yC2 zR2 cC1"),
    ("cC2", "yC3 cC2"),
    ("cC3 gradC0", None),
)
TILE = 256
LINK_WORK = 10 << 30
F32 = jnp.float32
BF16 = jnp.bfloat16


def after(value, *earlier):
    return lax.optimization_barrier((value,) + earlier)[0]


def whole(count):
    return [pl.BlockSpec(memory_space=pltpu.VMEM)] * count


def call(kernel, mib, name, moved=0, **keywords):
    return pl.pallas_call(
        kernel,
        compiler_params=pltpu.CompilerParams(vmem_limit_bytes=mib << 20),
        cost_estimate=pl.CostEstimate(flops=moved, bytes_accessed=0, transcendentals=0),
        name=name,
        **keywords,
    )


def experts_of(plane, experts, rows):
    ahead = lax.broadcasted_iota(jnp.int32, (experts, rows), 0) + plane
    return jnp.where(ahead >= experts, ahead - experts, ahead)


def placing_of(routes, plane, experts, capacity):
    rows = routes.shape[1]
    expert = experts_of(plane, experts, rows)
    member = jnp.zeros((experts, rows), jnp.bool_)
    for k in range(routes.shape[0]):
        member = member | (routes[k : k + 1, :] == expert)
    first = lax.broadcasted_iota(jnp.int32, (rows, rows), 0)
    second = lax.broadcasted_iota(jnp.int32, (rows, rows), 1)
    upto = (first <= second).astype(F32).astype(BF16)
    ones = member.astype(F32)
    count = jnp.dot(ones.astype(BF16), upto, preferred_element_type=F32)
    place = (ones * count).astype(jnp.int32) - 1
    slots = lax.broadcasted_iota(jnp.int32, (capacity, rows), 0)
    return [(slots == place[s : s + 1, :]).astype(F32) for s in range(experts)]


def gates_of(routes, numbers, plane, experts):
    expert = experts_of(plane, experts, routes.shape[1])
    numerators = numbers.astype(F32)
    gates = numerators / jnp.sum(numerators, 0, keepdims=True)
    gate = jnp.zeros(expert.shape, F32)
    for k in range(routes.shape[0]):
        gate = gate + jnp.where(routes[k : k + 1, :] == expert, gates[k : k + 1, :], 0.0)
    return gate


def fetch(semaphores, *pairs):
    copies = [
        pltpu.make_async_copy(source, target, semaphores.at[i])
        for i, (source, target) in enumerate(pairs)
    ]
    for copy in copies:
        copy.start()
    return copies


def send_kernel(experts, plane_ref, *refs):
    sources, refs = refs[:5], refs[5:]
    row_outs, grad_outs = refs[:experts], refs[experts : 2 * experts]
    targets, semaphores = refs[2 * experts : -1], refs[-1]
    tokens_ref, cot_ref, routes_ref, nums_ref, gain_ref = targets
    copies = fetch(semaphores, *zip(sources, targets))
    copies[2].wait()
    copies[3].wait()
    routes = routes_ref[...]
    placings = placing_of(routes, plane_ref[0], experts, row_outs[0].shape[0])
    gates = gates_of(routes, nums_ref[...], plane_ref[0], experts)
    copies[4].wait()
    copies[0].wait()
    frames = tokens_ref[...].astype(F32)
    inverse = lax.rsqrt(jnp.mean(frames * frames, -1, keepdims=True) + 1e-06)
    normed = (frames * inverse * gain_ref[...]).astype(BF16)
    for out, placing in zip(row_outs, placings):
        out[...] = jnp.dot(placing.astype(BF16), normed, preferred_element_type=F32).astype(BF16)
    copies[1].wait()
    cot = cot_ref[...]
    for s, (out, placing) in enumerate(zip(grad_outs, placings)):
        picked = jnp.dot(placing.astype(BF16), cot, preferred_element_type=F32)
        gate = jnp.sum(placing * gates[s : s + 1, :], -1, keepdims=True)
        out[...] = (gate * picked).astype(BF16)


def load_kernel(*refs):
    sources, outs, semaphores = refs[:3], refs[3:6], refs[6]
    copies = fetch(semaphores, *[(s.at[0], o) for s, o in zip(sources, outs)])
    for copy in copies:
        copy.wait()


def pair_kernel(first_ref, second_ref, out_ref):
    rows = first_ref.shape[0]
    out_ref[:rows, :] = first_ref[...]
    out_ref[rows:, :] = second_ref[...]


def fold_kernel(keep_ref, crossed_ref, out_ref):
    rows = out_ref.shape[0]
    total = keep_ref[rows:, :].astype(F32) + crossed_ref[rows:, :].astype(F32)
    out_ref[...] = total.astype(BF16)


def total_kernel(keep_ref, crossed_ref, came_ref, *outs):
    at = 0
    for out in outs:
        part = slice(at, at + out.shape[0])
        total = keep_ref[part, :].astype(F32) + crossed_ref[part, :].astype(F32)
        out[...] = (total + came_ref[part, :].astype(F32)).astype(BF16)
        at += out.shape[0]


def nothing(*refs):
    pass


def through(values, name, moved=0):
    count = len(values)
    return call(
        nothing,
        4,
        name,
        moved,
        out_shape=[jax.ShapeDtypeStruct(v.shape, v.dtype) for v in values],
        in_specs=whole(count),
        out_specs=whole(count),
        input_output_aliases={i: i for i in range(count)},
    )(*values)


def ffn_kernel(count, *refs):
    pieces, refs = refs[:count], refs[count:]
    gate_ref, up_ref, down_ref, turned_ref, keep_ref, send_ref, rows_ref, hidden_ref = refs
    at = 0
    for piece in pieces:
        rows_ref[at : at + piece.shape[0], :] = piece[...]
        at += piece.shape[0]
    rows = rows_ref[...]
    half = keep_ref.shape[0]
    for j in range(gate_ref.shape[1] // TILE):
        columns = slice(j * TILE, (j + 1) * TILE)
        pre_gate = jnp.dot(rows, gate_ref[:, columns], preferred_element_type=F32)
        pre_up = jnp.dot(rows, up_ref[:, columns], preferred_element_type=F32)
        hidden = pre_gate * lax.logistic(pre_gate) * pre_up
        hidden_ref[:, columns] = hidden.astype(BF16)
        turned_ref[columns, :] = hidden.T.astype(BF16)
    for j in range(down_ref.shape[1] // TILE):
        columns = slice(j * TILE, (j + 1) * TILE)
        value = jnp.dot(
            hidden_ref[...], down_ref[:, columns], preferred_element_type=F32
        ).astype(BF16)
        keep_ref[:, columns] = value[:half]
        send_ref[:, columns] = value[half:]


def gather_grad(plan, refs, hidden_ref, cot_ref):
    at = 0
    for turned, column, piece, row, count in plan:
        hidden_ref[:, at : at + count] = refs[turned][:, column : column + count]
        cot_ref[at : at + count, :] = refs[piece][row : row + count, :]
        at += count


def first_grad_kernel(plan, *refs):
    out_ref, hidden_ref, cot_ref = refs[-3:]
    gather_grad(plan, refs, hidden_ref, cot_ref)
    for j in range(out_ref.shape[0] // TILE):
        part = slice(j * TILE, (j + 1) * TILE)
        out_ref[part, :] = jnp.dot(
            hidden_ref[part, :], cot_ref[...], preferred_element_type=F32
        )


def last_grad_kernel(plan, first_ref, *refs):
    out_hbm, out_ref, hidden_ref, cot_ref, semaphores = refs[-5:]
    gather_grad(plan, refs, hidden_ref, cot_ref)
    copies = []
    for j in range(first_ref.shape[0] // TILE):
        part = slice(j * TILE, (j + 1) * TILE)
        total = jnp.dot(hidden_ref[part, :], cot_ref[...], preferred_element_type=F32)
        out_ref[part, :] = (first_ref[part, :] + total).astype(BF16)
        copies.append(
            pltpu.make_async_copy(out_ref.at[part, :], out_hbm.at[0, part, :], semaphores.at[j])
        )
        copies[-1].start()
    for copy in copies:
        copy.wait()


def combine_kernel(experts, plane_ref, tokens_ref, routes_ref, nums_ref, *refs):
    values, out = refs[:-1], refs[-1]
    routes = routes_ref[...]
    placings = placing_of(routes, plane_ref[0], experts, values[0].shape[0])
    gates = gates_of(routes, nums_ref[...], plane_ref[0], experts)
    fill = -experts % 8
    if fill:
        gates = jnp.concatenate([gates, jnp.zeros((fill, gates.shape[1]), F32)], 0)
    gates = gates.T
    total = tokens_ref[...].astype(F32)
    for s, value in enumerate(values):
        picked = lax.dot_general(
            placings[s].astype(BF16),
            value[...],
            (((0,), (0,)), ((), ())),
            preferred_element_type=F32,
        )
        total = total + gates[:, s : s + 1] * picked
    out[...] = total.astype(BF16)


def on_device(tokens, cotangent, routes, gate_nums, gain, w_gate, w_up, w_down):
    devices = lax.axis_size("expert")
    experts = devices // HSPLIT
    rows_here, width = tokens.shape
    hidden_width = w_gate.shape[2]
    top_count = routes.shape[1]
    capacity = HSPLIT * (3 * top_count * rows_here // (2 * experts * HSPLIT))
    capacity = -(-capacity // 16) * 16
    shifts = max(1, experts // GROUPS)
    turns = sorted(range(experts), key=lambda s: (min(s, experts - s), s))
    groups = [turns[g : g + shifts] for g in range(0, experts, shifts)]
    height = shifts * capacity
    plane = (lax.axis_index("expert") // HSPLIT).astype(jnp.int32).reshape(1)
    routes, gate_nums, gain = routes.T, gate_nums.T, gain.reshape(1, -1)
    scalar = pl.BlockSpec(memory_space=pltpu.SMEM)
    anywhere = pl.BlockSpec(memory_space=pl.ANY)
    piece = jax.ShapeDtypeStruct((capacity, width), BF16)
    live = {}

    def swap(value, mask):
        return lax.ppermute(value, "expert", [(i, i ^ mask) for i in range(devices)])

    def turn(value, steps):
        to = [(i, (i + steps * HSPLIT) % devices) for i in range(devices)]
        return lax.ppermute(value, "expert", to)

    def sync():
        values = lax.optimization_barrier(tuple(live.values()))
        live.update(zip(list(live), values))

    def join(parts):
        return parts[0] if len(parts) == 1 else jnp.concatenate(parts, 0)

    flying, slow = {}, []

    def small(kernel, name, outs, *values):
        return call(
            kernel,
            8,
            name,
            out_shape=[jax.ShapeDtypeStruct((rows, width), BF16) for rows in outs],
            in_specs=whole(len(values)),
            out_specs=whole(len(outs)),
        )(*values)

    def land(*names):
        names = [n for name in names for n in flights_of(name)]
        quick = [name for name in names if name[0] == "c"]
        names = [name for name in names if name[0] != "c"]
        values = [flying.pop(name) for name in names]
        if not names:
            names, values = [("C", groups[-1][-1])], [live["C", groups[-1][-1]]]
        values = through(values, "land", LINK_WORK)
        landed = list(zip(names, values))
        if quick:
            cores = tuple(flying.pop(name) for name in quick) + (values[0],)
            cores = lax.optimization_barrier(cores)[: len(quick)]
            landed += list(zip(quick, through(cores, "land_core")))
        live.update(landed)
        sync()

    def flights_of(name):
        axis, kind, g = name
        return [(kind, s) for s in groups[g] if s] if axis == "z" else [name]

    def z(kind, g):
        for s in groups[g]:
            if s:
                flying[kind, s] = turn(live[kind, s], -s if kind == "R" else s)

    def y(kind, g):
        if kind == "R":
            keep, crossed = live["keep", (g,)], live["c", "R", g]
            (value,) = small(fold_kernel, "fold", [height], keep, crossed)
        else:
            value = join([live.pop((kind, s)) for s in groups[g]])
            live["sent", kind, g] = value
        flying["y", kind, g] = swap(value, 2)

    def c(kind, g):
        if kind == "R":
            value = live.pop(("send", (g,)))
        else:
            here, came = live.pop(("sent", kind, g)), live.pop(("y", kind, g))
            (value,) = small(pair_kernel, "pair", [2 * height], here, came)
            live[kind, "own", (g,)] = value
        flying["c", kind, g] = swap(value, 1)

    def total(g):
        values = live.pop(("keep", (g,))), live.pop(("c", "R", g)), live.pop(("y", "R", g))
        outs = small(total_kernel, "total", [capacity] * shifts, *values)
        live.update({("R", s): out for s, out in zip(groups[g], outs)})

    def ffn(*gs):
        pieces = [live.pop(("N", "own", gs)), live.pop(("c", "N", gs[0]))]
        half = jax.ShapeDtypeStruct(pieces[0].shape, BF16)
        rows = 2 * half.shape[0]
        live["turned", gs], live["keep", gs], live["send", gs] = call(
            functools.partial(ffn_kernel, len(pieces)),
            24,
            "ffn",
            out_shape=[jax.ShapeDtypeStruct((hidden_width, rows), BF16), half, half],
            in_specs=whole(len(pieces) + 3),
            out_specs=whole(3),
            scratch_shapes=[
                pltpu.VMEM((rows, width), BF16),
                pltpu.VMEM((rows, hidden_width), BF16),
            ],
        )(*pieces, live["w", 0], live["w", 1], live["w", 2])

    def in_hbm(*values):
        return [pltpu.with_memory_space_constraint(v, pltpu.HBM) for v in values]

    def send():
        sources = (tokens, cotangent, routes, gate_nums, gain)
        values = call(
            functools.partial(send_kernel, experts),
            16,
            "send",
            out_shape=[piece] * (2 * experts),
            in_specs=[scalar] + [anywhere] * len(sources),
            out_specs=whole(2 * experts),
            scratch_shapes=[pltpu.VMEM(v.shape, v.dtype) for v in sources]
            + [pltpu.SemaphoreType.DMA((len(sources),))],
        )(plane, *in_hbm(*sources))
        live.update({("N", s): value for s, value in enumerate(values[:experts])})
        live.update({("C", s): value for s, value in enumerate(values[experts:])})

    def load():
        weight = jax.ShapeDtypeStruct((width, hidden_width), BF16)
        values = call(
            load_kernel,
            16,
            "load",
            out_shape=[weight, weight, jax.ShapeDtypeStruct((hidden_width, width), BF16)],
            in_specs=[anywhere] * 3,
            out_specs=whole(3),
            scratch_shapes=[pltpu.SemaphoreType.DMA((3,))],
        )(*in_hbm(after(w_gate, live["C", groups[-1][-1]]), w_up, w_down))
        live.update({("w", i): value for i, value in enumerate(values)})

    def grad_call(turned, pieces):
        columns = {}
        for i, gs in enumerate(turned):
            at = 0
            for half in ("own", "other"):
                for side in range(2):
                    for g in gs:
                        columns[half, side, g] = (i, at)
                        at += height
        plan = []
        for i, name in enumerate(pieces):
            half = "other" if name[0] == "c" else "own"
            g = name[-1] if half == "other" else name[-1][0]
            for side in range(2):
                where, at = columns[half, side, g]
                plan.append((where, at, len(turned) + i, side * height, height))
        rows = sum(step[-1] for step in plan)
        sides = [pltpu.VMEM((hidden_width, rows), BF16), pltpu.VMEM((rows, width), BF16)]
        values = [live["turned", gs] for gs in turned]
        values += [live[name] for name in pieces]
        return plan, sides, values

    def first_grad(turned, pieces):
        plan, sides, values = grad_call(turned, pieces)
        live["first"] = call(
            functools.partial(first_grad_kernel, plan),
            24,
            "first_grad",
            out_shape=jax.ShapeDtypeStruct((hidden_width, width), F32),
            in_specs=whole(len(values)),
            out_specs=whole(1)[0],
            scratch_shapes=sides,
        )(*values)

    def last_grad(turned, pieces):
        plan, sides, values = grad_call(turned, pieces)
        return call(
            functools.partial(last_grad_kernel, plan),
            24,
            "last_grad",
            out_shape=jax.ShapeDtypeStruct((1, hidden_width, width), BF16),
            in_specs=whole(1 + len(values)),
            out_specs=anywhere,
            scratch_shapes=[pltpu.VMEM((hidden_width, width), BF16)]
            + sides
            + [pltpu.SemaphoreType.DMA((hidden_width // TILE,))],
        )(live["first"], *values)

    steps = {
        "z": z,
        "y": y,
        "c": c,
        "ffn": lambda kind, g: ffn(g),
        "total": lambda kind, g: total(g),
        "load": lambda kind, g: load(),
        "grad": lambda kind, g: first_grad(
            [(0,), (1,), (2,)],
            [("C", "own", (i,)) for i in range(3)] + [("c", "C", i) for i in range(3)],
        ),
    }
    send()
    if shifts > 1:
        z("N", 0)
        z("C", 0)
        land(("z", "N", 0), ("z", "C", 0))
    sync()
    for starts, lands in PLAN:
        for act in starts.split():
            steps[act[:-2]](act[-2], int(act[-1]))
        if lands is None:
            break
        land(*[(act[:-2], act[-2], int(act[-1])) for act in lands.split()])
    live["c", "C", 3] = flying.pop(("c", "C", 3))
    grad_down = last_grad([(3,)], [("C", "own", (3,)), ("c", "C", 3)])
    mixed = call(
        functools.partial(combine_kernel, experts),
        16,
        "combine",
        out_shape=jax.ShapeDtypeStruct(tokens.shape, BF16),
        in_specs=[scalar] + whole(3 + experts),
        out_specs=whole(1)[0],
    )(plane, tokens, routes, gate_nums, *[live["R", s] for s in range(experts)])
    return (mixed, grad_down)


def solution(mesh):
    placed = (
        P(("group", "expert"), None),
        P(("group", "expert"), None),
        P(("group", "expert"), None),
        P(("group", "expert"), None),
        P(),
        P("expert", None, None),
        P("expert", None, None),
        P("expert", None, None),
    )
    return jax.shard_map(
        on_device,
        mesh=mesh,
        in_specs=placed,
        out_specs=(P(("group", "expert"), None), P(("group", "expert"), None, None)),
        check_vma=False,
    )
```

```python
import functools

import jax
import jax.numpy as jnp
from jax import lax
from jax.experimental import pallas as pl
from jax.experimental.pallas import tpu as pltpu
from jax.sharding import PartitionSpec as P

HSPLIT = 4
GROUPS = 4
PLAN = (
    ("zN1 zN2 yN0 loadW0", ""),
    ("yC0", "yN0 zN1 zN2"),
    ("cN0 yN1 zN3", "yC0 cN0"),
    ("ffnN0 cR0 yN2", "yN1 zN3 cR0"),
    ("cN1 yN3 zC1 zC2", "yN2 cN1"),
    ("ffnN1 cR1N2 yR0", "yN3 zC1 zC2 cR1N2"),
    ("ffnN2 cR2N3 yR1 zC3", "yR0 cR2N3"),
    ("ffnN3 cR3 totalR0 yR2", "yR1 zC3 cR3"),
    ("totalR1 zR1 yR3 cC0", "yR2 cC0"),
    ("totalR2 zR2 yC1", "yR3 zR1"),
    ("totalR3 zR3 yC2", "yC1 zR2"),
    ("cC1 yC3", "yC2 cC1"),
    ("cC2 gradC0", "yC3 zR3 cC2"),
    ("cC3", None),
)
TILE = 256
LINK_WORK = 10 << 30
F32 = jnp.float32
BF16 = jnp.bfloat16


def after(value, *earlier):
    return lax.optimization_barrier((value,) + earlier)[0]


def whole(count):
    return [pl.BlockSpec(memory_space=pltpu.VMEM)] * count


def call(kernel, mib, name, moved=0, **keywords):
    return pl.pallas_call(
        kernel,
        compiler_params=pltpu.CompilerParams(vmem_limit_bytes=mib << 20),
        cost_estimate=pl.CostEstimate(flops=moved, bytes_accessed=0, transcendentals=0),
        name=name,
        **keywords,
    )


def experts_of(plane, experts, rows):
    ahead = lax.broadcasted_iota(jnp.int32, (experts, rows), 0) + plane
    return jnp.where(ahead >= experts, ahead - experts, ahead)


def placing_of(routes, plane, experts, capacity):
    rows = routes.shape[1]
    expert = experts_of(plane, experts, rows)
    member = jnp.zeros((experts, rows), jnp.bool_)
    for k in range(routes.shape[0]):
        member = member | (routes[k : k + 1, :] == expert)
    first = lax.broadcasted_iota(jnp.int32, (rows, rows), 0)
    second = lax.broadcasted_iota(jnp.int32, (rows, rows), 1)
    upto = (first <= second).astype(F32).astype(BF16)
    ones = member.astype(F32)
    count = jnp.dot(ones.astype(BF16), upto, preferred_element_type=F32)
    place = (ones * count).astype(jnp.int32) - 1
    slots = lax.broadcasted_iota(jnp.int32, (capacity, rows), 0)
    return [(slots == place[s : s + 1, :]).astype(F32) for s in range(experts)]


def gates_of(routes, numbers, plane, experts):
    expert = experts_of(plane, experts, routes.shape[1])
    numerators = numbers.astype(F32)
    gates = numerators / jnp.sum(numerators, 0, keepdims=True)
    gate = jnp.zeros(expert.shape, F32)
    for k in range(routes.shape[0]):
        gate = gate + jnp.where(routes[k : k + 1, :] == expert, gates[k : k + 1, :], 0.0)
    return gate


def fetch(semaphores, *pairs):
    copies = [
        pltpu.make_async_copy(source, target, semaphores.at[i])
        for i, (source, target) in enumerate(pairs)
    ]
    for copy in copies:
        copy.start()
    return copies


def send_kernel(experts, plane_ref, *refs):
    sources, refs = refs[:5], refs[5:]
    row_outs, grad_outs = refs[:experts], refs[experts : 2 * experts]
    targets, semaphores = refs[2 * experts : -1], refs[-1]
    tokens_ref, cot_ref, routes_ref, nums_ref, gain_ref = targets
    copies = fetch(semaphores, *zip(sources, targets))
    copies[2].wait()
    copies[3].wait()
    routes = routes_ref[...]
    placings = placing_of(routes, plane_ref[0], experts, row_outs[0].shape[0])
    gates = gates_of(routes, nums_ref[...], plane_ref[0], experts)
    copies[4].wait()
    copies[0].wait()
    frames = tokens_ref[...].astype(F32)
    inverse = lax.rsqrt(jnp.mean(frames * frames, -1, keepdims=True) + 1e-06)
    normed = (frames * inverse * gain_ref[...]).astype(BF16)
    for out, placing in zip(row_outs, placings):
        out[...] = jnp.dot(placing.astype(BF16), normed, preferred_element_type=F32).astype(BF16)
    copies[1].wait()
    cot = cot_ref[...]
    for s, (out, placing) in enumerate(zip(grad_outs, placings)):
        picked = jnp.dot(placing.astype(BF16), cot, preferred_element_type=F32)
        gate = jnp.sum(placing * gates[s : s + 1, :], -1, keepdims=True)
        out[...] = (gate * picked).astype(BF16)


def load_kernel(*refs):
    sources, outs, semaphores = refs[:3], refs[3:6], refs[6]
    copies = fetch(semaphores, *[(s.at[0], o) for s, o in zip(sources, outs)])
    for copy in copies:
        copy.wait()


def pair_kernel(first_ref, second_ref, out_ref):
    rows = first_ref.shape[0]
    out_ref[:rows, :] = first_ref[...]
    out_ref[rows:, :] = second_ref[...]


def split_kernel(both_ref, first_ref, second_ref):
    rows = first_ref.shape[0]
    first_ref[...] = both_ref[:rows, :]
    second_ref[...] = both_ref[rows:, :]


def fold_kernel(keep_ref, crossed_ref, out_ref):
    rows = out_ref.shape[0]
    total = keep_ref[rows:, :].astype(F32) + crossed_ref[rows:, :].astype(F32)
    out_ref[...] = total.astype(BF16)


def total_kernel(keep_ref, crossed_ref, came_ref, *outs):
    at = 0
    for out in outs:
        part = slice(at, at + out.shape[0])
        total = keep_ref[part, :].astype(F32) + crossed_ref[part, :].astype(F32)
        out[...] = (total + came_ref[part, :].astype(F32)).astype(BF16)
        at += out.shape[0]


def nothing(*refs):
    pass


def through(values, name, moved=0):
    count = len(values)
    return call(
        nothing,
        4,
        name,
        moved,
        out_shape=[jax.ShapeDtypeStruct(v.shape, v.dtype) for v in values],
        in_specs=whole(count),
        out_specs=whole(count),
        input_output_aliases={i: i for i in range(count)},
    )(*values)


def ffn_kernel(count, *refs):
    pieces, refs = refs[:count], refs[count:]
    gate_ref, up_ref, down_ref, turned_ref, keep_ref, send_ref, rows_ref, hidden_ref = refs
    at = 0
    for piece in pieces:
        rows_ref[at : at + piece.shape[0], :] = piece[...]
        at += piece.shape[0]
    rows = rows_ref[...]
    half = keep_ref.shape[0]
    for j in range(gate_ref.shape[1] // TILE):
        columns = slice(j * TILE, (j + 1) * TILE)
        pre_gate = jnp.dot(rows, gate_ref[:, columns], preferred_element_type=F32)
        pre_up = jnp.dot(rows, up_ref[:, columns], preferred_element_type=F32)
        hidden = pre_gate * lax.logistic(pre_gate) * pre_up
        hidden_ref[:, columns] = hidden.astype(BF16)
        turned_ref[columns, :] = hidden.T.astype(BF16)
    for j in range(down_ref.shape[1] // TILE):
        columns = slice(j * TILE, (j + 1) * TILE)
        value = jnp.dot(
            hidden_ref[...], down_ref[:, columns], preferred_element_type=F32
        ).astype(BF16)
        keep_ref[:, columns] = value[:half]
        send_ref[:, columns] = value[half:]


def gather_grad(plan, refs, hidden_ref, cot_ref):
    at = 0
    for turned, column, piece, row, count in plan:
        hidden_ref[:, at : at + count] = refs[turned][:, column : column + count]
        cot_ref[at : at + count, :] = refs[piece][row : row + count, :]
        at += count


def first_grad_kernel(plan, *refs):
    out_ref, hidden_ref, cot_ref = refs[-3:]
    gather_grad(plan, refs, hidden_ref, cot_ref)
    for j in range(out_ref.shape[0] // TILE):
        part = slice(j * TILE, (j + 1) * TILE)
        out_ref[part, :] = jnp.dot(
            hidden_ref[part, :], cot_ref[...], preferred_element_type=F32
        )


def last_grad_kernel(plan, first_ref, *refs):
    out_hbm, out_ref, hidden_ref, cot_ref, semaphores = refs[-5:]
    gather_grad(plan, refs, hidden_ref, cot_ref)
    copies = []
    for j in range(first_ref.shape[0] // TILE):
        part = slice(j * TILE, (j + 1) * TILE)
        total = jnp.dot(hidden_ref[part, :], cot_ref[...], preferred_element_type=F32)
        out_ref[part, :] = (first_ref[part, :] + total).astype(BF16)
        copies.append(
            pltpu.make_async_copy(out_ref.at[part, :], out_hbm.at[0, part, :], semaphores.at[j])
        )
        copies[-1].start()
    for copy in copies:
        copy.wait()


def combine_kernel(experts, plane_ref, tokens_ref, routes_ref, nums_ref, *refs):
    values, out = refs[:-1], refs[-1]
    routes = routes_ref[...]
    placings = placing_of(routes, plane_ref[0], experts, values[0].shape[0])
    gates = gates_of(routes, nums_ref[...], plane_ref[0], experts)
    fill = -experts % 8
    if fill:
        gates = jnp.concatenate([gates, jnp.zeros((fill, gates.shape[1]), F32)], 0)
    gates = gates.T
    total = tokens_ref[...].astype(F32)
    for s, value in enumerate(values):
        picked = lax.dot_general(
            placings[s].astype(BF16),
            value[...],
            (((0,), (0,)), ((), ())),
            preferred_element_type=F32,
        )
        total = total + gates[:, s : s + 1] * picked
    out[...] = total.astype(BF16)


def on_device(tokens, cotangent, routes, gate_nums, gain, w_gate, w_up, w_down):
    devices = lax.axis_size("expert")
    experts = devices // HSPLIT
    rows_here, width = tokens.shape
    hidden_width = w_gate.shape[2]
    top_count = routes.shape[1]
    capacity = HSPLIT * (3 * top_count * rows_here // (2 * experts * HSPLIT))
    capacity = -(-capacity // 16) * 16
    shifts = max(1, experts // GROUPS)
    turns = sorted(range(experts), key=lambda s: (min(s, experts - s), s))
    groups = [turns[g : g + shifts] for g in range(0, experts, shifts)]
    height = shifts * capacity
    plane = (lax.axis_index("expert") // HSPLIT).astype(jnp.int32).reshape(1)
    routes, gate_nums, gain = routes.T, gate_nums.T, gain.reshape(1, -1)
    scalar = pl.BlockSpec(memory_space=pltpu.SMEM)
    anywhere = pl.BlockSpec(memory_space=pl.ANY)
    piece = jax.ShapeDtypeStruct((capacity, width), BF16)
    live = {}

    def swap(value, mask):
        return lax.ppermute(value, "expert", [(i, i ^ mask) for i in range(devices)])

    def turn(value, steps):
        to = [(i, (i + steps * HSPLIT) % devices) for i in range(devices)]
        return lax.ppermute(value, "expert", to)

    def sync():
        values = lax.optimization_barrier(tuple(live.values()))
        live.update(zip(list(live), values))

    def join(parts):
        return parts[0] if len(parts) == 1 else jnp.concatenate(parts, 0)

    flying, slow = {}, []

    def small(kernel, name, outs, *values):
        return call(
            kernel,
            8,
            name,
            out_shape=[jax.ShapeDtypeStruct((rows, width), BF16) for rows in outs],
            in_specs=whole(len(values)),
            out_specs=whole(len(outs)),
        )(*values)

    def land(*names):
        names = [n for name in names for n in flights_of(name)]
        quick = [name for name in names if name[0] == "c"]
        names = [name for name in names if name[0] != "c"]
        values = [flying.pop(name) for name in names]
        if not names:
            names, values = [("C", groups[-1][-1])], [live["C", groups[-1][-1]]]
        values = through(values, "land", LINK_WORK)
        landed = list(zip(names, values))
        if quick:
            cores = tuple(flying.pop(name) for name in quick) + (values[0],)
            cores = lax.optimization_barrier(cores)[: len(quick)]
            landed += list(zip(quick, through(cores, "land_core")))
        live.update(landed)
        sync()
        for name in quick:
            values = [live.pop(name)]
            if len(name) > 2:
                values = small(split_kernel, "split", [2 * height] * 2, *values)
            live.update({("c",) + item: value for item, value in zip(name[1:], values)})

    def flights_of(name):
        if name[0] == "c":
            return [name]
        axis, kind, g = name
        return [(kind, s) for s in groups[g] if s] if axis == "z" else [name]

    def z(kind, g):
        for s in groups[g]:
            if s:
                flying[kind, s] = turn(live[kind, s], -s if kind == "R" else s)

    def y(kind, g):
        if kind == "R":
            keep, crossed = live["keep", (g,)], live["c", "R", g]
            (value,) = small(fold_kernel, "fold", [height], keep, crossed)
        else:
            value = join([live.pop((kind, s)) for s in groups[g]])
            live["sent", kind, g] = value
        flying["y", kind, g] = swap(value, 2)

    def c(*items):
        values = []
        for kind, g in items:
            if kind == "R":
                values.append(live.pop(("send", (g,))))
                continue
            here, came = live.pop(("sent", kind, g)), live.pop(("y", kind, g))
            (value,) = small(pair_kernel, "pair", [2 * height], here, came)
            live[kind, "own", (g,)] = value
            values.append(value)
        if len(values) > 1:
            values = small(pair_kernel, "pair", [4 * height], *values)
        flying[("c",) + items] = swap(values[0], 1)

    def total(g):
        values = live.pop(("keep", (g,))), live.pop(("c", "R", g)), live.pop(("y", "R", g))
        outs = small(total_kernel, "total", [capacity] * shifts, *values)
        live.update({("R", s): out for s, out in zip(groups[g], outs)})

    def ffn(*gs):
        pieces = [live.pop(("N", "own", gs)), live.pop(("c", "N", gs[0]))]
        half = jax.ShapeDtypeStruct(pieces[0].shape, BF16)
        rows = 2 * half.shape[0]
        live["turned", gs], live["keep", gs], live["send", gs] = call(
            functools.partial(ffn_kernel, len(pieces)),
            24,
            "ffn",
            out_shape=[jax.ShapeDtypeStruct((hidden_width, rows), BF16), half, half],
            in_specs=whole(len(pieces) + 3),
            out_specs=whole(3),
            scratch_shapes=[
                pltpu.VMEM((rows, width), BF16),
                pltpu.VMEM((rows, hidden_width), BF16),
            ],
        )(*pieces, live["w", 0], live["w", 1], live["w", 2])

    def in_hbm(*values):
        return [pltpu.with_memory_space_constraint(v, pltpu.HBM) for v in values]

    def send():
        sources = (tokens, cotangent, routes, gate_nums, gain)
        values = call(
            functools.partial(send_kernel, experts),
            16,
            "send",
            out_shape=[piece] * (2 * experts),
            in_specs=[scalar] + [anywhere] * len(sources),
            out_specs=whole(2 * experts),
            scratch_shapes=[pltpu.VMEM(v.shape, v.dtype) for v in sources]
            + [pltpu.SemaphoreType.DMA((len(sources),))],
        )(plane, *in_hbm(*sources))
        live.update({("N", s): value for s, value in enumerate(values[:experts])})
        live.update({("C", s): value for s, value in enumerate(values[experts:])})

    def load():
        weight = jax.ShapeDtypeStruct((width, hidden_width), BF16)
        values = call(
            load_kernel,
            16,
            "load",
            out_shape=[weight, weight, jax.ShapeDtypeStruct((hidden_width, width), BF16)],
            in_specs=[anywhere] * 3,
            out_specs=whole(3),
            scratch_shapes=[pltpu.SemaphoreType.DMA((3,))],
        )(*in_hbm(after(w_gate, live["C", groups[-1][-1]]), w_up, w_down))
        live.update({("w", i): value for i, value in enumerate(values)})

    def grad_call(turned, pieces):
        columns = {}
        for i, gs in enumerate(turned):
            at = 0
            for half in ("own", "other"):
                for side in range(2):
                    for g in gs:
                        columns[half, side, g] = (i, at)
                        at += height
        plan = []
        for i, name in enumerate(pieces):
            half = "other" if name[0] == "c" else "own"
            g = name[-1] if half == "other" else name[-1][0]
            for side in range(2):
                where, at = columns[half, side, g]
                plan.append((where, at, len(turned) + i, side * height, height))
        rows = sum(step[-1] for step in plan)
        sides = [pltpu.VMEM((hidden_width, rows), BF16), pltpu.VMEM((rows, width), BF16)]
        values = [live["turned", gs] for gs in turned]
        values += [live[name] for name in pieces]
        return plan, sides, values

    def first_grad(turned, pieces):
        plan, sides, values = grad_call(turned, pieces)
        live["first"] = call(
            functools.partial(first_grad_kernel, plan),
            24,
            "first_grad",
            out_shape=jax.ShapeDtypeStruct((hidden_width, width), F32),
            in_specs=whole(len(values)),
            out_specs=whole(1)[0],
            scratch_shapes=sides,
        )(*values)

    def last_grad(turned, pieces):
        plan, sides, values = grad_call(turned, pieces)
        return call(
            functools.partial(last_grad_kernel, plan),
            24,
            "last_grad",
            out_shape=jax.ShapeDtypeStruct((1, hidden_width, width), BF16),
            in_specs=whole(1 + len(values)),
            out_specs=anywhere,
            scratch_shapes=[pltpu.VMEM((hidden_width, width), BF16)]
            + sides
            + [pltpu.SemaphoreType.DMA((hidden_width // TILE,))],
        )(live["first"], *values)

    steps = {
        "z": z,
        "y": y,
        "c": c,
        "ffn": lambda kind, g: ffn(g),
        "total": lambda kind, g: total(g),
        "load": lambda kind, g: load(),
        "grad": lambda kind, g: first_grad(
            [(0,), (1,)],
            [("C", "own", (0,)), ("C", "own", (1,)), ("c", "C", 0), ("c", "C", 1)],
        ),
    }
    def name_of(act):
        marks = act.lstrip("abcdefghijklmnopqrstuvwxyz")
        items = [(marks[i], int(marks[i + 1])) for i in range(0, len(marks), 2)]
        return (act[: len(act) - len(marks)],) + tuple(items)

    send()
    if shifts > 1:
        z("N", 0)
        z("C", 0)
        land(("z", "N", 0), ("z", "C", 0))
    sync()
    for starts, lands in PLAN:
        for act in starts.split():
            name = name_of(act)
            steps[name[0]](*(name[1:] if name[0] == "c" else name[1]))
        if lands is None:
            break
        land(*[n if n[0] == "c" else (n[0],) + n[1] for n in map(name_of, lands.split())])
    live["c", "C", 3] = flying.pop(("c", ("C", 3)))
    grad_down = last_grad(
        [(2,), (3,)],
        [("C", "own", (2,)), ("C", "own", (3,)), ("c", "C", 2), ("c", "C", 3)],
    )
    mixed = call(
        functools.partial(combine_kernel, experts),
        16,
        "combine",
        out_shape=jax.ShapeDtypeStruct(tokens.shape, BF16),
        in_specs=[scalar] + whole(3 + experts),
        out_specs=whole(1)[0],
    )(plane, tokens, routes, gate_nums, *[live["R", s] for s in range(experts)])
    return (mixed, grad_down)


def solution(mesh):
    placed = (
        P(("group", "expert"), None),
        P(("group", "expert"), None),
        P(("group", "expert"), None),
        P(("group", "expert"), None),
        P(),
        P("expert", None, None),
        P("expert", None, None),
        P("expert", None, None),
    )
    return jax.shard_map(
        on_device,
        mesh=mesh,
        in_specs=placed,
        out_specs=(P(("group", "expert"), None), P(("group", "expert"), None, None)),
        check_vma=False,
    )
```

```python
import functools

import jax
import jax.numpy as jnp
from jax import lax
from jax.experimental import pallas as pl
from jax.experimental.pallas import tpu as pltpu
from jax.sharding import PartitionSpec as P

HSPLIT = 4
GROUPS = 4
PLAN = (
    ("zN1 zN2 yN0 loadW0", ""),
    ("yC0 zN3", "yN0 zN1 zN2"),
    ("cN0 yN1", "yC0 cN0"),
    ("ffnN0 yN2", "yN1 zN3"),
    ("cR0N1 yN3 zC1 zC2", "yN2 cR0N1"),
    ("ffnN1 cN2 yR0", "yN3 zC1 zC2 cN2"),
    ("cR1N3 ffnN2 yC1 zC3", "yR0 cR1N3"),
    ("cR2 ffnN3 yR1 totalR0", "yC1 zC3 cR2"),
    ("cR3 yR2", "yR1 cR3"),
    ("totalR1 zR1 yR3 cC0", "yR2 cC0"),
    ("totalR2 zR2 yC2", "yR3 zR1"),
    ("totalR3 zR3 yC3 cC1", "yC2 zR2 cC1"),
    ("cC2 gradC0", "yC3 zR3 cC2"),
    ("cC3", None),
)
TILE = 256
LINK_WORK = 10 << 30
F32 = jnp.float32
BF16 = jnp.bfloat16


def after(value, *earlier):
    return lax.optimization_barrier((value,) + earlier)[0]


def whole(count):
    return [pl.BlockSpec(memory_space=pltpu.VMEM)] * count


def call(kernel, mib, name, moved=0, **keywords):
    return pl.pallas_call(
        kernel,
        compiler_params=pltpu.CompilerParams(vmem_limit_bytes=mib << 20),
        cost_estimate=pl.CostEstimate(flops=moved, bytes_accessed=0, transcendentals=0),
        name=name,
        **keywords,
    )


def experts_of(plane, experts, rows):
    ahead = lax.broadcasted_iota(jnp.int32, (experts, rows), 0) + plane
    return jnp.where(ahead >= experts, ahead - experts, ahead)


def placing_of(routes, plane, experts, capacity):
    rows = routes.shape[1]
    expert = experts_of(plane, experts, rows)
    member = jnp.zeros((experts, rows), jnp.bool_)
    for k in range(routes.shape[0]):
        member = member | (routes[k : k + 1, :] == expert)
    first = lax.broadcasted_iota(jnp.int32, (rows, rows), 0)
    second = lax.broadcasted_iota(jnp.int32, (rows, rows), 1)
    upto = (first <= second).astype(F32).astype(BF16)
    ones = member.astype(F32)
    count = jnp.dot(ones.astype(BF16), upto, preferred_element_type=F32)
    place = (ones * count).astype(jnp.int32) - 1
    slots = lax.broadcasted_iota(jnp.int32, (capacity, rows), 0)
    return [(slots == place[s : s + 1, :]).astype(F32) for s in range(experts)]


def gates_of(routes, numbers, plane, experts):
    expert = experts_of(plane, experts, routes.shape[1])
    numerators = numbers.astype(F32)
    gates = numerators / jnp.sum(numerators, 0, keepdims=True)
    gate = jnp.zeros(expert.shape, F32)
    for k in range(routes.shape[0]):
        gate = gate + jnp.where(routes[k : k + 1, :] == expert, gates[k : k + 1, :], 0.0)
    return gate


def fetch(semaphores, *pairs):
    copies = [
        pltpu.make_async_copy(source, target, semaphores.at[i])
        for i, (source, target) in enumerate(pairs)
    ]
    for copy in copies:
        copy.start()
    return copies


def send_kernel(experts, plane_ref, *refs):
    sources, refs = refs[:5], refs[5:]
    row_outs, grad_outs = refs[:experts], refs[experts : 2 * experts]
    targets, semaphores = refs[2 * experts : -1], refs[-1]
    tokens_ref, cot_ref, routes_ref, nums_ref, gain_ref = targets
    copies = fetch(semaphores, *zip(sources, targets))
    copies[2].wait()
    copies[3].wait()
    routes = routes_ref[...]
    placings = placing_of(routes, plane_ref[0], experts, row_outs[0].shape[0])
    gates = gates_of(routes, nums_ref[...], plane_ref[0], experts)
    copies[4].wait()
    copies[0].wait()
    frames = tokens_ref[...].astype(F32)
    inverse = lax.rsqrt(jnp.mean(frames * frames, -1, keepdims=True) + 1e-06)
    normed = (frames * inverse * gain_ref[...]).astype(BF16)
    for out, placing in zip(row_outs, placings):
        out[...] = jnp.dot(placing.astype(BF16), normed, preferred_element_type=F32).astype(BF16)
    copies[1].wait()
    cot = cot_ref[...]
    for s, (out, placing) in enumerate(zip(grad_outs, placings)):
        picked = jnp.dot(placing.astype(BF16), cot, preferred_element_type=F32)
        gate = jnp.sum(placing * gates[s : s + 1, :], -1, keepdims=True)
        out[...] = (gate * picked).astype(BF16)


def load_kernel(*refs):
    sources, outs, semaphores = refs[:3], refs[3:6], refs[6]
    copies = fetch(semaphores, *[(s.at[0], o) for s, o in zip(sources, outs)])
    for copy in copies:
        copy.wait()


def pair_kernel(first_ref, second_ref, out_ref):
    rows = first_ref.shape[0]
    out_ref[:rows, :] = first_ref[...]
    out_ref[rows:, :] = second_ref[...]


def split_kernel(both_ref, first_ref, second_ref):
    rows = first_ref.shape[0]
    first_ref[...] = both_ref[:rows, :]
    second_ref[...] = both_ref[rows:, :]


def fold_kernel(keep_ref, crossed_ref, out_ref):
    rows = out_ref.shape[0]
    total = keep_ref[rows:, :].astype(F32) + crossed_ref[rows:, :].astype(F32)
    out_ref[...] = total.astype(BF16)


def total_kernel(keep_ref, crossed_ref, came_ref, *outs):
    at = 0
    for out in outs:
        part = slice(at, at + out.shape[0])
        total = keep_ref[part, :].astype(F32) + crossed_ref[part, :].astype(F32)
        out[...] = (total + came_ref[part, :].astype(F32)).astype(BF16)
        at += out.shape[0]


def nothing(*refs):
    pass


def through(values, name, moved=0, earlier=()):
    count = len(values)
    return call(
        nothing,
        4,
        name,
        moved,
        out_shape=[jax.ShapeDtypeStruct(v.shape, v.dtype) for v in values],
        in_specs=whole(count) + [pl.BlockSpec(memory_space=pl.ANY)] * len(earlier),
        out_specs=whole(count),
        input_output_aliases={i: i for i in range(count)},
    )(*values, *earlier)


def ffn_kernel(count, *refs):
    pieces, refs = refs[:count], refs[count:]
    gate_ref, up_ref, down_ref, turned_ref, keep_ref, send_ref, rows_ref, hidden_ref = refs
    at = 0
    for piece in pieces:
        rows_ref[at : at + piece.shape[0], :] = piece[...]
        at += piece.shape[0]
    rows = rows_ref[...]
    half = keep_ref.shape[0]
    for j in range(gate_ref.shape[1] // TILE):
        columns = slice(j * TILE, (j + 1) * TILE)
        pre_gate = jnp.dot(rows, gate_ref[:, columns], preferred_element_type=F32)
        pre_up = jnp.dot(rows, up_ref[:, columns], preferred_element_type=F32)
        hidden = pre_gate * lax.logistic(pre_gate) * pre_up
        hidden_ref[:, columns] = hidden.astype(BF16)
        turned_ref[columns, :] = hidden.T.astype(BF16)
    for j in range(down_ref.shape[1] // TILE):
        columns = slice(j * TILE, (j + 1) * TILE)
        value = jnp.dot(
            hidden_ref[...], down_ref[:, columns], preferred_element_type=F32
        ).astype(BF16)
        keep_ref[:, columns] = value[:half]
        send_ref[:, columns] = value[half:]


def gather_grad(plan, refs, hidden_ref, cot_ref):
    at = 0
    for turned, column, piece, row, count in plan:
        hidden_ref[:, at : at + count] = refs[turned][:, column : column + count]
        cot_ref[at : at + count, :] = refs[piece][row : row + count, :]
        at += count


def first_grad_kernel(plan, *refs):
    out_ref, hidden_ref, cot_ref = refs[-3:]
    gather_grad(plan, refs, hidden_ref, cot_ref)
    for j in range(out_ref.shape[0] // TILE):
        part = slice(j * TILE, (j + 1) * TILE)
        out_ref[part, :] = jnp.dot(
            hidden_ref[part, :], cot_ref[...], preferred_element_type=F32
        )


def last_grad_kernel(plan, first_ref, *refs):
    out_hbm, out_ref, hidden_ref, cot_ref, semaphores = refs[-5:]
    gather_grad(plan, refs, hidden_ref, cot_ref)
    copies = []
    for j in range(first_ref.shape[0] // TILE):
        part = slice(j * TILE, (j + 1) * TILE)
        total = jnp.dot(hidden_ref[part, :], cot_ref[...], preferred_element_type=F32)
        out_ref[part, :] = (first_ref[part, :] + total).astype(BF16)
        copies.append(
            pltpu.make_async_copy(out_ref.at[part, :], out_hbm.at[0, part, :], semaphores.at[j])
        )
        copies[-1].start()
    for copy in copies:
        copy.wait()


def combine_kernel(experts, plane_ref, tokens_ref, routes_ref, nums_ref, *refs):
    values, out = refs[:-1], refs[-1]
    routes = routes_ref[...]
    placings = placing_of(routes, plane_ref[0], experts, values[0].shape[0])
    gates = gates_of(routes, nums_ref[...], plane_ref[0], experts)
    fill = -experts % 8
    if fill:
        gates = jnp.concatenate([gates, jnp.zeros((fill, gates.shape[1]), F32)], 0)
    gates = gates.T
    total = tokens_ref[...].astype(F32)
    for s, value in enumerate(values):
        picked = lax.dot_general(
            placings[s].astype(BF16),
            value[...],
            (((0,), (0,)), ((), ())),
            preferred_element_type=F32,
        )
        total = total + gates[:, s : s + 1] * picked
    out[...] = total.astype(BF16)


def on_device(tokens, cotangent, routes, gate_nums, gain, w_gate, w_up, w_down):
    devices = lax.axis_size("expert")
    experts = devices // HSPLIT
    rows_here, width = tokens.shape
    hidden_width = w_gate.shape[2]
    top_count = routes.shape[1]
    capacity = HSPLIT * (3 * top_count * rows_here // (2 * experts * HSPLIT))
    capacity = -(-capacity // 16) * 16
    shifts = max(1, experts // GROUPS)
    turns = sorted(range(experts), key=lambda s: (min(s, experts - s), s))
    groups = [turns[g : g + shifts] for g in range(0, experts, shifts)]
    height = shifts * capacity
    plane = (lax.axis_index("expert") // HSPLIT).astype(jnp.int32).reshape(1)
    routes, gate_nums, gain = routes.T, gate_nums.T, gain.reshape(1, -1)
    scalar = pl.BlockSpec(memory_space=pltpu.SMEM)
    anywhere = pl.BlockSpec(memory_space=pl.ANY)
    piece = jax.ShapeDtypeStruct((capacity, width), BF16)
    live = {}

    def swap(value, mask):
        return lax.ppermute(value, "expert", [(i, i ^ mask) for i in range(devices)])

    def turn(value, steps):
        to = [(i, (i + steps * HSPLIT) % devices) for i in range(devices)]
        return lax.ppermute(value, "expert", to)

    def sync():
        values = lax.optimization_barrier(tuple(live.values()))
        live.update(zip(list(live), values))

    def join(parts):
        return parts[0] if len(parts) == 1 else jnp.concatenate(parts, 0)

    flying, slow = {}, []

    def small(kernel, name, outs, *values):
        return call(
            kernel,
            8,
            name,
            out_shape=[jax.ShapeDtypeStruct((rows, width), BF16) for rows in outs],
            in_specs=whole(len(values)),
            out_specs=whole(len(outs)),
        )(*values)

    def land(*names, earlier=()):
        names = [n for name in names for n in flights_of(name)]
        quick = [name for name in names if name[0] == "c"]
        names = [name for name in names if name[0] != "c"]
        values = [flying.pop(name) for name in names]
        if not names:
            names, values = [("C", groups[-1][-1])], [live["C", groups[-1][-1]]]
        values = through(values, "land", LINK_WORK, earlier)
        landed = list(zip(names, values))
        if quick:
            cores = tuple(flying.pop(name) for name in quick) + (values[0],)
            cores = lax.optimization_barrier(cores)[: len(quick)]
            landed += list(zip(quick, through(cores, "land_core")))
        live.update(landed)
        sync()
        for name in quick:
            values = [live.pop(name)]
            if len(name) > 2:
                values = small(split_kernel, "split", [2 * height] * 2, *values)
            live.update({("c",) + item: value for item, value in zip(name[1:], values)})

    def flights_of(name):
        if name[0] == "c":
            return [name]
        axis, kind, g = name
        return [(kind, s) for s in groups[g] if s] if axis == "z" else [name]

    def z(kind, g):
        for s in groups[g]:
            if s:
                flying[kind, s] = turn(live[kind, s], -s if kind == "R" else s)

    def y(kind, g):
        if kind == "R":
            keep, crossed = live["keep", (g,)], live["c", "R", g]
            (value,) = small(fold_kernel, "fold", [height], keep, crossed)
        else:
            value = join([live.pop((kind, s)) for s in groups[g]])
            live["sent", kind, g] = value
        flying["y", kind, g] = swap(value, 2)

    def c(*items):
        values = []
        for kind, g in items:
            if kind == "R":
                values.append(live.pop(("send", (g,))))
                continue
            here, came = live.pop(("sent", kind, g)), live.pop(("y", kind, g))
            (value,) = small(pair_kernel, "pair", [2 * height], here, came)
            live[kind, "own", (g,)] = value
            values.append(value)
        if len(values) > 1:
            values = small(pair_kernel, "pair", [4 * height], *values)
        flying[("c",) + items] = swap(values[0], 1)

    def total(g):
        values = live.pop(("keep", (g,))), live.pop(("c", "R", g)), live.pop(("y", "R", g))
        outs = small(total_kernel, "total", [capacity] * shifts, *values)
        live.update({("R", s): out for s, out in zip(groups[g], outs)})

    def ffn(*gs):
        pieces = [live.pop(("N", "own", gs)), live.pop(("c", "N", gs[0]))]
        half = jax.ShapeDtypeStruct(pieces[0].shape, BF16)
        rows = 2 * half.shape[0]
        live["turned", gs], live["keep", gs], live["send", gs] = call(
            functools.partial(ffn_kernel, len(pieces)),
            24,
            "ffn",
            out_shape=[jax.ShapeDtypeStruct((hidden_width, rows), BF16), half, half],
            in_specs=whole(len(pieces) + 3),
            out_specs=whole(3),
            scratch_shapes=[
                pltpu.VMEM((rows, width), BF16),
                pltpu.VMEM((rows, hidden_width), BF16),
            ],
        )(*pieces, live["w", 0], live["w", 1], live["w", 2])

    def in_hbm(*values):
        return [pltpu.with_memory_space_constraint(v, pltpu.HBM) for v in values]

    def send():
        sources = (tokens, cotangent, routes, gate_nums, gain)
        values = call(
            functools.partial(send_kernel, experts),
            16,
            "send",
            out_shape=[piece] * (2 * experts),
            in_specs=[scalar] + [anywhere] * len(sources),
            out_specs=whole(2 * experts),
            scratch_shapes=[pltpu.VMEM(v.shape, v.dtype) for v in sources]
            + [pltpu.SemaphoreType.DMA((len(sources),))],
        )(plane, *in_hbm(*sources))
        live.update({("N", s): value for s, value in enumerate(values[:experts])})
        live.update({("C", s): value for s, value in enumerate(values[experts:])})

    def load():
        weight = jax.ShapeDtypeStruct((width, hidden_width), BF16)
        values = call(
            load_kernel,
            16,
            "load",
            out_shape=[weight, weight, jax.ShapeDtypeStruct((hidden_width, width), BF16)],
            in_specs=[anywhere] * 3,
            out_specs=whole(3),
            scratch_shapes=[pltpu.SemaphoreType.DMA((3,))],
        )(*in_hbm(after(w_gate, live["C", groups[-1][-1]]), w_up, w_down))
        live.update({("w", i): value for i, value in enumerate(values)})

    def grad_call(turned, pieces):
        columns = {}
        for i, gs in enumerate(turned):
            at = 0
            for half in ("own", "other"):
                for side in range(2):
                    for g in gs:
                        columns[half, side, g] = (i, at)
                        at += height
        plan = []
        for i, name in enumerate(pieces):
            half = "other" if name[0] == "c" else "own"
            g = name[-1] if half == "other" else name[-1][0]
            for side in range(2):
                where, at = columns[half, side, g]
                plan.append((where, at, len(turned) + i, side * height, height))
        rows = sum(step[-1] for step in plan)
        sides = [pltpu.VMEM((hidden_width, rows), BF16), pltpu.VMEM((rows, width), BF16)]
        values = [live["turned", gs] for gs in turned]
        values += [live[name] for name in pieces]
        return plan, sides, values

    def first_grad(turned, pieces):
        plan, sides, values = grad_call(turned, pieces)
        live["first"] = call(
            functools.partial(first_grad_kernel, plan),
            24,
            "first_grad",
            out_shape=jax.ShapeDtypeStruct((hidden_width, width), F32),
            in_specs=whole(len(values)),
            out_specs=whole(1)[0],
            scratch_shapes=sides,
        )(*values)

    def last_grad(turned, pieces):
        plan, sides, values = grad_call(turned, pieces)
        return call(
            functools.partial(last_grad_kernel, plan),
            24,
            "last_grad",
            out_shape=jax.ShapeDtypeStruct((1, hidden_width, width), BF16),
            in_specs=whole(1 + len(values)),
            out_specs=anywhere,
            scratch_shapes=[pltpu.VMEM((hidden_width, width), BF16)]
            + sides
            + [pltpu.SemaphoreType.DMA((hidden_width // TILE,))],
        )(live["first"], *values)

    steps = {
        "z": z,
        "y": y,
        "c": c,
        "ffn": lambda kind, g: ffn(g),
        "total": lambda kind, g: total(g),
        "load": lambda kind, g: load(),
        "grad": lambda kind, g: first_grad(
            [(0,), (1,)],
            [("C", "own", (0,)), ("C", "own", (1,)), ("c", "C", 0), ("c", "C", 1)],
        ),
    }
    def name_of(act):
        marks = act.lstrip("abcdefghijklmnopqrstuvwxyz")
        items = [(marks[i], int(marks[i + 1])) for i in range(0, len(marks), 2)]
        return (act[: len(act) - len(marks)],) + tuple(items)

    send()
    if shifts > 1:
        z("N", 0)
        z("C", 0)
        land(("z", "N", 0), ("z", "C", 0))
    sync()
    for starts, lands in PLAN:
        kernels = []
        for act in starts.split():
            name = name_of(act)
            steps[name[0]](*(name[1:] if name[0] == "c" else name[1]))
            if name[0] == "ffn":
                kernels.append(live["turned", name[1][1:]])
            if name[0] == "grad":
                kernels.append(live["first"])
        if lands is None:
            break
        names = [n if n[0] == "c" else (n[0],) + n[1] for n in map(name_of, lands.split())]
        land(*names, earlier=kernels)
    live["c", "C", 3] = flying.pop(("c", ("C", 3)))
    grad_down = last_grad(
        [(2,), (3,)],
        [("C", "own", (2,)), ("C", "own", (3,)), ("c", "C", 2), ("c", "C", 3)],
    )
    mixed = call(
        functools.partial(combine_kernel, experts),
        16,
        "combine",
        out_shape=jax.ShapeDtypeStruct(tokens.shape, BF16),
        in_specs=[scalar] + whole(3 + experts),
        out_specs=whole(1)[0],
    )(plane, tokens, routes, gate_nums, *[live["R", s] for s in range(experts)])
    return (mixed, grad_down)


def solution(mesh):
    placed = (
        P(("group", "expert"), None),
        P(("group", "expert"), None),
        P(("group", "expert"), None),
        P(("group", "expert"), None),
        P(),
        P("expert", None, None),
        P("expert", None, None),
        P("expert", None, None),
    )
    return jax.shard_map(
        on_device,
        mesh=mesh,
        in_specs=placed,
        out_specs=(P(("group", "expert"), None), P(("group", "expert"), None, None)),
        check_vma=False,
    )
```

```python
import functools

import jax
import jax.numpy as jnp
from jax import lax
from jax.experimental import pallas as pl
from jax.experimental.pallas import tpu as pltpu
from jax.sharding import PartitionSpec as P

HSPLIT = 4
GROUPS = 4
PLAN = (
    ("yN0 zN1 zN2", ""),
    ("yC0 zN3 loadW0", "yN0 zN1 zN2"),
    ("cN0 yN1", "yC0 cN0"),
    ("ffnN0 yN2 zC1", "yN1 zN3"),
    ("cR0N1 yN3 zC2", "yN2 zC1 cR0N1"),
    ("cN2 ffnN1 cR1 yR0", "yN3 zC2 cN2 cR1"),
    ("cN3 ffnN2 cR2 yR1 zC3", "yR0 cN3 cR2"),
    ("ffnN3 cR3 yR2 totalR0", "yR1 zC3 cR3"),
    ("totalR1 zR1 yR3 cC0", "yR2 cC0"),
    ("totalR2 zR2 yC1", "yR3 zR1"),
    ("totalR3 zR3 yC2", "yC1 zR2"),
    ("cC1 yC3", "yC2 zR3 cC1"),
    ("cC2 gradC0", "yC3 cC2"),
    ("cC3", None),
)
TILE = 256
LINK_WORK = 10 << 30
F32 = jnp.float32
BF16 = jnp.bfloat16


def after(value, *earlier):
    return lax.optimization_barrier((value,) + earlier)[0]


def whole(count):
    return [pl.BlockSpec(memory_space=pltpu.VMEM)] * count


def call(kernel, mib, name, moved=0, **keywords):
    return pl.pallas_call(
        kernel,
        compiler_params=pltpu.CompilerParams(vmem_limit_bytes=mib << 20),
        cost_estimate=pl.CostEstimate(flops=moved, bytes_accessed=0, transcendentals=0),
        name=name,
        **keywords,
    )


def experts_of(plane, experts, rows):
    ahead = lax.broadcasted_iota(jnp.int32, (experts, rows), 0) + plane
    return jnp.where(ahead >= experts, ahead - experts, ahead)


def placing_of(routes, plane, experts, capacity):
    rows = routes.shape[1]
    expert = experts_of(plane, experts, rows)
    member = jnp.zeros((experts, rows), jnp.bool_)
    for k in range(routes.shape[0]):
        member = member | (routes[k : k + 1, :] == expert)
    first = lax.broadcasted_iota(jnp.int32, (rows, rows), 0)
    second = lax.broadcasted_iota(jnp.int32, (rows, rows), 1)
    upto = (first <= second).astype(F32).astype(BF16)
    ones = member.astype(F32)
    count = jnp.dot(ones.astype(BF16), upto, preferred_element_type=F32)
    place = (ones * count).astype(jnp.int32) - 1
    slots = lax.broadcasted_iota(jnp.int32, (capacity, rows), 0)
    return [(slots == place[s : s + 1, :]).astype(F32) for s in range(experts)]


def gates_of(routes, numbers, plane, experts):
    expert = experts_of(plane, experts, routes.shape[1])
    numerators = numbers.astype(F32)
    gates = numerators / jnp.sum(numerators, 0, keepdims=True)
    gate = jnp.zeros(expert.shape, F32)
    for k in range(routes.shape[0]):
        gate = gate + jnp.where(routes[k : k + 1, :] == expert, gates[k : k + 1, :], 0.0)
    return gate


def fetch(semaphores, *pairs):
    copies = [
        pltpu.make_async_copy(source, target, semaphores.at[i])
        for i, (source, target) in enumerate(pairs)
    ]
    for copy in copies:
        copy.start()
    return copies


def send_kernel(experts, plane_ref, *refs):
    sources, refs = refs[:5], refs[5:]
    row_outs, grad_outs = refs[:experts], refs[experts : 2 * experts]
    targets, semaphores = refs[2 * experts : -1], refs[-1]
    tokens_ref, cot_ref, routes_ref, nums_ref, gain_ref = targets
    copies = fetch(semaphores, *zip(sources, targets))
    copies[2].wait()
    copies[3].wait()
    routes = routes_ref[...]
    placings = placing_of(routes, plane_ref[0], experts, row_outs[0].shape[0])
    gates = gates_of(routes, nums_ref[...], plane_ref[0], experts)
    copies[4].wait()
    copies[0].wait()
    frames = tokens_ref[...].astype(F32)
    inverse = lax.rsqrt(jnp.mean(frames * frames, -1, keepdims=True) + 1e-06)
    normed = (frames * inverse * gain_ref[...]).astype(BF16)
    for out, placing in zip(row_outs, placings):
        out[...] = jnp.dot(placing.astype(BF16), normed, preferred_element_type=F32).astype(BF16)
    copies[1].wait()
    cot = cot_ref[...]
    for s, (out, placing) in enumerate(zip(grad_outs, placings)):
        picked = jnp.dot(placing.astype(BF16), cot, preferred_element_type=F32)
        gate = jnp.sum(placing * gates[s : s + 1, :], -1, keepdims=True)
        out[...] = (gate * picked).astype(BF16)


def load_kernel(*refs):
    sources, outs, semaphores = refs[:3], refs[3:6], refs[6]
    copies = fetch(semaphores, *[(s.at[0], o) for s, o in zip(sources, outs)])
    for copy in copies:
        copy.wait()


def pair_kernel(first_ref, second_ref, out_ref):
    rows = first_ref.shape[0]
    out_ref[:rows, :] = first_ref[...]
    out_ref[rows:, :] = second_ref[...]


def split_kernel(both_ref, first_ref, second_ref):
    rows = first_ref.shape[0]
    first_ref[...] = both_ref[:rows, :]
    second_ref[...] = both_ref[rows:, :]


def fold_kernel(keep_ref, crossed_ref, out_ref):
    rows = out_ref.shape[0]
    total = keep_ref[rows:, :].astype(F32) + crossed_ref[rows:, :].astype(F32)
    out_ref[...] = total.astype(BF16)


def total_kernel(keep_ref, crossed_ref, came_ref, *outs):
    at = 0
    for out in outs:
        part = slice(at, at + out.shape[0])
        total = keep_ref[part, :].astype(F32) + crossed_ref[part, :].astype(F32)
        out[...] = (total + came_ref[part, :].astype(F32)).astype(BF16)
        at += out.shape[0]


def nothing(*refs):
    pass


def through(values, name, moved=0, earlier=()):
    count = len(values)
    return call(
        nothing,
        4,
        name,
        moved,
        out_shape=[jax.ShapeDtypeStruct(v.shape, v.dtype) for v in values],
        in_specs=whole(count) + [pl.BlockSpec(memory_space=pl.ANY)] * len(earlier),
        out_specs=whole(count),
        input_output_aliases={i: i for i in range(count)},
    )(*values, *earlier)


def ffn_kernel(count, *refs):
    pieces, refs = refs[:count], refs[count:]
    gate_ref, up_ref, down_ref, turned_ref, keep_ref, send_ref, rows_ref, hidden_ref = refs
    at = 0
    for piece in pieces:
        rows_ref[at : at + piece.shape[0], :] = piece[...]
        at += piece.shape[0]
    rows = rows_ref[...]
    half = keep_ref.shape[0]
    for j in range(gate_ref.shape[1] // TILE):
        columns = slice(j * TILE, (j + 1) * TILE)
        pre_gate = jnp.dot(rows, gate_ref[:, columns], preferred_element_type=F32)
        pre_up = jnp.dot(rows, up_ref[:, columns], preferred_element_type=F32)
        hidden = pre_gate * lax.logistic(pre_gate) * pre_up
        hidden_ref[:, columns] = hidden.astype(BF16)
        turned_ref[columns, :] = hidden.T.astype(BF16)
    for j in range(down_ref.shape[1] // TILE):
        columns = slice(j * TILE, (j + 1) * TILE)
        value = jnp.dot(
            hidden_ref[...], down_ref[:, columns], preferred_element_type=F32
        ).astype(BF16)
        keep_ref[:, columns] = value[:half]
        send_ref[:, columns] = value[half:]


def gather_grad(plan, refs, hidden_ref, cot_ref):
    at = 0
    for turned, column, piece, row, count in plan:
        hidden_ref[:, at : at + count] = refs[turned][:, column : column + count]
        cot_ref[at : at + count, :] = refs[piece][row : row + count, :]
        at += count


def first_grad_kernel(plan, *refs):
    out_ref, hidden_ref, cot_ref = refs[-3:]
    gather_grad(plan, refs, hidden_ref, cot_ref)
    for j in range(out_ref.shape[0] // TILE):
        part = slice(j * TILE, (j + 1) * TILE)
        out_ref[part, :] = jnp.dot(
            hidden_ref[part, :], cot_ref[...], preferred_element_type=F32
        )


def last_grad_kernel(plan, first_ref, *refs):
    out_hbm, out_ref, hidden_ref, cot_ref, semaphores = refs[-5:]
    gather_grad(plan, refs, hidden_ref, cot_ref)
    copies = []
    for j in range(first_ref.shape[0] // TILE):
        part = slice(j * TILE, (j + 1) * TILE)
        total = jnp.dot(hidden_ref[part, :], cot_ref[...], preferred_element_type=F32)
        out_ref[part, :] = (first_ref[part, :] + total).astype(BF16)
        copies.append(
            pltpu.make_async_copy(out_ref.at[part, :], out_hbm.at[0, part, :], semaphores.at[j])
        )
        copies[-1].start()
    for copy in copies:
        copy.wait()


def combine_kernel(experts, plane_ref, tokens_ref, routes_ref, nums_ref, *refs):
    values, out = refs[:-1], refs[-1]
    routes = routes_ref[...]
    placings = placing_of(routes, plane_ref[0], experts, values[0].shape[0])
    gates = gates_of(routes, nums_ref[...], plane_ref[0], experts)
    fill = -experts % 8
    if fill:
        gates = jnp.concatenate([gates, jnp.zeros((fill, gates.shape[1]), F32)], 0)
    gates = gates.T
    total = tokens_ref[...].astype(F32)
    for s, value in enumerate(values):
        picked = lax.dot_general(
            placings[s].astype(BF16),
            value[...],
            (((0,), (0,)), ((), ())),
            preferred_element_type=F32,
        )
        total = total + gates[:, s : s + 1] * picked
    out[...] = total.astype(BF16)


def on_device(tokens, cotangent, routes, gate_nums, gain, w_gate, w_up, w_down):
    devices = lax.axis_size("expert")
    experts = devices // HSPLIT
    rows_here, width = tokens.shape
    hidden_width = w_gate.shape[2]
    top_count = routes.shape[1]
    capacity = HSPLIT * (3 * top_count * rows_here // (2 * experts * HSPLIT))
    capacity = -(-capacity // 16) * 16
    shifts = max(1, experts // GROUPS)
    turns = sorted(range(experts), key=lambda s: (min(s, experts - s), s))
    groups = [turns[g : g + shifts] for g in range(0, experts, shifts)]
    height = shifts * capacity
    plane = (lax.axis_index("expert") // HSPLIT).astype(jnp.int32).reshape(1)
    routes, gate_nums, gain = routes.T, gate_nums.T, gain.reshape(1, -1)
    scalar = pl.BlockSpec(memory_space=pltpu.SMEM)
    anywhere = pl.BlockSpec(memory_space=pl.ANY)
    piece = jax.ShapeDtypeStruct((capacity, width), BF16)
    live = {}

    def swap(value, mask):
        return lax.ppermute(value, "expert", [(i, i ^ mask) for i in range(devices)])

    def turn(value, steps):
        to = [(i, (i + steps * HSPLIT) % devices) for i in range(devices)]
        return lax.ppermute(value, "expert", to)

    def sync():
        values = lax.optimization_barrier(tuple(live.values()))
        live.update(zip(list(live), values))

    def join(parts):
        return parts[0] if len(parts) == 1 else jnp.concatenate(parts, 0)

    flying, slow = {}, []

    def small(kernel, name, outs, *values):
        return call(
            kernel,
            8,
            name,
            out_shape=[jax.ShapeDtypeStruct((rows, width), BF16) for rows in outs],
            in_specs=whole(len(values)),
            out_specs=whole(len(outs)),
        )(*values)

    def land(*names, earlier=()):
        names = [n for name in names for n in flights_of(name)]
        quick = [name for name in names if name[0] == "c"]
        names = [name for name in names if name[0] != "c"]
        values = [flying.pop(name) for name in names]
        if not names:
            names, values = [("C", groups[-1][-1])], [live["C", groups[-1][-1]]]
        values = through(values, "land", LINK_WORK, earlier)
        landed = list(zip(names, values))
        if quick:
            cores = tuple(flying.pop(name) for name in quick) + (values[0],)
            cores = lax.optimization_barrier(cores)[: len(quick)]
            landed += list(zip(quick, through(cores, "land_core")))
        live.update(landed)
        sync()
        for name in quick:
            values = [live.pop(name)]
            if len(name) > 2:
                values = small(split_kernel, "split", [2 * height] * 2, *values)
            live.update({("c",) + item: value for item, value in zip(name[1:], values)})

    def flights_of(name):
        if name[0] == "c":
            return [name]
        axis, kind, g = name
        return [(kind, s) for s in groups[g] if s] if axis == "z" else [name]

    def z(kind, g):
        for s in groups[g]:
            if s:
                flying[kind, s] = turn(live[kind, s], -s if kind == "R" else s)

    def y(kind, g):
        if kind == "R":
            keep, crossed = live["keep", (g,)], live["c", "R", g]
            (value,) = small(fold_kernel, "fold", [height], keep, crossed)
        else:
            value = join([live.pop((kind, s)) for s in groups[g]])
            live["sent", kind, g] = value
        flying["y", kind, g] = swap(value, 2)

    def c(*items):
        values = []
        for kind, g in items:
            if kind == "R":
                values.append(live.pop(("send", (g,))))
                continue
            here, came = live.pop(("sent", kind, g)), live.pop(("y", kind, g))
            (value,) = small(pair_kernel, "pair", [2 * height], here, came)
            live[kind, "own", (g,)] = value
            values.append(value)
        if len(values) > 1:
            values = small(pair_kernel, "pair", [4 * height], *values)
        flying[("c",) + items] = swap(values[0], 1)

    def total(g):
        values = live.pop(("keep", (g,))), live.pop(("c", "R", g)), live.pop(("y", "R", g))
        outs = small(total_kernel, "total", [capacity] * shifts, *values)
        live.update({("R", s): out for s, out in zip(groups[g], outs)})

    def ffn(*gs):
        pieces = [live.pop(("N", "own", gs)), live.pop(("c", "N", gs[0]))]
        half = jax.ShapeDtypeStruct(pieces[0].shape, BF16)
        rows = 2 * half.shape[0]
        live["turned", gs], live["keep", gs], live["send", gs] = call(
            functools.partial(ffn_kernel, len(pieces)),
            24,
            "ffn",
            out_shape=[jax.ShapeDtypeStruct((hidden_width, rows), BF16), half, half],
            in_specs=whole(len(pieces) + 3),
            out_specs=whole(3),
            scratch_shapes=[
                pltpu.VMEM((rows, width), BF16),
                pltpu.VMEM((rows, hidden_width), BF16),
            ],
        )(*pieces, live["w", 0], live["w", 1], live["w", 2])

    def in_hbm(*values):
        return [pltpu.with_memory_space_constraint(v, pltpu.HBM) for v in values]

    def send():
        sources = (tokens, cotangent, routes, gate_nums, gain)
        values = call(
            functools.partial(send_kernel, experts),
            16,
            "send",
            out_shape=[piece] * (2 * experts),
            in_specs=[scalar] + [anywhere] * len(sources),
            out_specs=whole(2 * experts),
            scratch_shapes=[pltpu.VMEM(v.shape, v.dtype) for v in sources]
            + [pltpu.SemaphoreType.DMA((len(sources),))],
        )(plane, *in_hbm(*sources))
        live.update({("N", s): value for s, value in enumerate(values[:experts])})
        live.update({("C", s): value for s, value in enumerate(values[experts:])})

    def load():
        weight = jax.ShapeDtypeStruct((width, hidden_width), BF16)
        values = call(
            load_kernel,
            16,
            "load",
            out_shape=[weight, weight, jax.ShapeDtypeStruct((hidden_width, width), BF16)],
            in_specs=[anywhere] * 3,
            out_specs=whole(3),
            scratch_shapes=[pltpu.SemaphoreType.DMA((3,))],
        )(*in_hbm(after(w_gate, live["C", groups[-1][-1]]), w_up, w_down))
        live.update({("w", i): value for i, value in enumerate(values)})

    def grad_call(turned, pieces):
        columns = {}
        for i, gs in enumerate(turned):
            at = 0
            for half in ("own", "other"):
                for side in range(2):
                    for g in gs:
                        columns[half, side, g] = (i, at)
                        at += height
        plan = []
        for i, name in enumerate(pieces):
            half = "other" if name[0] == "c" else "own"
            g = name[-1] if half == "other" else name[-1][0]
            for side in range(2):
                where, at = columns[half, side, g]
                plan.append((where, at, len(turned) + i, side * height, height))
        rows = sum(step[-1] for step in plan)
        sides = [pltpu.VMEM((hidden_width, rows), BF16), pltpu.VMEM((rows, width), BF16)]
        values = [live["turned", gs] for gs in turned]
        values += [live[name] for name in pieces]
        return plan, sides, values

    def first_grad(turned, pieces):
        plan, sides, values = grad_call(turned, pieces)
        live["first"] = call(
            functools.partial(first_grad_kernel, plan),
            24,
            "first_grad",
            out_shape=jax.ShapeDtypeStruct((hidden_width, width), F32),
            in_specs=whole(len(values)),
            out_specs=whole(1)[0],
            scratch_shapes=sides,
        )(*values)

    def last_grad(turned, pieces):
        plan, sides, values = grad_call(turned, pieces)
        return call(
            functools.partial(last_grad_kernel, plan),
            24,
            "last_grad",
            out_shape=jax.ShapeDtypeStruct((1, hidden_width, width), BF16),
            in_specs=whole(1 + len(values)),
            out_specs=anywhere,
            scratch_shapes=[pltpu.VMEM((hidden_width, width), BF16)]
            + sides
            + [pltpu.SemaphoreType.DMA((hidden_width // TILE,))],
        )(live["first"], *values)

    steps = {
        "z": z,
        "y": y,
        "c": c,
        "ffn": lambda kind, g: ffn(g),
        "total": lambda kind, g: total(g),
        "load": lambda kind, g: load(),
        "grad": lambda kind, g: first_grad(
            [(0,), (1,)],
            [("C", "own", (0,)), ("C", "own", (1,)), ("c", "C", 0), ("c", "C", 1)],
        ),
    }
    def name_of(act):
        marks = act.lstrip("abcdefghijklmnopqrstuvwxyz")
        items = [(marks[i], int(marks[i + 1])) for i in range(0, len(marks), 2)]
        return (act[: len(act) - len(marks)],) + tuple(items)

    send()
    if shifts > 1:
        z("N", 0)
        z("C", 0)
        land(("z", "N", 0), ("z", "C", 0))
    sync()
    for starts, lands in PLAN:
        kernels = []
        for act in starts.split():
            name = name_of(act)
            steps[name[0]](*(name[1:] if name[0] == "c" else name[1]))
            if name[0] == "ffn":
                kernels.append(live["turned", name[1][1:]])
            if name[0] == "grad":
                kernels.append(live["first"])
        if lands is None:
            break
        names = [n if n[0] == "c" else (n[0],) + n[1] for n in map(name_of, lands.split())]
        land(*names, earlier=kernels)
    live["c", "C", 3] = flying.pop(("c", ("C", 3)))
    grad_down = last_grad(
        [(2,), (3,)],
        [("C", "own", (2,)), ("C", "own", (3,)), ("c", "C", 2), ("c", "C", 3)],
    )
    mixed = call(
        functools.partial(combine_kernel, experts),
        16,
        "combine",
        out_shape=jax.ShapeDtypeStruct(tokens.shape, BF16),
        in_specs=[scalar] + whole(3 + experts),
        out_specs=whole(1)[0],
    )(plane, tokens, routes, gate_nums, *[live["R", s] for s in range(experts)])
    return (mixed, grad_down)


def solution(mesh):
    placed = (
        P(("group", "expert"), None),
        P(("group", "expert"), None),
        P(("group", "expert"), None),
        P(("group", "expert"), None),
        P(),
        P("expert", None, None),
        P("expert", None, None),
        P("expert", None, None),
    )
    return jax.shard_map(
        on_device,
        mesh=mesh,
        in_specs=placed,
        out_specs=(P(("group", "expert"), None), P(("group", "expert"), None, None)),
        check_vma=False,
    )
```

```python
import functools

import jax
import jax.numpy as jnp
from jax import lax
from jax.experimental import pallas as pl
from jax.experimental.pallas import tpu as pltpu
from jax.sharding import PartitionSpec as P

HSPLIT = 4
GROUPS = 4
PLAN = (
    ("yN0 zN1 zN2 loadW0", ""),
    ("yC0 zN3", "zN1 zN2 yN0"),
    ("cN0 yN1", "yC0 cN0"),
    ("ffnN0 yN2", "yN1 zN3"),
    ("cR0N1 yN3 zC1 zC2", "yN2 cR0N1"),
    ("ffnN1 cN2 yR0", "yN3 zC1 zC2 cN2"),
    ("cR1N3 ffnN2 yC1 zC3", "yR0 cR1N3"),
    ("cR2 ffnN3 yR1 totalR0", "yC1 zC3 cR2"),
    ("", "yR1"),
    ("yR2 totalR1 zR1 cR3", "cR3"),
    ("yR3 yC2", "yR2 zR1"),
    ("totalR2 zR2 yC3 cC0", "yR3 yC2 cC0"),
    ("totalR3 zR3 cC1C2", "yC3 zR2 cC1C2"),
    ("cC3 gradC0", "zR3 cC3"),
)
TILE = 256
LINK_WORK = 10 << 30
F32 = jnp.float32
BF16 = jnp.bfloat16


def after(value, *earlier):
    return lax.optimization_barrier((value,) + earlier)[0]


def whole(count):
    return [pl.BlockSpec(memory_space=pltpu.VMEM)] * count


def call(kernel, mib, name, moved=0, **keywords):
    return pl.pallas_call(
        kernel,
        compiler_params=pltpu.CompilerParams(vmem_limit_bytes=mib << 20),
        cost_estimate=pl.CostEstimate(flops=moved, bytes_accessed=0, transcendentals=0),
        name=name,
        **keywords,
    )


def experts_of(plane, experts, rows):
    ahead = lax.broadcasted_iota(jnp.int32, (experts, rows), 0) + plane
    return jnp.where(ahead >= experts, ahead - experts, ahead)


def placing_of(routes, plane, experts, capacity):
    rows = routes.shape[1]
    expert = experts_of(plane, experts, rows)
    member = jnp.zeros((experts, rows), jnp.bool_)
    for k in range(routes.shape[0]):
        member = member | (routes[k : k + 1, :] == expert)
    first = lax.broadcasted_iota(jnp.int32, (rows, rows), 0)
    second = lax.broadcasted_iota(jnp.int32, (rows, rows), 1)
    upto = (first <= second).astype(F32).astype(BF16)
    ones = member.astype(F32)
    count = jnp.dot(ones.astype(BF16), upto, preferred_element_type=F32)
    place = (ones * count).astype(jnp.int32) - 1
    slots = lax.broadcasted_iota(jnp.int32, (capacity, rows), 0)
    return [(slots == place[s : s + 1, :]).astype(F32) for s in range(experts)]


def gates_of(routes, numbers, plane, experts):
    expert = experts_of(plane, experts, routes.shape[1])
    numerators = numbers.astype(F32)
    gates = numerators / jnp.sum(numerators, 0, keepdims=True)
    gate = jnp.zeros(expert.shape, F32)
    for k in range(routes.shape[0]):
        gate = gate + jnp.where(routes[k : k + 1, :] == expert, gates[k : k + 1, :], 0.0)
    return gate


def fetch(semaphores, *pairs):
    copies = [
        pltpu.make_async_copy(source, target, semaphores.at[i])
        for i, (source, target) in enumerate(pairs)
    ]
    for copy in copies:
        copy.start()
    return copies


def send_kernel(experts, plane_ref, *refs):
    sources, refs = refs[:5], refs[5:]
    row_outs, grad_outs = refs[:experts], refs[experts : 2 * experts]
    targets, semaphores = refs[2 * experts : -1], refs[-1]
    tokens_ref, cot_ref, routes_ref, nums_ref, gain_ref = targets
    copies = fetch(semaphores, *zip(sources, targets))
    copies[2].wait()
    copies[3].wait()
    routes = routes_ref[...]
    placings = placing_of(routes, plane_ref[0], experts, row_outs[0].shape[0])
    gates = gates_of(routes, nums_ref[...], plane_ref[0], experts)
    copies[4].wait()
    copies[0].wait()
    frames = tokens_ref[...].astype(F32)
    inverse = lax.rsqrt(jnp.mean(frames * frames, -1, keepdims=True) + 1e-06)
    normed = (frames * inverse * gain_ref[...]).astype(BF16)
    for out, placing in zip(row_outs, placings):
        out[...] = jnp.dot(placing.astype(BF16), normed, preferred_element_type=F32).astype(BF16)
    copies[1].wait()
    cot = cot_ref[...]
    for s, (out, placing) in enumerate(zip(grad_outs, placings)):
        picked = jnp.dot(placing.astype(BF16), cot, preferred_element_type=F32)
        gate = jnp.sum(placing * gates[s : s + 1, :], -1, keepdims=True)
        out[...] = (gate * picked).astype(BF16)


def load_kernel(*refs):
    sources, outs, semaphores = refs[:3], refs[3:6], refs[6]
    copies = fetch(semaphores, *[(s.at[0], o) for s, o in zip(sources, outs)])
    for copy in copies:
        copy.wait()


def pair_kernel(first_ref, second_ref, out_ref):
    rows = first_ref.shape[0]
    out_ref[:rows, :] = first_ref[...]
    out_ref[rows:, :] = second_ref[...]


def split_kernel(both_ref, first_ref, second_ref):
    rows = first_ref.shape[0]
    first_ref[...] = both_ref[:rows, :]
    second_ref[...] = both_ref[rows:, :]


def fold_kernel(keep_ref, crossed_ref, out_ref):
    rows = out_ref.shape[0]
    total = keep_ref[rows:, :].astype(F32) + crossed_ref[rows:, :].astype(F32)
    out_ref[...] = total.astype(BF16)


def total_kernel(keep_ref, crossed_ref, came_ref, *outs):
    at = 0
    for out in outs:
        part = slice(at, at + out.shape[0])
        total = keep_ref[part, :].astype(F32) + crossed_ref[part, :].astype(F32)
        out[...] = (total + came_ref[part, :].astype(F32)).astype(BF16)
        at += out.shape[0]


def nothing(*refs):
    pass


def through(values, name, moved=0, earlier=()):
    count = len(values)
    return call(
        nothing,
        4,
        name,
        moved,
        out_shape=[jax.ShapeDtypeStruct(v.shape, v.dtype) for v in values],
        in_specs=whole(count) + [pl.BlockSpec(memory_space=pl.ANY)] * len(earlier),
        out_specs=whole(count),
        input_output_aliases={i: i for i in range(count)},
    )(*values, *earlier)


def ffn_kernel(count, *refs):
    pieces, refs = refs[:count], refs[count:]
    gate_ref, up_ref, down_ref, turned_ref, keep_ref, send_ref, rows_ref, hidden_ref = refs
    at = 0
    for piece in pieces:
        rows_ref[at : at + piece.shape[0], :] = piece[...]
        at += piece.shape[0]
    rows = rows_ref[...]
    half = keep_ref.shape[0]
    for j in range(gate_ref.shape[1] // TILE):
        columns = slice(j * TILE, (j + 1) * TILE)
        pre_gate = jnp.dot(rows, gate_ref[:, columns], preferred_element_type=F32)
        pre_up = jnp.dot(rows, up_ref[:, columns], preferred_element_type=F32)
        hidden = pre_gate * lax.logistic(pre_gate) * pre_up
        hidden_ref[:, columns] = hidden.astype(BF16)
        turned_ref[columns, :] = hidden.T.astype(BF16)
    for j in range(down_ref.shape[1] // TILE):
        columns = slice(j * TILE, (j + 1) * TILE)
        value = jnp.dot(
            hidden_ref[...], down_ref[:, columns], preferred_element_type=F32
        ).astype(BF16)
        keep_ref[:, columns] = value[:half]
        send_ref[:, columns] = value[half:]


def gather_grad(plan, refs, hidden_ref, cot_ref):
    at = 0
    for turned, column, piece, row, count in plan:
        hidden_ref[:, at : at + count] = refs[turned][:, column : column + count]
        cot_ref[at : at + count, :] = refs[piece][row : row + count, :]
        at += count


def first_grad_kernel(plan, *refs):
    out_ref, hidden_ref, cot_ref = refs[-3:]
    gather_grad(plan, refs, hidden_ref, cot_ref)
    for j in range(out_ref.shape[0] // TILE):
        part = slice(j * TILE, (j + 1) * TILE)
        out_ref[part, :] = jnp.dot(
            hidden_ref[part, :], cot_ref[...], preferred_element_type=F32
        )


def last_grad_kernel(plan, first_ref, *refs):
    out_hbm, out_ref, hidden_ref, cot_ref, semaphores = refs[-5:]
    gather_grad(plan, refs, hidden_ref, cot_ref)
    copies = []
    for j in range(first_ref.shape[0] // TILE):
        part = slice(j * TILE, (j + 1) * TILE)
        total = jnp.dot(hidden_ref[part, :], cot_ref[...], preferred_element_type=F32)
        out_ref[part, :] = (first_ref[part, :] + total).astype(BF16)
        copies.append(
            pltpu.make_async_copy(out_ref.at[part, :], out_hbm.at[0, part, :], semaphores.at[j])
        )
        copies[-1].start()
    for copy in copies:
        copy.wait()


def combine_kernel(experts, plane_ref, tokens_ref, routes_ref, nums_ref, *refs):
    values, out = refs[:-1], refs[-1]
    routes = routes_ref[...]
    placings = placing_of(routes, plane_ref[0], experts, values[0].shape[0])
    gates = gates_of(routes, nums_ref[...], plane_ref[0], experts)
    fill = -experts % 8
    if fill:
        gates = jnp.concatenate([gates, jnp.zeros((fill, gates.shape[1]), F32)], 0)
    gates = gates.T
    total = tokens_ref[...].astype(F32)
    for s, value in enumerate(values):
        picked = lax.dot_general(
            placings[s].astype(BF16),
            value[...],
            (((0,), (0,)), ((), ())),
            preferred_element_type=F32,
        )
        total = total + gates[:, s : s + 1] * picked
    out[...] = total.astype(BF16)


def on_device(tokens, cotangent, routes, gate_nums, gain, w_gate, w_up, w_down):
    devices = lax.axis_size("expert")
    experts = devices // HSPLIT
    rows_here, width = tokens.shape
    hidden_width = w_gate.shape[2]
    top_count = routes.shape[1]
    capacity = HSPLIT * (3 * top_count * rows_here // (2 * experts * HSPLIT))
    capacity = -(-capacity // 16) * 16
    shifts = max(1, experts // GROUPS)
    turns = sorted(range(experts), key=lambda s: (min(s, experts - s), s))
    groups = [turns[g : g + shifts] for g in range(0, experts, shifts)]
    height = shifts * capacity
    plane = (lax.axis_index("expert") // HSPLIT).astype(jnp.int32).reshape(1)
    routes, gate_nums, gain = routes.T, gate_nums.T, gain.reshape(1, -1)
    scalar = pl.BlockSpec(memory_space=pltpu.SMEM)
    anywhere = pl.BlockSpec(memory_space=pl.ANY)
    piece = jax.ShapeDtypeStruct((capacity, width), BF16)
    live = {}

    def swap(value, mask):
        return lax.ppermute(value, "expert", [(i, i ^ mask) for i in range(devices)])

    def turn(value, steps):
        to = [(i, (i + steps * HSPLIT) % devices) for i in range(devices)]
        return lax.ppermute(value, "expert", to)

    def sync():
        values = lax.optimization_barrier(tuple(live.values()))
        live.update(zip(list(live), values))

    def join(parts):
        return parts[0] if len(parts) == 1 else jnp.concatenate(parts, 0)

    flying, slow = {}, []

    def small(kernel, name, outs, *values):
        return call(
            kernel,
            8,
            name,
            out_shape=[jax.ShapeDtypeStruct((rows, width), BF16) for rows in outs],
            in_specs=whole(len(values)),
            out_specs=whole(len(outs)),
        )(*values)

    def land(*names, earlier=()):
        names = [n for name in names for n in flights_of(name)]
        quick = [name for name in names if name[0] == "c"]
        names = [name for name in names if name[0] != "c"]
        values = [flying.pop(name) for name in names]
        if not names:
            names, values = [("C", groups[-1][-1])], [live["C", groups[-1][-1]]]
        values = through(values, "land", LINK_WORK, earlier)
        landed = list(zip(names, values))
        if quick:
            cores = tuple(flying.pop(name) for name in quick) + (values[0],)
            cores = lax.optimization_barrier(cores)[: len(quick)]
            landed += list(zip(quick, through(cores, "land_core")))
        live.update(landed)
        sync()
        for name in quick:
            values = [live.pop(name)]
            if len(name) > 2:
                values = small(split_kernel, "split", [2 * height] * 2, *values)
            live.update({("c",) + item: value for item, value in zip(name[1:], values)})

    def flights_of(name):
        if name[0] == "c":
            return [name]
        axis, kind, g = name
        return [(kind, s) for s in groups[g] if s] if axis == "z" else [name]

    def z(kind, g):
        for s in groups[g]:
            if s:
                flying[kind, s] = turn(live[kind, s], -s if kind == "R" else s)

    def y(kind, g):
        if kind == "R":
            keep, crossed = live["keep", (g,)], live["c", "R", g]
            (value,) = small(fold_kernel, "fold", [height], keep, crossed)
        else:
            value = join([live.pop((kind, s)) for s in groups[g]])
            live["sent", kind, g] = value
        flying["y", kind, g] = swap(value, 2)

    def c(*items):
        values = []
        for kind, g in items:
            if kind == "R":
                values.append(live.pop(("send", (g,))))
                continue
            here, came = live.pop(("sent", kind, g)), live.pop(("y", kind, g))
            (value,) = small(pair_kernel, "pair", [2 * height], here, came)
            live[kind, "own", (g,)] = value
            values.append(value)
        if len(values) > 1:
            values = small(pair_kernel, "pair", [4 * height], *values)
        flying[("c",) + items] = swap(values[0], 1)

    def total(g):
        values = live.pop(("keep", (g,))), live.pop(("c", "R", g)), live.pop(("y", "R", g))
        outs = small(total_kernel, "total", [capacity] * shifts, *values)
        live.update({("R", s): out for s, out in zip(groups[g], outs)})

    def ffn(*gs):
        pieces = [live.pop(("N", "own", gs)), live.pop(("c", "N", gs[0]))]
        half = jax.ShapeDtypeStruct(pieces[0].shape, BF16)
        rows = 2 * half.shape[0]
        live["turned", gs], live["keep", gs], live["send", gs] = call(
            functools.partial(ffn_kernel, len(pieces)),
            24,
            "ffn",
            out_shape=[jax.ShapeDtypeStruct((hidden_width, rows), BF16), half, half],
            in_specs=whole(len(pieces) + 3),
            out_specs=whole(3),
            scratch_shapes=[
                pltpu.VMEM((rows, width), BF16),
                pltpu.VMEM((rows, hidden_width), BF16),
            ],
        )(*pieces, live["w", 0], live["w", 1], live["w", 2])

    def in_hbm(*values):
        return [pltpu.with_memory_space_constraint(v, pltpu.HBM) for v in values]

    def send():
        sources = (tokens, cotangent, routes, gate_nums, gain)
        values = call(
            functools.partial(send_kernel, experts),
            16,
            "send",
            out_shape=[piece] * (2 * experts),
            in_specs=[scalar] + [anywhere] * len(sources),
            out_specs=whole(2 * experts),
            scratch_shapes=[pltpu.VMEM(v.shape, v.dtype) for v in sources]
            + [pltpu.SemaphoreType.DMA((len(sources),))],
        )(plane, *in_hbm(*sources))
        live.update({("N", s): value for s, value in enumerate(values[:experts])})
        live.update({("C", s): value for s, value in enumerate(values[experts:])})

    def load():
        weight = jax.ShapeDtypeStruct((width, hidden_width), BF16)
        values = call(
            load_kernel,
            16,
            "load",
            out_shape=[weight, weight, jax.ShapeDtypeStruct((hidden_width, width), BF16)],
            in_specs=[anywhere] * 3,
            out_specs=whole(3),
            scratch_shapes=[pltpu.SemaphoreType.DMA((3,))],
        )(*in_hbm(after(w_gate, live["C", groups[-1][-1]]), w_up, w_down))
        live.update({("w", i): value for i, value in enumerate(values)})

    def grad_call(turned, pieces):
        columns = {}
        for i, gs in enumerate(turned):
            at = 0
            for half in ("own", "other"):
                for side in range(2):
                    for g in gs:
                        columns[half, side, g] = (i, at)
                        at += height
        plan = []
        for i, name in enumerate(pieces):
            half = "other" if name[0] == "c" else "own"
            g = name[-1] if half == "other" else name[-1][0]
            for side in range(2):
                where, at = columns[half, side, g]
                plan.append((where, at, len(turned) + i, side * height, height))
        rows = sum(step[-1] for step in plan)
        sides = [pltpu.VMEM((hidden_width, rows), BF16), pltpu.VMEM((rows, width), BF16)]
        values = [live["turned", gs] for gs in turned]
        values += [live[name] for name in pieces]
        return plan, sides, values

    def first_grad(turned, pieces):
        plan, sides, values = grad_call(turned, pieces)
        live["first"] = call(
            functools.partial(first_grad_kernel, plan),
            24,
            "first_grad",
            out_shape=jax.ShapeDtypeStruct((hidden_width, width), F32),
            in_specs=whole(len(values)),
            out_specs=whole(1)[0],
            scratch_shapes=sides,
        )(*values)

    def last_grad(turned, pieces):
        plan, sides, values = grad_call(turned, pieces)
        return call(
            functools.partial(last_grad_kernel, plan),
            24,
            "last_grad",
            out_shape=jax.ShapeDtypeStruct((1, hidden_width, width), BF16),
            in_specs=whole(1 + len(values)),
            out_specs=anywhere,
            scratch_shapes=[pltpu.VMEM((hidden_width, width), BF16)]
            + sides
            + [pltpu.SemaphoreType.DMA((hidden_width // TILE,))],
        )(live["first"], *values)

    steps = {
        "z": z,
        "y": y,
        "c": c,
        "ffn": lambda kind, g: ffn(g),
        "total": lambda kind, g: total(g),
        "load": lambda kind, g: load(),
        "grad": lambda kind, g: first_grad(
            [(0,), (1,), (2,)],
            [("C", "own", (i,)) for i in range(3)] + [("c", "C", i) for i in range(3)],
        ),
    }
    def name_of(act):
        marks = act.lstrip("abcdefghijklmnopqrstuvwxyz")
        items = [(marks[i], int(marks[i + 1])) for i in range(0, len(marks), 2)]
        return (act[: len(act) - len(marks)],) + tuple(items)

    send()
    if shifts > 1:
        z("N", 0)
        z("C", 0)
        land(("z", "N", 0), ("z", "C", 0))
    sync()
    for starts, lands in PLAN:
        kernels = []
        for act in starts.split():
            name = name_of(act)
            steps[name[0]](*(name[1:] if name[0] == "c" else name[1]))
            if name[0] == "ffn":
                kernels.append(live["turned", name[1][1:]])
            if name[0] == "grad":
                kernels.append(live["first"])
        names = [n if n[0] == "c" else (n[0],) + n[1] for n in map(name_of, lands.split())]
        land(*names, earlier=kernels)
    grad_down = last_grad(
        [(3,)],
        [("C", "own", (3,)), ("c", "C", 3)],
    )
    mixed = call(
        functools.partial(combine_kernel, experts),
        16,
        "combine",
        out_shape=jax.ShapeDtypeStruct(tokens.shape, BF16),
        in_specs=[scalar] + whole(3 + experts),
        out_specs=whole(1)[0],
    )(plane, tokens, routes, gate_nums, *[live["R", s] for s in range(experts)])
    return (mixed, grad_down)


def solution(mesh):
    placed = (
        P(("group", "expert"), None),
        P(("group", "expert"), None),
        P(("group", "expert"), None),
        P(("group", "expert"), None),
        P(),
        P("expert", None, None),
        P("expert", None, None),
        P("expert", None, None),
    )
    return jax.shard_map(
        on_device,
        mesh=mesh,
        in_specs=placed,
        out_specs=(P(("group", "expert"), None), P(("group", "expert"), None, None)),
        check_vma=False,
    )
```

```python
import functools

import jax
import jax.numpy as jnp
from jax import lax
from jax.experimental import pallas as pl
from jax.experimental.pallas import tpu as pltpu
from jax.sharding import PartitionSpec as P

HSPLIT = 4
GROUPS = 4
PLAN = (
    ("yN0 zN1 zN2 loadW0", ""),
    ("yC0 zN3", "zN1 zN2 yN0"),
    ("cN0 yN1", "yC0 cN0"),
    ("ffnN0 yN2", "yN1 zN3"),
    ("cR0N1 yN3 zC1 zC2", "yN2 cR0N1"),
    ("ffnN1 cN2 yR0", "yN3 zC1 zC2 cN2"),
    ("cR1N3 ffnN2 yC1 zC3", "yR0 cR1N3"),
    ("cR2 ffnN3 yR1 totalR0", "yC1 zC3 cR2"),
    ("", "yR1"),
    ("yR2 totalR1 zR1 cR3", "cR3"),
    ("yR3", "yR2 zR1"),
    ("totalR2 zR2 yC2 yC3 cC0", "yR3 cC0"),
    ("totalR3 zR3 cC1", "yC2 yC3 zR2 cC1"),
    ("cC2C3 gradC0", "zR3 cC2C3"),
)
TILE = 256
LINK_WORK = 10 << 30
F32 = jnp.float32
BF16 = jnp.bfloat16


def after(value, *earlier):
    return lax.optimization_barrier((value,) + earlier)[0]


def whole(count):
    return [pl.BlockSpec(memory_space=pltpu.VMEM)] * count


def call(kernel, mib, name, moved=0, **keywords):
    return pl.pallas_call(
        kernel,
        compiler_params=pltpu.CompilerParams(vmem_limit_bytes=mib << 20),
        cost_estimate=pl.CostEstimate(flops=moved, bytes_accessed=0, transcendentals=0),
        name=name,
        **keywords,
    )


def experts_of(plane, experts, rows):
    ahead = lax.broadcasted_iota(jnp.int32, (experts, rows), 0) + plane
    return jnp.where(ahead >= experts, ahead - experts, ahead)


def placing_of(routes, plane, experts, capacity):
    rows = routes.shape[1]
    expert = experts_of(plane, experts, rows)
    member = jnp.zeros((experts, rows), jnp.bool_)
    for k in range(routes.shape[0]):
        member = member | (routes[k : k + 1, :] == expert)
    first = lax.broadcasted_iota(jnp.int32, (rows, rows), 0)
    second = lax.broadcasted_iota(jnp.int32, (rows, rows), 1)
    upto = (first <= second).astype(F32).astype(BF16)
    ones = member.astype(F32)
    count = jnp.dot(ones.astype(BF16), upto, preferred_element_type=F32)
    place = (ones * count).astype(jnp.int32) - 1
    slots = lax.broadcasted_iota(jnp.int32, (capacity, rows), 0)
    return [(slots == place[s : s + 1, :]).astype(F32) for s in range(experts)]


def gates_of(routes, numbers, plane, experts):
    expert = experts_of(plane, experts, routes.shape[1])
    numerators = numbers.astype(F32)
    gates = numerators / jnp.sum(numerators, 0, keepdims=True)
    gate = jnp.zeros(expert.shape, F32)
    for k in range(routes.shape[0]):
        gate = gate + jnp.where(routes[k : k + 1, :] == expert, gates[k : k + 1, :], 0.0)
    return gate


def fetch(semaphores, *pairs):
    copies = [
        pltpu.make_async_copy(source, target, semaphores.at[i])
        for i, (source, target) in enumerate(pairs)
    ]
    for copy in copies:
        copy.start()
    return copies


def send_kernel(experts, plane_ref, *refs):
    sources, refs = refs[:5], refs[5:]
    row_outs, grad_outs = refs[:experts], refs[experts : 2 * experts]
    targets, semaphores = refs[2 * experts : -1], refs[-1]
    tokens_ref, cot_ref, routes_ref, nums_ref, gain_ref = targets
    copies = fetch(semaphores, *zip(sources, targets))
    copies[2].wait()
    copies[3].wait()
    routes = routes_ref[...]
    placings = placing_of(routes, plane_ref[0], experts, row_outs[0].shape[0])
    gates = gates_of(routes, nums_ref[...], plane_ref[0], experts)
    copies[4].wait()
    copies[0].wait()
    frames = tokens_ref[...].astype(F32)
    inverse = lax.rsqrt(jnp.mean(frames * frames, -1, keepdims=True) + 1e-06)
    normed = (frames * inverse * gain_ref[...]).astype(BF16)
    for out, placing in zip(row_outs, placings):
        out[...] = jnp.dot(placing.astype(BF16), normed, preferred_element_type=F32).astype(BF16)
    copies[1].wait()
    cot = cot_ref[...]
    for s, (out, placing) in enumerate(zip(grad_outs, placings)):
        picked = jnp.dot(placing.astype(BF16), cot, preferred_element_type=F32)
        gate = jnp.sum(placing * gates[s : s + 1, :], -1, keepdims=True)
        out[...] = (gate * picked).astype(BF16)


def load_kernel(*refs):
    sources, outs, semaphores = refs[:3], refs[3:6], refs[6]
    copies = fetch(semaphores, *[(s.at[0], o) for s, o in zip(sources, outs)])
    for copy in copies:
        copy.wait()


def pair_kernel(first_ref, second_ref, out_ref):
    rows = first_ref.shape[0]
    out_ref[:rows, :] = first_ref[...]
    out_ref[rows:, :] = second_ref[...]


def split_kernel(both_ref, first_ref, second_ref):
    rows = first_ref.shape[0]
    first_ref[...] = both_ref[:rows, :]
    second_ref[...] = both_ref[rows:, :]


def fold_kernel(keep_ref, crossed_ref, out_ref):
    rows = out_ref.shape[0]
    total = keep_ref[rows:, :].astype(F32) + crossed_ref[rows:, :].astype(F32)
    out_ref[...] = total.astype(BF16)


def total_kernel(keep_ref, crossed_ref, came_ref, *outs):
    at = 0
    for out in outs:
        part = slice(at, at + out.shape[0])
        total = keep_ref[part, :].astype(F32) + crossed_ref[part, :].astype(F32)
        out[...] = (total + came_ref[part, :].astype(F32)).astype(BF16)
        at += out.shape[0]


def nothing(*refs):
    pass


def through(values, name, moved=0, earlier=()):
    count = len(values)
    return call(
        nothing,
        4,
        name,
        moved,
        out_shape=[jax.ShapeDtypeStruct(v.shape, v.dtype) for v in values],
        in_specs=whole(count) + [pl.BlockSpec(memory_space=pl.ANY)] * len(earlier),
        out_specs=whole(count),
        input_output_aliases={i: i for i in range(count)},
    )(*values, *earlier)


def ffn_kernel(count, *refs):
    pieces, refs = refs[:count], refs[count:]
    gate_ref, up_ref, down_ref, turned_ref, keep_ref, send_ref, rows_ref, hidden_ref = refs
    at = 0
    for piece in pieces:
        rows_ref[at : at + piece.shape[0], :] = piece[...]
        at += piece.shape[0]
    rows = rows_ref[...]
    half = keep_ref.shape[0]
    for j in range(gate_ref.shape[1] // TILE):
        columns = slice(j * TILE, (j + 1) * TILE)
        pre_gate = jnp.dot(rows, gate_ref[:, columns], preferred_element_type=F32)
        pre_up = jnp.dot(rows, up_ref[:, columns], preferred_element_type=F32)
        hidden = pre_gate * lax.logistic(pre_gate) * pre_up
        hidden_ref[:, columns] = hidden.astype(BF16)
        turned_ref[columns, :] = hidden.T.astype(BF16)
    for j in range(down_ref.shape[1] // TILE):
        columns = slice(j * TILE, (j + 1) * TILE)
        value = jnp.dot(
            hidden_ref[...], down_ref[:, columns], preferred_element_type=F32
        ).astype(BF16)
        keep_ref[:, columns] = value[:half]
        send_ref[:, columns] = value[half:]


def gather_grad(plan, refs, hidden_ref, cot_ref):
    at = 0
    for turned, column, piece, row, count in plan:
        hidden_ref[:, at : at + count] = refs[turned][:, column : column + count]
        cot_ref[at : at + count, :] = refs[piece][row : row + count, :]
        at += count


def first_grad_kernel(plan, *refs):
    out_ref, hidden_ref, cot_ref = refs[-3:]
    gather_grad(plan, refs, hidden_ref, cot_ref)
    for j in range(out_ref.shape[0] // TILE):
        part = slice(j * TILE, (j + 1) * TILE)
        out_ref[part, :] = jnp.dot(
            hidden_ref[part, :], cot_ref[...], preferred_element_type=F32
        )


def last_grad_kernel(plan, first_ref, *refs):
    out_hbm, out_ref, hidden_ref, cot_ref, semaphores = refs[-5:]
    gather_grad(plan, refs, hidden_ref, cot_ref)
    copies = []
    for j in range(first_ref.shape[0] // TILE):
        part = slice(j * TILE, (j + 1) * TILE)
        total = jnp.dot(hidden_ref[part, :], cot_ref[...], preferred_element_type=F32)
        out_ref[part, :] = (first_ref[part, :] + total).astype(BF16)
        copies.append(
            pltpu.make_async_copy(out_ref.at[part, :], out_hbm.at[0, part, :], semaphores.at[j])
        )
        copies[-1].start()
    for copy in copies:
        copy.wait()


def combine_kernel(experts, plane_ref, tokens_ref, routes_ref, nums_ref, *refs):
    values, out = refs[:-1], refs[-1]
    routes = routes_ref[...]
    placings = placing_of(routes, plane_ref[0], experts, values[0].shape[0])
    gates = gates_of(routes, nums_ref[...], plane_ref[0], experts)
    fill = -experts % 8
    if fill:
        gates = jnp.concatenate([gates, jnp.zeros((fill, gates.shape[1]), F32)], 0)
    gates = gates.T
    total = tokens_ref[...].astype(F32)
    for s, value in enumerate(values):
        picked = lax.dot_general(
            placings[s].astype(BF16),
            value[...],
            (((0,), (0,)), ((), ())),
            preferred_element_type=F32,
        )
        total = total + gates[:, s : s + 1] * picked
    out[...] = total.astype(BF16)


def on_device(tokens, cotangent, routes, gate_nums, gain, w_gate, w_up, w_down):
    devices = lax.axis_size("expert")
    experts = devices // HSPLIT
    rows_here, width = tokens.shape
    hidden_width = w_gate.shape[2]
    top_count = routes.shape[1]
    capacity = HSPLIT * (3 * top_count * rows_here // (2 * experts * HSPLIT))
    capacity = -(-capacity // 16) * 16
    shifts = max(1, experts // GROUPS)
    turns = sorted(range(experts), key=lambda s: (min(s, experts - s), s))
    groups = [turns[g : g + shifts] for g in range(0, experts, shifts)]
    height = shifts * capacity
    plane = (lax.axis_index("expert") // HSPLIT).astype(jnp.int32).reshape(1)
    routes, gate_nums, gain = routes.T, gate_nums.T, gain.reshape(1, -1)
    scalar = pl.BlockSpec(memory_space=pltpu.SMEM)
    anywhere = pl.BlockSpec(memory_space=pl.ANY)
    piece = jax.ShapeDtypeStruct((capacity, width), BF16)
    live = {}

    def swap(value, mask):
        return lax.ppermute(value, "expert", [(i, i ^ mask) for i in range(devices)])

    def turn(value, steps):
        to = [(i, (i + steps * HSPLIT) % devices) for i in range(devices)]
        return lax.ppermute(value, "expert", to)

    def sync():
        values = lax.optimization_barrier(tuple(live.values()))
        live.update(zip(list(live), values))

    def join(parts):
        return parts[0] if len(parts) == 1 else jnp.concatenate(parts, 0)

    flying, slow = {}, []

    def small(kernel, name, outs, *values):
        return call(
            kernel,
            8,
            name,
            out_shape=[jax.ShapeDtypeStruct((rows, width), BF16) for rows in outs],
            in_specs=whole(len(values)),
            out_specs=whole(len(outs)),
        )(*values)

    def land(*names, earlier=()):
        names = [n for name in names for n in flights_of(name)]
        quick = [name for name in names if name[0] == "c"]
        names = [name for name in names if name[0] != "c"]
        if not names:
            names, quick = quick, []
        cores = [name for name in names + quick if name[0] == "c"]
        values = [flying.pop(name) for name in names]
        if not names:
            names, values = [("C", groups[-1][-1])], [live["C", groups[-1][-1]]]
        values = through(values, "land", LINK_WORK, earlier)
        landed = list(zip(names, values))
        if quick:
            crossed = tuple(flying.pop(name) for name in quick) + (values[0],)
            crossed = lax.optimization_barrier(crossed)[: len(quick)]
            landed += list(zip(quick, through(crossed, "land_core")))
        live.update(landed)
        sync()
        for name in cores:
            values = [live.pop(name)]
            if len(name) > 2:
                values = small(split_kernel, "split", [2 * height] * 2, *values)
            live.update({("c",) + item: value for item, value in zip(name[1:], values)})

    def flights_of(name):
        if name[0] == "c":
            return [name]
        axis, kind, g = name
        return [(kind, s) for s in groups[g] if s] if axis == "z" else [name]

    def z(kind, g):
        for s in groups[g]:
            if s:
                flying[kind, s] = turn(live[kind, s], -s if kind == "R" else s)

    def y(kind, g):
        if kind == "R":
            keep, crossed = live["keep", (g,)], live["c", "R", g]
            (value,) = small(fold_kernel, "fold", [height], keep, crossed)
        else:
            value = join([live.pop((kind, s)) for s in groups[g]])
            live["sent", kind, g] = value
        flying["y", kind, g] = swap(value, 2)

    def c(*items):
        values = []
        for kind, g in items:
            if kind == "R":
                values.append(live.pop(("send", (g,))))
                continue
            here, came = live.pop(("sent", kind, g)), live.pop(("y", kind, g))
            (value,) = small(pair_kernel, "pair", [2 * height], here, came)
            live[kind, "own", (g,)] = value
            values.append(value)
        if len(values) > 1:
            values = small(pair_kernel, "pair", [4 * height], *values)
        flying[("c",) + items] = swap(values[0], 1)

    def total(g):
        values = live.pop(("keep", (g,))), live.pop(("c", "R", g)), live.pop(("y", "R", g))
        outs = small(total_kernel, "total", [capacity] * shifts, *values)
        live.update({("R", s): out for s, out in zip(groups[g], outs)})

    def ffn(*gs):
        pieces = [live.pop(("N", "own", gs)), live.pop(("c", "N", gs[0]))]
        half = jax.ShapeDtypeStruct(pieces[0].shape, BF16)
        rows = 2 * half.shape[0]
        live["turned", gs], live["keep", gs], live["send", gs] = call(
            functools.partial(ffn_kernel, len(pieces)),
            24,
            "ffn",
            out_shape=[jax.ShapeDtypeStruct((hidden_width, rows), BF16), half, half],
            in_specs=whole(len(pieces) + 3),
            out_specs=whole(3),
            scratch_shapes=[
                pltpu.VMEM((rows, width), BF16),
                pltpu.VMEM((rows, hidden_width), BF16),
            ],
        )(*pieces, live["w", 0], live["w", 1], live["w", 2])

    def in_hbm(*values):
        return [pltpu.with_memory_space_constraint(v, pltpu.HBM) for v in values]

    def send():
        sources = (tokens, cotangent, routes, gate_nums, gain)
        values = call(
            functools.partial(send_kernel, experts),
            16,
            "send",
            out_shape=[piece] * (2 * experts),
            in_specs=[scalar] + [anywhere] * len(sources),
            out_specs=whole(2 * experts),
            scratch_shapes=[pltpu.VMEM(v.shape, v.dtype) for v in sources]
            + [pltpu.SemaphoreType.DMA((len(sources),))],
        )(plane, *in_hbm(*sources))
        live.update({("N", s): value for s, value in enumerate(values[:experts])})
        live.update({("C", s): value for s, value in enumerate(values[experts:])})

    def load():
        weight = jax.ShapeDtypeStruct((width, hidden_width), BF16)
        values = call(
            load_kernel,
            16,
            "load",
            out_shape=[weight, weight, jax.ShapeDtypeStruct((hidden_width, width), BF16)],
            in_specs=[anywhere] * 3,
            out_specs=whole(3),
            scratch_shapes=[pltpu.SemaphoreType.DMA((3,))],
        )(*in_hbm(after(w_gate, live["C", groups[-1][-1]]), w_up, w_down))
        live.update({("w", i): value for i, value in enumerate(values)})

    def grad_call(turned, pieces):
        columns = {}
        for i, gs in enumerate(turned):
            at = 0
            for half in ("own", "other"):
                for side in range(2):
                    for g in gs:
                        columns[half, side, g] = (i, at)
                        at += height
        plan = []
        for i, name in enumerate(pieces):
            half = "other" if name[0] == "c" else "own"
            g = name[-1] if half == "other" else name[-1][0]
            for side in range(2):
                where, at = columns[half, side, g]
                plan.append((where, at, len(turned) + i, side * height, height))
        rows = sum(step[-1] for step in plan)
        sides = [pltpu.VMEM((hidden_width, rows), BF16), pltpu.VMEM((rows, width), BF16)]
        values = [live["turned", gs] for gs in turned]
        values += [live[name] for name in pieces]
        return plan, sides, values

    def first_grad(turned, pieces):
        plan, sides, values = grad_call(turned, pieces)
        live["first"] = call(
            functools.partial(first_grad_kernel, plan),
            24,
            "first_grad",
            out_shape=jax.ShapeDtypeStruct((hidden_width, width), F32),
            in_specs=whole(len(values)),
            out_specs=whole(1)[0],
            scratch_shapes=sides,
        )(*values)

    def last_grad(turned, pieces):
        plan, sides, values = grad_call(turned, pieces)
        return call(
            functools.partial(last_grad_kernel, plan),
            24,
            "last_grad",
            out_shape=jax.ShapeDtypeStruct((1, hidden_width, width), BF16),
            in_specs=whole(1 + len(values)),
            out_specs=anywhere,
            scratch_shapes=[pltpu.VMEM((hidden_width, width), BF16)]
            + sides
            + [pltpu.SemaphoreType.DMA((hidden_width // TILE,))],
        )(live["first"], *values)

    steps = {
        "z": z,
        "y": y,
        "c": c,
        "ffn": lambda kind, g: ffn(g),
        "total": lambda kind, g: total(g),
        "load": lambda kind, g: load(),
        "grad": lambda kind, g: first_grad(
            [(0,), (1,)],
            [("C", "own", (0,)), ("C", "own", (1,)), ("c", "C", 0), ("c", "C", 1)],
        ),
    }
    def name_of(act):
        marks = act.lstrip("abcdefghijklmnopqrstuvwxyz")
        items = [(marks[i], int(marks[i + 1])) for i in range(0, len(marks), 2)]
        return (act[: len(act) - len(marks)],) + tuple(items)

    send()
    if shifts > 1:
        z("N", 0)
        z("C", 0)
        land(("z", "N", 0), ("z", "C", 0))
    sync()
    for starts, lands in PLAN:
        kernels = []
        for act in starts.split():
            name = name_of(act)
            steps[name[0]](*(name[1:] if name[0] == "c" else name[1]))
            if name[0] == "ffn":
                kernels.append(live["turned", name[1][1:]])
            if name[0] == "grad":
                kernels.append(live["first"])
        names = [n if n[0] == "c" else (n[0],) + n[1] for n in map(name_of, lands.split())]
        land(*names, earlier=kernels)
    grad_down = last_grad(
        [(2,), (3,)],
        [("C", "own", (2,)), ("C", "own", (3,)), ("c", "C", 2), ("c", "C", 3)],
    )
    mixed = call(
        functools.partial(combine_kernel, experts),
        16,
        "combine",
        out_shape=jax.ShapeDtypeStruct(tokens.shape, BF16),
        in_specs=[scalar] + whole(3 + experts),
        out_specs=whole(1)[0],
    )(plane, tokens, routes, gate_nums, *[live["R", s] for s in range(experts)])
    return (mixed, grad_down)


def solution(mesh):
    placed = (
        P(("group", "expert"), None),
        P(("group", "expert"), None),
        P(("group", "expert"), None),
        P(("group", "expert"), None),
        P(),
        P("expert", None, None),
        P("expert", None, None),
        P("expert", None, None),
    )
    return jax.shard_map(
        on_device,
        mesh=mesh,
        in_specs=placed,
        out_specs=(P(("group", "expert"), None), P(("group", "expert"), None, None)),
        check_vma=False,
    )
```

```python
import functools

import jax
import jax.numpy as jnp
from jax import lax
from jax.experimental import pallas as pl
from jax.experimental.pallas import tpu as pltpu
from jax.sharding import PartitionSpec as P

HSPLIT = 4
GROUPS = 4
PLAN = (
    ("yN0 zN1 zN2 loadW0", ""),
    ("yC0 zN3", "zN1 zN2 yN0"),
    ("cN0 yN1", "yC0 cN0"),
    ("ffnN0 yN2", "yN1 zN3"),
    ("cR0N1 yN3 zC1 zC2", "yN2 cR0N1"),
    ("ffnN1 cN2 yR0", "yN3 zC1 zC2 cN2"),
    ("cR1N3 ffnN2 yC1C2 zC3", "yR0 cR1N3"),
    ("cR2 ffnN3 cR3 yR1 totalR0", "yC1C2 zC3 cR2"),
    ("", "yR1 cR3"),
    ("yR2 yR3 totalR1 zR1", "yR2 zR1"),
    ("totalR2 zR2 yC3 cC0", "yR3 cC0"),
    ("totalR3 zR3 cC1C2", "yC3 zR2 cC1C2"),
    ("cC3 gradC0", "zR3 cC3"),
)
TILE = 256
LINK_WORK = 10 << 30
F32 = jnp.float32
BF16 = jnp.bfloat16


def after(value, *earlier):
    return lax.optimization_barrier((value,) + earlier)[0]


def whole(count):
    return [pl.BlockSpec(memory_space=pltpu.VMEM)] * count


def call(kernel, mib, name, moved=0, **keywords):
    return pl.pallas_call(
        kernel,
        compiler_params=pltpu.CompilerParams(vmem_limit_bytes=mib << 20),
        cost_estimate=pl.CostEstimate(flops=moved, bytes_accessed=0, transcendentals=0),
        name=name,
        **keywords,
    )


def experts_of(plane, experts, rows):
    ahead = lax.broadcasted_iota(jnp.int32, (experts, rows), 0) + plane
    return jnp.where(ahead >= experts, ahead - experts, ahead)


def placing_of(routes, plane, experts, capacity):
    rows = routes.shape[1]
    expert = experts_of(plane, experts, rows)
    member = jnp.zeros((experts, rows), jnp.bool_)
    for k in range(routes.shape[0]):
        member = member | (routes[k : k + 1, :] == expert)
    first = lax.broadcasted_iota(jnp.int32, (rows, rows), 0)
    second = lax.broadcasted_iota(jnp.int32, (rows, rows), 1)
    upto = (first <= second).astype(F32).astype(BF16)
    ones = member.astype(F32)
    count = jnp.dot(ones.astype(BF16), upto, preferred_element_type=F32)
    place = (ones * count).astype(jnp.int32) - 1
    slots = lax.broadcasted_iota(jnp.int32, (capacity, rows), 0)
    return [(slots == place[s : s + 1, :]).astype(F32) for s in range(experts)]


def gates_of(routes, numbers, plane, experts):
    expert = experts_of(plane, experts, routes.shape[1])
    numerators = numbers.astype(F32)
    gates = numerators / jnp.sum(numerators, 0, keepdims=True)
    gate = jnp.zeros(expert.shape, F32)
    for k in range(routes.shape[0]):
        gate = gate + jnp.where(routes[k : k + 1, :] == expert, gates[k : k + 1, :], 0.0)
    return gate


def fetch(semaphores, *pairs):
    copies = [
        pltpu.make_async_copy(source, target, semaphores.at[i])
        for i, (source, target) in enumerate(pairs)
    ]
    for copy in copies:
        copy.start()
    return copies


def send_kernel(experts, plane_ref, *refs):
    sources, refs = refs[:5], refs[5:]
    row_outs, grad_outs = refs[:experts], refs[experts : 2 * experts]
    targets, semaphores = refs[2 * experts : -1], refs[-1]
    tokens_ref, cot_ref, routes_ref, nums_ref, gain_ref = targets
    copies = fetch(semaphores, *zip(sources, targets))
    copies[2].wait()
    copies[3].wait()
    routes = routes_ref[...]
    placings = placing_of(routes, plane_ref[0], experts, row_outs[0].shape[0])
    gates = gates_of(routes, nums_ref[...], plane_ref[0], experts)
    copies[4].wait()
    copies[0].wait()
    frames = tokens_ref[...].astype(F32)
    inverse = lax.rsqrt(jnp.mean(frames * frames, -1, keepdims=True) + 1e-06)
    normed = (frames * inverse * gain_ref[...]).astype(BF16)
    for out, placing in zip(row_outs, placings):
        out[...] = jnp.dot(placing.astype(BF16), normed, preferred_element_type=F32).astype(BF16)
    copies[1].wait()
    cot = cot_ref[...]
    for s, (out, placing) in enumerate(zip(grad_outs, placings)):
        picked = jnp.dot(placing.astype(BF16), cot, preferred_element_type=F32)
        gate = jnp.sum(placing * gates[s : s + 1, :], -1, keepdims=True)
        out[...] = (gate * picked).astype(BF16)


def load_kernel(*refs):
    sources, outs, semaphores = refs[:3], refs[3:6], refs[6]
    copies = fetch(semaphores, *[(s.at[0], o) for s, o in zip(sources, outs)])
    for copy in copies:
        copy.wait()


def pair_kernel(first_ref, second_ref, out_ref):
    rows = first_ref.shape[0]
    out_ref[:rows, :] = first_ref[...]
    out_ref[rows:, :] = second_ref[...]


def split_kernel(both_ref, first_ref, second_ref):
    rows = first_ref.shape[0]
    first_ref[...] = both_ref[:rows, :]
    second_ref[...] = both_ref[rows:, :]


def fold_kernel(keep_ref, crossed_ref, out_ref):
    rows = out_ref.shape[0]
    total = keep_ref[rows:, :].astype(F32) + crossed_ref[rows:, :].astype(F32)
    out_ref[...] = total.astype(BF16)


def total_kernel(keep_ref, crossed_ref, came_ref, *outs):
    at = 0
    for out in outs:
        part = slice(at, at + out.shape[0])
        total = keep_ref[part, :].astype(F32) + crossed_ref[part, :].astype(F32)
        out[...] = (total + came_ref[part, :].astype(F32)).astype(BF16)
        at += out.shape[0]


def nothing(*refs):
    pass


def through(values, name, moved=0, earlier=()):
    count = len(values)
    return call(
        nothing,
        4,
        name,
        moved,
        out_shape=[jax.ShapeDtypeStruct(v.shape, v.dtype) for v in values],
        in_specs=whole(count) + [pl.BlockSpec(memory_space=pl.ANY)] * len(earlier),
        out_specs=whole(count),
        input_output_aliases={i: i for i in range(count)},
    )(*values, *earlier)


def ffn_kernel(count, *refs):
    pieces, refs = refs[:count], refs[count:]
    gate_ref, up_ref, down_ref, turned_ref, keep_ref, send_ref, rows_ref, hidden_ref = refs
    at = 0
    for piece in pieces:
        rows_ref[at : at + piece.shape[0], :] = piece[...]
        at += piece.shape[0]
    rows = rows_ref[...]
    half = keep_ref.shape[0]
    for j in range(gate_ref.shape[1] // TILE):
        columns = slice(j * TILE, (j + 1) * TILE)
        pre_gate = jnp.dot(rows, gate_ref[:, columns], preferred_element_type=F32)
        pre_up = jnp.dot(rows, up_ref[:, columns], preferred_element_type=F32)
        hidden = pre_gate * lax.logistic(pre_gate) * pre_up
        hidden_ref[:, columns] = hidden.astype(BF16)
        turned_ref[columns, :] = hidden.T.astype(BF16)
    for j in range(down_ref.shape[1] // TILE):
        columns = slice(j * TILE, (j + 1) * TILE)
        value = jnp.dot(
            hidden_ref[...], down_ref[:, columns], preferred_element_type=F32
        ).astype(BF16)
        keep_ref[:, columns] = value[:half]
        send_ref[:, columns] = value[half:]


def gather_grad(plan, refs, hidden_ref, cot_ref):
    at = 0
    for turned, column, piece, row, count in plan:
        hidden_ref[:, at : at + count] = refs[turned][:, column : column + count]
        cot_ref[at : at + count, :] = refs[piece][row : row + count, :]
        at += count


def first_grad_kernel(plan, *refs):
    out_ref, hidden_ref, cot_ref = refs[-3:]
    gather_grad(plan, refs, hidden_ref, cot_ref)
    for j in range(out_ref.shape[0] // TILE):
        part = slice(j * TILE, (j + 1) * TILE)
        out_ref[part, :] = jnp.dot(
            hidden_ref[part, :], cot_ref[...], preferred_element_type=F32
        )


def last_grad_kernel(plan, first_ref, *refs):
    out_hbm, out_ref, hidden_ref, cot_ref, semaphores = refs[-5:]
    gather_grad(plan, refs, hidden_ref, cot_ref)
    copies = []
    for j in range(first_ref.shape[0] // TILE):
        part = slice(j * TILE, (j + 1) * TILE)
        total = jnp.dot(hidden_ref[part, :], cot_ref[...], preferred_element_type=F32)
        out_ref[part, :] = (first_ref[part, :] + total).astype(BF16)
        copies.append(
            pltpu.make_async_copy(out_ref.at[part, :], out_hbm.at[0, part, :], semaphores.at[j])
        )
        copies[-1].start()
    for copy in copies:
        copy.wait()


def combine_kernel(experts, plane_ref, tokens_ref, routes_ref, nums_ref, *refs):
    values, out = refs[:-1], refs[-1]
    routes = routes_ref[...]
    placings = placing_of(routes, plane_ref[0], experts, values[0].shape[0])
    gates = gates_of(routes, nums_ref[...], plane_ref[0], experts)
    fill = -experts % 8
    if fill:
        gates = jnp.concatenate([gates, jnp.zeros((fill, gates.shape[1]), F32)], 0)
    gates = gates.T
    total = tokens_ref[...].astype(F32)
    for s, value in enumerate(values):
        picked = lax.dot_general(
            placings[s].astype(BF16),
            value[...],
            (((0,), (0,)), ((), ())),
            preferred_element_type=F32,
        )
        total = total + gates[:, s : s + 1] * picked
    out[...] = total.astype(BF16)


def on_device(tokens, cotangent, routes, gate_nums, gain, w_gate, w_up, w_down):
    devices = lax.axis_size("expert")
    experts = devices // HSPLIT
    rows_here, width = tokens.shape
    hidden_width = w_gate.shape[2]
    top_count = routes.shape[1]
    capacity = HSPLIT * (3 * top_count * rows_here // (2 * experts * HSPLIT))
    capacity = -(-capacity // 16) * 16
    shifts = max(1, experts // GROUPS)
    turns = sorted(range(experts), key=lambda s: (min(s, experts - s), s))
    groups = [turns[g : g + shifts] for g in range(0, experts, shifts)]
    height = shifts * capacity
    plane = (lax.axis_index("expert") // HSPLIT).astype(jnp.int32).reshape(1)
    routes, gate_nums, gain = routes.T, gate_nums.T, gain.reshape(1, -1)
    scalar = pl.BlockSpec(memory_space=pltpu.SMEM)
    anywhere = pl.BlockSpec(memory_space=pl.ANY)
    piece = jax.ShapeDtypeStruct((capacity, width), BF16)
    live = {}

    def swap(value, mask):
        return lax.ppermute(value, "expert", [(i, i ^ mask) for i in range(devices)])

    def turn(value, steps):
        to = [(i, (i + steps * HSPLIT) % devices) for i in range(devices)]
        return lax.ppermute(value, "expert", to)

    def sync():
        values = lax.optimization_barrier(tuple(live.values()))
        live.update(zip(list(live), values))

    def join(parts):
        return parts[0] if len(parts) == 1 else jnp.concatenate(parts, 0)

    flying, slow = {}, []

    def small(kernel, name, outs, *values):
        return call(
            kernel,
            8,
            name,
            out_shape=[jax.ShapeDtypeStruct((rows, width), BF16) for rows in outs],
            in_specs=whole(len(values)),
            out_specs=whole(len(outs)),
        )(*values)

    def land(*names, earlier=()):
        names = [n for name in names for n in flights_of(name)]
        quick = [name for name in names if name[0] == "c"]
        names = [name for name in names if name[0] != "c"]
        if not names:
            names, quick = quick, []
        joined = [name for name in names + quick if name[0] in "cy"]
        values = [flying.pop(name) for name in names]
        if not names:
            names, values = [("C", groups[-1][-1])], [live["C", groups[-1][-1]]]
        values = through(values, "land", LINK_WORK, earlier)
        landed = list(zip(names, values))
        if quick:
            crossed = tuple(flying.pop(name) for name in quick) + (values[0],)
            crossed = lax.optimization_barrier(crossed)[: len(quick)]
            landed += list(zip(quick, through(crossed, "land_core")))
        live.update(landed)
        sync()
        for name in joined:
            values = [live.pop(name)]
            if len(name) > 2:
                values = small(split_kernel, "split", [values[0].shape[0] // 2] * 2, *values)
            live.update({(name[0],) + item: value for item, value in zip(name[1:], values)})

    def flights_of(name):
        if name[0] != "z":
            return [name]
        kind, g = name[1]
        return [(kind, s) for s in groups[g] if s]

    def z(kind, g):
        for s in groups[g]:
            if s:
                flying[kind, s] = turn(live[kind, s], -s if kind == "R" else s)

    def y(*items):
        values = [to_row(*item) for item in items]
        if len(values) > 1:
            values = small(pair_kernel, "pair", [2 * height], *values)
        flying[("y",) + items] = swap(values[0], 2)

    def to_row(kind, g):
        if kind == "R":
            keep, crossed = live["keep", (g,)], live["c", "R", g]
            (value,) = small(fold_kernel, "fold", [height], keep, crossed)
        else:
            value = join([live.pop((kind, s)) for s in groups[g]])
            live["sent", kind, g] = value
        return value

    def c(*items):
        values = []
        for kind, g in items:
            if kind == "R":
                values.append(live.pop(("send", (g,))))
                continue
            here, came = live.pop(("sent", kind, g)), live.pop(("y", kind, g))
            (value,) = small(pair_kernel, "pair", [2 * height], here, came)
            live[kind, "own", (g,)] = value
            values.append(value)
        if len(values) > 1:
            values = small(pair_kernel, "pair", [4 * height], *values)
        flying[("c",) + items] = swap(values[0], 1)

    def total(g):
        values = live.pop(("keep", (g,))), live.pop(("c", "R", g)), live.pop(("y", "R", g))
        outs = small(total_kernel, "total", [capacity] * shifts, *values)
        live.update({("R", s): out for s, out in zip(groups[g], outs)})

    def ffn(*gs):
        pieces = [live.pop(("N", "own", gs)), live.pop(("c", "N", gs[0]))]
        half = jax.ShapeDtypeStruct(pieces[0].shape, BF16)
        rows = 2 * half.shape[0]
        live["turned", gs], live["keep", gs], live["send", gs] = call(
            functools.partial(ffn_kernel, len(pieces)),
            24,
            "ffn",
            out_shape=[jax.ShapeDtypeStruct((hidden_width, rows), BF16), half, half],
            in_specs=whole(len(pieces) + 3),
            out_specs=whole(3),
            scratch_shapes=[
                pltpu.VMEM((rows, width), BF16),
                pltpu.VMEM((rows, hidden_width), BF16),
            ],
        )(*pieces, live["w", 0], live["w", 1], live["w", 2])

    def in_hbm(*values):
        return [pltpu.with_memory_space_constraint(v, pltpu.HBM) for v in values]

    def send():
        sources = (tokens, cotangent, routes, gate_nums, gain)
        values = call(
            functools.partial(send_kernel, experts),
            16,
            "send",
            out_shape=[piece] * (2 * experts),
            in_specs=[scalar] + [anywhere] * len(sources),
            out_specs=whole(2 * experts),
            scratch_shapes=[pltpu.VMEM(v.shape, v.dtype) for v in sources]
            + [pltpu.SemaphoreType.DMA((len(sources),))],
        )(plane, *in_hbm(*sources))
        live.update({("N", s): value for s, value in enumerate(values[:experts])})
        live.update({("C", s): value for s, value in enumerate(values[experts:])})

    def load():
        weight = jax.ShapeDtypeStruct((width, hidden_width), BF16)
        values = call(
            load_kernel,
            16,
            "load",
            out_shape=[weight, weight, jax.ShapeDtypeStruct((hidden_width, width), BF16)],
            in_specs=[anywhere] * 3,
            out_specs=whole(3),
            scratch_shapes=[pltpu.SemaphoreType.DMA((3,))],
        )(*in_hbm(after(w_gate, live["C", groups[-1][-1]]), w_up, w_down))
        live.update({("w", i): value for i, value in enumerate(values)})

    def grad_call(turned, pieces):
        columns = {}
        for i, gs in enumerate(turned):
            at = 0
            for half in ("own", "other"):
                for side in range(2):
                    for g in gs:
                        columns[half, side, g] = (i, at)
                        at += height
        plan = []
        for i, name in enumerate(pieces):
            half = "other" if name[0] == "c" else "own"
            g = name[-1] if half == "other" else name[-1][0]
            for side in range(2):
                where, at = columns[half, side, g]
                plan.append((where, at, len(turned) + i, side * height, height))
        rows = sum(step[-1] for step in plan)
        sides = [pltpu.VMEM((hidden_width, rows), BF16), pltpu.VMEM((rows, width), BF16)]
        values = [live["turned", gs] for gs in turned]
        values += [live[name] for name in pieces]
        return plan, sides, values

    def first_grad(turned, pieces):
        plan, sides, values = grad_call(turned, pieces)
        live["first"] = call(
            functools.partial(first_grad_kernel, plan),
            24,
            "first_grad",
            out_shape=jax.ShapeDtypeStruct((hidden_width, width), F32),
            in_specs=whole(len(values)),
            out_specs=whole(1)[0],
            scratch_shapes=sides,
        )(*values)

    def last_grad(turned, pieces):
        plan, sides, values = grad_call(turned, pieces)
        return call(
            functools.partial(last_grad_kernel, plan),
            24,
            "last_grad",
            out_shape=jax.ShapeDtypeStruct((1, hidden_width, width), BF16),
            in_specs=whole(1 + len(values)),
            out_specs=anywhere,
            scratch_shapes=[pltpu.VMEM((hidden_width, width), BF16)]
            + sides
            + [pltpu.SemaphoreType.DMA((hidden_width // TILE,))],
        )(live["first"], *values)

    steps = {
        "z": z,
        "y": y,
        "c": c,
        "ffn": lambda kind, g: ffn(g),
        "total": lambda kind, g: total(g),
        "load": lambda kind, g: load(),
        "grad": lambda kind, g: first_grad(
            [(0,), (1,), (2,)],
            [("C", "own", (i,)) for i in range(3)] + [("c", "C", i) for i in range(3)],
        ),
    }
    def name_of(act):
        marks = act.lstrip("abcdefghijklmnopqrstuvwxyz")
        items = [(marks[i], int(marks[i + 1])) for i in range(0, len(marks), 2)]
        return (act[: len(act) - len(marks)],) + tuple(items)

    send()
    if shifts > 1:
        z("N", 0)
        z("C", 0)
        land(("z", ("N", 0)), ("z", ("C", 0)))
    sync()
    for starts, lands in PLAN:
        kernels = []
        for act in starts.split():
            name = name_of(act)
            steps[name[0]](*(name[1:] if name[0] in ("c", "y") else name[1]))
            if name[0] == "ffn":
                kernels.append(live["turned", name[1][1:]])
            if name[0] == "grad":
                kernels.append(live["first"])
        land(*map(name_of, lands.split()), earlier=kernels)
    grad_down = last_grad(
        [(3,)],
        [("C", "own", (3,)), ("c", "C", 3)],
    )
    mixed = call(
        functools.partial(combine_kernel, experts),
        16,
        "combine",
        out_shape=jax.ShapeDtypeStruct(tokens.shape, BF16),
        in_specs=[scalar] + whole(3 + experts),
        out_specs=whole(1)[0],
    )(plane, tokens, routes, gate_nums, *[live["R", s] for s in range(experts)])
    return (mixed, grad_down)


def solution(mesh):
    placed = (
        P(("group", "expert"), None),
        P(("group", "expert"), None),
        P(("group", "expert"), None),
        P(("group", "expert"), None),
        P(),
        P("expert", None, None),
        P("expert", None, None),
        P("expert", None, None),
    )
    return jax.shard_map(
        on_device,
        mesh=mesh,
        in_specs=placed,
        out_specs=(P(("group", "expert"), None), P(("group", "expert"), None, None)),
        check_vma=False,
    )
```

```python
import functools

import jax
import jax.numpy as jnp
from jax import lax
from jax.experimental import pallas as pl
from jax.experimental.pallas import tpu as pltpu
from jax.sharding import PartitionSpec as P

HSPLIT = 4
GROUPS = 4
PLAN = (
    ("yN0 zN1 zN2 loadW0", ""),
    ("yC0 zN3", "zN1 zN2 yN0"),
    ("cN0 yN1", "yC0 cN0"),
    ("ffnN0 yN2", "yN1 zN3"),
    ("cR0N1 yN3 zC1 zC2", "yN2 cR0N1"),
    ("ffnN1 cN2 yR0", "yN3 zC1 zC2 cN2"),
    ("cR1N3 ffnN2 yC1 zC3", "yR0 cR1N3"),
    ("cR2 ffnN3 yR1 totalR0", "yC1 zC3 cR2"),
    ("cR3 yR2", "yR1"),
    ("totalR1 zR1", "cR3"),
    ("yR3 cC0", "yR2 cC0"),
    ("totalR2 zR2 yC2", "yR3 zR1"),
    ("totalR3 zR3 yC3 cC1", "yC2 zR2 cC1"),
    ("cC2 gradC0", "yC3 zR3 cC2"),
    ("cC3", None),
)
TILE = 256
LINK_WORK = 10 << 30
F32 = jnp.float32
BF16 = jnp.bfloat16


def after(value, *earlier):
    return lax.optimization_barrier((value,) + earlier)[0]


def whole(count):
    return [pl.BlockSpec(memory_space=pltpu.VMEM)] * count


def call(kernel, mib, name, moved=0, **keywords):
    return pl.pallas_call(
        kernel,
        compiler_params=pltpu.CompilerParams(vmem_limit_bytes=mib << 20),
        cost_estimate=pl.CostEstimate(flops=moved, bytes_accessed=0, transcendentals=0),
        name=name,
        **keywords,
    )


def experts_of(plane, experts, rows):
    ahead = lax.broadcasted_iota(jnp.int32, (experts, rows), 0) + plane
    return jnp.where(ahead >= experts, ahead - experts, ahead)


def placing_of(routes, plane, experts, capacity):
    rows = routes.shape[1]
    expert = experts_of(plane, experts, rows)
    member = jnp.zeros((experts, rows), jnp.bool_)
    for k in range(routes.shape[0]):
        member = member | (routes[k : k + 1, :] == expert)
    first = lax.broadcasted_iota(jnp.int32, (rows, rows), 0)
    second = lax.broadcasted_iota(jnp.int32, (rows, rows), 1)
    upto = (first <= second).astype(F32).astype(BF16)
    ones = member.astype(F32)
    count = jnp.dot(ones.astype(BF16), upto, preferred_element_type=F32)
    place = (ones * count).astype(jnp.int32) - 1
    slots = lax.broadcasted_iota(jnp.int32, (capacity, rows), 0)
    return [(slots == place[s : s + 1, :]).astype(F32) for s in range(experts)]


def gates_of(routes, numbers, plane, experts):
    expert = experts_of(plane, experts, routes.shape[1])
    numerators = numbers.astype(F32)
    gates = numerators / jnp.sum(numerators, 0, keepdims=True)
    gate = jnp.zeros(expert.shape, F32)
    for k in range(routes.shape[0]):
        gate = gate + jnp.where(routes[k : k + 1, :] == expert, gates[k : k + 1, :], 0.0)
    return gate


def fetch(semaphores, *pairs):
    copies = [
        pltpu.make_async_copy(source, target, semaphores.at[i])
        for i, (source, target) in enumerate(pairs)
    ]
    for copy in copies:
        copy.start()
    return copies


def send_kernel(experts, plane_ref, *refs):
    sources, refs = refs[:5], refs[5:]
    row_outs, grad_outs = refs[:experts], refs[experts : 2 * experts]
    targets, semaphores = refs[2 * experts : -1], refs[-1]
    tokens_ref, cot_ref, routes_ref, nums_ref, gain_ref = targets
    copies = fetch(semaphores, *zip(sources, targets))
    copies[2].wait()
    copies[3].wait()
    routes = routes_ref[...]
    placings = placing_of(routes, plane_ref[0], experts, row_outs[0].shape[0])
    gates = gates_of(routes, nums_ref[...], plane_ref[0], experts)
    copies[4].wait()
    copies[0].wait()
    frames = tokens_ref[...].astype(F32)
    inverse = lax.rsqrt(jnp.mean(frames * frames, -1, keepdims=True) + 1e-06)
    normed = (frames * inverse * gain_ref[...]).astype(BF16)
    for out, placing in zip(row_outs, placings):
        out[...] = jnp.dot(placing.astype(BF16), normed, preferred_element_type=F32).astype(BF16)
    copies[1].wait()
    cot = cot_ref[...]
    for s, (out, placing) in enumerate(zip(grad_outs, placings)):
        picked = jnp.dot(placing.astype(BF16), cot, preferred_element_type=F32)
        gate = jnp.sum(placing * gates[s : s + 1, :], -1, keepdims=True)
        out[...] = (gate * picked).astype(BF16)


def load_kernel(*refs):
    sources, outs, semaphores = refs[:3], refs[3:6], refs[6]
    copies = fetch(semaphores, *[(s.at[0], o) for s, o in zip(sources, outs)])
    for copy in copies:
        copy.wait()


def pair_kernel(first_ref, second_ref, out_ref):
    rows = first_ref.shape[0]
    out_ref[:rows, :] = first_ref[...]
    out_ref[rows:, :] = second_ref[...]


def split_kernel(both_ref, first_ref, second_ref):
    rows = first_ref.shape[0]
    first_ref[...] = both_ref[:rows, :]
    second_ref[...] = both_ref[rows:, :]


def fold_kernel(keep_ref, crossed_ref, out_ref):
    rows = out_ref.shape[0]
    total = keep_ref[rows:, :].astype(F32) + crossed_ref[rows:, :].astype(F32)
    out_ref[...] = total.astype(BF16)


def total_kernel(keep_ref, crossed_ref, came_ref, *outs):
    at = 0
    for out in outs:
        part = slice(at, at + out.shape[0])
        total = keep_ref[part, :].astype(F32) + crossed_ref[part, :].astype(F32)
        out[...] = (total + came_ref[part, :].astype(F32)).astype(BF16)
        at += out.shape[0]


def nothing(*refs):
    pass


def through(values, name, moved=0, earlier=()):
    count = len(values)
    return call(
        nothing,
        4,
        name,
        moved,
        out_shape=[jax.ShapeDtypeStruct(v.shape, v.dtype) for v in values],
        in_specs=whole(count) + [pl.BlockSpec(memory_space=pl.ANY)] * len(earlier),
        out_specs=whole(count),
        input_output_aliases={i: i for i in range(count)},
    )(*values, *earlier)


def ffn_kernel(count, *refs):
    pieces, refs = refs[:count], refs[count:]
    gate_ref, up_ref, down_ref, turned_ref, keep_ref, send_ref, rows_ref, hidden_ref = refs
    at = 0
    for piece in pieces:
        rows_ref[at : at + piece.shape[0], :] = piece[...]
        at += piece.shape[0]
    rows = rows_ref[...]
    half = keep_ref.shape[0]
    for j in range(gate_ref.shape[1] // TILE):
        columns = slice(j * TILE, (j + 1) * TILE)
        pre_gate = jnp.dot(rows, gate_ref[:, columns], preferred_element_type=F32)
        pre_up = jnp.dot(rows, up_ref[:, columns], preferred_element_type=F32)
        hidden = pre_gate * lax.logistic(pre_gate) * pre_up
        hidden_ref[:, columns] = hidden.astype(BF16)
        turned_ref[columns, :] = hidden.T.astype(BF16)
    for j in range(down_ref.shape[1] // TILE):
        columns = slice(j * TILE, (j + 1) * TILE)
        value = jnp.dot(
            hidden_ref[...], down_ref[:, columns], preferred_element_type=F32
        ).astype(BF16)
        keep_ref[:, columns] = value[:half]
        send_ref[:, columns] = value[half:]


def gather_grad(plan, refs, hidden_ref, cot_ref):
    at = 0
    for turned, column, piece, row, count in plan:
        hidden_ref[:, at : at + count] = refs[turned][:, column : column + count]
        cot_ref[at : at + count, :] = refs[piece][row : row + count, :]
        at += count


def first_grad_kernel(plan, *refs):
    out_ref, hidden_ref, cot_ref = refs[-3:]
    gather_grad(plan, refs, hidden_ref, cot_ref)
    for j in range(out_ref.shape[0] // TILE):
        part = slice(j * TILE, (j + 1) * TILE)
        out_ref[part, :] = jnp.dot(
            hidden_ref[part, :], cot_ref[...], preferred_element_type=F32
        )


def last_grad_kernel(plan, first_ref, *refs):
    out_hbm, out_ref, hidden_ref, cot_ref, semaphores = refs[-5:]
    gather_grad(plan, refs, hidden_ref, cot_ref)
    copies = []
    for j in range(first_ref.shape[0] // TILE):
        part = slice(j * TILE, (j + 1) * TILE)
        total = jnp.dot(hidden_ref[part, :], cot_ref[...], preferred_element_type=F32)
        out_ref[part, :] = (first_ref[part, :] + total).astype(BF16)
        copies.append(
            pltpu.make_async_copy(out_ref.at[part, :], out_hbm.at[0, part, :], semaphores.at[j])
        )
        copies[-1].start()
    for copy in copies:
        copy.wait()


def combine_kernel(experts, plane_ref, tokens_ref, routes_ref, nums_ref, *refs):
    values, out = refs[:-1], refs[-1]
    routes = routes_ref[...]
    placings = placing_of(routes, plane_ref[0], experts, values[0].shape[0])
    gates = gates_of(routes, nums_ref[...], plane_ref[0], experts)
    fill = -experts % 8
    if fill:
        gates = jnp.concatenate([gates, jnp.zeros((fill, gates.shape[1]), F32)], 0)
    gates = gates.T
    total = tokens_ref[...].astype(F32)
    for s, value in enumerate(values):
        picked = lax.dot_general(
            placings[s].astype(BF16),
            value[...],
            (((0,), (0,)), ((), ())),
            preferred_element_type=F32,
        )
        total = total + gates[:, s : s + 1] * picked
    out[...] = total.astype(BF16)


def on_device(tokens, cotangent, routes, gate_nums, gain, w_gate, w_up, w_down):
    devices = lax.axis_size("expert")
    experts = devices // HSPLIT
    rows_here, width = tokens.shape
    hidden_width = w_gate.shape[2]
    top_count = routes.shape[1]
    capacity = HSPLIT * (3 * top_count * rows_here // (2 * experts * HSPLIT))
    capacity = -(-capacity // 16) * 16
    shifts = max(1, experts // GROUPS)
    turns = sorted(range(experts), key=lambda s: (min(s, experts - s), s))
    groups = [turns[g : g + shifts] for g in range(0, experts, shifts)]
    height = shifts * capacity
    plane = (lax.axis_index("expert") // HSPLIT).astype(jnp.int32).reshape(1)
    routes, gate_nums, gain = routes.T, gate_nums.T, gain.reshape(1, -1)
    scalar = pl.BlockSpec(memory_space=pltpu.SMEM)
    anywhere = pl.BlockSpec(memory_space=pl.ANY)
    piece = jax.ShapeDtypeStruct((capacity, width), BF16)
    live = {}

    def swap(value, mask):
        return lax.ppermute(value, "expert", [(i, i ^ mask) for i in range(devices)])

    def turn(value, steps):
        to = [(i, (i + steps * HSPLIT) % devices) for i in range(devices)]
        return lax.ppermute(value, "expert", to)

    def sync():
        values = lax.optimization_barrier(tuple(live.values()))
        live.update(zip(list(live), values))

    def join(parts):
        return parts[0] if len(parts) == 1 else jnp.concatenate(parts, 0)

    flying, slow = {}, []

    def small(kernel, name, outs, *values):
        return call(
            kernel,
            8,
            name,
            out_shape=[jax.ShapeDtypeStruct((rows, width), BF16) for rows in outs],
            in_specs=whole(len(values)),
            out_specs=whole(len(outs)),
        )(*values)

    def land(*names, earlier=()):
        names = [n for name in names for n in flights_of(name)]
        quick = [name for name in names if name[0] == "c"]
        names = [name for name in names if name[0] != "c"]
        if not names:
            names, quick = quick, []
        joined = [name for name in names + quick if name[0] in "cy"]
        values = [flying.pop(name) for name in names]
        if not names:
            names, values = [("C", groups[-1][-1])], [live["C", groups[-1][-1]]]
        values = through(values, "land", LINK_WORK, earlier)
        landed = list(zip(names, values))
        if quick:
            crossed = tuple(flying.pop(name) for name in quick) + (values[0],)
            crossed = lax.optimization_barrier(crossed)[: len(quick)]
            landed += list(zip(quick, through(crossed, "land_core")))
        live.update(landed)
        sync()
        for name in joined:
            values = [live.pop(name)]
            if len(name) > 2:
                values = small(split_kernel, "split", [values[0].shape[0] // 2] * 2, *values)
            live.update({(name[0],) + item: value for item, value in zip(name[1:], values)})

    def flights_of(name):
        if name[0] != "z":
            return [name]
        kind, g = name[1]
        return [(kind, s) for s in groups[g] if s]

    def z(kind, g):
        for s in groups[g]:
            if s:
                flying[kind, s] = turn(live[kind, s], -s if kind == "R" else s)

    def y(*items):
        values = [to_row(*item) for item in items]
        if len(values) > 1:
            values = small(pair_kernel, "pair", [2 * height], *values)
        flying[("y",) + items] = swap(values[0], 2)

    def to_row(kind, g):
        if kind == "R":
            keep, crossed = live["keep", (g,)], live["c", "R", g]
            (value,) = small(fold_kernel, "fold", [height], keep, crossed)
        else:
            value = join([live.pop((kind, s)) for s in groups[g]])
            live["sent", kind, g] = value
        return value

    def c(*items):
        values = []
        for kind, g in items:
            if kind == "R":
                values.append(live.pop(("send", (g,))))
                continue
            here, came = live.pop(("sent", kind, g)), live.pop(("y", kind, g))
            (value,) = small(pair_kernel, "pair", [2 * height], here, came)
            live[kind, "own", (g,)] = value
            values.append(value)
        if len(values) > 1:
            values = small(pair_kernel, "pair", [4 * height], *values)
        flying[("c",) + items] = swap(values[0], 1)

    def total(g):
        values = live.pop(("keep", (g,))), live.pop(("c", "R", g)), live.pop(("y", "R", g))
        outs = small(total_kernel, "total", [capacity] * shifts, *values)
        live.update({("R", s): out for s, out in zip(groups[g], outs)})

    def ffn(*gs):
        pieces = [live.pop(("N", "own", gs)), live.pop(("c", "N", gs[0]))]
        half = jax.ShapeDtypeStruct(pieces[0].shape, BF16)
        rows = 2 * half.shape[0]
        live["turned", gs], live["keep", gs], live["send", gs] = call(
            functools.partial(ffn_kernel, len(pieces)),
            24,
            "ffn",
            out_shape=[jax.ShapeDtypeStruct((hidden_width, rows), BF16), half, half],
            in_specs=whole(len(pieces) + 3),
            out_specs=whole(3),
            scratch_shapes=[
                pltpu.VMEM((rows, width), BF16),
                pltpu.VMEM((rows, hidden_width), BF16),
            ],
        )(*pieces, live["w", 0], live["w", 1], live["w", 2])

    def in_hbm(*values):
        return [pltpu.with_memory_space_constraint(v, pltpu.HBM) for v in values]

    def send():
        sources = (tokens, cotangent, routes, gate_nums, gain)
        values = call(
            functools.partial(send_kernel, experts),
            16,
            "send",
            out_shape=[piece] * (2 * experts),
            in_specs=[scalar] + [anywhere] * len(sources),
            out_specs=whole(2 * experts),
            scratch_shapes=[pltpu.VMEM(v.shape, v.dtype) for v in sources]
            + [pltpu.SemaphoreType.DMA((len(sources),))],
        )(plane, *in_hbm(*sources))
        live.update({("N", s): value for s, value in enumerate(values[:experts])})
        live.update({("C", s): value for s, value in enumerate(values[experts:])})

    def load():
        weight = jax.ShapeDtypeStruct((width, hidden_width), BF16)
        values = call(
            load_kernel,
            16,
            "load",
            out_shape=[weight, weight, jax.ShapeDtypeStruct((hidden_width, width), BF16)],
            in_specs=[anywhere] * 3,
            out_specs=whole(3),
            scratch_shapes=[pltpu.SemaphoreType.DMA((3,))],
        )(*in_hbm(after(w_gate, live["C", groups[-1][-1]]), w_up, w_down))
        live.update({("w", i): value for i, value in enumerate(values)})

    def grad_call(turned, pieces):
        columns = {}
        for i, gs in enumerate(turned):
            at = 0
            for half in ("own", "other"):
                for side in range(2):
                    for g in gs:
                        columns[half, side, g] = (i, at)
                        at += height
        plan = []
        for i, name in enumerate(pieces):
            half = "other" if name[0] == "c" else "own"
            g = name[-1] if half == "other" else name[-1][0]
            for side in range(2):
                where, at = columns[half, side, g]
                plan.append((where, at, len(turned) + i, side * height, height))
        rows = sum(step[-1] for step in plan)
        sides = [pltpu.VMEM((hidden_width, rows), BF16), pltpu.VMEM((rows, width), BF16)]
        values = [live["turned", gs] for gs in turned]
        values += [live[name] for name in pieces]
        return plan, sides, values

    def first_grad(turned, pieces):
        plan, sides, values = grad_call(turned, pieces)
        live["first"] = call(
            functools.partial(first_grad_kernel, plan),
            24,
            "first_grad",
            out_shape=jax.ShapeDtypeStruct((hidden_width, width), F32),
            in_specs=whole(len(values)),
            out_specs=whole(1)[0],
            scratch_shapes=sides,
        )(*values)

    def last_grad(turned, pieces):
        plan, sides, values = grad_call(turned, pieces)
        return call(
            functools.partial(last_grad_kernel, plan),
            24,
            "last_grad",
            out_shape=jax.ShapeDtypeStruct((1, hidden_width, width), BF16),
            in_specs=whole(1 + len(values)),
            out_specs=anywhere,
            scratch_shapes=[pltpu.VMEM((hidden_width, width), BF16)]
            + sides
            + [pltpu.SemaphoreType.DMA((hidden_width // TILE,))],
        )(live["first"], *values)

    steps = {
        "z": z,
        "y": y,
        "c": c,
        "ffn": lambda kind, g: ffn(g),
        "total": lambda kind, g: total(g),
        "load": lambda kind, g: load(),
        "grad": lambda kind, g: first_grad(
            [(0,), (1,)],
            [("C", "own", (0,)), ("C", "own", (1,)), ("c", "C", 0), ("c", "C", 1)],
        ),
    }
    def name_of(act):
        marks = act.lstrip("abcdefghijklmnopqrstuvwxyz")
        items = [(marks[i], int(marks[i + 1])) for i in range(0, len(marks), 2)]
        return (act[: len(act) - len(marks)],) + tuple(items)

    send()
    if shifts > 1:
        z("N", 0)
        z("C", 0)
        land(("z", ("N", 0)), ("z", ("C", 0)))
    sync()
    for starts, lands in PLAN:
        kernels = []
        for act in starts.split():
            name = name_of(act)
            steps[name[0]](*(name[1:] if name[0] in ("c", "y") else name[1]))
            if name[0] == "ffn":
                kernels.append(live["turned", name[1][1:]])
            if name[0] == "grad":
                kernels.append(live["first"])
        if lands is None:
            break
        land(*map(name_of, lands.split()), earlier=kernels)
    if ("c", ("C", 3)) in flying:
        live["c", "C", 3] = flying.pop(("c", ("C", 3)))
    grad_down = last_grad(
        [(2,), (3,)],
        [("C", "own", (2,)), ("C", "own", (3,)), ("c", "C", 2), ("c", "C", 3)],
    )
    mixed = call(
        functools.partial(combine_kernel, experts),
        16,
        "combine",
        out_shape=jax.ShapeDtypeStruct(tokens.shape, BF16),
        in_specs=[scalar] + whole(3 + experts),
        out_specs=whole(1)[0],
    )(plane, tokens, routes, gate_nums, *[live["R", s] for s in range(experts)])
    return (mixed, grad_down)


def solution(mesh):
    placed = (
        P(("group", "expert"), None),
        P(("group", "expert"), None),
        P(("group", "expert"), None),
        P(("group", "expert"), None),
        P(),
        P("expert", None, None),
        P("expert", None, None),
        P("expert", None, None),
    )
    return jax.shard_map(
        on_device,
        mesh=mesh,
        in_specs=placed,
        out_specs=(P(("group", "expert"), None), P(("group", "expert"), None, None)),
        check_vma=False,
    )
```

```python
import functools

import jax
import jax.numpy as jnp
from jax import lax
from jax.experimental import pallas as pl
from jax.experimental.pallas import tpu as pltpu
from jax.sharding import PartitionSpec as P

HSPLIT = 4
GROUPS = 4
PLAN = (
    ("yN0 zN1 zN2 loadW0", ""),
    ("yC0 zN3", "zN1 zN2 yN0"),
    ("cN0 yN1", "yC0 cN0"),
    ("ffnN0 yN2", "yN1 zN3"),
    ("cR0N1 yN3 zC1 zC2", "yN2 cR0N1"),
    ("ffnN1 cN2 yR0", "yN3 zC1 zC2 cN2"),
    ("cR1N3 ffnN2 yC1 zC3", "yR0 cR1N3"),
    ("cR2 ffnN3 cR3 yR1 totalR0", "yC1 zC3 cR2"),
    ("yR2", "yR1 cR3"),
    ("totalR1 zR1 yR3", "yR2"),
    ("totalR2 zR2 yC2 cC0", "zR1 yR3 cC0"),
    ("totalR3 zR3 yC3 cC1", "yC2 zR2 cC1"),
    ("cC2 gradC0", "yC3 zR3 cC2"),
    ("cC3", None),
)
TILE = 256
LINK_WORK = 10 << 30
F32 = jnp.float32
BF16 = jnp.bfloat16


def after(value, *earlier):
    return lax.optimization_barrier((value,) + earlier)[0]


def whole(count):
    return [pl.BlockSpec(memory_space=pltpu.VMEM)] * count


def call(kernel, mib, name, moved=0, **keywords):
    return pl.pallas_call(
        kernel,
        compiler_params=pltpu.CompilerParams(vmem_limit_bytes=mib << 20),
        cost_estimate=pl.CostEstimate(flops=moved, bytes_accessed=0, transcendentals=0),
        name=name,
        **keywords,
    )


def experts_of(plane, experts, rows):
    ahead = lax.broadcasted_iota(jnp.int32, (experts, rows), 0) + plane
    return jnp.where(ahead >= experts, ahead - experts, ahead)


def placing_of(routes, plane, experts, capacity):
    rows = routes.shape[1]
    expert = experts_of(plane, experts, rows)
    member = jnp.zeros((experts, rows), jnp.bool_)
    for k in range(routes.shape[0]):
        member = member | (routes[k : k + 1, :] == expert)
    first = lax.broadcasted_iota(jnp.int32, (rows, rows), 0)
    second = lax.broadcasted_iota(jnp.int32, (rows, rows), 1)
    upto = (first <= second).astype(F32).astype(BF16)
    ones = member.astype(F32)
    count = jnp.dot(ones.astype(BF16), upto, preferred_element_type=F32)
    place = (ones * count).astype(jnp.int32) - 1
    slots = lax.broadcasted_iota(jnp.int32, (capacity, rows), 0)
    return [(slots == place[s : s + 1, :]).astype(F32) for s in range(experts)]


def gates_of(routes, numbers, plane, experts):
    expert = experts_of(plane, experts, routes.shape[1])
    numerators = numbers.astype(F32)
    gates = numerators / jnp.sum(numerators, 0, keepdims=True)
    gate = jnp.zeros(expert.shape, F32)
    for k in range(routes.shape[0]):
        gate = gate + jnp.where(routes[k : k + 1, :] == expert, gates[k : k + 1, :], 0.0)
    return gate


def fetch(semaphores, *pairs):
    copies = [
        pltpu.make_async_copy(source, target, semaphores.at[i])
        for i, (source, target) in enumerate(pairs)
    ]
    for copy in copies:
        copy.start()
    return copies


def send_kernel(experts, plane_ref, *refs):
    sources, refs = refs[:5], refs[5:]
    row_outs, grad_outs = refs[:experts], refs[experts : 2 * experts]
    targets, semaphores = refs[2 * experts : -1], refs[-1]
    tokens_ref, cot_ref, routes_ref, nums_ref, gain_ref = targets
    copies = fetch(semaphores, *zip(sources, targets))
    copies[2].wait()
    copies[3].wait()
    routes = routes_ref[...]
    placings = placing_of(routes, plane_ref[0], experts, row_outs[0].shape[0])
    gates = gates_of(routes, nums_ref[...], plane_ref[0], experts)
    copies[4].wait()
    copies[0].wait()
    frames = tokens_ref[...].astype(F32)
    inverse = lax.rsqrt(jnp.mean(frames * frames, -1, keepdims=True) + 1e-06)
    normed = (frames * inverse * gain_ref[...]).astype(BF16)
    for out, placing in zip(row_outs, placings):
        out[...] = jnp.dot(placing.astype(BF16), normed, preferred_element_type=F32).astype(BF16)
    copies[1].wait()
    cot = cot_ref[...]
    for s, (out, placing) in enumerate(zip(grad_outs, placings)):
        picked = jnp.dot(placing.astype(BF16), cot, preferred_element_type=F32)
        gate = jnp.sum(placing * gates[s : s + 1, :], -1, keepdims=True)
        out[...] = (gate * picked).astype(BF16)


def load_kernel(*refs):
    sources, outs, semaphores = refs[:3], refs[3:6], refs[6]
    copies = fetch(semaphores, *[(s.at[0], o) for s, o in zip(sources, outs)])
    for copy in copies:
        copy.wait()


def pair_kernel(first_ref, second_ref, out_ref):
    rows = first_ref.shape[0]
    out_ref[:rows, :] = first_ref[...]
    out_ref[rows:, :] = second_ref[...]


def split_kernel(both_ref, first_ref, second_ref):
    rows = first_ref.shape[0]
    first_ref[...] = both_ref[:rows, :]
    second_ref[...] = both_ref[rows:, :]


def fold_kernel(keep_ref, crossed_ref, out_ref):
    rows = out_ref.shape[0]
    total = keep_ref[rows:, :].astype(F32) + crossed_ref[rows:, :].astype(F32)
    out_ref[...] = total.astype(BF16)


def total_kernel(keep_ref, crossed_ref, came_ref, *outs):
    at = 0
    for out in outs:
        part = slice(at, at + out.shape[0])
        total = keep_ref[part, :].astype(F32) + crossed_ref[part, :].astype(F32)
        out[...] = (total + came_ref[part, :].astype(F32)).astype(BF16)
        at += out.shape[0]


def nothing(*refs):
    pass


def through(values, name, moved=0, earlier=()):
    count = len(values)
    return call(
        nothing,
        4,
        name,
        moved,
        out_shape=[jax.ShapeDtypeStruct(v.shape, v.dtype) for v in values],
        in_specs=whole(count) + [pl.BlockSpec(memory_space=pl.ANY)] * len(earlier),
        out_specs=whole(count),
        input_output_aliases={i: i for i in range(count)},
    )(*values, *earlier)


def ffn_kernel(count, *refs):
    pieces, refs = refs[:count], refs[count:]
    gate_ref, up_ref, down_ref, turned_ref, keep_ref, send_ref, rows_ref, hidden_ref = refs
    at = 0
    for piece in pieces:
        rows_ref[at : at + piece.shape[0], :] = piece[...]
        at += piece.shape[0]
    rows = rows_ref[...]
    half = keep_ref.shape[0]
    for j in range(gate_ref.shape[1] // TILE):
        columns = slice(j * TILE, (j + 1) * TILE)
        pre_gate = jnp.dot(rows, gate_ref[:, columns], preferred_element_type=F32)
        pre_up = jnp.dot(rows, up_ref[:, columns], preferred_element_type=F32)
        hidden = pre_gate * lax.logistic(pre_gate) * pre_up
        hidden_ref[:, columns] = hidden.astype(BF16)
        turned_ref[columns, :] = hidden.T.astype(BF16)
    for j in range(down_ref.shape[1] // TILE):
        columns = slice(j * TILE, (j + 1) * TILE)
        value = jnp.dot(
            hidden_ref[...], down_ref[:, columns], preferred_element_type=F32
        ).astype(BF16)
        keep_ref[:, columns] = value[:half]
        send_ref[:, columns] = value[half:]


def gather_grad(plan, refs, hidden_ref, cot_ref):
    at = 0
    for turned, column, piece, row, count in plan:
        hidden_ref[:, at : at + count] = refs[turned][:, column : column + count]
        cot_ref[at : at + count, :] = refs[piece][row : row + count, :]
        at += count


def first_grad_kernel(plan, *refs):
    out_ref, hidden_ref, cot_ref = refs[-3:]
    gather_grad(plan, refs, hidden_ref, cot_ref)
    for j in range(out_ref.shape[0] // TILE):
        part = slice(j * TILE, (j + 1) * TILE)
        out_ref[part, :] = jnp.dot(
            hidden_ref[part, :], cot_ref[...], preferred_element_type=F32
        )


def last_grad_kernel(plan, first_ref, *refs):
    out_hbm, out_ref, hidden_ref, cot_ref, semaphores = refs[-5:]
    gather_grad(plan, refs, hidden_ref, cot_ref)
    copies = []
    for j in range(first_ref.shape[0] // TILE):
        part = slice(j * TILE, (j + 1) * TILE)
        total = jnp.dot(hidden_ref[part, :], cot_ref[...], preferred_element_type=F32)
        out_ref[part, :] = (first_ref[part, :] + total).astype(BF16)
        copies.append(
            pltpu.make_async_copy(out_ref.at[part, :], out_hbm.at[0, part, :], semaphores.at[j])
        )
        copies[-1].start()
    for copy in copies:
        copy.wait()


def combine_kernel(experts, plane_ref, tokens_ref, routes_ref, nums_ref, *refs):
    values, out = refs[:-1], refs[-1]
    routes = routes_ref[...]
    placings = placing_of(routes, plane_ref[0], experts, values[0].shape[0])
    gates = gates_of(routes, nums_ref[...], plane_ref[0], experts)
    fill = -experts % 8
    if fill:
        gates = jnp.concatenate([gates, jnp.zeros((fill, gates.shape[1]), F32)], 0)
    gates = gates.T
    total = tokens_ref[...].astype(F32)
    for s, value in enumerate(values):
        picked = lax.dot_general(
            placings[s].astype(BF16),
            value[...],
            (((0,), (0,)), ((), ())),
            preferred_element_type=F32,
        )
        total = total + gates[:, s : s + 1] * picked
    out[...] = total.astype(BF16)


def on_device(tokens, cotangent, routes, gate_nums, gain, w_gate, w_up, w_down):
    devices = lax.axis_size("expert")
    experts = devices // HSPLIT
    rows_here, width = tokens.shape
    hidden_width = w_gate.shape[2]
    top_count = routes.shape[1]
    capacity = HSPLIT * (3 * top_count * rows_here // (2 * experts * HSPLIT))
    capacity = -(-capacity // 16) * 16
    shifts = max(1, experts // GROUPS)
    turns = sorted(range(experts), key=lambda s: (min(s, experts - s), s))
    groups = [turns[g : g + shifts] for g in range(0, experts, shifts)]
    height = shifts * capacity
    plane = (lax.axis_index("expert") // HSPLIT).astype(jnp.int32).reshape(1)
    routes, gate_nums, gain = routes.T, gate_nums.T, gain.reshape(1, -1)
    scalar = pl.BlockSpec(memory_space=pltpu.SMEM)
    anywhere = pl.BlockSpec(memory_space=pl.ANY)
    piece = jax.ShapeDtypeStruct((capacity, width), BF16)
    live = {}

    def swap(value, mask):
        return lax.ppermute(value, "expert", [(i, i ^ mask) for i in range(devices)])

    def turn(value, steps):
        to = [(i, (i + steps * HSPLIT) % devices) for i in range(devices)]
        return lax.ppermute(value, "expert", to)

    def sync():
        values = lax.optimization_barrier(tuple(live.values()))
        live.update(zip(list(live), values))

    def join(parts):
        return parts[0] if len(parts) == 1 else jnp.concatenate(parts, 0)

    flying, slow = {}, []

    def small(kernel, name, outs, *values):
        return call(
            kernel,
            8,
            name,
            out_shape=[jax.ShapeDtypeStruct((rows, width), BF16) for rows in outs],
            in_specs=whole(len(values)),
            out_specs=whole(len(outs)),
        )(*values)

    def land(*names, earlier=()):
        names = [n for name in names for n in flights_of(name)]
        quick = [name for name in names if name[0] == "c"]
        names = [name for name in names if name[0] != "c"]
        if not names:
            names, quick = quick, []
        joined = [name for name in names + quick if name[0] in "cy"]
        values = [flying.pop(name) for name in names]
        if not names:
            names, values = [("C", groups[-1][-1])], [live["C", groups[-1][-1]]]
        values = through(values, "land", LINK_WORK, earlier)
        landed = list(zip(names, values))
        if quick:
            crossed = tuple(flying.pop(name) for name in quick) + (values[0],)
            crossed = lax.optimization_barrier(crossed)[: len(quick)]
            landed += list(zip(quick, through(crossed, "land_core")))
        live.update(landed)
        sync()
        for name in joined:
            values = [live.pop(name)]
            if len(name) > 2:
                values = small(split_kernel, "split", [values[0].shape[0] // 2] * 2, *values)
            live.update({(name[0],) + item: value for item, value in zip(name[1:], values)})

    def flights_of(name):
        if name[0] != "z":
            return [name]
        kind, g = name[1]
        return [(kind, s) for s in groups[g] if s]

    def z(kind, g):
        for s in groups[g]:
            if s:
                flying[kind, s] = turn(live[kind, s], -s if kind == "R" else s)

    def y(*items):
        values = [to_row(*item) for item in items]
        if len(values) > 1:
            values = small(pair_kernel, "pair", [2 * height], *values)
        flying[("y",) + items] = swap(values[0], 2)

    def to_row(kind, g):
        if kind == "R":
            keep, crossed = live["keep", (g,)], live["c", "R", g]
            (value,) = small(fold_kernel, "fold", [height], keep, crossed)
        else:
            value = join([live.pop((kind, s)) for s in groups[g]])
            live["sent", kind, g] = value
        return value

    def c(*items):
        values = []
        for kind, g in items:
            if kind == "R":
                values.append(live.pop(("send", (g,))))
                continue
            here, came = live.pop(("sent", kind, g)), live.pop(("y", kind, g))
            (value,) = small(pair_kernel, "pair", [2 * height], here, came)
            live[kind, "own", (g,)] = value
            values.append(value)
        if len(values) > 1:
            values = small(pair_kernel, "pair", [4 * height], *values)
        flying[("c",) + items] = swap(values[0], 1)

    def total(g):
        values = live.pop(("keep", (g,))), live.pop(("c", "R", g)), live.pop(("y", "R", g))
        outs = small(total_kernel, "total", [capacity] * shifts, *values)
        live.update({("R", s): out for s, out in zip(groups[g], outs)})

    def ffn(*gs):
        pieces = [live.pop(("N", "own", gs)), live.pop(("c", "N", gs[0]))]
        half = jax.ShapeDtypeStruct(pieces[0].shape, BF16)
        rows = 2 * half.shape[0]
        live["turned", gs], live["keep", gs], live["send", gs] = call(
            functools.partial(ffn_kernel, len(pieces)),
            24,
            "ffn",
            out_shape=[jax.ShapeDtypeStruct((hidden_width, rows), BF16), half, half],
            in_specs=whole(len(pieces) + 3),
            out_specs=whole(3),
            scratch_shapes=[
                pltpu.VMEM((rows, width), BF16),
                pltpu.VMEM((rows, hidden_width), BF16),
            ],
        )(*pieces, live["w", 0], live["w", 1], live["w", 2])

    def in_hbm(*values):
        return [pltpu.with_memory_space_constraint(v, pltpu.HBM) for v in values]

    def send():
        sources = (tokens, cotangent, routes, gate_nums, gain)
        values = call(
            functools.partial(send_kernel, experts),
            16,
            "send",
            out_shape=[piece] * (2 * experts),
            in_specs=[scalar] + [anywhere] * len(sources),
            out_specs=whole(2 * experts),
            scratch_shapes=[pltpu.VMEM(v.shape, v.dtype) for v in sources]
            + [pltpu.SemaphoreType.DMA((len(sources),))],
        )(plane, *in_hbm(*sources))
        live.update({("N", s): value for s, value in enumerate(values[:experts])})
        live.update({("C", s): value for s, value in enumerate(values[experts:])})

    def load():
        weight = jax.ShapeDtypeStruct((width, hidden_width), BF16)
        values = call(
            load_kernel,
            16,
            "load",
            out_shape=[weight, weight, jax.ShapeDtypeStruct((hidden_width, width), BF16)],
            in_specs=[anywhere] * 3,
            out_specs=whole(3),
            scratch_shapes=[pltpu.SemaphoreType.DMA((3,))],
        )(*in_hbm(after(w_gate, live["C", groups[-1][-1]]), w_up, w_down))
        live.update({("w", i): value for i, value in enumerate(values)})

    def grad_call(turned, pieces):
        columns = {}
        for i, gs in enumerate(turned):
            at = 0
            for half in ("own", "other"):
                for side in range(2):
                    for g in gs:
                        columns[half, side, g] = (i, at)
                        at += height
        plan = []
        for i, name in enumerate(pieces):
            half = "other" if name[0] == "c" else "own"
            g = name[-1] if half == "other" else name[-1][0]
            for side in range(2):
                where, at = columns[half, side, g]
                plan.append((where, at, len(turned) + i, side * height, height))
        rows = sum(step[-1] for step in plan)
        sides = [pltpu.VMEM((hidden_width, rows), BF16), pltpu.VMEM((rows, width), BF16)]
        values = [live["turned", gs] for gs in turned]
        values += [live[name] for name in pieces]
        return plan, sides, values

    def first_grad(turned, pieces):
        plan, sides, values = grad_call(turned, pieces)
        live["first"] = call(
            functools.partial(first_grad_kernel, plan),
            24,
            "first_grad",
            out_shape=jax.ShapeDtypeStruct((hidden_width, width), F32),
            in_specs=whole(len(values)),
            out_specs=whole(1)[0],
            scratch_shapes=sides,
        )(*values)

    def last_grad(turned, pieces):
        plan, sides, values = grad_call(turned, pieces)
        return call(
            functools.partial(last_grad_kernel, plan),
            24,
            "last_grad",
            out_shape=jax.ShapeDtypeStruct((1, hidden_width, width), BF16),
            in_specs=whole(1 + len(values)),
            out_specs=anywhere,
            scratch_shapes=[pltpu.VMEM((hidden_width, width), BF16)]
            + sides
            + [pltpu.SemaphoreType.DMA((hidden_width // TILE,))],
        )(live["first"], *values)

    steps = {
        "z": z,
        "y": y,
        "c": c,
        "ffn": lambda kind, g: ffn(g),
        "total": lambda kind, g: total(g),
        "load": lambda kind, g: load(),
        "grad": lambda kind, g: first_grad(
            [(0,), (1,)],
            [("C", "own", (0,)), ("C", "own", (1,)), ("c", "C", 0), ("c", "C", 1)],
        ),
    }
    def name_of(act):
        marks = act.lstrip("abcdefghijklmnopqrstuvwxyz")
        items = [(marks[i], int(marks[i + 1])) for i in range(0, len(marks), 2)]
        return (act[: len(act) - len(marks)],) + tuple(items)

    send()
    if shifts > 1:
        z("N", 0)
        z("C", 0)
        land(("z", ("N", 0)), ("z", ("C", 0)))
    sync()
    for starts, lands in PLAN:
        kernels = []
        for act in starts.split():
            name = name_of(act)
            steps[name[0]](*(name[1:] if name[0] in ("c", "y") else name[1]))
            if name[0] == "ffn":
                kernels.append(live["turned", name[1][1:]])
            if name[0] == "grad":
                kernels.append(live["first"])
        if lands is None:
            break
        land(*map(name_of, lands.split()), earlier=kernels)
    if ("c", ("C", 3)) in flying:
        live["c", "C", 3] = flying.pop(("c", ("C", 3)))
    grad_down = last_grad(
        [(2,), (3,)],
        [("C", "own", (2,)), ("C", "own", (3,)), ("c", "C", 2), ("c", "C", 3)],
    )
    mixed = call(
        functools.partial(combine_kernel, experts),
        16,
        "combine",
        out_shape=jax.ShapeDtypeStruct(tokens.shape, BF16),
        in_specs=[scalar] + whole(3 + experts),
        out_specs=whole(1)[0],
    )(plane, tokens, routes, gate_nums, *[live["R", s] for s in range(experts)])
    return (mixed, grad_down)


def solution(mesh):
    placed = (
        P(("group", "expert"), None),
        P(("group", "expert"), None),
        P(("group", "expert"), None),
        P(("group", "expert"), None),
        P(),
        P("expert", None, None),
        P("expert", None, None),
        P("expert", None, None),
    )
    return jax.shard_map(
        on_device,
        mesh=mesh,
        in_specs=placed,
        out_specs=(P(("group", "expert"), None), P(("group", "expert"), None, None)),
        check_vma=False,
    )
```

```python
import functools

import jax
import jax.numpy as jnp
from jax import lax
from jax.experimental import pallas as pl
from jax.experimental.pallas import tpu as pltpu
from jax.sharding import PartitionSpec as P

HSPLIT = 4
GROUPS = 4
PLAN = (
    ("yN0 zN1 zN2 loadW0", ""),
    ("yC0 zN3", "zN1 zN2 yN0"),
    ("cN0 yN1", "yC0 cN0"),
    ("ffnN0 yN2", "yN1 zN3"),
    ("cR0N1 yN3 zC3", "yN2 cR0N1"),
    ("ffnN1 cN2 yR0", "yN3 zC3 cN2"),
    ("cR1N3 ffnN2 yC3 zC1", "yR0 cR1N3"),
    ("cR2 ffnN3 yR1 zC2 totalR0", "zC1 yC3 cR2"),
    ("cR3 yR2", "yR1 zC2"),
    ("totalR1 zR1", "cR3"),
    ("yR3 cC0", "yR2 cC0"),
    ("totalR2 zR2 yC1", "zR1 yR3"),
    ("totalR3 zR3 yC2 cC3", "yC1 zR2 cC3"),
    ("cC1 gradC0", "yC2 zR3 cC1"),
    ("cC2", None),
)
TILE = 256
LINK_WORK = 10 << 30
F32 = jnp.float32
BF16 = jnp.bfloat16


def after(value, *earlier):
    return lax.optimization_barrier((value,) + earlier)[0]


def whole(count):
    return [pl.BlockSpec(memory_space=pltpu.VMEM)] * count


def call(kernel, mib, name, moved=0, **keywords):
    return pl.pallas_call(
        kernel,
        compiler_params=pltpu.CompilerParams(vmem_limit_bytes=mib << 20),
        cost_estimate=pl.CostEstimate(flops=moved, bytes_accessed=0, transcendentals=0),
        name=name,
        **keywords,
    )


def experts_of(plane, experts, rows):
    ahead = lax.broadcasted_iota(jnp.int32, (experts, rows), 0) + plane
    return jnp.where(ahead >= experts, ahead - experts, ahead)


def placing_of(routes, plane, experts, capacity):
    rows = routes.shape[1]
    expert = experts_of(plane, experts, rows)
    member = jnp.zeros((experts, rows), jnp.bool_)
    for k in range(routes.shape[0]):
        member = member | (routes[k : k + 1, :] == expert)
    first = lax.broadcasted_iota(jnp.int32, (rows, rows), 0)
    second = lax.broadcasted_iota(jnp.int32, (rows, rows), 1)
    upto = (first <= second).astype(F32).astype(BF16)
    ones = member.astype(F32)
    count = jnp.dot(ones.astype(BF16), upto, preferred_element_type=F32)
    place = (ones * count).astype(jnp.int32) - 1
    slots = lax.broadcasted_iota(jnp.int32, (capacity, rows), 0)
    return [(slots == place[s : s + 1, :]).astype(F32) for s in range(experts)]


def gates_of(routes, numbers, plane, experts):
    expert = experts_of(plane, experts, routes.shape[1])
    numerators = numbers.astype(F32)
    gates = numerators / jnp.sum(numerators, 0, keepdims=True)
    gate = jnp.zeros(expert.shape, F32)
    for k in range(routes.shape[0]):
        gate = gate + jnp.where(routes[k : k + 1, :] == expert, gates[k : k + 1, :], 0.0)
    return gate


def fetch(semaphores, *pairs):
    copies = [
        pltpu.make_async_copy(source, target, semaphores.at[i])
        for i, (source, target) in enumerate(pairs)
    ]
    for copy in copies:
        copy.start()
    return copies


def send_kernel(experts, plane_ref, *refs):
    sources, refs = refs[:5], refs[5:]
    row_outs, grad_outs = refs[:experts], refs[experts : 2 * experts]
    targets, semaphores = refs[2 * experts : -1], refs[-1]
    tokens_ref, cot_ref, routes_ref, nums_ref, gain_ref = targets
    copies = fetch(semaphores, *zip(sources, targets))
    copies[2].wait()
    copies[3].wait()
    routes = routes_ref[...]
    placings = placing_of(routes, plane_ref[0], experts, row_outs[0].shape[0])
    gates = gates_of(routes, nums_ref[...], plane_ref[0], experts)
    copies[4].wait()
    copies[0].wait()
    frames = tokens_ref[...].astype(F32)
    inverse = lax.rsqrt(jnp.mean(frames * frames, -1, keepdims=True) + 1e-06)
    normed = (frames * inverse * gain_ref[...]).astype(BF16)
    for out, placing in zip(row_outs, placings):
        out[...] = jnp.dot(placing.astype(BF16), normed, preferred_element_type=F32).astype(BF16)
    copies[1].wait()
    cot = cot_ref[...]
    for s, (out, placing) in enumerate(zip(grad_outs, placings)):
        picked = jnp.dot(placing.astype(BF16), cot, preferred_element_type=F32)
        gate = jnp.sum(placing * gates[s : s + 1, :], -1, keepdims=True)
        out[...] = (gate * picked).astype(BF16)


def load_kernel(*refs):
    sources, outs, semaphores = refs[:3], refs[3:6], refs[6]
    copies = fetch(semaphores, *[(s.at[0], o) for s, o in zip(sources, outs)])
    for copy in copies:
        copy.wait()


def pair_kernel(first_ref, second_ref, out_ref):
    rows = first_ref.shape[0]
    out_ref[:rows, :] = first_ref[...]
    out_ref[rows:, :] = second_ref[...]


def split_kernel(both_ref, first_ref, second_ref):
    rows = first_ref.shape[0]
    first_ref[...] = both_ref[:rows, :]
    second_ref[...] = both_ref[rows:, :]


def fold_kernel(keep_ref, crossed_ref, out_ref):
    rows = out_ref.shape[0]
    total = keep_ref[rows:, :].astype(F32) + crossed_ref[rows:, :].astype(F32)
    out_ref[...] = total.astype(BF16)


def total_kernel(keep_ref, crossed_ref, came_ref, *outs):
    at = 0
    for out in outs:
        part = slice(at, at + out.shape[0])
        total = keep_ref[part, :].astype(F32) + crossed_ref[part, :].astype(F32)
        out[...] = (total + came_ref[part, :].astype(F32)).astype(BF16)
        at += out.shape[0]


def nothing(*refs):
    pass


def through(values, name, moved=0, earlier=()):
    count = len(values)
    return call(
        nothing,
        4,
        name,
        moved,
        out_shape=[jax.ShapeDtypeStruct(v.shape, v.dtype) for v in values],
        in_specs=whole(count) + [pl.BlockSpec(memory_space=pl.ANY)] * len(earlier),
        out_specs=whole(count),
        input_output_aliases={i: i for i in range(count)},
    )(*values, *earlier)


def ffn_kernel(count, *refs):
    pieces, refs = refs[:count], refs[count:]
    gate_ref, up_ref, down_ref, turned_ref, keep_ref, send_ref, rows_ref, hidden_ref = refs
    at = 0
    for piece in pieces:
        rows_ref[at : at + piece.shape[0], :] = piece[...]
        at += piece.shape[0]
    rows = rows_ref[...]
    half = keep_ref.shape[0]
    for j in range(gate_ref.shape[1] // TILE):
        columns = slice(j * TILE, (j + 1) * TILE)
        pre_gate = jnp.dot(rows, gate_ref[:, columns], preferred_element_type=F32)
        pre_up = jnp.dot(rows, up_ref[:, columns], preferred_element_type=F32)
        hidden = pre_gate * lax.logistic(pre_gate) * pre_up
        hidden_ref[:, columns] = hidden.astype(BF16)
        turned_ref[columns, :] = hidden.T.astype(BF16)
    for j in range(down_ref.shape[1] // TILE):
        columns = slice(j * TILE, (j + 1) * TILE)
        value = jnp.dot(
            hidden_ref[...], down_ref[:, columns], preferred_element_type=F32
        ).astype(BF16)
        keep_ref[:, columns] = value[:half]
        send_ref[:, columns] = value[half:]


def gather_grad(plan, refs, hidden_ref, cot_ref):
    at = 0
    for turned, column, piece, row, count in plan:
        hidden_ref[:, at : at + count] = refs[turned][:, column : column + count]
        cot_ref[at : at + count, :] = refs[piece][row : row + count, :]
        at += count


def first_grad_kernel(plan, *refs):
    out_ref, hidden_ref, cot_ref = refs[-3:]
    gather_grad(plan, refs, hidden_ref, cot_ref)
    for j in range(out_ref.shape[0] // TILE):
        part = slice(j * TILE, (j + 1) * TILE)
        out_ref[part, :] = jnp.dot(
            hidden_ref[part, :], cot_ref[...], preferred_element_type=F32
        )


def last_grad_kernel(plan, first_ref, *refs):
    out_hbm, out_ref, hidden_ref, cot_ref, semaphores = refs[-5:]
    gather_grad(plan, refs, hidden_ref, cot_ref)
    copies = []
    for j in range(first_ref.shape[0] // TILE):
        part = slice(j * TILE, (j + 1) * TILE)
        total = jnp.dot(hidden_ref[part, :], cot_ref[...], preferred_element_type=F32)
        out_ref[part, :] = (first_ref[part, :] + total).astype(BF16)
        copies.append(
            pltpu.make_async_copy(out_ref.at[part, :], out_hbm.at[0, part, :], semaphores.at[j])
        )
        copies[-1].start()
    for copy in copies:
        copy.wait()


def combine_kernel(experts, plane_ref, tokens_ref, routes_ref, nums_ref, *refs):
    values, out = refs[:-1], refs[-1]
    routes = routes_ref[...]
    placings = placing_of(routes, plane_ref[0], experts, values[0].shape[0])
    gates = gates_of(routes, nums_ref[...], plane_ref[0], experts)
    fill = -experts % 8
    if fill:
        gates = jnp.concatenate([gates, jnp.zeros((fill, gates.shape[1]), F32)], 0)
    gates = gates.T
    total = tokens_ref[...].astype(F32)
    for s, value in enumerate(values):
        picked = lax.dot_general(
            placings[s].astype(BF16),
            value[...],
            (((0,), (0,)), ((), ())),
            preferred_element_type=F32,
        )
        total = total + gates[:, s : s + 1] * picked
    out[...] = total.astype(BF16)


def on_device(tokens, cotangent, routes, gate_nums, gain, w_gate, w_up, w_down):
    devices = lax.axis_size("expert")
    experts = devices // HSPLIT
    rows_here, width = tokens.shape
    hidden_width = w_gate.shape[2]
    top_count = routes.shape[1]
    capacity = HSPLIT * (3 * top_count * rows_here // (2 * experts * HSPLIT))
    capacity = -(-capacity // 16) * 16
    shifts = max(1, experts // GROUPS)
    turns = sorted(range(experts), key=lambda s: (min(s, experts - s), s))
    groups = [turns[g : g + shifts] for g in range(0, experts, shifts)]
    height = shifts * capacity
    plane = (lax.axis_index("expert") // HSPLIT).astype(jnp.int32).reshape(1)
    routes, gate_nums, gain = routes.T, gate_nums.T, gain.reshape(1, -1)
    scalar = pl.BlockSpec(memory_space=pltpu.SMEM)
    anywhere = pl.BlockSpec(memory_space=pl.ANY)
    piece = jax.ShapeDtypeStruct((capacity, width), BF16)
    live = {}

    def swap(value, mask):
        return lax.ppermute(value, "expert", [(i, i ^ mask) for i in range(devices)])

    def turn(value, steps):
        to = [(i, (i + steps * HSPLIT) % devices) for i in range(devices)]
        return lax.ppermute(value, "expert", to)

    def sync():
        values = lax.optimization_barrier(tuple(live.values()))
        live.update(zip(list(live), values))

    def join(parts):
        return parts[0] if len(parts) == 1 else jnp.concatenate(parts, 0)

    flying, slow = {}, []

    def small(kernel, name, outs, *values):
        return call(
            kernel,
            8,
            name,
            out_shape=[jax.ShapeDtypeStruct((rows, width), BF16) for rows in outs],
            in_specs=whole(len(values)),
            out_specs=whole(len(outs)),
        )(*values)

    def land(*names, earlier=()):
        names = [n for name in names for n in flights_of(name)]
        quick = [name for name in names if name[0] == "c"]
        names = [name for name in names if name[0] != "c"]
        if not names:
            names, quick = quick, []
        joined = [name for name in names + quick if name[0] in "cy"]
        values = [flying.pop(name) for name in names]
        if not names:
            names, values = [("C", groups[-1][-1])], [live["C", groups[-1][-1]]]
        values = through(values, "land", LINK_WORK, earlier)
        landed = list(zip(names, values))
        if quick:
            crossed = tuple(flying.pop(name) for name in quick) + (values[0],)
            crossed = lax.optimization_barrier(crossed)[: len(quick)]
            landed += list(zip(quick, through(crossed, "land_core")))
        live.update(landed)
        sync()
        for name in joined:
            values = [live.pop(name)]
            if len(name) > 2:
                values = small(split_kernel, "split", [values[0].shape[0] // 2] * 2, *values)
            live.update({(name[0],) + item: value for item, value in zip(name[1:], values)})

    def flights_of(name):
        if name[0] != "z":
            return [name]
        kind, g = name[1]
        return [(kind, s) for s in groups[g] if s]

    def z(kind, g):
        for s in groups[g]:
            if s:
                flying[kind, s] = turn(live[kind, s], -s if kind == "R" else s)

    def y(*items):
        values = [to_row(*item) for item in items]
        if len(values) > 1:
            values = small(pair_kernel, "pair", [2 * height], *values)
        flying[("y",) + items] = swap(values[0], 2)

    def to_row(kind, g):
        if kind == "R":
            keep, crossed = live["keep", (g,)], live["c", "R", g]
            (value,) = small(fold_kernel, "fold", [height], keep, crossed)
        else:
            value = join([live.pop((kind, s)) for s in groups[g]])
            live["sent", kind, g] = value
        return value

    def c(*items):
        values = []
        for kind, g in items:
            if kind == "R":
                values.append(live.pop(("send", (g,))))
                continue
            here, came = live.pop(("sent", kind, g)), live.pop(("y", kind, g))
            (value,) = small(pair_kernel, "pair", [2 * height], here, came)
            live[kind, "own", (g,)] = value
            values.append(value)
        if len(values) > 1:
            values = small(pair_kernel, "pair", [4 * height], *values)
        flying[("c",) + items] = swap(values[0], 1)

    def total(g):
        values = live.pop(("keep", (g,))), live.pop(("c", "R", g)), live.pop(("y", "R", g))
        outs = small(total_kernel, "total", [capacity] * shifts, *values)
        live.update({("R", s): out for s, out in zip(groups[g], outs)})

    def ffn(*gs):
        pieces = [live.pop(("N", "own", gs)), live.pop(("c", "N", gs[0]))]
        half = jax.ShapeDtypeStruct(pieces[0].shape, BF16)
        rows = 2 * half.shape[0]
        live["turned", gs], live["keep", gs], live["send", gs] = call(
            functools.partial(ffn_kernel, len(pieces)),
            24,
            "ffn",
            out_shape=[jax.ShapeDtypeStruct((hidden_width, rows), BF16), half, half],
            in_specs=whole(len(pieces) + 3),
            out_specs=whole(3),
            scratch_shapes=[
                pltpu.VMEM((rows, width), BF16),
                pltpu.VMEM((rows, hidden_width), BF16),
            ],
        )(*pieces, live["w", 0], live["w", 1], live["w", 2])

    def in_hbm(*values):
        return [pltpu.with_memory_space_constraint(v, pltpu.HBM) for v in values]

    def send():
        sources = (tokens, cotangent, routes, gate_nums, gain)
        values = call(
            functools.partial(send_kernel, experts),
            16,
            "send",
            out_shape=[piece] * (2 * experts),
            in_specs=[scalar] + [anywhere] * len(sources),
            out_specs=whole(2 * experts),
            scratch_shapes=[pltpu.VMEM(v.shape, v.dtype) for v in sources]
            + [pltpu.SemaphoreType.DMA((len(sources),))],
        )(plane, *in_hbm(*sources))
        live.update({("N", s): value for s, value in enumerate(values[:experts])})
        live.update({("C", s): value for s, value in enumerate(values[experts:])})

    def load():
        weight = jax.ShapeDtypeStruct((width, hidden_width), BF16)
        values = call(
            load_kernel,
            16,
            "load",
            out_shape=[weight, weight, jax.ShapeDtypeStruct((hidden_width, width), BF16)],
            in_specs=[anywhere] * 3,
            out_specs=whole(3),
            scratch_shapes=[pltpu.SemaphoreType.DMA((3,))],
        )(*in_hbm(after(w_gate, live["C", groups[-1][-1]]), w_up, w_down))
        live.update({("w", i): value for i, value in enumerate(values)})

    def grad_call(turned, pieces):
        columns = {}
        for i, gs in enumerate(turned):
            at = 0
            for half in ("own", "other"):
                for side in range(2):
                    for g in gs:
                        columns[half, side, g] = (i, at)
                        at += height
        plan = []
        for i, name in enumerate(pieces):
            half = "other" if name[0] == "c" else "own"
            g = name[-1] if half == "other" else name[-1][0]
            for side in range(2):
                where, at = columns[half, side, g]
                plan.append((where, at, len(turned) + i, side * height, height))
        rows = sum(step[-1] for step in plan)
        sides = [pltpu.VMEM((hidden_width, rows), BF16), pltpu.VMEM((rows, width), BF16)]
        values = [live["turned", gs] for gs in turned]
        values += [live[name] for name in pieces]
        return plan, sides, values

    def first_grad(turned, pieces):
        plan, sides, values = grad_call(turned, pieces)
        live["first"] = call(
            functools.partial(first_grad_kernel, plan),
            24,
            "first_grad",
            out_shape=jax.ShapeDtypeStruct((hidden_width, width), F32),
            in_specs=whole(len(values)),
            out_specs=whole(1)[0],
            scratch_shapes=sides,
        )(*values)

    def last_grad(turned, pieces):
        plan, sides, values = grad_call(turned, pieces)
        return call(
            functools.partial(last_grad_kernel, plan),
            24,
            "last_grad",
            out_shape=jax.ShapeDtypeStruct((1, hidden_width, width), BF16),
            in_specs=whole(1 + len(values)),
            out_specs=anywhere,
            scratch_shapes=[pltpu.VMEM((hidden_width, width), BF16)]
            + sides
            + [pltpu.SemaphoreType.DMA((hidden_width // TILE,))],
        )(live["first"], *values)

    steps = {
        "z": z,
        "y": y,
        "c": c,
        "ffn": lambda kind, g: ffn(g),
        "total": lambda kind, g: total(g),
        "load": lambda kind, g: load(),
        "grad": lambda kind, g: first_grad(
            [(0,), (3,), (1,)],
            [("C", "own", (i,)) for i in (0, 3, 1)] + [("c", "C", i) for i in (0, 3)],
        ),
    }
    def name_of(act):
        marks = act.lstrip("abcdefghijklmnopqrstuvwxyz")
        items = [(marks[i], int(marks[i + 1])) for i in range(0, len(marks), 2)]
        return (act[: len(act) - len(marks)],) + tuple(items)

    send()
    if shifts > 1:
        z("N", 0)
        z("C", 0)
        land(("z", ("N", 0)), ("z", ("C", 0)))
    sync()
    for starts, lands in PLAN:
        kernels = []
        for act in starts.split():
            name = name_of(act)
            steps[name[0]](*(name[1:] if name[0] in ("c", "y") else name[1]))
            if name[0] == "ffn":
                kernels.append(live["turned", name[1][1:]])
            if name[0] == "grad":
                kernels.append(live["first"])
        if lands is None:
            break
        land(*map(name_of, lands.split()), earlier=kernels)
    live["c", "C", 2] = flying.pop(("c", ("C", 2)))
    grad_down = last_grad(
        [(1,), (2,)],
        [("C", "own", (2,)), ("c", "C", 1), ("c", "C", 2)],
    )
    mixed = call(
        functools.partial(combine_kernel, experts),
        16,
        "combine",
        out_shape=jax.ShapeDtypeStruct(tokens.shape, BF16),
        in_specs=[scalar] + whole(3 + experts),
        out_specs=whole(1)[0],
    )(plane, tokens, routes, gate_nums, *[live["R", s] for s in range(experts)])
    return (mixed, grad_down)


def solution(mesh):
    placed = (
        P(("group", "expert"), None),
        P(("group", "expert"), None),
        P(("group", "expert"), None),
        P(("group", "expert"), None),
        P(),
        P("expert", None, None),
        P("expert", None, None),
        P("expert", None, None),
    )
    return jax.shard_map(
        on_device,
        mesh=mesh,
        in_specs=placed,
        out_specs=(P(("group", "expert"), None), P(("group", "expert"), None, None)),
        check_vma=False,
    )
```

```python
import functools

import jax
import jax.numpy as jnp
from jax import lax
from jax.experimental import pallas as pl
from jax.experimental.pallas import tpu as pltpu
from jax.sharding import PartitionSpec as P

HSPLIT = 4
GROUPS = 4
PLAN = (
    ("yN0 zN1 zN2 loadW0", ""),
    ("yC0 zN3", "zN1 zN2 yN0"),
    ("cN0 yN1", "yC0 cN0"),
    ("ffnN0 yN2", "yN1 zN3"),
    ("cR0N1 yN3 zC3", "yN2 cR0N1"),
    ("ffnN1 cN2 yR0", "yN3 zC3 cN2"),
    ("cR1N3 ffnN2 yC3 zC1", "yR0 cR1N3"),
    ("cR2 ffnN3 yR1 totalR0", "zC1 yC3 cR2"),
    ("cR3 yR2 zC2", "yR1"),
    ("totalR1 zR1", "zC2 cR3"),
    ("yR3 cC0", "yR2 cC0"),
    ("totalR2 zR2 yC1", "zR1 yR3"),
    ("totalR3 zR3 yC2 cC3", "yC1 zR2 cC3"),
    ("cC1 gradC0", "yC2 zR3 cC1"),
    ("cC2", None),
)
TILE = 256
LINK_WORK = 10 << 30
F32 = jnp.float32
BF16 = jnp.bfloat16


def after(value, *earlier):
    return lax.optimization_barrier((value,) + earlier)[0]


def whole(count):
    return [pl.BlockSpec(memory_space=pltpu.VMEM)] * count


def call(kernel, mib, name, moved=0, **keywords):
    return pl.pallas_call(
        kernel,
        compiler_params=pltpu.CompilerParams(vmem_limit_bytes=mib << 20),
        cost_estimate=pl.CostEstimate(flops=moved, bytes_accessed=0, transcendentals=0),
        name=name,
        **keywords,
    )


def experts_of(plane, experts, rows):
    ahead = lax.broadcasted_iota(jnp.int32, (experts, rows), 0) + plane
    return jnp.where(ahead >= experts, ahead - experts, ahead)


def placing_of(routes, plane, experts, capacity):
    rows = routes.shape[1]
    expert = experts_of(plane, experts, rows)
    member = jnp.zeros((experts, rows), jnp.bool_)
    for k in range(routes.shape[0]):
        member = member | (routes[k : k + 1, :] == expert)
    first = lax.broadcasted_iota(jnp.int32, (rows, rows), 0)
    second = lax.broadcasted_iota(jnp.int32, (rows, rows), 1)
    upto = (first <= second).astype(F32).astype(BF16)
    ones = member.astype(F32)
    count = jnp.dot(ones.astype(BF16), upto, preferred_element_type=F32)
    place = (ones * count).astype(jnp.int32) - 1
    slots = lax.broadcasted_iota(jnp.int32, (capacity, rows), 0)
    return [(slots == place[s : s + 1, :]).astype(F32) for s in range(experts)]


def gates_of(routes, numbers, plane, experts):
    expert = experts_of(plane, experts, routes.shape[1])
    numerators = numbers.astype(F32)
    gates = numerators / jnp.sum(numerators, 0, keepdims=True)
    gate = jnp.zeros(expert.shape, F32)
    for k in range(routes.shape[0]):
        gate = gate + jnp.where(routes[k : k + 1, :] == expert, gates[k : k + 1, :], 0.0)
    return gate


def fetch(semaphores, *pairs):
    copies = [
        pltpu.make_async_copy(source, target, semaphores.at[i])
        for i, (source, target) in enumerate(pairs)
    ]
    for copy in copies:
        copy.start()
    return copies


def send_kernel(experts, plane_ref, *refs):
    sources, refs = refs[:5], refs[5:]
    row_outs, grad_outs = refs[:experts], refs[experts : 2 * experts]
    targets, semaphores = refs[2 * experts : -1], refs[-1]
    tokens_ref, cot_ref, routes_ref, nums_ref, gain_ref = targets
    copies = fetch(semaphores, *zip(sources, targets))
    copies[2].wait()
    copies[3].wait()
    routes = routes_ref[...]
    placings = placing_of(routes, plane_ref[0], experts, row_outs[0].shape[0])
    gates = gates_of(routes, nums_ref[...], plane_ref[0], experts)
    copies[4].wait()
    copies[0].wait()
    frames = tokens_ref[...].astype(F32)
    inverse = lax.rsqrt(jnp.mean(frames * frames, -1, keepdims=True) + 1e-06)
    normed = (frames * inverse * gain_ref[...]).astype(BF16)
    for out, placing in zip(row_outs, placings):
        out[...] = jnp.dot(placing.astype(BF16), normed, preferred_element_type=F32).astype(BF16)
    copies[1].wait()
    cot = cot_ref[...]
    for s, (out, placing) in enumerate(zip(grad_outs, placings)):
        picked = jnp.dot(placing.astype(BF16), cot, preferred_element_type=F32)
        gate = jnp.sum(placing * gates[s : s + 1, :], -1, keepdims=True)
        out[...] = (gate * picked).astype(BF16)


def load_kernel(*refs):
    sources, outs, semaphores = refs[:3], refs[3:6], refs[6]
    copies = fetch(semaphores, *[(s.at[0], o) for s, o in zip(sources, outs)])
    for copy in copies:
        copy.wait()


def pair_kernel(first_ref, second_ref, out_ref):
    rows = first_ref.shape[0]
    out_ref[:rows, :] = first_ref[...]
    out_ref[rows:, :] = second_ref[...]


def split_kernel(both_ref, first_ref, second_ref):
    rows = first_ref.shape[0]
    first_ref[...] = both_ref[:rows, :]
    second_ref[...] = both_ref[rows:, :]


def fold_kernel(keep_ref, crossed_ref, out_ref):
    rows = out_ref.shape[0]
    total = keep_ref[rows:, :].astype(F32) + crossed_ref[rows:, :].astype(F32)
    out_ref[...] = total.astype(BF16)


def total_kernel(keep_ref, crossed_ref, came_ref, *outs):
    at = 0
    for out in outs:
        part = slice(at, at + out.shape[0])
        total = keep_ref[part, :].astype(F32) + crossed_ref[part, :].astype(F32)
        out[...] = (total + came_ref[part, :].astype(F32)).astype(BF16)
        at += out.shape[0]


def nothing(*refs):
    pass


def through(values, name, moved=0, earlier=()):
    count = len(values)
    return call(
        nothing,
        4,
        name,
        moved,
        out_shape=[jax.ShapeDtypeStruct(v.shape, v.dtype) for v in values],
        in_specs=whole(count) + [pl.BlockSpec(memory_space=pl.ANY)] * len(earlier),
        out_specs=whole(count),
        input_output_aliases={i: i for i in range(count)},
    )(*values, *earlier)


def ffn_kernel(count, *refs):
    pieces, refs = refs[:count], refs[count:]
    gate_ref, up_ref, down_ref, turned_ref, keep_ref, send_ref, rows_ref, hidden_ref = refs
    at = 0
    for piece in pieces:
        rows_ref[at : at + piece.shape[0], :] = piece[...]
        at += piece.shape[0]
    rows = rows_ref[...]
    half = keep_ref.shape[0]
    for j in range(gate_ref.shape[1] // TILE):
        columns = slice(j * TILE, (j + 1) * TILE)
        pre_gate = jnp.dot(rows, gate_ref[:, columns], preferred_element_type=F32)
        pre_up = jnp.dot(rows, up_ref[:, columns], preferred_element_type=F32)
        hidden = pre_gate * lax.logistic(pre_gate) * pre_up
        hidden_ref[:, columns] = hidden.astype(BF16)
        turned_ref[columns, :] = hidden.T.astype(BF16)
    for j in range(down_ref.shape[1] // TILE):
        columns = slice(j * TILE, (j + 1) * TILE)
        value = jnp.dot(
            hidden_ref[...], down_ref[:, columns], preferred_element_type=F32
        ).astype(BF16)
        keep_ref[:, columns] = value[:half]
        send_ref[:, columns] = value[half:]


def gather_grad(plan, refs, hidden_ref, cot_ref):
    at = 0
    for turned, column, piece, row, count in plan:
        hidden_ref[:, at : at + count] = refs[turned][:, column : column + count]
        cot_ref[at : at + count, :] = refs[piece][row : row + count, :]
        at += count


def first_grad_kernel(plan, *refs):
    out_ref, hidden_ref, cot_ref = refs[-3:]
    gather_grad(plan, refs, hidden_ref, cot_ref)
    for j in range(out_ref.shape[0] // TILE):
        part = slice(j * TILE, (j + 1) * TILE)
        out_ref[part, :] = jnp.dot(
            hidden_ref[part, :], cot_ref[...], preferred_element_type=F32
        )


def last_grad_kernel(plan, first_ref, *refs):
    out_hbm, out_ref, hidden_ref, cot_ref, semaphores = refs[-5:]
    gather_grad(plan, refs, hidden_ref, cot_ref)
    copies = []
    for j in range(first_ref.shape[0] // TILE):
        part = slice(j * TILE, (j + 1) * TILE)
        total = jnp.dot(hidden_ref[part, :], cot_ref[...], preferred_element_type=F32)
        out_ref[part, :] = (first_ref[part, :] + total).astype(BF16)
        copies.append(
            pltpu.make_async_copy(out_ref.at[part, :], out_hbm.at[0, part, :], semaphores.at[j])
        )
        copies[-1].start()
    for copy in copies:
        copy.wait()


def combine_kernel(experts, plane_ref, tokens_ref, routes_ref, nums_ref, *refs):
    values, out = refs[:-1], refs[-1]
    routes = routes_ref[...]
    placings = placing_of(routes, plane_ref[0], experts, values[0].shape[0])
    gates = gates_of(routes, nums_ref[...], plane_ref[0], experts)
    fill = -experts % 8
    if fill:
        gates = jnp.concatenate([gates, jnp.zeros((fill, gates.shape[1]), F32)], 0)
    gates = gates.T
    total = tokens_ref[...].astype(F32)
    for s, value in enumerate(values):
        picked = lax.dot_general(
            placings[s].astype(BF16),
            value[...],
            (((0,), (0,)), ((), ())),
            preferred_element_type=F32,
        )
        total = total + gates[:, s : s + 1] * picked
    out[...] = total.astype(BF16)


def on_device(tokens, cotangent, routes, gate_nums, gain, w_gate, w_up, w_down):
    devices = lax.axis_size("expert")
    experts = devices // HSPLIT
    rows_here, width = tokens.shape
    hidden_width = w_gate.shape[2]
    top_count = routes.shape[1]
    capacity = HSPLIT * (3 * top_count * rows_here // (2 * experts * HSPLIT))
    capacity = -(-capacity // 16) * 16
    shifts = max(1, experts // GROUPS)
    turns = sorted(range(experts), key=lambda s: (min(s, experts - s), s))
    groups = [turns[g : g + shifts] for g in range(0, experts, shifts)]
    height = shifts * capacity
    plane = (lax.axis_index("expert") // HSPLIT).astype(jnp.int32).reshape(1)
    routes, gate_nums, gain = routes.T, gate_nums.T, gain.reshape(1, -1)
    scalar = pl.BlockSpec(memory_space=pltpu.SMEM)
    anywhere = pl.BlockSpec(memory_space=pl.ANY)
    piece = jax.ShapeDtypeStruct((capacity, width), BF16)
    live = {}

    def swap(value, mask):
        return lax.ppermute(value, "expert", [(i, i ^ mask) for i in range(devices)])

    def turn(value, steps):
        to = [(i, (i + steps * HSPLIT) % devices) for i in range(devices)]
        return lax.ppermute(value, "expert", to)

    def sync():
        values = lax.optimization_barrier(tuple(live.values()))
        live.update(zip(list(live), values))

    def join(parts):
        return parts[0] if len(parts) == 1 else jnp.concatenate(parts, 0)

    flying, slow = {}, []

    def small(kernel, name, outs, *values):
        return call(
            kernel,
            8,
            name,
            out_shape=[jax.ShapeDtypeStruct((rows, width), BF16) for rows in outs],
            in_specs=whole(len(values)),
            out_specs=whole(len(outs)),
        )(*values)

    def land(*names, earlier=()):
        names = [n for name in names for n in flights_of(name)]
        quick = [name for name in names if name[0] == "c"]
        names = [name for name in names if name[0] != "c"]
        if not names:
            names, quick = quick, []
        joined = [name for name in names + quick if name[0] in "cy"]
        values = [flying.pop(name) for name in names]
        if not names:
            names, values = [("C", groups[-1][-1])], [live["C", groups[-1][-1]]]
        values = through(values, "land", LINK_WORK, earlier)
        landed = list(zip(names, values))
        if quick:
            crossed = tuple(flying.pop(name) for name in quick) + (values[0],)
            crossed = lax.optimization_barrier(crossed)[: len(quick)]
            landed += list(zip(quick, through(crossed, "land_core")))
        live.update(landed)
        sync()
        for name in joined:
            values = [live.pop(name)]
            if len(name) > 2:
                values = small(split_kernel, "split", [values[0].shape[0] // 2] * 2, *values)
            live.update({(name[0],) + item: value for item, value in zip(name[1:], values)})

    def flights_of(name):
        if name[0] != "z":
            return [name]
        kind, g = name[1]
        return [(kind, s) for s in groups[g] if s]

    def z(kind, g):
        for s in groups[g]:
            if s:
                flying[kind, s] = turn(live[kind, s], -s if kind == "R" else s)

    def y(*items):
        values = [to_row(*item) for item in items]
        if len(values) > 1:
            values = small(pair_kernel, "pair", [2 * height], *values)
        flying[("y",) + items] = swap(values[0], 2)

    def to_row(kind, g):
        if kind == "R":
            keep, crossed = live["keep", (g,)], live["c", "R", g]
            (value,) = small(fold_kernel, "fold", [height], keep, crossed)
        else:
            value = join([live.pop((kind, s)) for s in groups[g]])
            live["sent", kind, g] = value
        return value

    def c(*items):
        values = []
        for kind, g in items:
            if kind == "R":
                values.append(live.pop(("send", (g,))))
                continue
            here, came = live.pop(("sent", kind, g)), live.pop(("y", kind, g))
            (value,) = small(pair_kernel, "pair", [2 * height], here, came)
            live[kind, "own", (g,)] = value
            values.append(value)
        if len(values) > 1:
            values = small(pair_kernel, "pair", [4 * height], *values)
        flying[("c",) + items] = swap(values[0], 1)

    def total(g):
        values = live.pop(("keep", (g,))), live.pop(("c", "R", g)), live.pop(("y", "R", g))
        outs = small(total_kernel, "total", [capacity] * shifts, *values)
        live.update({("R", s): out for s, out in zip(groups[g], outs)})

    def ffn(*gs):
        pieces = [live.pop(("N", "own", gs)), live.pop(("c", "N", gs[0]))]
        half = jax.ShapeDtypeStruct(pieces[0].shape, BF16)
        rows = 2 * half.shape[0]
        live["turned", gs], live["keep", gs], live["send", gs] = call(
            functools.partial(ffn_kernel, len(pieces)),
            24,
            "ffn",
            out_shape=[jax.ShapeDtypeStruct((hidden_width, rows), BF16), half, half],
            in_specs=whole(len(pieces) + 3),
            out_specs=whole(3),
            scratch_shapes=[
                pltpu.VMEM((rows, width), BF16),
                pltpu.VMEM((rows, hidden_width), BF16),
            ],
        )(*pieces, live["w", 0], live["w", 1], live["w", 2])

    def in_hbm(*values):
        return [pltpu.with_memory_space_constraint(v, pltpu.HBM) for v in values]

    def send():
        sources = (tokens, cotangent, routes, gate_nums, gain)
        values = call(
            functools.partial(send_kernel, experts),
            16,
            "send",
            out_shape=[piece] * (2 * experts),
            in_specs=[scalar] + [anywhere] * len(sources),
            out_specs=whole(2 * experts),
            scratch_shapes=[pltpu.VMEM(v.shape, v.dtype) for v in sources]
            + [pltpu.SemaphoreType.DMA((len(sources),))],
        )(plane, *in_hbm(*sources))
        live.update({("N", s): value for s, value in enumerate(values[:experts])})
        live.update({("C", s): value for s, value in enumerate(values[experts:])})

    def load():
        weight = jax.ShapeDtypeStruct((width, hidden_width), BF16)
        values = call(
            load_kernel,
            16,
            "load",
            out_shape=[weight, weight, jax.ShapeDtypeStruct((hidden_width, width), BF16)],
            in_specs=[anywhere] * 3,
            out_specs=whole(3),
            scratch_shapes=[pltpu.SemaphoreType.DMA((3,))],
        )(*in_hbm(after(w_gate, live["C", groups[-1][-1]]), w_up, w_down))
        live.update({("w", i): value for i, value in enumerate(values)})

    def grad_call(turned, pieces):
        columns = {}
        for i, gs in enumerate(turned):
            at = 0
            for half in ("own", "other"):
                for side in range(2):
                    for g in gs:
                        columns[half, side, g] = (i, at)
                        at += height
        plan = []
        for i, name in enumerate(pieces):
            half = "other" if name[0] == "c" else "own"
            g = name[-1] if half == "other" else name[-1][0]
            for side in range(2):
                where, at = columns[half, side, g]
                plan.append((where, at, len(turned) + i, side * height, height))
        rows = sum(step[-1] for step in plan)
        sides = [pltpu.VMEM((hidden_width, rows), BF16), pltpu.VMEM((rows, width), BF16)]
        values = [live["turned", gs] for gs in turned]
        values += [live[name] for name in pieces]
        return plan, sides, values

    def first_grad(turned, pieces):
        plan, sides, values = grad_call(turned, pieces)
        live["first"] = call(
            functools.partial(first_grad_kernel, plan),
            24,
            "first_grad",
            out_shape=jax.ShapeDtypeStruct((hidden_width, width), F32),
            in_specs=whole(len(values)),
            out_specs=whole(1)[0],
            scratch_shapes=sides,
        )(*values)

    def last_grad(turned, pieces):
        plan, sides, values = grad_call(turned, pieces)
        return call(
            functools.partial(last_grad_kernel, plan),
            24,
            "last_grad",
            out_shape=jax.ShapeDtypeStruct((1, hidden_width, width), BF16),
            in_specs=whole(1 + len(values)),
            out_specs=anywhere,
            scratch_shapes=[pltpu.VMEM((hidden_width, width), BF16)]
            + sides
            + [pltpu.SemaphoreType.DMA((hidden_width // TILE,))],
        )(live["first"], *values)

    steps = {
        "z": z,
        "y": y,
        "c": c,
        "ffn": lambda kind, g: ffn(g),
        "total": lambda kind, g: total(g),
        "load": lambda kind, g: load(),
        "grad": lambda kind, g: first_grad(
            [(0,), (3,), (1,)],
            [("C", "own", (i,)) for i in (0, 3, 1)] + [("c", "C", i) for i in (0, 3)],
        ),
    }
    def name_of(act):
        marks = act.lstrip("abcdefghijklmnopqrstuvwxyz")
        items = [(marks[i], int(marks[i + 1])) for i in range(0, len(marks), 2)]
        return (act[: len(act) - len(marks)],) + tuple(items)

    send()
    if shifts > 1:
        z("N", 0)
        z("C", 0)
        land(("z", ("N", 0)), ("z", ("C", 0)))
    sync()
    for starts, lands in PLAN:
        kernels = []
        for act in starts.split():
            name = name_of(act)
            steps[name[0]](*(name[1:] if name[0] in ("c", "y") else name[1]))
            if name[0] == "ffn":
                kernels.append(live["turned", name[1][1:]])
            if name[0] == "grad":
                kernels.append(live["first"])
        if lands is None:
            break
        land(*map(name_of, lands.split()), earlier=kernels)
    live["c", "C", 2] = flying.pop(("c", ("C", 2)))
    grad_down = last_grad(
        [(1,), (2,)],
        [("C", "own", (2,)), ("c", "C", 1), ("c", "C", 2)],
    )
    mixed = call(
        functools.partial(combine_kernel, experts),
        16,
        "combine",
        out_shape=jax.ShapeDtypeStruct(tokens.shape, BF16),
        in_specs=[scalar] + whole(3 + experts),
        out_specs=whole(1)[0],
    )(plane, tokens, routes, gate_nums, *[live["R", s] for s in range(experts)])
    return (mixed, grad_down)


def solution(mesh):
    placed = (
        P(("group", "expert"), None),
        P(("group", "expert"), None),
        P(("group", "expert"), None),
        P(("group", "expert"), None),
        P(),
        P("expert", None, None),
        P("expert", None, None),
        P("expert", None, None),
    )
    return jax.shard_map(
        on_device,
        mesh=mesh,
        in_specs=placed,
        out_specs=(P(("group", "expert"), None), P(("group", "expert"), None, None)),
        check_vma=False,
    )
```

```python
import functools

import jax
import jax.numpy as jnp
from jax import lax
from jax.experimental import pallas as pl
from jax.experimental.pallas import tpu as pltpu
from jax.sharding import PartitionSpec as P

HSPLIT = 4
GROUPS = 4
PLAN = (
    ("yN0 zN1 zN2 sendC0 loadW0", ""),
    ("yC0 zN3", "zN1 zN2 yN0"),
    ("cN0 yN1", "yC0 cN0"),
    ("ffnN0 yN2", "yN1 zN3"),
    ("cR0N1 yN3 zC1 zC2", "yN2 cR0N1"),
    ("ffnN1 cN2 yR0", "yN3 zC1 zC2 cN2"),
    ("cR1N3 ffnN2 yC1 zC3", "yR0 cR1N3"),
    ("cR2 ffnN3 cR3 yR1 totalR0", "yC1 zC3 cR2"),
    ("yR2", "yR1 cR3"),
    ("totalR1 zR1 yR3", "yR2"),
    ("totalR2 zR2 yC2 cC0", "zR1 yR3 cC0"),
    ("totalR3 zR3 yC3 cC1", "yC2 zR2 cC1"),
    ("cC2 gradC0", "yC3 zR3 cC2"),
    ("cC3", None),
)
TILE = 256
LINK_WORK = 10 << 30
F32 = jnp.float32
BF16 = jnp.bfloat16


def after(value, *earlier):
    return lax.optimization_barrier((value,) + earlier)[0]


def whole(count):
    return [pl.BlockSpec(memory_space=pltpu.VMEM)] * count


def call(kernel, mib, name, moved=0, **keywords):
    return pl.pallas_call(
        kernel,
        compiler_params=pltpu.CompilerParams(vmem_limit_bytes=mib << 20),
        cost_estimate=pl.CostEstimate(flops=moved, bytes_accessed=0, transcendentals=0),
        name=name,
        **keywords,
    )


def experts_of(plane, experts, rows):
    ahead = lax.broadcasted_iota(jnp.int32, (experts, rows), 0) + plane
    return jnp.where(ahead >= experts, ahead - experts, ahead)


def placing_of(routes, plane, experts, capacity):
    rows = routes.shape[1]
    expert = experts_of(plane, experts, rows)
    member = jnp.zeros((experts, rows), jnp.bool_)
    for k in range(routes.shape[0]):
        member = member | (routes[k : k + 1, :] == expert)
    first = lax.broadcasted_iota(jnp.int32, (rows, rows), 0)
    second = lax.broadcasted_iota(jnp.int32, (rows, rows), 1)
    upto = (first <= second).astype(F32).astype(BF16)
    ones = member.astype(F32)
    count = jnp.dot(ones.astype(BF16), upto, preferred_element_type=F32)
    place = (ones * count).astype(jnp.int32) - 1
    slots = lax.broadcasted_iota(jnp.int32, (capacity, rows), 0)
    return [(slots == place[s : s + 1, :]).astype(F32) for s in range(experts)]


def gates_of(routes, numbers, plane, experts):
    expert = experts_of(plane, experts, routes.shape[1])
    numerators = numbers.astype(F32)
    gates = numerators / jnp.sum(numerators, 0, keepdims=True)
    gate = jnp.zeros(expert.shape, F32)
    for k in range(routes.shape[0]):
        gate = gate + jnp.where(routes[k : k + 1, :] == expert, gates[k : k + 1, :], 0.0)
    return gate


def fetch(semaphores, *pairs):
    copies = [
        pltpu.make_async_copy(source, target, semaphores.at[i])
        for i, (source, target) in enumerate(pairs)
    ]
    for copy in copies:
        copy.start()
    return copies


def send_rows_kernel(experts, plane_ref, *refs):
    sources, outs, targets, semaphores = refs[:3], refs[3 : 3 + experts], refs[-4:-1], refs[-1]
    tokens_ref, routes_ref, gain_ref = targets
    copies = fetch(semaphores, *zip(sources, targets))
    copies[1].wait()
    placings = placing_of(routes_ref[...], plane_ref[0], experts, outs[0].shape[0])
    copies[2].wait()
    copies[0].wait()
    frames = tokens_ref[...].astype(F32)
    inverse = lax.rsqrt(jnp.mean(frames * frames, -1, keepdims=True) + 1e-06)
    normed = (frames * inverse * gain_ref[...]).astype(BF16)
    for out, placing in zip(outs, placings):
        out[...] = jnp.dot(placing.astype(BF16), normed, preferred_element_type=F32).astype(BF16)


def send_grads_kernel(experts, plane_ref, *refs):
    sources, outs, targets, semaphores = refs[:3], refs[3 : 3 + experts], refs[-4:-1], refs[-1]
    cot_ref, routes_ref, nums_ref = targets
    copies = fetch(semaphores, *zip(sources, targets))
    copies[1].wait()
    copies[2].wait()
    routes = routes_ref[...]
    placings = placing_of(routes, plane_ref[0], experts, outs[0].shape[0])
    gates = gates_of(routes, nums_ref[...], plane_ref[0], experts)
    copies[0].wait()
    cot = cot_ref[...]
    for s, (out, placing) in enumerate(zip(outs, placings)):
        picked = jnp.dot(placing.astype(BF16), cot, preferred_element_type=F32)
        gate = jnp.sum(placing * gates[s : s + 1, :], -1, keepdims=True)
        out[...] = (gate * picked).astype(BF16)


def load_kernel(*refs):
    sources, outs, semaphores = refs[:3], refs[3:6], refs[6]
    copies = fetch(semaphores, *[(s.at[0], o) for s, o in zip(sources, outs)])
    for copy in copies:
        copy.wait()


def pair_kernel(first_ref, second_ref, out_ref):
    rows = first_ref.shape[0]
    out_ref[:rows, :] = first_ref[...]
    out_ref[rows:, :] = second_ref[...]


def split_kernel(both_ref, first_ref, second_ref):
    rows = first_ref.shape[0]
    first_ref[...] = both_ref[:rows, :]
    second_ref[...] = both_ref[rows:, :]


def fold_kernel(keep_ref, crossed_ref, out_ref):
    rows = out_ref.shape[0]
    total = keep_ref[rows:, :].astype(F32) + crossed_ref[rows:, :].astype(F32)
    out_ref[...] = total.astype(BF16)


def total_kernel(keep_ref, crossed_ref, came_ref, *outs):
    at = 0
    for out in outs:
        part = slice(at, at + out.shape[0])
        total = keep_ref[part, :].astype(F32) + crossed_ref[part, :].astype(F32)
        out[...] = (total + came_ref[part, :].astype(F32)).astype(BF16)
        at += out.shape[0]


def nothing(*refs):
    pass


def through(values, name, moved=0, earlier=()):
    count = len(values)
    return call(
        nothing,
        4,
        name,
        moved,
        out_shape=[jax.ShapeDtypeStruct(v.shape, v.dtype) for v in values],
        in_specs=whole(count) + [pl.BlockSpec(memory_space=pl.ANY)] * len(earlier),
        out_specs=whole(count),
        input_output_aliases={i: i for i in range(count)},
    )(*values, *earlier)


def ffn_kernel(count, *refs):
    pieces, refs = refs[:count], refs[count:]
    gate_ref, up_ref, down_ref, turned_ref, keep_ref, send_ref, rows_ref, hidden_ref = refs
    at = 0
    for piece in pieces:
        rows_ref[at : at + piece.shape[0], :] = piece[...]
        at += piece.shape[0]
    rows = rows_ref[...]
    half = keep_ref.shape[0]
    for j in range(gate_ref.shape[1] // TILE):
        columns = slice(j * TILE, (j + 1) * TILE)
        pre_gate = jnp.dot(rows, gate_ref[:, columns], preferred_element_type=F32)
        pre_up = jnp.dot(rows, up_ref[:, columns], preferred_element_type=F32)
        hidden = pre_gate * lax.logistic(pre_gate) * pre_up
        hidden_ref[:, columns] = hidden.astype(BF16)
        turned_ref[columns, :] = hidden.T.astype(BF16)
    for j in range(down_ref.shape[1] // TILE):
        columns = slice(j * TILE, (j + 1) * TILE)
        value = jnp.dot(
            hidden_ref[...], down_ref[:, columns], preferred_element_type=F32
        ).astype(BF16)
        keep_ref[:, columns] = value[:half]
        send_ref[:, columns] = value[half:]


def gather_grad(plan, refs, hidden_ref, cot_ref):
    at = 0
    for turned, column, piece, row, count in plan:
        hidden_ref[:, at : at + count] = refs[turned][:, column : column + count]
        cot_ref[at : at + count, :] = refs[piece][row : row + count, :]
        at += count


def first_grad_kernel(plan, *refs):
    out_ref, hidden_ref, cot_ref = refs[-3:]
    gather_grad(plan, refs, hidden_ref, cot_ref)
    for j in range(out_ref.shape[0] // TILE):
        part = slice(j * TILE, (j + 1) * TILE)
        out_ref[part, :] = jnp.dot(
            hidden_ref[part, :], cot_ref[...], preferred_element_type=F32
        )


def last_grad_kernel(plan, first_ref, *refs):
    out_hbm, out_ref, hidden_ref, cot_ref, semaphores = refs[-5:]
    gather_grad(plan, refs, hidden_ref, cot_ref)
    copies = []
    for j in range(first_ref.shape[0] // TILE):
        part = slice(j * TILE, (j + 1) * TILE)
        total = jnp.dot(hidden_ref[part, :], cot_ref[...], preferred_element_type=F32)
        out_ref[part, :] = (first_ref[part, :] + total).astype(BF16)
        copies.append(
            pltpu.make_async_copy(out_ref.at[part, :], out_hbm.at[0, part, :], semaphores.at[j])
        )
        copies[-1].start()
    for copy in copies:
        copy.wait()


def combine_kernel(experts, plane_ref, tokens_ref, routes_ref, nums_ref, *refs):
    values, out = refs[:-1], refs[-1]
    routes = routes_ref[...]
    placings = placing_of(routes, plane_ref[0], experts, values[0].shape[0])
    gates = gates_of(routes, nums_ref[...], plane_ref[0], experts)
    fill = -experts % 8
    if fill:
        gates = jnp.concatenate([gates, jnp.zeros((fill, gates.shape[1]), F32)], 0)
    gates = gates.T
    total = tokens_ref[...].astype(F32)
    for s, value in enumerate(values):
        picked = lax.dot_general(
            placings[s].astype(BF16),
            value[...],
            (((0,), (0,)), ((), ())),
            preferred_element_type=F32,
        )
        total = total + gates[:, s : s + 1] * picked
    out[...] = total.astype(BF16)


def on_device(tokens, cotangent, routes, gate_nums, gain, w_gate, w_up, w_down):
    devices = lax.axis_size("expert")
    experts = devices // HSPLIT
    rows_here, width = tokens.shape
    hidden_width = w_gate.shape[2]
    top_count = routes.shape[1]
    capacity = HSPLIT * (3 * top_count * rows_here // (2 * experts * HSPLIT))
    capacity = -(-capacity // 16) * 16
    shifts = max(1, experts // GROUPS)
    turns = sorted(range(experts), key=lambda s: (min(s, experts - s), s))
    groups = [turns[g : g + shifts] for g in range(0, experts, shifts)]
    height = shifts * capacity
    plane = (lax.axis_index("expert") // HSPLIT).astype(jnp.int32).reshape(1)
    routes, gate_nums, gain = routes.T, gate_nums.T, gain.reshape(1, -1)
    scalar = pl.BlockSpec(memory_space=pltpu.SMEM)
    anywhere = pl.BlockSpec(memory_space=pl.ANY)
    piece = jax.ShapeDtypeStruct((capacity, width), BF16)
    live = {}

    def swap(value, mask):
        return lax.ppermute(value, "expert", [(i, i ^ mask) for i in range(devices)])

    def turn(value, steps):
        to = [(i, (i + steps * HSPLIT) % devices) for i in range(devices)]
        return lax.ppermute(value, "expert", to)

    def sync():
        values = lax.optimization_barrier(tuple(live.values()))
        live.update(zip(list(live), values))

    def join(parts):
        return parts[0] if len(parts) == 1 else jnp.concatenate(parts, 0)

    flying, slow = {}, []

    def small(kernel, name, outs, *values):
        return call(
            kernel,
            8,
            name,
            out_shape=[jax.ShapeDtypeStruct((rows, width), BF16) for rows in outs],
            in_specs=whole(len(values)),
            out_specs=whole(len(outs)),
        )(*values)

    def land(*names, earlier=()):
        names = [n for name in names for n in flights_of(name)]
        quick = [name for name in names if name[0] == "c"]
        names = [name for name in names if name[0] != "c"]
        if not names:
            names, quick = quick, []
        joined = [name for name in names + quick if name[0] in "cy"]
        values = [flying.pop(name) for name in names]
        if not names:
            names, values = [("N", groups[-1][-1])], [live["N", groups[-1][-1]]]
        values = through(values, "land", LINK_WORK, earlier)
        landed = list(zip(names, values))
        if quick:
            crossed = tuple(flying.pop(name) for name in quick) + (values[0],)
            crossed = lax.optimization_barrier(crossed)[: len(quick)]
            landed += list(zip(quick, through(crossed, "land_core")))
        live.update(landed)
        sync()
        for name in joined:
            values = [live.pop(name)]
            if len(name) > 2:
                values = small(split_kernel, "split", [values[0].shape[0] // 2] * 2, *values)
            live.update({(name[0],) + item: value for item, value in zip(name[1:], values)})

    def flights_of(name):
        if name[0] != "z":
            return [name]
        kind, g = name[1]
        return [(kind, s) for s in groups[g] if s]

    def z(kind, g):
        for s in groups[g]:
            if s:
                flying[kind, s] = turn(live[kind, s], -s if kind == "R" else s)

    def y(*items):
        values = [to_row(*item) for item in items]
        if len(values) > 1:
            values = small(pair_kernel, "pair", [2 * height], *values)
        flying[("y",) + items] = swap(values[0], 2)

    def to_row(kind, g):
        if kind == "R":
            keep, crossed = live["keep", (g,)], live["c", "R", g]
            (value,) = small(fold_kernel, "fold", [height], keep, crossed)
        else:
            value = join([live.pop((kind, s)) for s in groups[g]])
            live["sent", kind, g] = value
        return value

    def c(*items):
        values = []
        for kind, g in items:
            if kind == "R":
                values.append(live.pop(("send", (g,))))
                continue
            here, came = live.pop(("sent", kind, g)), live.pop(("y", kind, g))
            (value,) = small(pair_kernel, "pair", [2 * height], here, came)
            live[kind, "own", (g,)] = value
            values.append(value)
        if len(values) > 1:
            values = small(pair_kernel, "pair", [4 * height], *values)
        flying[("c",) + items] = swap(values[0], 1)

    def total(g):
        values = live.pop(("keep", (g,))), live.pop(("c", "R", g)), live.pop(("y", "R", g))
        outs = small(total_kernel, "total", [capacity] * shifts, *values)
        live.update({("R", s): out for s, out in zip(groups[g], outs)})

    def ffn(*gs):
        pieces = [live.pop(("N", "own", gs)), live.pop(("c", "N", gs[0]))]
        half = jax.ShapeDtypeStruct(pieces[0].shape, BF16)
        rows = 2 * half.shape[0]
        live["turned", gs], live["keep", gs], live["send", gs] = call(
            functools.partial(ffn_kernel, len(pieces)),
            24,
            "ffn",
            out_shape=[jax.ShapeDtypeStruct((hidden_width, rows), BF16), half, half],
            in_specs=whole(len(pieces) + 3),
            out_specs=whole(3),
            scratch_shapes=[
                pltpu.VMEM((rows, width), BF16),
                pltpu.VMEM((rows, hidden_width), BF16),
            ],
        )(*pieces, live["w", 0], live["w", 1], live["w", 2])

    def in_hbm(*values):
        return [pltpu.with_memory_space_constraint(v, pltpu.HBM) for v in values]

    def send(kind, kernel, sources):
        values = call(
            functools.partial(kernel, experts),
            16,
            kernel.__name__[:-7],
            out_shape=[piece] * experts,
            in_specs=[scalar] + [anywhere] * 3,
            out_specs=whole(experts),
            scratch_shapes=[pltpu.VMEM(v.shape, v.dtype) for v in sources]
            + [pltpu.SemaphoreType.DMA((3,))],
        )(plane, *in_hbm(*sources))
        live.update({(kind, s): value for s, value in enumerate(values)})

    def send_grads(kind, g):
        if (kind, groups[-1][-1]) in live:
            return
        first = after(cotangent, live["N", groups[-1][-1]])
        send(kind, send_grads_kernel, (first, routes, gate_nums))

    def load():
        weight = jax.ShapeDtypeStruct((width, hidden_width), BF16)
        values = call(
            load_kernel,
            16,
            "load",
            out_shape=[weight, weight, jax.ShapeDtypeStruct((hidden_width, width), BF16)],
            in_specs=[anywhere] * 3,
            out_specs=whole(3),
            scratch_shapes=[pltpu.SemaphoreType.DMA((3,))],
        )(*in_hbm(after(w_gate, live["N", groups[-1][-1]]), w_up, w_down))
        live.update({("w", i): value for i, value in enumerate(values)})

    def grad_call(turned, pieces):
        columns = {}
        for i, gs in enumerate(turned):
            at = 0
            for half in ("own", "other"):
                for side in range(2):
                    for g in gs:
                        columns[half, side, g] = (i, at)
                        at += height
        plan = []
        for i, name in enumerate(pieces):
            half = "other" if name[0] == "c" else "own"
            g = name[-1] if half == "other" else name[-1][0]
            for side in range(2):
                where, at = columns[half, side, g]
                plan.append((where, at, len(turned) + i, side * height, height))
        rows = sum(step[-1] for step in plan)
        sides = [pltpu.VMEM((hidden_width, rows), BF16), pltpu.VMEM((rows, width), BF16)]
        values = [live["turned", gs] for gs in turned]
        values += [live[name] for name in pieces]
        return plan, sides, values

    def first_grad(turned, pieces):
        plan, sides, values = grad_call(turned, pieces)
        live["first"] = call(
            functools.partial(first_grad_kernel, plan),
            24,
            "first_grad",
            out_shape=jax.ShapeDtypeStruct((hidden_width, width), F32),
            in_specs=whole(len(values)),
            out_specs=whole(1)[0],
            scratch_shapes=sides,
        )(*values)

    def last_grad(turned, pieces):
        plan, sides, values = grad_call(turned, pieces)
        return call(
            functools.partial(last_grad_kernel, plan),
            24,
            "last_grad",
            out_shape=jax.ShapeDtypeStruct((1, hidden_width, width), BF16),
            in_specs=whole(1 + len(values)),
            out_specs=anywhere,
            scratch_shapes=[pltpu.VMEM((hidden_width, width), BF16)]
            + sides
            + [pltpu.SemaphoreType.DMA((hidden_width // TILE,))],
        )(live["first"], *values)

    steps = {
        "z": z,
        "y": y,
        "c": c,
        "ffn": lambda kind, g: ffn(g),
        "total": lambda kind, g: total(g),
        "load": lambda kind, g: load(),
        "send": send_grads,
        "grad": lambda kind, g: first_grad(
            [(0,), (1,), (2,)],
            [("C", "own", (i,)) for i in (0, 1, 2)] + [("c", "C", i) for i in (0, 1)],
        ),
    }
    def name_of(act):
        marks = act.lstrip("abcdefghijklmnopqrstuvwxyz")
        items = [(marks[i], int(marks[i + 1])) for i in range(0, len(marks), 2)]
        return (act[: len(act) - len(marks)],) + tuple(items)

    send("N", send_rows_kernel, (tokens, routes, gain))
    if shifts > 1:
        send_grads("C", 0)
        z("N", 0)
        z("C", 0)
        land(("z", ("N", 0)), ("z", ("C", 0)))
    sync()
    for starts, lands in PLAN:
        kernels = []
        for act in starts.split():
            name = name_of(act)
            steps[name[0]](*(name[1:] if name[0] in ("c", "y") else name[1]))
            if name[0] == "ffn":
                kernels.append(live["turned", name[1][1:]])
            if name[0] == "grad":
                kernels.append(live["first"])
        if lands is None:
            break
        if lands == "none":
            name = "C", groups[-1][-1]
            (live[name],) = through([live[name]], "step")
            sync()
            continue
        land(*map(name_of, lands.split()), earlier=kernels)
    live["c", "C", 3] = flying.pop(("c", ("C", 3)))
    grad_down = last_grad(
        [(2,), (3,)],
        [("C", "own", (3,)), ("c", "C", 2), ("c", "C", 3)],
    )
    mixed = call(
        functools.partial(combine_kernel, experts),
        16,
        "combine",
        out_shape=jax.ShapeDtypeStruct(tokens.shape, BF16),
        in_specs=[scalar] + whole(3 + experts),
        out_specs=whole(1)[0],
    )(plane, tokens, routes, gate_nums, *[live["R", s] for s in range(experts)])
    return (mixed, grad_down)


def solution(mesh):
    placed = (
        P(("group", "expert"), None),
        P(("group", "expert"), None),
        P(("group", "expert"), None),
        P(("group", "expert"), None),
        P(),
        P("expert", None, None),
        P("expert", None, None),
        P("expert", None, None),
    )
    return jax.shard_map(
        on_device,
        mesh=mesh,
        in_specs=placed,
        out_specs=(P(("group", "expert"), None), P(("group", "expert"), None, None)),
        check_vma=False,
    )
```

```python
import functools

import jax
import jax.numpy as jnp
from jax import lax
from jax.experimental import pallas as pl
from jax.experimental.pallas import tpu as pltpu
from jax.sharding import PartitionSpec as P

HSPLIT = 4
GROUPS = 4
PLAN = (
    ("yN0 zN1 zN2 sendC0 loadW0", ""),
    ("yC0 zN3", "zN1 zN2 yN0"),
    ("cN0 yN1", "yC0 cN0"),
    ("ffnN0 yN2", "yN1 zN3"),
    ("cR0N1 yN3 zC1 zC2", "yN2 cR0N1"),
    ("ffnN1 cN2C0", "yN3 zC1 zC2 cN2C0"),
    ("cR1N3 ffnN2 yC1 zC3", "cR1N3"),
    ("cR2 ffnN3 cR3 yR1", "yC1 zC3 cR2"),
    ("yR2", "yR1 cR3"),
    ("totalR1 zR1 yR3", "yR2"),
    ("totalR2 zR2 yC2R0", "zR1 yR3"),
    ("totalR3 zR3 yC3 cC1", "yC2R0 zR2 cC1"),
    ("totalR0 cC2 gradC0", "yC3 zR3 cC2"),
    ("cC3", None),
)
TILE = 256
LINK_WORK = 10 << 30
F32 = jnp.float32
BF16 = jnp.bfloat16


def after(value, *earlier):
    return lax.optimization_barrier((value,) + earlier)[0]


def whole(count):
    return [pl.BlockSpec(memory_space=pltpu.VMEM)] * count


def call(kernel, mib, name, moved=0, **keywords):
    return pl.pallas_call(
        kernel,
        compiler_params=pltpu.CompilerParams(vmem_limit_bytes=mib << 20),
        cost_estimate=pl.CostEstimate(flops=moved, bytes_accessed=0, transcendentals=0),
        name=name,
        **keywords,
    )


def experts_of(plane, experts, rows):
    ahead = lax.broadcasted_iota(jnp.int32, (experts, rows), 0) + plane
    return jnp.where(ahead >= experts, ahead - experts, ahead)


def placing_of(routes, plane, experts, capacity):
    rows = routes.shape[1]
    expert = experts_of(plane, experts, rows)
    member = jnp.zeros((experts, rows), jnp.bool_)
    for k in range(routes.shape[0]):
        member = member | (routes[k : k + 1, :] == expert)
    first = lax.broadcasted_iota(jnp.int32, (rows, rows), 0)
    second = lax.broadcasted_iota(jnp.int32, (rows, rows), 1)
    upto = (first <= second).astype(F32).astype(BF16)
    ones = member.astype(F32)
    count = jnp.dot(ones.astype(BF16), upto, preferred_element_type=F32)
    place = (ones * count).astype(jnp.int32) - 1
    slots = lax.broadcasted_iota(jnp.int32, (capacity, rows), 0)
    return [(slots == place[s : s + 1, :]).astype(F32) for s in range(experts)]


def gates_of(routes, numbers, plane, experts):
    expert = experts_of(plane, experts, routes.shape[1])
    numerators = numbers.astype(F32)
    gates = numerators / jnp.sum(numerators, 0, keepdims=True)
    gate = jnp.zeros(expert.shape, F32)
    for k in range(routes.shape[0]):
        gate = gate + jnp.where(routes[k : k + 1, :] == expert, gates[k : k + 1, :], 0.0)
    return gate


def fetch(semaphores, *pairs):
    copies = [
        pltpu.make_async_copy(source, target, semaphores.at[i])
        for i, (source, target) in enumerate(pairs)
    ]
    for copy in copies:
        copy.start()
    return copies


def send_rows_kernel(experts, plane_ref, *refs):
    sources, outs, targets, semaphores = refs[:3], refs[3 : 3 + experts], refs[-4:-1], refs[-1]
    tokens_ref, routes_ref, gain_ref = targets
    copies = fetch(semaphores, *zip(sources, targets))
    copies[1].wait()
    placings = placing_of(routes_ref[...], plane_ref[0], experts, outs[0].shape[0])
    copies[2].wait()
    copies[0].wait()
    frames = tokens_ref[...].astype(F32)
    inverse = lax.rsqrt(jnp.mean(frames * frames, -1, keepdims=True) + 1e-06)
    normed = (frames * inverse * gain_ref[...]).astype(BF16)
    for out, placing in zip(outs, placings):
        out[...] = jnp.dot(placing.astype(BF16), normed, preferred_element_type=F32).astype(BF16)


def send_grads_kernel(experts, plane_ref, *refs):
    sources, outs, targets, semaphores = refs[:3], refs[3 : 3 + experts], refs[-4:-1], refs[-1]
    cot_ref, routes_ref, nums_ref = targets
    copies = fetch(semaphores, *zip(sources, targets))
    copies[1].wait()
    copies[2].wait()
    routes = routes_ref[...]
    placings = placing_of(routes, plane_ref[0], experts, outs[0].shape[0])
    gates = gates_of(routes, nums_ref[...], plane_ref[0], experts)
    copies[0].wait()
    cot = cot_ref[...]
    for s, (out, placing) in enumerate(zip(outs, placings)):
        picked = jnp.dot(placing.astype(BF16), cot, preferred_element_type=F32)
        gate = jnp.sum(placing * gates[s : s + 1, :], -1, keepdims=True)
        out[...] = (gate * picked).astype(BF16)


def load_kernel(*refs):
    sources, outs, semaphores = refs[:3], refs[3:6], refs[6]
    copies = fetch(semaphores, *[(s.at[0], o) for s, o in zip(sources, outs)])
    for copy in copies:
        copy.wait()


def pair_kernel(first_ref, second_ref, out_ref):
    rows = first_ref.shape[0]
    out_ref[:rows, :] = first_ref[...]
    out_ref[rows:, :] = second_ref[...]


def split_kernel(both_ref, first_ref, second_ref):
    rows = first_ref.shape[0]
    first_ref[...] = both_ref[:rows, :]
    second_ref[...] = both_ref[rows:, :]


def fold_kernel(keep_ref, crossed_ref, out_ref):
    rows = out_ref.shape[0]
    total = keep_ref[rows:, :].astype(F32) + crossed_ref[rows:, :].astype(F32)
    out_ref[...] = total.astype(BF16)


def total_kernel(keep_ref, crossed_ref, came_ref, *outs):
    at = 0
    for out in outs:
        part = slice(at, at + out.shape[0])
        total = keep_ref[part, :].astype(F32) + crossed_ref[part, :].astype(F32)
        out[...] = (total + came_ref[part, :].astype(F32)).astype(BF16)
        at += out.shape[0]


def nothing(*refs):
    pass


def through(values, name, moved=0, earlier=()):
    count = len(values)
    return call(
        nothing,
        4,
        name,
        moved,
        out_shape=[jax.ShapeDtypeStruct(v.shape, v.dtype) for v in values],
        in_specs=whole(count) + [pl.BlockSpec(memory_space=pl.ANY)] * len(earlier),
        out_specs=whole(count),
        input_output_aliases={i: i for i in range(count)},
    )(*values, *earlier)


def ffn_kernel(count, *refs):
    pieces, refs = refs[:count], refs[count:]
    gate_ref, up_ref, down_ref, turned_ref, keep_ref, send_ref, rows_ref, hidden_ref = refs
    at = 0
    for piece in pieces:
        rows_ref[at : at + piece.shape[0], :] = piece[...]
        at += piece.shape[0]
    rows = rows_ref[...]
    half = keep_ref.shape[0]
    for j in range(gate_ref.shape[1] // TILE):
        columns = slice(j * TILE, (j + 1) * TILE)
        pre_gate = jnp.dot(rows, gate_ref[:, columns], preferred_element_type=F32)
        pre_up = jnp.dot(rows, up_ref[:, columns], preferred_element_type=F32)
        hidden = pre_gate * lax.logistic(pre_gate) * pre_up
        hidden_ref[:, columns] = hidden.astype(BF16)
        turned_ref[columns, :] = hidden.T.astype(BF16)
    for j in range(down_ref.shape[1] // TILE):
        columns = slice(j * TILE, (j + 1) * TILE)
        value = jnp.dot(
            hidden_ref[...], down_ref[:, columns], preferred_element_type=F32
        ).astype(BF16)
        keep_ref[:, columns] = value[:half]
        send_ref[:, columns] = value[half:]


def gather_grad(plan, refs, hidden_ref, cot_ref):
    at = 0
    for turned, column, piece, row, count in plan:
        hidden_ref[:, at : at + count] = refs[turned][:, column : column + count]
        cot_ref[at : at + count, :] = refs[piece][row : row + count, :]
        at += count


def first_grad_kernel(plan, *refs):
    out_ref, hidden_ref, cot_ref = refs[-3:]
    gather_grad(plan, refs, hidden_ref, cot_ref)
    for j in range(out_ref.shape[0] // TILE):
        part = slice(j * TILE, (j + 1) * TILE)
        out_ref[part, :] = jnp.dot(
            hidden_ref[part, :], cot_ref[...], preferred_element_type=F32
        )


def last_grad_kernel(plan, first_ref, *refs):
    out_hbm, out_ref, hidden_ref, cot_ref, semaphores = refs[-5:]
    gather_grad(plan, refs, hidden_ref, cot_ref)
    copies = []
    for j in range(first_ref.shape[0] // TILE):
        part = slice(j * TILE, (j + 1) * TILE)
        total = jnp.dot(hidden_ref[part, :], cot_ref[...], preferred_element_type=F32)
        out_ref[part, :] = (first_ref[part, :] + total).astype(BF16)
        copies.append(
            pltpu.make_async_copy(out_ref.at[part, :], out_hbm.at[0, part, :], semaphores.at[j])
        )
        copies[-1].start()
    for copy in copies:
        copy.wait()


def combine_kernel(experts, plane_ref, tokens_ref, routes_ref, nums_ref, *refs):
    values, out = refs[:-1], refs[-1]
    routes = routes_ref[...]
    placings = placing_of(routes, plane_ref[0], experts, values[0].shape[0])
    gates = gates_of(routes, nums_ref[...], plane_ref[0], experts)
    fill = -experts % 8
    if fill:
        gates = jnp.concatenate([gates, jnp.zeros((fill, gates.shape[1]), F32)], 0)
    gates = gates.T
    total = tokens_ref[...].astype(F32)
    for s, value in enumerate(values):
        picked = lax.dot_general(
            placings[s].astype(BF16),
            value[...],
            (((0,), (0,)), ((), ())),
            preferred_element_type=F32,
        )
        total = total + gates[:, s : s + 1] * picked
    out[...] = total.astype(BF16)


def on_device(tokens, cotangent, routes, gate_nums, gain, w_gate, w_up, w_down):
    devices = lax.axis_size("expert")
    experts = devices // HSPLIT
    rows_here, width = tokens.shape
    hidden_width = w_gate.shape[2]
    top_count = routes.shape[1]
    capacity = HSPLIT * (3 * top_count * rows_here // (2 * experts * HSPLIT))
    capacity = -(-capacity // 16) * 16
    shifts = max(1, experts // GROUPS)
    turns = sorted(range(experts), key=lambda s: (min(s, experts - s), s))
    groups = [turns[g : g + shifts] for g in range(0, experts, shifts)]
    height = shifts * capacity
    plane = (lax.axis_index("expert") // HSPLIT).astype(jnp.int32).reshape(1)
    routes, gate_nums, gain = routes.T, gate_nums.T, gain.reshape(1, -1)
    scalar = pl.BlockSpec(memory_space=pltpu.SMEM)
    anywhere = pl.BlockSpec(memory_space=pl.ANY)
    piece = jax.ShapeDtypeStruct((capacity, width), BF16)
    live = {}

    def swap(value, mask):
        return lax.ppermute(value, "expert", [(i, i ^ mask) for i in range(devices)])

    def turn(value, steps):
        to = [(i, (i + steps * HSPLIT) % devices) for i in range(devices)]
        return lax.ppermute(value, "expert", to)

    def sync():
        values = lax.optimization_barrier(tuple(live.values()))
        live.update(zip(list(live), values))

    def join(parts):
        return parts[0] if len(parts) == 1 else jnp.concatenate(parts, 0)

    flying, slow = {}, []

    def small(kernel, name, outs, *values):
        return call(
            kernel,
            8,
            name,
            out_shape=[jax.ShapeDtypeStruct((rows, width), BF16) for rows in outs],
            in_specs=whole(len(values)),
            out_specs=whole(len(outs)),
        )(*values)

    def land(*names, earlier=()):
        names = [n for name in names for n in flights_of(name)]
        quick = [name for name in names if name[0] == "c"]
        names = [name for name in names if name[0] != "c"]
        if not names:
            names, quick = quick, []
        joined = [name for name in names + quick if name[0] in "cy"]
        values = [flying.pop(name) for name in names]
        if not names:
            names, values = [("N", groups[-1][-1])], [live["N", groups[-1][-1]]]
        values = through(values, "land", LINK_WORK, earlier)
        landed = list(zip(names, values))
        if quick:
            crossed = tuple(flying.pop(name) for name in quick) + (values[0],)
            crossed = lax.optimization_barrier(crossed)[: len(quick)]
            landed += list(zip(quick, through(crossed, "land_core")))
        live.update(landed)
        sync()
        for name in joined:
            values = [live.pop(name)]
            if len(name) > 2:
                values = small(split_kernel, "split", [values[0].shape[0] // 2] * 2, *values)
            live.update({(name[0],) + item: value for item, value in zip(name[1:], values)})

    def flights_of(name):
        if name[0] != "z":
            return [name]
        kind, g = name[1]
        return [(kind, s) for s in groups[g] if s]

    def z(kind, g):
        for s in groups[g]:
            if s:
                flying[kind, s] = turn(live[kind, s], -s if kind == "R" else s)

    def y(*items):
        values = [to_row(*item) for item in items]
        if len(values) > 1:
            values = small(pair_kernel, "pair", [2 * height], *values)
        flying[("y",) + items] = swap(values[0], 2)

    def to_row(kind, g):
        if kind == "R":
            keep, crossed = live["keep", (g,)], live["c", "R", g]
            (value,) = small(fold_kernel, "fold", [height], keep, crossed)
        else:
            value = join([live.pop((kind, s)) for s in groups[g]])
            live["sent", kind, g] = value
        return value

    def c(*items):
        values = []
        for kind, g in items:
            if kind == "R":
                values.append(live.pop(("send", (g,))))
                continue
            here, came = live.pop(("sent", kind, g)), live.pop(("y", kind, g))
            (value,) = small(pair_kernel, "pair", [2 * height], here, came)
            live[kind, "own", (g,)] = value
            values.append(value)
        if len(values) > 1:
            values = small(pair_kernel, "pair", [4 * height], *values)
        flying[("c",) + items] = swap(values[0], 1)

    def total(g):
        values = live.pop(("keep", (g,))), live.pop(("c", "R", g)), live.pop(("y", "R", g))
        outs = small(total_kernel, "total", [capacity] * shifts, *values)
        live.update({("R", s): out for s, out in zip(groups[g], outs)})

    def ffn(*gs):
        pieces = [live.pop(("N", "own", gs)), live.pop(("c", "N", gs[0]))]
        half = jax.ShapeDtypeStruct(pieces[0].shape, BF16)
        rows = 2 * half.shape[0]
        live["turned", gs], live["keep", gs], live["send", gs] = call(
            functools.partial(ffn_kernel, len(pieces)),
            24,
            "ffn",
            out_shape=[jax.ShapeDtypeStruct((hidden_width, rows), BF16), half, half],
            in_specs=whole(len(pieces) + 3),
            out_specs=whole(3),
            scratch_shapes=[
                pltpu.VMEM((rows, width), BF16),
                pltpu.VMEM((rows, hidden_width), BF16),
            ],
        )(*pieces, live["w", 0], live["w", 1], live["w", 2])

    def in_hbm(*values):
        return [pltpu.with_memory_space_constraint(v, pltpu.HBM) for v in values]

    def send(kind, kernel, sources):
        values = call(
            functools.partial(kernel, experts),
            16,
            kernel.__name__[:-7],
            out_shape=[piece] * experts,
            in_specs=[scalar] + [anywhere] * 3,
            out_specs=whole(experts),
            scratch_shapes=[pltpu.VMEM(v.shape, v.dtype) for v in sources]
            + [pltpu.SemaphoreType.DMA((3,))],
        )(plane, *in_hbm(*sources))
        live.update({(kind, s): value for s, value in enumerate(values)})

    def send_grads(kind, g):
        if (kind, groups[-1][-1]) in live:
            return
        first = after(cotangent, live["N", groups[-1][-1]])
        send(kind, send_grads_kernel, (first, routes, gate_nums))

    def load():
        weight = jax.ShapeDtypeStruct((width, hidden_width), BF16)
        values = call(
            load_kernel,
            16,
            "load",
            out_shape=[weight, weight, jax.ShapeDtypeStruct((hidden_width, width), BF16)],
            in_specs=[anywhere] * 3,
            out_specs=whole(3),
            scratch_shapes=[pltpu.SemaphoreType.DMA((3,))],
        )(*in_hbm(after(w_gate, live["N", groups[-1][-1]]), w_up, w_down))
        live.update({("w", i): value for i, value in enumerate(values)})

    def grad_call(turned, pieces):
        columns = {}
        for i, gs in enumerate(turned):
            at = 0
            for half in ("own", "other"):
                for side in range(2):
                    for g in gs:
                        columns[half, side, g] = (i, at)
                        at += height
        plan = []
        for i, name in enumerate(pieces):
            half = "other" if name[0] == "c" else "own"
            g = name[-1] if half == "other" else name[-1][0]
            for side in range(2):
                where, at = columns[half, side, g]
                plan.append((where, at, len(turned) + i, side * height, height))
        rows = sum(step[-1] for step in plan)
        sides = [pltpu.VMEM((hidden_width, rows), BF16), pltpu.VMEM((rows, width), BF16)]
        values = [live["turned", gs] for gs in turned]
        values += [live[name] for name in pieces]
        return plan, sides, values

    def first_grad(turned, pieces):
        plan, sides, values = grad_call(turned, pieces)
        live["first"] = call(
            functools.partial(first_grad_kernel, plan),
            24,
            "first_grad",
            out_shape=jax.ShapeDtypeStruct((hidden_width, width), F32),
            in_specs=whole(len(values)),
            out_specs=whole(1)[0],
            scratch_shapes=sides,
        )(*values)

    def last_grad(turned, pieces):
        plan, sides, values = grad_call(turned, pieces)
        return call(
            functools.partial(last_grad_kernel, plan),
            24,
            "last_grad",
            out_shape=jax.ShapeDtypeStruct((1, hidden_width, width), BF16),
            in_specs=whole(1 + len(values)),
            out_specs=anywhere,
            scratch_shapes=[pltpu.VMEM((hidden_width, width), BF16)]
            + sides
            + [pltpu.SemaphoreType.DMA((hidden_width // TILE,))],
        )(live["first"], *values)

    steps = {
        "z": z,
        "y": y,
        "c": c,
        "ffn": lambda kind, g: ffn(g),
        "total": lambda kind, g: total(g),
        "load": lambda kind, g: load(),
        "send": send_grads,
        "grad": lambda kind, g: first_grad(
            [(0,), (1,), (2,)],
            [("C", "own", (i,)) for i in (0, 1, 2)] + [("c", "C", i) for i in (0, 1)],
        ),
    }
    def name_of(act):
        marks = act.lstrip("abcdefghijklmnopqrstuvwxyz")
        items = [(marks[i], int(marks[i + 1])) for i in range(0, len(marks), 2)]
        return (act[: len(act) - len(marks)],) + tuple(items)

    send("N", send_rows_kernel, (tokens, routes, gain))
    if shifts > 1:
        send_grads("C", 0)
        z("N", 0)
        z("C", 0)
        land(("z", ("N", 0)), ("z", ("C", 0)))
    sync()
    for starts, lands in PLAN:
        kernels = []
        for act in starts.split():
            name = name_of(act)
            steps[name[0]](*(name[1:] if name[0] in ("c", "y") else name[1]))
            if name[0] == "ffn":
                kernels.append(live["turned", name[1][1:]])
            if name[0] == "grad":
                kernels.append(live["first"])
        if lands is None:
            break
        if lands == "none":
            name = "C", groups[-1][-1]
            (live[name],) = through([live[name]], "step")
            sync()
            continue
        land(*map(name_of, lands.split()), earlier=kernels)
    live["c", "C", 3] = flying.pop(("c", ("C", 3)))
    grad_down = last_grad(
        [(2,), (3,)],
        [("C", "own", (3,)), ("c", "C", 2), ("c", "C", 3)],
    )
    mixed = call(
        functools.partial(combine_kernel, experts),
        16,
        "combine",
        out_shape=jax.ShapeDtypeStruct(tokens.shape, BF16),
        in_specs=[scalar] + whole(3 + experts),
        out_specs=whole(1)[0],
    )(plane, tokens, routes, gate_nums, *[live["R", s] for s in range(experts)])
    return (mixed, grad_down)


def solution(mesh):
    placed = (
        P(("group", "expert"), None),
        P(("group", "expert"), None),
        P(("group", "expert"), None),
        P(("group", "expert"), None),
        P(),
        P("expert", None, None),
        P("expert", None, None),
        P("expert", None, None),
    )
    return jax.shard_map(
        on_device,
        mesh=mesh,
        in_specs=placed,
        out_specs=(P(("group", "expert"), None), P(("group", "expert"), None, None)),
        check_vma=False,
    )
```

```python
import functools

import jax
import jax.numpy as jnp
from jax import lax
from jax.experimental import pallas as pl
from jax.experimental.pallas import tpu as pltpu
from jax.sharding import PartitionSpec as P

HSPLIT = 4
GROUPS = 4
PLAN = (
    ("yN0 zN2 zN1 sendC0 loadW0", ""),
    ("yC0 zN3", "zN2 zN1 yN0"),
    ("cN0 yN1", "yC0 cN0"),
    ("ffnN0 yN2", "yN1 zN3"),
    ("cR0N1 yN3 zC2 zC1", "yN2 cR0N1"),
    ("ffnN1 cN2 yR0", "yN3 zC2 zC1 cN2"),
    ("cR1N3 ffnN2 yC1 zC3", "yR0 cR1N3"),
    ("cR2 ffnN3 cR3 yR1 totalR0", "yC1 zC3 cR2"),
    ("yR2", "yR1 cR3"),
    ("totalR1 zR1 yR3", "yR2"),
    ("totalR2 zR2 yC2 cC0", "zR1 yR3 cC0"),
    ("totalR3 zR3 yC3 cC1", "yC2 zR2 cC1"),
    ("cC2 gradC0", "yC3 zR3 cC2"),
    ("cC3", None),
)
TILE = 256
LINK_WORK = 10 << 30
F32 = jnp.float32
BF16 = jnp.bfloat16


def after(value, *earlier):
    return lax.optimization_barrier((value,) + earlier)[0]


def whole(count):
    return [pl.BlockSpec(memory_space=pltpu.VMEM)] * count


def call(kernel, mib, name, moved=0, **keywords):
    return pl.pallas_call(
        kernel,
        compiler_params=pltpu.CompilerParams(vmem_limit_bytes=mib << 20),
        cost_estimate=pl.CostEstimate(flops=moved, bytes_accessed=0, transcendentals=0),
        name=name,
        **keywords,
    )


def experts_of(plane, experts, rows):
    ahead = lax.broadcasted_iota(jnp.int32, (experts, rows), 0) + plane
    return jnp.where(ahead >= experts, ahead - experts, ahead)


def placing_of(routes, plane, experts, capacity):
    rows = routes.shape[1]
    expert = experts_of(plane, experts, rows)
    member = jnp.zeros((experts, rows), jnp.bool_)
    for k in range(routes.shape[0]):
        member = member | (routes[k : k + 1, :] == expert)
    first = lax.broadcasted_iota(jnp.int32, (rows, rows), 0)
    second = lax.broadcasted_iota(jnp.int32, (rows, rows), 1)
    upto = (first <= second).astype(F32).astype(BF16)
    ones = member.astype(F32)
    count = jnp.dot(ones.astype(BF16), upto, preferred_element_type=F32)
    place = (ones * count).astype(jnp.int32) - 1
    slots = lax.broadcasted_iota(jnp.int32, (capacity, rows), 0)
    return [(slots == place[s : s + 1, :]).astype(F32) for s in range(experts)]


def gates_of(routes, numbers, plane, experts):
    expert = experts_of(plane, experts, routes.shape[1])
    numerators = numbers.astype(F32)
    gates = numerators / jnp.sum(numerators, 0, keepdims=True)
    gate = jnp.zeros(expert.shape, F32)
    for k in range(routes.shape[0]):
        gate = gate + jnp.where(routes[k : k + 1, :] == expert, gates[k : k + 1, :], 0.0)
    return gate


def fetch(semaphores, *pairs):
    copies = [
        pltpu.make_async_copy(source, target, semaphores.at[i])
        for i, (source, target) in enumerate(pairs)
    ]
    for copy in copies:
        copy.start()
    return copies


def send_rows_kernel(experts, plane_ref, *refs):
    sources, outs, targets, semaphores = refs[:3], refs[3 : 3 + experts], refs[-4:-1], refs[-1]
    tokens_ref, routes_ref, gain_ref = targets
    copies = fetch(semaphores, *zip(sources, targets))
    copies[1].wait()
    placings = placing_of(routes_ref[...], plane_ref[0], experts, outs[0].shape[0])
    copies[2].wait()
    copies[0].wait()
    frames = tokens_ref[...].astype(F32)
    inverse = lax.rsqrt(jnp.mean(frames * frames, -1, keepdims=True) + 1e-06)
    normed = (frames * inverse * gain_ref[...]).astype(BF16)
    for out, placing in zip(outs, placings):
        out[...] = jnp.dot(placing.astype(BF16), normed, preferred_element_type=F32).astype(BF16)


def send_grads_kernel(experts, plane_ref, *refs):
    sources, outs, targets, semaphores = refs[:3], refs[3 : 3 + experts], refs[-4:-1], refs[-1]
    cot_ref, routes_ref, nums_ref = targets
    copies = fetch(semaphores, *zip(sources, targets))
    copies[1].wait()
    copies[2].wait()
    routes = routes_ref[...]
    placings = placing_of(routes, plane_ref[0], experts, outs[0].shape[0])
    gates = gates_of(routes, nums_ref[...], plane_ref[0], experts)
    copies[0].wait()
    cot = cot_ref[...]
    for s, (out, placing) in enumerate(zip(outs, placings)):
        picked = jnp.dot(placing.astype(BF16), cot, preferred_element_type=F32)
        gate = jnp.sum(placing * gates[s : s + 1, :], -1, keepdims=True)
        out[...] = (gate * picked).astype(BF16)


def load_kernel(*refs):
    sources, outs, semaphores = refs[:3], refs[3:6], refs[6]
    copies = fetch(semaphores, *[(s.at[0], o) for s, o in zip(sources, outs)])
    for copy in copies:
        copy.wait()


def pair_kernel(first_ref, second_ref, out_ref):
    rows = first_ref.shape[0]
    out_ref[:rows, :] = first_ref[...]
    out_ref[rows:, :] = second_ref[...]


def split_kernel(both_ref, first_ref, second_ref):
    rows = first_ref.shape[0]
    first_ref[...] = both_ref[:rows, :]
    second_ref[...] = both_ref[rows:, :]


def fold_kernel(keep_ref, crossed_ref, out_ref):
    rows = out_ref.shape[0]
    total = keep_ref[rows:, :].astype(F32) + crossed_ref[rows:, :].astype(F32)
    out_ref[...] = total.astype(BF16)


def total_kernel(keep_ref, crossed_ref, came_ref, *outs):
    at = 0
    for out in outs:
        part = slice(at, at + out.shape[0])
        total = keep_ref[part, :].astype(F32) + crossed_ref[part, :].astype(F32)
        out[...] = (total + came_ref[part, :].astype(F32)).astype(BF16)
        at += out.shape[0]


def nothing(*refs):
    pass


def through(values, name, moved=0, earlier=()):
    count = len(values)
    return call(
        nothing,
        4,
        name,
        moved,
        out_shape=[jax.ShapeDtypeStruct(v.shape, v.dtype) for v in values],
        in_specs=whole(count) + [pl.BlockSpec(memory_space=pl.ANY)] * len(earlier),
        out_specs=whole(count),
        input_output_aliases={i: i for i in range(count)},
    )(*values, *earlier)


def ffn_kernel(count, *refs):
    pieces, refs = refs[:count], refs[count:]
    gate_ref, up_ref, down_ref, turned_ref, keep_ref, send_ref, rows_ref, hidden_ref = refs
    at = 0
    for piece in pieces:
        rows_ref[at : at + piece.shape[0], :] = piece[...]
        at += piece.shape[0]
    rows = rows_ref[...]
    half = keep_ref.shape[0]
    for j in range(gate_ref.shape[1] // TILE):
        columns = slice(j * TILE, (j + 1) * TILE)
        pre_gate = jnp.dot(rows, gate_ref[:, columns], preferred_element_type=F32)
        pre_up = jnp.dot(rows, up_ref[:, columns], preferred_element_type=F32)
        hidden = pre_gate * lax.logistic(pre_gate) * pre_up
        hidden_ref[:, columns] = hidden.astype(BF16)
        turned_ref[columns, :] = hidden.T.astype(BF16)
    for j in range(down_ref.shape[1] // TILE):
        columns = slice(j * TILE, (j + 1) * TILE)
        value = jnp.dot(
            hidden_ref[...], down_ref[:, columns], preferred_element_type=F32
        ).astype(BF16)
        keep_ref[:, columns] = value[:half]
        send_ref[:, columns] = value[half:]


def gather_grad(plan, refs, hidden_ref, cot_ref):
    at = 0
    for turned, column, piece, row, count in plan:
        hidden_ref[:, at : at + count] = refs[turned][:, column : column + count]
        cot_ref[at : at + count, :] = refs[piece][row : row + count, :]
        at += count


def first_grad_kernel(plan, *refs):
    out_ref, hidden_ref, cot_ref = refs[-3:]
    gather_grad(plan, refs, hidden_ref, cot_ref)
    for j in range(out_ref.shape[0] // TILE):
        part = slice(j * TILE, (j + 1) * TILE)
        out_ref[part, :] = jnp.dot(
            hidden_ref[part, :], cot_ref[...], preferred_element_type=F32
        )


def last_grad_kernel(plan, first_ref, *refs):
    out_hbm, out_ref, hidden_ref, cot_ref, semaphores = refs[-5:]
    gather_grad(plan, refs, hidden_ref, cot_ref)
    copies = []
    for j in range(first_ref.shape[0] // TILE):
        part = slice(j * TILE, (j + 1) * TILE)
        total = jnp.dot(hidden_ref[part, :], cot_ref[...], preferred_element_type=F32)
        out_ref[part, :] = (first_ref[part, :] + total).astype(BF16)
        copies.append(
            pltpu.make_async_copy(out_ref.at[part, :], out_hbm.at[0, part, :], semaphores.at[j])
        )
        copies[-1].start()
    for copy in copies:
        copy.wait()


def combine_kernel(experts, plane_ref, tokens_ref, routes_ref, nums_ref, *refs):
    values, out = refs[:-1], refs[-1]
    routes = routes_ref[...]
    placings = placing_of(routes, plane_ref[0], experts, values[0].shape[0])
    gates = gates_of(routes, nums_ref[...], plane_ref[0], experts)
    fill = -experts % 8
    if fill:
        gates = jnp.concatenate([gates, jnp.zeros((fill, gates.shape[1]), F32)], 0)
    gates = gates.T
    total = tokens_ref[...].astype(F32)
    for s, value in enumerate(values):
        picked = lax.dot_general(
            placings[s].astype(BF16),
            value[...],
            (((0,), (0,)), ((), ())),
            preferred_element_type=F32,
        )
        total = total + gates[:, s : s + 1] * picked
    out[...] = total.astype(BF16)


def on_device(tokens, cotangent, routes, gate_nums, gain, w_gate, w_up, w_down):
    devices = lax.axis_size("expert")
    experts = devices // HSPLIT
    rows_here, width = tokens.shape
    hidden_width = w_gate.shape[2]
    top_count = routes.shape[1]
    capacity = HSPLIT * (3 * top_count * rows_here // (2 * experts * HSPLIT))
    capacity = -(-capacity // 16) * 16
    shifts = max(1, experts // GROUPS)
    turns = sorted(range(experts), key=lambda s: (min(s, experts - s), s))
    groups = [turns[g : g + shifts] for g in range(0, experts, shifts)]
    height = shifts * capacity
    plane = (lax.axis_index("expert") // HSPLIT).astype(jnp.int32).reshape(1)
    routes, gate_nums, gain = routes.T, gate_nums.T, gain.reshape(1, -1)
    scalar = pl.BlockSpec(memory_space=pltpu.SMEM)
    anywhere = pl.BlockSpec(memory_space=pl.ANY)
    piece = jax.ShapeDtypeStruct((capacity, width), BF16)
    live = {}

    def swap(value, mask):
        return lax.ppermute(value, "expert", [(i, i ^ mask) for i in range(devices)])

    def turn(value, steps):
        to = [(i, (i + steps * HSPLIT) % devices) for i in range(devices)]
        return lax.ppermute(value, "expert", to)

    def sync():
        values = lax.optimization_barrier(tuple(live.values()))
        live.update(zip(list(live), values))

    def join(parts):
        return parts[0] if len(parts) == 1 else jnp.concatenate(parts, 0)

    flying, slow = {}, []

    def small(kernel, name, outs, *values):
        return call(
            kernel,
            8,
            name,
            out_shape=[jax.ShapeDtypeStruct((rows, width), BF16) for rows in outs],
            in_specs=whole(len(values)),
            out_specs=whole(len(outs)),
        )(*values)

    def land(*names, earlier=()):
        names = [n for name in names for n in flights_of(name)]
        quick = [name for name in names if name[0] == "c"]
        names = [name for name in names if name[0] != "c"]
        if not names:
            names, quick = quick, []
        joined = [name for name in names + quick if name[0] in "cy"]
        values = [flying.pop(name) for name in names]
        if not names:
            names, values = [("N", groups[-1][-1])], [live["N", groups[-1][-1]]]
        values = through(values, "land", LINK_WORK, earlier)
        landed = list(zip(names, values))
        if quick:
            crossed = tuple(flying.pop(name) for name in quick) + (values[0],)
            crossed = lax.optimization_barrier(crossed)[: len(quick)]
            landed += list(zip(quick, through(crossed, "land_core")))
        live.update(landed)
        sync()
        for name in joined:
            values = [live.pop(name)]
            if len(name) > 2:
                values = small(split_kernel, "split", [values[0].shape[0] // 2] * 2, *values)
            live.update({(name[0],) + item: value for item, value in zip(name[1:], values)})

    def flights_of(name):
        if name[0] != "z":
            return [name]
        kind, g = name[1]
        return [(kind, s) for s in groups[g] if s]

    def z(kind, g):
        for s in groups[g]:
            if s:
                flying[kind, s] = turn(live[kind, s], -s if kind == "R" else s)

    def y(*items):
        values = [to_row(*item) for item in items]
        if len(values) > 1:
            values = small(pair_kernel, "pair", [2 * height], *values)
        flying[("y",) + items] = swap(values[0], 2)

    def to_row(kind, g):
        if kind == "R":
            keep, crossed = live["keep", (g,)], live["c", "R", g]
            (value,) = small(fold_kernel, "fold", [height], keep, crossed)
        else:
            value = join([live.pop((kind, s)) for s in groups[g]])
            live["sent", kind, g] = value
        return value

    def c(*items):
        values = []
        for kind, g in items:
            if kind == "R":
                values.append(live.pop(("send", (g,))))
                continue
            here, came = live.pop(("sent", kind, g)), live.pop(("y", kind, g))
            (value,) = small(pair_kernel, "pair", [2 * height], here, came)
            live[kind, "own", (g,)] = value
            values.append(value)
        if len(values) > 1:
            values = small(pair_kernel, "pair", [4 * height], *values)
        flying[("c",) + items] = swap(values[0], 1)

    def total(g):
        values = live.pop(("keep", (g,))), live.pop(("c", "R", g)), live.pop(("y", "R", g))
        outs = small(total_kernel, "total", [capacity] * shifts, *values)
        live.update({("R", s): out for s, out in zip(groups[g], outs)})

    def ffn(*gs):
        pieces = [live.pop(("N", "own", gs)), live.pop(("c", "N", gs[0]))]
        half = jax.ShapeDtypeStruct(pieces[0].shape, BF16)
        rows = 2 * half.shape[0]
        live["turned", gs], live["keep", gs], live["send", gs] = call(
            functools.partial(ffn_kernel, len(pieces)),
            24,
            "ffn",
            out_shape=[jax.ShapeDtypeStruct((hidden_width, rows), BF16), half, half],
            in_specs=whole(len(pieces) + 3),
            out_specs=whole(3),
            scratch_shapes=[
                pltpu.VMEM((rows, width), BF16),
                pltpu.VMEM((rows, hidden_width), BF16),
            ],
        )(*pieces, live["w", 0], live["w", 1], live["w", 2])

    def in_hbm(*values):
        return [pltpu.with_memory_space_constraint(v, pltpu.HBM) for v in values]

    def send(kind, kernel, sources):
        values = call(
            functools.partial(kernel, experts),
            16,
            kernel.__name__[:-7],
            out_shape=[piece] * experts,
            in_specs=[scalar] + [anywhere] * 3,
            out_specs=whole(experts),
            scratch_shapes=[pltpu.VMEM(v.shape, v.dtype) for v in sources]
            + [pltpu.SemaphoreType.DMA((3,))],
        )(plane, *in_hbm(*sources))
        live.update({(kind, s): value for s, value in enumerate(values)})

    def send_grads(kind, g):
        if (kind, groups[-1][-1]) in live:
            return
        first = after(cotangent, live["N", groups[-1][-1]])
        send(kind, send_grads_kernel, (first, routes, gate_nums))

    def load():
        weight = jax.ShapeDtypeStruct((width, hidden_width), BF16)
        values = call(
            load_kernel,
            16,
            "load",
            out_shape=[weight, weight, jax.ShapeDtypeStruct((hidden_width, width), BF16)],
            in_specs=[anywhere] * 3,
            out_specs=whole(3),
            scratch_shapes=[pltpu.SemaphoreType.DMA((3,))],
        )(*in_hbm(after(w_gate, live["N", groups[-1][-1]]), w_up, w_down))
        live.update({("w", i): value for i, value in enumerate(values)})

    def grad_call(turned, pieces):
        columns = {}
        for i, gs in enumerate(turned):
            at = 0
            for half in ("own", "other"):
                for side in range(2):
                    for g in gs:
                        columns[half, side, g] = (i, at)
                        at += height
        plan = []
        for i, name in enumerate(pieces):
            half = "other" if name[0] == "c" else "own"
            g = name[-1] if half == "other" else name[-1][0]
            for side in range(2):
                where, at = columns[half, side, g]
                plan.append((where, at, len(turned) + i, side * height, height))
        rows = sum(step[-1] for step in plan)
        sides = [pltpu.VMEM((hidden_width, rows), BF16), pltpu.VMEM((rows, width), BF16)]
        values = [live["turned", gs] for gs in turned]
        values += [live[name] for name in pieces]
        return plan, sides, values

    def first_grad(turned, pieces):
        plan, sides, values = grad_call(turned, pieces)
        live["first"] = call(
            functools.partial(first_grad_kernel, plan),
            24,
            "first_grad",
            out_shape=jax.ShapeDtypeStruct((hidden_width, width), F32),
            in_specs=whole(len(values)),
            out_specs=whole(1)[0],
            scratch_shapes=sides,
        )(*values)

    def last_grad(turned, pieces):
        plan, sides, values = grad_call(turned, pieces)
        return call(
            functools.partial(last_grad_kernel, plan),
            24,
            "last_grad",
            out_shape=jax.ShapeDtypeStruct((1, hidden_width, width), BF16),
            in_specs=whole(1 + len(values)),
            out_specs=anywhere,
            scratch_shapes=[pltpu.VMEM((hidden_width, width), BF16)]
            + sides
            + [pltpu.SemaphoreType.DMA((hidden_width // TILE,))],
        )(live["first"], *values)

    steps = {
        "z": z,
        "y": y,
        "c": c,
        "ffn": lambda kind, g: ffn(g),
        "total": lambda kind, g: total(g),
        "load": lambda kind, g: load(),
        "send": send_grads,
        "grad": lambda kind, g: first_grad(
            [(0,), (1,), (2,)],
            [("C", "own", (i,)) for i in (0, 1, 2)] + [("c", "C", i) for i in (0, 1)],
        ),
    }
    def name_of(act):
        marks = act.lstrip("abcdefghijklmnopqrstuvwxyz")
        items = [(marks[i], int(marks[i + 1])) for i in range(0, len(marks), 2)]
        return (act[: len(act) - len(marks)],) + tuple(items)

    send("N", send_rows_kernel, (tokens, routes, gain))
    if shifts > 1:
        send_grads("C", 0)
        z("N", 0)
        z("C", 0)
        land(("z", ("N", 0)), ("z", ("C", 0)))
    sync()
    for starts, lands in PLAN:
        kernels = []
        for act in starts.split():
            name = name_of(act)
            steps[name[0]](*(name[1:] if name[0] in ("c", "y") else name[1]))
            if name[0] == "ffn":
                kernels.append(live["turned", name[1][1:]])
            if name[0] == "grad":
                kernels.append(live["first"])
        if lands is None:
            break
        if lands == "none":
            name = "C", groups[-1][-1]
            (live[name],) = through([live[name]], "step")
            sync()
            continue
        land(*map(name_of, lands.split()), earlier=kernels)
    live["c", "C", 3] = flying.pop(("c", ("C", 3)))
    grad_down = last_grad(
        [(2,), (3,)],
        [("C", "own", (3,)), ("c", "C", 2), ("c", "C", 3)],
    )
    mixed = call(
        functools.partial(combine_kernel, experts),
        16,
        "combine",
        out_shape=jax.ShapeDtypeStruct(tokens.shape, BF16),
        in_specs=[scalar] + whole(3 + experts),
        out_specs=whole(1)[0],
    )(plane, tokens, routes, gate_nums, *[live["R", s] for s in range(experts)])
    return (mixed, grad_down)


def solution(mesh):
    placed = (
        P(("group", "expert"), None),
        P(("group", "expert"), None),
        P(("group", "expert"), None),
        P(("group", "expert"), None),
        P(),
        P("expert", None, None),
        P("expert", None, None),
        P("expert", None, None),
    )
    return jax.shard_map(
        on_device,
        mesh=mesh,
        in_specs=placed,
        out_specs=(P(("group", "expert"), None), P(("group", "expert"), None, None)),
        check_vma=False,
    )
```

```python
import functools

import jax
import jax.numpy as jnp
from jax import lax
from jax.experimental import pallas as pl
from jax.experimental.pallas import tpu as pltpu
from jax.sharding import PartitionSpec as P

HSPLIT = 4
GROUPS = 4
PLAN = (
    ("yN0 zN2 zN1 sendC0 loadW0", ""),
    ("yC0 zN3", "zN2 zN1 yN0"),
    ("cN0 yN1", "yC0 cN0"),
    ("ffnN0 yN2", "yN1 zN3"),
    ("cR0N1 yN3 zC2 zC1", "yN2 cR0N1"),
    ("ffnN1 cN2 yR0", "yN3 zC2 zC1 cN2"),
    ("cR1N3 ffnN2 yC1 zC3", "yR0 cR1N3"),
    ("cR2 ffnN3 cR3 yR1 totalR0", "yC1 zC3 cR2"),
    ("yR2", "yR1 cR3"),
    ("totalR1 zR1 yR3 cC0", "yR2 cC0"),
    ("totalR2 zR2 yC2", "zR1 yR3"),
    ("totalR3 zR3 yC3 cC1", "yC2 zR2 cC1"),
    ("cC2 gradC0", "yC3 zR3 cC2"),
    ("cC3", None),
)
TILE = 256
LINK_WORK = 10 << 30
F32 = jnp.float32
BF16 = jnp.bfloat16


def after(value, *earlier):
    return lax.optimization_barrier((value,) + earlier)[0]


def whole(count):
    return [pl.BlockSpec(memory_space=pltpu.VMEM)] * count


def call(kernel, mib, name, moved=0, **keywords):
    return pl.pallas_call(
        kernel,
        compiler_params=pltpu.CompilerParams(vmem_limit_bytes=mib << 20),
        cost_estimate=pl.CostEstimate(flops=moved, bytes_accessed=0, transcendentals=0),
        name=name,
        **keywords,
    )


def experts_of(plane, experts, rows):
    ahead = lax.broadcasted_iota(jnp.int32, (experts, rows), 0) + plane
    return jnp.where(ahead >= experts, ahead - experts, ahead)


def placing_of(routes, plane, experts, capacity):
    rows = routes.shape[1]
    expert = experts_of(plane, experts, rows)
    member = jnp.zeros((experts, rows), jnp.bool_)
    for k in range(routes.shape[0]):
        member = member | (routes[k : k + 1, :] == expert)
    first = lax.broadcasted_iota(jnp.int32, (rows, rows), 0)
    second = lax.broadcasted_iota(jnp.int32, (rows, rows), 1)
    upto = (first <= second).astype(F32).astype(BF16)
    ones = member.astype(F32)
    count = jnp.dot(ones.astype(BF16), upto, preferred_element_type=F32)
    place = (ones * count).astype(jnp.int32) - 1
    slots = lax.broadcasted_iota(jnp.int32, (capacity, rows), 0)
    return [(slots == place[s : s + 1, :]).astype(F32) for s in range(experts)]


def gates_of(routes, numbers, plane, experts):
    expert = experts_of(plane, experts, routes.shape[1])
    numerators = numbers.astype(F32)
    gates = numerators / jnp.sum(numerators, 0, keepdims=True)
    gate = jnp.zeros(expert.shape, F32)
    for k in range(routes.shape[0]):
        gate = gate + jnp.where(routes[k : k + 1, :] == expert, gates[k : k + 1, :], 0.0)
    return gate


def fetch(semaphores, *pairs):
    copies = [
        pltpu.make_async_copy(source, target, semaphores.at[i])
        for i, (source, target) in enumerate(pairs)
    ]
    for copy in copies:
        copy.start()
    return copies


def send_rows_kernel(experts, plane_ref, *refs):
    sources, outs, targets, semaphores = refs[:3], refs[3 : 3 + experts], refs[-4:-1], refs[-1]
    tokens_ref, routes_ref, gain_ref = targets
    copies = fetch(semaphores, *zip(sources, targets))
    copies[1].wait()
    placings = placing_of(routes_ref[...], plane_ref[0], experts, outs[0].shape[0])
    copies[2].wait()
    copies[0].wait()
    frames = tokens_ref[...].astype(F32)
    inverse = lax.rsqrt(jnp.mean(frames * frames, -1, keepdims=True) + 1e-06)
    normed = (frames * inverse * gain_ref[...]).astype(BF16)
    for out, placing in zip(outs, placings):
        out[...] = jnp.dot(placing.astype(BF16), normed, preferred_element_type=F32).astype(BF16)


def send_grads_kernel(experts, plane_ref, *refs):
    sources, outs, targets, semaphores = refs[:3], refs[3 : 3 + experts], refs[-4:-1], refs[-1]
    cot_ref, routes_ref, nums_ref = targets
    copies = fetch(semaphores, *zip(sources, targets))
    copies[1].wait()
    copies[2].wait()
    routes = routes_ref[...]
    placings = placing_of(routes, plane_ref[0], experts, outs[0].shape[0])
    gates = gates_of(routes, nums_ref[...], plane_ref[0], experts)
    copies[0].wait()
    cot = cot_ref[...]
    for s, (out, placing) in enumerate(zip(outs, placings)):
        picked = jnp.dot(placing.astype(BF16), cot, preferred_element_type=F32)
        gate = jnp.sum(placing * gates[s : s + 1, :], -1, keepdims=True)
        out[...] = (gate * picked).astype(BF16)


def load_kernel(*refs):
    sources, outs, semaphores = refs[:3], refs[3:6], refs[6]
    copies = fetch(semaphores, *[(s.at[0], o) for s, o in zip(sources, outs)])
    for copy in copies:
        copy.wait()


def pair_kernel(first_ref, second_ref, out_ref):
    rows = first_ref.shape[0]
    out_ref[:rows, :] = first_ref[...]
    out_ref[rows:, :] = second_ref[...]


def split_kernel(both_ref, first_ref, second_ref):
    rows = first_ref.shape[0]
    first_ref[...] = both_ref[:rows, :]
    second_ref[...] = both_ref[rows:, :]


def fold_kernel(keep_ref, crossed_ref, out_ref):
    rows = out_ref.shape[0]
    total = keep_ref[rows:, :].astype(F32) + crossed_ref[rows:, :].astype(F32)
    out_ref[...] = total.astype(BF16)


def total_kernel(keep_ref, crossed_ref, came_ref, *outs):
    at = 0
    for out in outs:
        part = slice(at, at + out.shape[0])
        total = keep_ref[part, :].astype(F32) + crossed_ref[part, :].astype(F32)
        out[...] = (total + came_ref[part, :].astype(F32)).astype(BF16)
        at += out.shape[0]


def nothing(*refs):
    pass


def through(values, name, moved=0, earlier=()):
    count = len(values)
    return call(
        nothing,
        4,
        name,
        moved,
        out_shape=[jax.ShapeDtypeStruct(v.shape, v.dtype) for v in values],
        in_specs=whole(count) + [pl.BlockSpec(memory_space=pl.ANY)] * len(earlier),
        out_specs=whole(count),
        input_output_aliases={i: i for i in range(count)},
    )(*values, *earlier)


def ffn_kernel(count, *refs):
    pieces, refs = refs[:count], refs[count:]
    gate_ref, up_ref, down_ref, turned_ref, keep_ref, send_ref, rows_ref, hidden_ref = refs
    at = 0
    for piece in pieces:
        rows_ref[at : at + piece.shape[0], :] = piece[...]
        at += piece.shape[0]
    rows = rows_ref[...]
    half = keep_ref.shape[0]
    for j in range(gate_ref.shape[1] // TILE):
        columns = slice(j * TILE, (j + 1) * TILE)
        pre_gate = jnp.dot(rows, gate_ref[:, columns], preferred_element_type=F32)
        pre_up = jnp.dot(rows, up_ref[:, columns], preferred_element_type=F32)
        hidden = pre_gate * lax.logistic(pre_gate) * pre_up
        hidden_ref[:, columns] = hidden.astype(BF16)
        turned_ref[columns, :] = hidden.T.astype(BF16)
    for j in range(down_ref.shape[1] // TILE):
        columns = slice(j * TILE, (j + 1) * TILE)
        value = jnp.dot(
            hidden_ref[...], down_ref[:, columns], preferred_element_type=F32
        ).astype(BF16)
        keep_ref[:, columns] = value[:half]
        send_ref[:, columns] = value[half:]


def gather_grad(plan, refs, hidden_ref, cot_ref):
    at = 0
    for turned, column, piece, row, count in plan:
        hidden_ref[:, at : at + count] = refs[turned][:, column : column + count]
        cot_ref[at : at + count, :] = refs[piece][row : row + count, :]
        at += count


def first_grad_kernel(plan, *refs):
    out_ref, hidden_ref, cot_ref = refs[-3:]
    gather_grad(plan, refs, hidden_ref, cot_ref)
    for j in range(out_ref.shape[0] // TILE):
        part = slice(j * TILE, (j + 1) * TILE)
        out_ref[part, :] = jnp.dot(
            hidden_ref[part, :], cot_ref[...], preferred_element_type=F32
        )


def last_grad_kernel(plan, first_ref, *refs):
    out_hbm, out_ref, hidden_ref, cot_ref, semaphores = refs[-5:]
    gather_grad(plan, refs, hidden_ref, cot_ref)
    copies = []
    for j in range(first_ref.shape[0] // TILE):
        part = slice(j * TILE, (j + 1) * TILE)
        total = jnp.dot(hidden_ref[part, :], cot_ref[...], preferred_element_type=F32)
        out_ref[part, :] = (first_ref[part, :] + total).astype(BF16)
        copies.append(
            pltpu.make_async_copy(out_ref.at[part, :], out_hbm.at[0, part, :], semaphores.at[j])
        )
        copies[-1].start()
    for copy in copies:
        copy.wait()


def combine_kernel(experts, plane_ref, tokens_ref, routes_ref, nums_ref, *refs):
    values, out = refs[:-1], refs[-1]
    routes = routes_ref[...]
    placings = placing_of(routes, plane_ref[0], experts, values[0].shape[0])
    gates = gates_of(routes, nums_ref[...], plane_ref[0], experts)
    fill = -experts % 8
    if fill:
        gates = jnp.concatenate([gates, jnp.zeros((fill, gates.shape[1]), F32)], 0)
    gates = gates.T
    total = tokens_ref[...].astype(F32)
    for s, value in enumerate(values):
        picked = lax.dot_general(
            placings[s].astype(BF16),
            value[...],
            (((0,), (0,)), ((), ())),
            preferred_element_type=F32,
        )
        total = total + gates[:, s : s + 1] * picked
    out[...] = total.astype(BF16)


def on_device(tokens, cotangent, routes, gate_nums, gain, w_gate, w_up, w_down):
    devices = lax.axis_size("expert")
    experts = devices // HSPLIT
    rows_here, width = tokens.shape
    hidden_width = w_gate.shape[2]
    top_count = routes.shape[1]
    capacity = HSPLIT * (3 * top_count * rows_here // (2 * experts * HSPLIT))
    capacity = -(-capacity // 16) * 16
    shifts = max(1, experts // GROUPS)
    turns = sorted(range(experts), key=lambda s: (min(s, experts - s), s))
    groups = [turns[g : g + shifts] for g in range(0, experts, shifts)]
    height = shifts * capacity
    plane = (lax.axis_index("expert") // HSPLIT).astype(jnp.int32).reshape(1)
    routes, gate_nums, gain = routes.T, gate_nums.T, gain.reshape(1, -1)
    scalar = pl.BlockSpec(memory_space=pltpu.SMEM)
    anywhere = pl.BlockSpec(memory_space=pl.ANY)
    piece = jax.ShapeDtypeStruct((capacity, width), BF16)
    live = {}

    def swap(value, mask):
        return lax.ppermute(value, "expert", [(i, i ^ mask) for i in range(devices)])

    def turn(value, steps):
        to = [(i, (i + steps * HSPLIT) % devices) for i in range(devices)]
        return lax.ppermute(value, "expert", to)

    def sync():
        values = lax.optimization_barrier(tuple(live.values()))
        live.update(zip(list(live), values))

    def join(parts):
        return parts[0] if len(parts) == 1 else jnp.concatenate(parts, 0)

    flying, slow = {}, []

    def small(kernel, name, outs, *values):
        return call(
            kernel,
            8,
            name,
            out_shape=[jax.ShapeDtypeStruct((rows, width), BF16) for rows in outs],
            in_specs=whole(len(values)),
            out_specs=whole(len(outs)),
        )(*values)

    def land(*names, earlier=()):
        names = [n for name in names for n in flights_of(name)]
        quick = [name for name in names if name[0] == "c"]
        names = [name for name in names if name[0] != "c"]
        if not names:
            names, quick = quick, []
        joined = [name for name in names + quick if name[0] in "cy"]
        values = [flying.pop(name) for name in names]
        if not names:
            names, values = [("N", groups[-1][-1])], [live["N", groups[-1][-1]]]
        values = through(values, "land", LINK_WORK, earlier)
        landed = list(zip(names, values))
        if quick:
            crossed = tuple(flying.pop(name) for name in quick) + (values[0],)
            crossed = lax.optimization_barrier(crossed)[: len(quick)]
            landed += list(zip(quick, through(crossed, "land_core")))
        live.update(landed)
        sync()
        for name in joined:
            values = [live.pop(name)]
            if len(name) > 2:
                values = small(split_kernel, "split", [values[0].shape[0] // 2] * 2, *values)
            live.update({(name[0],) + item: value for item, value in zip(name[1:], values)})

    def flights_of(name):
        if name[0] != "z":
            return [name]
        kind, g = name[1]
        return [(kind, s) for s in groups[g] if s]

    def z(kind, g):
        for s in groups[g]:
            if s:
                flying[kind, s] = turn(live[kind, s], -s if kind == "R" else s)

    def y(*items):
        values = [to_row(*item) for item in items]
        if len(values) > 1:
            values = small(pair_kernel, "pair", [2 * height], *values)
        flying[("y",) + items] = swap(values[0], 2)

    def to_row(kind, g):
        if kind == "R":
            keep, crossed = live["keep", (g,)], live["c", "R", g]
            (value,) = small(fold_kernel, "fold", [height], keep, crossed)
        else:
            value = join([live.pop((kind, s)) for s in groups[g]])
            live["sent", kind, g] = value
        return value

    def c(*items):
        values = []
        for kind, g in items:
            if kind == "R":
                values.append(live.pop(("send", (g,))))
                continue
            here, came = live.pop(("sent", kind, g)), live.pop(("y", kind, g))
            (value,) = small(pair_kernel, "pair", [2 * height], here, came)
            live[kind, "own", (g,)] = value
            values.append(value)
        if len(values) > 1:
            values = small(pair_kernel, "pair", [4 * height], *values)
        flying[("c",) + items] = swap(values[0], 1)

    def total(g):
        values = live.pop(("keep", (g,))), live.pop(("c", "R", g)), live.pop(("y", "R", g))
        outs = small(total_kernel, "total", [capacity] * shifts, *values)
        live.update({("R", s): out for s, out in zip(groups[g], outs)})

    def ffn(*gs):
        pieces = [live.pop(("N", "own", gs)), live.pop(("c", "N", gs[0]))]
        half = jax.ShapeDtypeStruct(pieces[0].shape, BF16)
        rows = 2 * half.shape[0]
        live["turned", gs], live["keep", gs], live["send", gs] = call(
            functools.partial(ffn_kernel, len(pieces)),
            24,
            "ffn",
            out_shape=[jax.ShapeDtypeStruct((hidden_width, rows), BF16), half, half],
            in_specs=whole(len(pieces) + 3),
            out_specs=whole(3),
            scratch_shapes=[
                pltpu.VMEM((rows, width), BF16),
                pltpu.VMEM((rows, hidden_width), BF16),
            ],
        )(*pieces, live["w", 0], live["w", 1], live["w", 2])

    def in_hbm(*values):
        return [pltpu.with_memory_space_constraint(v, pltpu.HBM) for v in values]

    def send(kind, kernel, sources):
        values = call(
            functools.partial(kernel, experts),
            16,
            kernel.__name__[:-7],
            out_shape=[piece] * experts,
            in_specs=[scalar] + [anywhere] * 3,
            out_specs=whole(experts),
            scratch_shapes=[pltpu.VMEM(v.shape, v.dtype) for v in sources]
            + [pltpu.SemaphoreType.DMA((3,))],
        )(plane, *in_hbm(*sources))
        live.update({(kind, s): value for s, value in enumerate(values)})

    def send_grads(kind, g):
        if (kind, groups[-1][-1]) in live:
            return
        first = after(cotangent, live["N", groups[-1][-1]])
        send(kind, send_grads_kernel, (first, routes, gate_nums))

    def load():
        weight = jax.ShapeDtypeStruct((width, hidden_width), BF16)
        values = call(
            load_kernel,
            16,
            "load",
            out_shape=[weight, weight, jax.ShapeDtypeStruct((hidden_width, width), BF16)],
            in_specs=[anywhere] * 3,
            out_specs=whole(3),
            scratch_shapes=[pltpu.SemaphoreType.DMA((3,))],
        )(*in_hbm(after(w_gate, live["N", groups[-1][-1]]), w_up, w_down))
        live.update({("w", i): value for i, value in enumerate(values)})

    def grad_call(turned, pieces):
        columns = {}
        for i, gs in enumerate(turned):
            at = 0
            for half in ("own", "other"):
                for side in range(2):
                    for g in gs:
                        columns[half, side, g] = (i, at)
                        at += height
        plan = []
        for i, name in enumerate(pieces):
            half = "other" if name[0] == "c" else "own"
            g = name[-1] if half == "other" else name[-1][0]
            for side in range(2):
                where, at = columns[half, side, g]
                plan.append((where, at, len(turned) + i, side * height, height))
        rows = sum(step[-1] for step in plan)
        sides = [pltpu.VMEM((hidden_width, rows), BF16), pltpu.VMEM((rows, width), BF16)]
        values = [live["turned", gs] for gs in turned]
        values += [live[name] for name in pieces]
        return plan, sides, values

    def first_grad(turned, pieces):
        plan, sides, values = grad_call(turned, pieces)
        live["first"] = call(
            functools.partial(first_grad_kernel, plan),
            24,
            "first_grad",
            out_shape=jax.ShapeDtypeStruct((hidden_width, width), F32),
            in_specs=whole(len(values)),
            out_specs=whole(1)[0],
            scratch_shapes=sides,
        )(*values)

    def last_grad(turned, pieces):
        plan, sides, values = grad_call(turned, pieces)
        return call(
            functools.partial(last_grad_kernel, plan),
            24,
            "last_grad",
            out_shape=jax.ShapeDtypeStruct((1, hidden_width, width), BF16),
            in_specs=whole(1 + len(values)),
            out_specs=anywhere,
            scratch_shapes=[pltpu.VMEM((hidden_width, width), BF16)]
            + sides
            + [pltpu.SemaphoreType.DMA((hidden_width // TILE,))],
        )(live["first"], *values)

    steps = {
        "z": z,
        "y": y,
        "c": c,
        "ffn": lambda kind, g: ffn(g),
        "total": lambda kind, g: total(g),
        "load": lambda kind, g: load(),
        "send": send_grads,
        "grad": lambda kind, g: first_grad(
            [(0,), (1,), (2,)],
            [("C", "own", (i,)) for i in (0, 1, 2)] + [("c", "C", i) for i in (0, 1)],
        ),
    }
    def name_of(act):
        marks = act.lstrip("abcdefghijklmnopqrstuvwxyz")
        items = [(marks[i], int(marks[i + 1])) for i in range(0, len(marks), 2)]
        return (act[: len(act) - len(marks)],) + tuple(items)

    send("N", send_rows_kernel, (tokens, routes, gain))
    if shifts > 1:
        send_grads("C", 0)
        z("N", 0)
        z("C", 0)
        land(("z", ("N", 0)), ("z", ("C", 0)))
    sync()
    for starts, lands in PLAN:
        kernels = []
        for act in starts.split():
            name = name_of(act)
            steps[name[0]](*(name[1:] if name[0] in ("c", "y") else name[1]))
            if name[0] == "ffn":
                kernels.append(live["turned", name[1][1:]])
            if name[0] == "grad":
                kernels.append(live["first"])
        if lands is None:
            break
        if lands == "none":
            name = "C", groups[-1][-1]
            (live[name],) = through([live[name]], "step")
            sync()
            continue
        land(*map(name_of, lands.split()), earlier=kernels)
    live["c", "C", 3] = flying.pop(("c", ("C", 3)))
    grad_down = last_grad(
        [(2,), (3,)],
        [("C", "own", (3,)), ("c", "C", 2), ("c", "C", 3)],
    )
    mixed = call(
        functools.partial(combine_kernel, experts),
        16,
        "combine",
        out_shape=jax.ShapeDtypeStruct(tokens.shape, BF16),
        in_specs=[scalar] + whole(3 + experts),
        out_specs=whole(1)[0],
    )(plane, tokens, routes, gate_nums, *[live["R", s] for s in range(experts)])
    return (mixed, grad_down)


def solution(mesh):
    placed = (
        P(("group", "expert"), None),
        P(("group", "expert"), None),
        P(("group", "expert"), None),
        P(("group", "expert"), None),
        P(),
        P("expert", None, None),
        P("expert", None, None),
        P("expert", None, None),
    )
    return jax.shard_map(
        on_device,
        mesh=mesh,
        in_specs=placed,
        out_specs=(P(("group", "expert"), None), P(("group", "expert"), None, None)),
        check_vma=False,
    )
```
